32 devices in a mesh: dp: 8 (over z, y), head: 4 (over x, core).
Axes of the slice: x: 2, y: 2, z: 4, core: 2. Of those that a mesh axis runs over, the one named last changes fastest.
Arguments:
- tokens: bfloat16 [16384, 512], P(('dp', 'head'))
- cotangent: bfloat16 [16384, 512], P(('dp', 'head'))
- seq_start: int32 [16384], P('dp'), may hold values from 0 to 2047, as said below
- time_bucket: int32 [16384], P('dp'), may hold values from 0 to 127
- proj_weight: float32 [512, 4, 512], P('dp', None, 'head'), may hold values from -0.25 to 0.25
- out_weight: float32 [512, 512], P('head', 'dp')
- small_params: float32 [8832], replicated, may hold values from -3 to 3
- proj_mean: float32 [512, 4, 512], P('dp', None, 'head'), may hold values from -0.0014648438 to 0.0014648438
- proj_square: float32 [512, 4, 512], P('dp', None, 'head'), may hold values from 7.5783296e-10 to 3.0313319e-09
- out_mean: float32 [512, 512], P('head', 'dp'), may hold values from -0.0014648438 to 0.0014648438
- out_square: float32 [512, 512], P('head', 'dp'), may hold values from 7.5783296e-10 to 3.0313319e-09
- small_mean: float32 [8832], replicated, may hold values from -0.00390625 to 0.00390625
- small_square: float32 [8832], replicated, may hold values from 6.8204966e-09 to 2.7281986e-08
Outputs:
- mixed: bfloat16 [16384, 512], P(('dp', 'head'))
- input_grad: float32 [16384, 512], P(('dp', 'head'))
- grad_proj: float32 [512, 4, 512], P('dp', None, 'head')
- grad_out: float32 [512, 512], P('head', 'dp')
- grad_small: float32 [8832], replicated
- grad_norm: float32 [], replicated
- new_proj: float32 [512, 4, 512], P('dp', None, 'head')
- mean_proj: float32 [512, 4, 512], P('dp', None, 'head')
- square_proj: float32 [512, 4, 512], P('dp', None, 'head')
- new_out: float32 [512, 512], P('head', 'dp')
- mean_out: float32 [512, 512], P('head', 'dp')
- square_out: float32 [512, 512], P('head', 'dp')
- new_small: float32 [8832], replicated
- mean_small: float32 [8832], replicated
- square_small: float32 [8832], replicated
The draws below stay inside these ranges and needn't reach their ends.
Inputs may be any that keep to these rules, and one draw needn't show every extreme that they name: `seq_start`: within each aligned group of 2048 tokens, the group-local index of the first token of the token's sequence; sequences are contiguous runs and the value equals a token's own index where its sequence begins; in every group one sequence begins within the first 512 tokens and ends within the last 512, the last token of the group is a sequence of its own, the others hold at most 256 tokens.
All inputs are finite; a program needn't handle non-finite values.
Results may differ from the reference program's by a relative error of at most 0.0089.
Values may be sent and summed in bfloat16 or wider, within the bound.
No kernel may reach another device: no remote copies, remote signals or barrier semaphores. Data moves between devices by JAX's collectives and lax.ppermute only.
A program may use at most 128 MiB of HBM per device.

```python
import math
import jax
import jax.numpy as jnp
from jax import lax

D = 512
HEADS = 8
HEAD_DIM = 64
HD = 512
TOK_DEV = 512
SESSION = 256
POS = 8192
NTB = 128
STEP = 10
GROUP = 2048
TOKENS = 16384
PARAMS = 1319552


def draw_tokens(key, part):
    key = jax.random.fold_in(key, 1)
    base = jax.random.normal(key, (TOKENS, D), jnp.float32)
    top = 3.0
    ramp = 1.0 + (top - 1.0) * jnp.arange(D, dtype=jnp.float32) / (D - 1)
    return (base * ramp[None, :]).astype(jnp.bfloat16)


def draw_cotangent(key, part):
    key = jax.random.fold_in(key, 2)
    base = jax.random.normal(key, (TOKENS, D), jnp.float32)
    top = 3.0
    ramp = 1.0 + (top - 1.0) * jnp.arange(D, dtype=jnp.float32) / (D - 1)
    return (base * ramp[None, :]).astype(jnp.bfloat16)


def draw_out_weight(key, part):
    key = jax.random.fold_in(key, 3)
    base = jax.random.normal(key, (HD, D), jnp.float32)
    top = 3.0
    ramp = 1.0 + (top - 1.0) * jnp.arange(HD, dtype=jnp.float32) / (HD - 1)
    return base * ramp[:, None] * HD ** (-0.5)


def draw_seq_start(key, part):
    key = jax.random.fold_in(key, 4)
    key_lead, key_tail = jax.random.split(key)
    groups = TOKENS // GROUP
    lead = jax.random.randint(key_lead, (groups, 1), 1, TOK_DEV)
    tail = jax.random.randint(key_tail, (groups, 1), 1, TOK_DEV)
    index = jnp.arange(GROUP, dtype=jnp.int32)[None, :]
    cut = GROUP - tail
    lead_start = index // SESSION * SESSION
    tail_start = cut + (index - cut) // SESSION * SESSION
    start = jnp.where(index < lead, lead_start, jnp.where(index < cut, lead, tail_start))
    start = jnp.where(index == GROUP - 1, GROUP - 1, start)
    return start.reshape(TOKENS).astype(jnp.int32)


def place_ends(values, own_key, low, high):
    shape = values.shape
    index_at = [jax.random.randint(jax.random.fold_in(own_key, axis), (), 0, shape[axis]) for axis in range(len(shape))]
    values = values.at[tuple(index_at)].set(low)
    longest = shape.index(max(shape))
    index_at[longest] = (index_at[longest] + 1) % shape[longest]
    return values.at[tuple(index_at)].set(high)


def shard_levels(rng, dims, cuts, least, high):
    loudness = 1.0
    for axis_at, shards_of in cuts:
        heights = jax.random.uniform(jax.random.fold_in(jax.random.fold_in(rng, 6), axis_at), (shards_of,), jnp.float32, least / len(cuts), high / len(cuts))
        loudness = loudness * jnp.repeat(jnp.exp(heights), dims[axis_at] // shards_of).reshape((-1,) + (1,) * (len(dims) - 1 - axis_at))
    return loudness


def gaussian(rng, shape, width, limit, cuts=(), kind=jnp.bfloat16):
    loudness = shard_levels(rng, shape, cuts, -0.22, 0.18) if cuts else 1.0
    values = jax.random.normal(rng, shape, jnp.float32) * width * loudness
    return jnp.minimum(jnp.maximum(values, -limit), limit).astype(kind)


def setup_inputs(seed: int = 0) -> dict:
    splits = jax.random.split(jax.random.key(seed), 14)
    return {
        "tokens": draw_tokens(jax.random.fold_in(splits[13], 71), 0),
        "cotangent": draw_cotangent(jax.random.fold_in(splits[13], 71), 0),
        "seq_start": draw_seq_start(jax.random.fold_in(splits[13], 71), 0),
        "time_bucket": place_ends(jax.random.randint(splits[3], (TOKENS,), 0, NTB), jax.random.fold_in(splits[3], 1), 0, NTB - 1).astype(jnp.int32),
        "proj_weight": gaussian(splits[4], (D, 4, HD), D ** -0.5, 0.25, ((0, 8), (2, 4)), jnp.float32),
        "out_weight": draw_out_weight(jax.random.fold_in(splits[13], 71), 0),
        "small_params": gaussian(splits[6], (D + POS + NTB,), 0.5, 3.0, (), jnp.float32),
        "proj_mean": gaussian(splits[7], (D, 4, HD), (0.11 / PARAMS ** 0.5), 0.0014648438, ((0, 8), (2, 4)), jnp.float32),
        "proj_square": jnp.clip(jnp.exp(math.log(3.0313318521990595e-09) - 1.3862944 * jax.random.uniform(splits[8], (D, 4, HD), jnp.float32) ** shard_levels(splits[8], (D, 4, HD), ((0, 8), (2, 4)), -0.2, 0.2)), 7.578329630497649e-10, 3.0313318521990595e-09),
        "out_mean": gaussian(splits[9], (HD, D), (0.11 / PARAMS ** 0.5), 0.0014648438, ((0, 4), (1, 8)), jnp.float32),
        "out_square": jnp.clip(jnp.exp(math.log(3.0313318521990595e-09) - 1.3862944 * jax.random.uniform(splits[10], (HD, D), jnp.float32) ** shard_levels(splits[10], (HD, D), ((0, 4), (1, 8)), -0.2, 0.2)), 7.578329630497649e-10, 3.0313318521990595e-09),
        "small_mean": gaussian(splits[11], (D + POS + NTB,), (0.33 / PARAMS ** 0.5), 0.00390625, (), jnp.float32),
        "small_square": jnp.clip(jnp.exp(jax.random.uniform(splits[12], (D + POS + NTB,), jnp.float32, math.log(6.820496611936733e-09), math.log(2.728198644774693e-08))), 6.820496611936733e-09, 2.728198644774693e-08),
    }


norm_epsilon = 1e-06
adam_epsilon = 1e-08
beta_one = 0.9
beta_two = 0.999
clip_norm = 1.0
rate_matrix = 0.05
rate_small = 0.3
decay_matrix = 0.1
HIGH = lax.Precision.HIGHEST

@jax.custom_vjp
def low(v):
    return lax.optimization_barrier(v.astype(jnp.bfloat16)).astype(jnp.float32)

@jax.custom_vjp
def low_back(v):
    return v

def low_keep(v):
    return (low(v), None)

def low_pass(kept, grad):
    return (grad,)

def back_keep(v):
    return (v, None)

def back_low(kept, grad):
    return (low(grad),)
low.defvjp(low_keep, low_pass)
low_back.defvjp(back_keep, back_low)

def block_output(query, keys, values, row_seq, col_seq, row_time, col_time, pos_table, time_table, row_index, col_index):
    product = jnp.dot(query, keys.T, precision=HIGH) * (1.0 / math.sqrt(HEAD_DIM))
    pos_index = jnp.clip(row_index[:, None] - col_index[None, :], 0, POS - 1)
    time_index = jnp.abs(row_time[:, None] - col_time[None, :])
    scores = low_back(product + pos_table[pos_index] + time_table[time_index])
    mask = ((row_seq[:, None] == col_seq[None, :]) & (col_index[None, :] <= row_index[:, None])).astype(jnp.float32)
    weights = low(jax.nn.silu(scores) * mask)
    return jnp.dot(weights, values, precision=HIGH)

def head_output(query, keys, values, starts, times, pos_table, time_table):
    rows = query.shape[0]
    step_rows = math.gcd(rows, 1024)
    pieces = []
    for first in range(0, rows, step_rows):
        last = first + step_rows
        pieces.append(jax.checkpoint(block_output)(query[first:last], keys[:last], values[:last], starts[first:last], starts[:last], times[first:last], times[:last], pos_table, time_table, jnp.arange(first, last, dtype=jnp.int32), jnp.arange(0, last, dtype=jnp.int32)))
    return jnp.concatenate(pieces, axis=0)

def forward(inputs, proj_weight, out_weight, small_params, seq_start, time_bucket):
    centred = inputs - lax.optimization_barrier(jnp.mean(inputs, -1, keepdims=True))
    normed = low(centred * lax.rsqrt(lax.optimization_barrier(jnp.mean(centred * centred, -1, keepdims=True)) + norm_epsilon))
    projected = low_back(jnp.einsum('td,dch->tch', normed, low(proj_weight), precision=HIGH))
    active = jax.nn.silu(projected)
    gating = active[:, 0]
    values = low(active[:, 1])
    queries = low(active[:, 2])
    keys_all = low(active[:, 3])
    groups = inputs.shape[0] // GROUP
    bias_out = small_params[:D]
    pos_table = small_params[D:D + POS]
    time_table = small_params[D + POS:]

    def by_heads(array):
        return array.reshape(groups, GROUP, HEADS, HEAD_DIM).transpose(0, 2, 1, 3)

    def per_group(items):
        group_q, group_k, group_v, starts, times = items

        def per_head(trio):
            return head_output(trio[0], trio[1], trio[2], starts, times, pos_table, time_table)
        return lax.map(per_head, (group_q, group_k, group_v))
    attn = lax.map(per_group, (by_heads(queries), by_heads(keys_all), by_heads(values), seq_start.reshape(groups, GROUP), time_bucket.reshape(groups, GROUP)))
    attn = low_back(attn.transpose(0, 2, 1, 3).reshape(inputs.shape[0], HD))
    centre_mid = attn - lax.optimization_barrier(jnp.mean(attn, -1, keepdims=True))
    attn_normed = centre_mid * lax.rsqrt(lax.optimization_barrier(jnp.mean(centre_mid * centre_mid, -1, keepdims=True)) + norm_epsilon)
    gated = low(attn_normed * gating)
    return jnp.dot(gated, low(out_weight), precision=HIGH) + bias_out + inputs

def adam_step(weight, grad, first, second, factor, rate, decay):
    clipped = grad * factor
    first_new = beta_one * first + (1.0 - beta_one) * clipped
    second_new = beta_two * second + (1.0 - beta_two) * clipped * clipped
    update = first_new / (1.0 - beta_one ** STEP) / (jnp.sqrt(second_new / (1.0 - beta_two ** STEP)) + adam_epsilon)
    return (weight - rate * (update + decay * weight), first_new, second_new)

def reference(tokens, cotangent, seq_start, time_bucket, proj_weight, out_weight, small_params, proj_mean, proj_square, out_mean, out_square, small_mean, small_square):

    def layer(inputs, weight_a, weight_b, params):
        return forward(inputs, weight_a, weight_b, params, seq_start, time_bucket)
    result, pullback = jax.vjp(layer, tokens.astype(jnp.float32), proj_weight, out_weight, small_params)
    input_grad, grad_proj, grad_out, grad_small = pullback(cotangent.astype(jnp.float32))
    total = jnp.sum(grad_proj * grad_proj) + jnp.sum(grad_out * grad_out) + jnp.sum(grad_small * grad_small)
    grad_norm = jnp.sqrt(total)
    factor = jnp.minimum(1.0, clip_norm / (grad_norm + 1e-06))
    new_proj, mean_proj, square_proj = adam_step(proj_weight, grad_proj, proj_mean, proj_square, factor, rate_matrix, decay_matrix)
    new_out, mean_out, square_out = adam_step(out_weight, grad_out, out_mean, out_square, factor, rate_matrix, decay_matrix)
    new_small, mean_small, square_small = adam_step(small_params, grad_small, small_mean, small_square, factor, rate_small, 0.0)
    return (result.astype(jnp.bfloat16), input_grad, grad_proj, grad_out, grad_small, grad_norm, new_proj, mean_proj, square_proj, new_out, mean_out, square_out, new_small, mean_small, square_small)
```

```python
import functools
import math

import jax
import jax.numpy as jnp
from jax import lax
from jax.experimental import pallas as pl
from jax.experimental.pallas import tpu as pltpu
from jax.sharding import PartitionSpec as P

D = 512
HEAD_DIM = 64
HD = 512
POS = 8192
NTB = 128
STEP = 10
TILE = 256
NEG = -1e9

norm_epsilon = 1e-06
adam_epsilon = 1e-08
beta_one = 0.9
beta_two = 0.999
clip_norm = 1.0
rate_matrix = 0.05
rate_small = 0.3
decay_matrix = 0.1

f32 = jnp.float32
bf16 = jnp.bfloat16
VMEM = pl.BlockSpec(memory_space=pltpu.VMEM)
SMEM = pl.BlockSpec(memory_space=pltpu.SMEM)
ANY = pl.BlockSpec(memory_space=pl.ANY)


def adam_step(weight, grad, first, second, factor, rate, decay):
    clipped = grad * factor
    first_new = beta_one * first + (1.0 - beta_one) * clipped
    second_new = beta_two * second + (1.0 - beta_two) * clipped * clipped
    update = (
        first_new
        / (1.0 - beta_one**STEP)
        / (jnp.sqrt(second_new / (1.0 - beta_two**STEP)) + adam_epsilon)
    )
    return (weight - rate * (update + decay * weight), first_new, second_new)


def swap(x, axis, k):
    n = lax.axis_size(axis)
    return lax.ppermute(x, axis, [(i, i ^ k) for i in range(n)])


def gather_head(x):
    n = lax.axis_size("head")
    pieces = [None] * n
    pieces[0] = x
    for k in range(2, n, 2):
        pieces[k] = swap(x, "head", k)
    pieces[1] = swap(x, "head", 1)
    for k in range(2, n, 2):
        pieces[k + 1] = swap(pieces[k], "head", 1)
    return pieces


def gather_dp(x):
    n = lax.axis_size("dp")
    arrays, offsets = [x], [[0]]
    k = n // 2
    while k:
        arrays.append(swap(jnp.concatenate(arrays, 0) if len(arrays) > 1 else x, "dp", k))
        offsets.append([o ^ k for group in offsets for o in group])
        k //= 2
    return arrays, offsets


def scatter_dp(x):
    n = lax.axis_size("dp")
    me = lax.axis_index("dp")
    low = 2 ** ((n.bit_length() - 1) // 2)
    high = n // low
    parts = x.reshape((high, low) + x.shape[1:])
    here = me % low
    total = lax.dynamic_index_in_dim(parts, here, 1, False).astype(f32)
    for k in range(1, low):
        sent = lax.dynamic_index_in_dim(parts, here ^ k, 1, False)
        total = total + swap(sent, "dp", k).astype(f32)
    row = me // low
    narrow = total.astype(bf16)
    mine = lax.dynamic_index_in_dim(total, row, 0, False)
    for k in range(1, high):
        sent = lax.dynamic_index_in_dim(narrow, row ^ k, 0, False)
        mine = mine + swap(sent, "dp", k * low).astype(f32)
    return mine


def scatter_head(x):
    n = lax.axis_size("head")
    me = lax.axis_index("head")
    core, chip = me % 2, me // 2
    parts = x.reshape(n // 2, 2, x.shape[0] // n, x.shape[1])
    total = lax.dynamic_index_in_dim(parts, core, 1, False).astype(f32)
    sent = lax.dynamic_index_in_dim(parts, 1 - core, 1, False)
    total = total + swap(sent, "head", 1).astype(f32)
    narrow = total.astype(bf16)
    mine = lax.dynamic_index_in_dim(total, chip, 0, False)
    for k in range(1, n // 2):
        sent = lax.dynamic_index_in_dim(narrow, chip ^ k, 0, False)
        mine = mine + swap(sent, "head", 2 * k).astype(f32)
    return mine


def sum_all(x):
    for axis in ("head", "dp"):
        k = 1
        while k < lax.axis_size(axis):
            x = x + swap(x, axis, k)
            k *= 2
    return x


def dot(a, b):
    return lax.dot_general(a, b, (((1,), (0,)), ((), ())), preferred_element_type=f32)


def dot_nt(a, b):
    return lax.dot_general(a, b, (((1,), (1,)), ((), ())), preferred_element_type=f32)


def flip(a):
    return jnp.transpose(a.astype(f32))


def lanes(i):
    return pl.ds(pl.multiple_of(i * TILE, TILE), TILE)


def by_head(block, heads):
    zero = jnp.zeros((HEAD_DIM, block.shape[1]), block.dtype)
    return jnp.concatenate(
        [
            jnp.concatenate(
                [block[g * HEAD_DIM : (g + 1) * HEAD_DIM] if g == h else zero for g in range(heads)], axis=0
            )
            for h in range(heads)
        ],
        axis=1,
    )


def diagonals(x):
    rows, cols = x.shape
    z = jnp.concatenate([x, jnp.zeros((rows, cols), f32)], axis=1)
    total = z[:8]
    for q in range(1, rows // 8):
        total = total + pltpu.roll(z[8 * q : 8 * q + 8], 2 * cols - 8 * q, 1)
    g = total[0:1]
    for r in range(1, 8):
        g = g + pltpu.roll(total, 2 * cols - r, 1)[r : r + 1]
    return g


def copy_pieces(pieces, target, sems, me):
    copies = [
        pltpu.make_async_copy(piece, target.at[me ^ k], sems.at[k]) for k, piece in enumerate(pieces)
    ]
    for copy in copies:
        copy.start()
    return copies


def forward_kernel(heads, n_head, offsets, me_ref, first_ref, *refs):
    refs = list(refs)
    take = lambda count: [refs.pop(0) for _ in range(count)]
    x_pieces, cot_pieces, w_pieces = take(n_head), take(n_head), take(len(offsets))
    tb_ref, ss_ref, small_ref = take(3)
    attn_ref, d_ref, gate_ref, gg_ref, stat_ref = take(5)
    kx_ref, kxt_ref, qxt_ref, v_ref, qm_ref, pos_ref, wt_ref = take(7)
    x_ref, cot_ref, w_ref, vt_ref, acc_ref, x_sem, cot_sem, w_sem = refs
    nb, width = attn_ref.shape[0], attn_ref.shape[1]
    per = x_ref.shape[1] // TILE
    copies = copy_pieces(x_pieces, x_ref, x_sem, me_ref[0]) + copy_pieces(cot_pieces, cot_ref, cot_sem, me_ref[0])
    count = 0
    for piece, group in zip(w_pieces, offsets):
        rows = piece.shape[0] // len(group)
        for at, offset in enumerate(group):
            start = pl.multiple_of((me_ref[1] ^ offset) * rows, 16)
            copy = pltpu.make_async_copy(
                piece.at[pl.ds(at * rows, rows)], w_ref.at[pl.ds(start, rows)], w_sem.at[count]
            )
            copy.start()
            copies.append(copy)
            count += 1

    for d in range(nb):
        here = small_ref[:, D + d * TILE : D + (d + 1) * TILE]
        before = here if d == 0 else small_ref[:, D + (d - 1) * TILE : D + d * TILE]
        row = jnp.concatenate([here, before], axis=1) * 0.5
        tile = pltpu.roll(
            jnp.broadcast_to(row, (TILE, 2 * TILE)), 0, 1, stride=1, stride_axis=0
        )[:, :TILE]
        if d == 0:
            b = lax.broadcasted_iota(jnp.int32, (TILE, TILE), 0)
            a = lax.broadcasted_iota(jnp.int32, (TILE, TILE), 1)
            tile = jnp.where(b <= a, tile, NEG)
        pos_ref[d] = tile
    table = small_ref[:, D + POS : D + POS + NTB]
    row = jnp.concatenate([table, table], axis=1)
    upper = pltpu.roll(jnp.broadcast_to(row, (NTB, 2 * NTB)), 0, 1, stride=1, stride_axis=0)[:, :NTB]
    a = lax.broadcasted_iota(jnp.int32, (NTB, NTB), 0)
    b = lax.broadcasted_iota(jnp.int32, (NTB, NTB), 1)
    upper = jnp.where(b >= a, upper, 0.0)
    square = (jnp.where(b > a, upper, jnp.transpose(upper)) * 0.5).astype(bf16)

    for copy in copies:
        copy.wait()
    wt_ref[...] = flip(w_ref[...]).astype(bf16)

    def project(i, _):
        rows = lanes(i % per)
        p = dot_nt(wt_ref[: 4 * width], x_ref[i // per, rows, :])
        sg = 0.5 + 0.5 * jnp.tanh(0.5 * p)
        act = p * sg
        d_ref[i] = sg + act * (1.0 - sg)
        gate_ref[i] = act[:width]
        gg_ref[i] = dot_nt(wt_ref[4 * width :], cot_ref[i // per, rows, :])
        vt = act[width : 2 * width]
        vt_ref[i] = vt.astype(bf16)
        v_ref[i] = flip(vt).astype(bf16)
        qt = act[2 * width : 3 * width].astype(bf16)
        kt = act[3 * width :]
        onehot = (lax.broadcasted_iota(jnp.int32, (NTB, TILE), 0) == tb_ref[:, lanes(i)]).astype(f32)
        low = onehot.astype(bf16)
        kxt_ref[i, :NTB] = low
        kxt_ref[i, NTB:] = kt.astype(bf16)
        kx_ref[i, :, :NTB] = flip(onehot).astype(bf16)
        kx_ref[i, :, NTB:] = flip(kt).astype(bf16)
        trow = dot(square, low).astype(bf16)
        qs = (qt.astype(f32) * (0.5 / math.sqrt(HEAD_DIM))).astype(bf16)
        qxt_ref[i, :NTB] = jnp.concatenate([trow] * heads, axis=1)
        qxt_ref[i, NTB:] = by_head(qs, heads)
        q = flip(qt).astype(bf16)
        lane = lax.broadcasted_iota(jnp.int32, (TILE, width), 1) // HEAD_DIM
        for h in range(heads):
            qm_ref[i, h * TILE : (h + 1) * TILE, :] = jnp.where(lane == h, q, jnp.zeros_like(q))
        return 0

    lax.fori_loop(0, nb, project, 0)
    key_index = lax.broadcasted_iota(jnp.int32, (TILE, TILE), 0)

    def rows(i, _):
        acc_ref[...] = jnp.zeros_like(acc_ref)
        start = ss_ref[:, lanes(i)]

        def cols(j, _):
            s = dot(kx_ref[j], qxt_ref[i]) + jnp.concatenate([pos_ref[i - j]] * heads, axis=1)
            seen = (key_index + j * TILE) >= start
            s = jnp.where(jnp.concatenate([seen] * heads, axis=1), s, NEG)
            w = (s + s * jnp.tanh(s)).astype(bf16)
            acc_ref[...] += dot(vt_ref[j], w)
            return 0

        lax.fori_loop(first_ref[i], i + 1, cols, 0)
        at = jnp.concatenate(
            [
                acc_ref[h * HEAD_DIM : (h + 1) * HEAD_DIM, h * TILE : (h + 1) * TILE]
                for h in range(heads)
            ],
            axis=0,
        )
        attn_ref[i] = at
        mean = jnp.sum(at, axis=0, keepdims=True) / width
        centred = at - mean
        grad = gg_ref[i] * gate_ref[i]
        stat_ref[i] = jnp.concatenate(
            [
                mean,
                jnp.sum(centred * centred, axis=0, keepdims=True),
                jnp.sum(grad, axis=0, keepdims=True),
                jnp.sum(grad * centred, axis=0, keepdims=True),
            ],
            axis=0,
        )
        return 0

    lax.fori_loop(0, nb, rows, 0)


def middle_kernel(heads, n_head, me_ref, *refs):
    refs = list(refs)
    take = lambda count: [refs.pop(0) for _ in range(count)]
    x_pieces, cot_pieces, stats = take(n_head), take(n_head), take(n_head)
    attn_ref, d_ref, gate_ref, gg_ref, wt_ref = take(5)
    dat_ref, gu_ref, branch_ref, wg_ref = take(4)
    x_ref, cot_ref, ow_ref, acc_ref, x_sem, cot_sem = refs
    nb, width = attn_ref.shape[0], attn_ref.shape[1]
    per = x_ref.shape[1] // TILE
    copies = copy_pieces(x_pieces, x_ref, x_sem, me_ref[0]) + copy_pieces(cot_pieces, cot_ref, cot_sem, me_ref[0])
    ow_ref[...] = wt_ref[4 * width :]
    acc_ref[...] = jnp.zeros_like(acc_ref)
    for copy in copies:
        copy.wait()

    def rows(i, _):
        parts = [s[i] for s in stats]
        mean = sum(p[0:1] for p in parts) / n_head
        spread = sum(p[1:2] + width * (p[0:1] - mean) * (p[0:1] - mean) for p in parts)
        scale = lax.rsqrt(spread / HD + norm_epsilon)
        first = sum(p[2:3] for p in parts) / HD
        second = scale * sum(p[3:4] + (p[0:1] - mean) * p[2:3] for p in parts) / HD
        normed = (attn_ref[i] - mean) * scale
        gate, gg = gate_ref[i], gg_ref[i]
        gated = normed * gate
        dat_ref[i] = scale * (gg * gate - first - normed * second)
        gu = (gg * normed * d_ref[i]).astype(bf16)
        gu_ref[i] = gu
        at = lanes(i % per)
        branch_ref[pl.ds(pl.multiple_of(i * TILE, TILE), TILE), :] = dot(
            flip(gated.astype(bf16)).astype(bf16), ow_ref[...]
        ).astype(bf16)
        acc_ref[:width] += dot(gu, x_ref[i // per, at, :])
        acc_ref[width:] += dot(gated.astype(bf16), cot_ref[i // per, at, :])
        return 0

    lax.fori_loop(0, nb, rows, 0)
    wg_ref[...] = flip(acc_ref[...]).astype(bf16)


def backward_kernel(heads, n_head, me_ref, first_ref, *refs):
    refs = list(refs)
    take = lambda count: [refs.pop(0) for _ in range(count)]
    x_pieces = take(n_head)
    wt_ref, d_ref, kx_ref, kxt_ref, qxt_ref, v_ref, qm_ref, pos_ref, dat_ref, gu_ref, ss_ref = take(11)
    wg_ref, gn_ref, pg_ref, tg_ref = take(4)
    x_ref, dax_ref, daxt_ref, accv_ref, acck_ref, accq_ref, posg_ref, m2_ref, gp_ref, acc_ref, x_sem = refs
    nb, width = dat_ref.shape[0], dat_ref.shape[1]
    per = x_ref.shape[1] // TILE
    copies = copy_pieces(x_pieces, x_ref, x_sem, me_ref[0])
    accv_ref[...] = jnp.zeros_like(accv_ref)
    acck_ref[...] = jnp.zeros_like(acck_ref)
    posg_ref[...] = jnp.zeros_like(posg_ref)
    m2_ref[...] = jnp.zeros_like(m2_ref)
    lane = lax.broadcasted_iota(jnp.int32, (TILE, width), 1) // HEAD_DIM
    key_index = lax.broadcasted_iota(jnp.int32, (TILE, TILE), 0)
    factor = 1.0 / math.sqrt(HEAD_DIM)

    def rows(i, _):
        grad = dat_ref[i]
        daxt_ref[...] = by_head((grad * 0.5).astype(bf16), heads)
        natural = flip(grad).astype(bf16)
        for h in range(heads):
            dax_ref[h * TILE : (h + 1) * TILE, :] = jnp.where(lane == h, natural, jnp.zeros_like(natural))
        accq_ref[...] = jnp.zeros_like(accq_ref)
        start = ss_ref[:, lanes(i)]

        def cols(j, _):
            s = dot(kx_ref[j], qxt_ref[i]) + jnp.concatenate([pos_ref[i - j]] * heads, axis=1)
            seen = (key_index + j * TILE) >= start
            s = jnp.where(jnp.concatenate([seen] * heads, axis=1), s, NEG)
            t = jnp.tanh(s)
            u = 1.0 + t
            w = s * u
            ds = dot(v_ref[j], daxt_ref[...]) * (u + w * (1.0 - t))
            low = ds.astype(bf16)
            accv_ref[j] += dot(w.astype(bf16), dax_ref[...])
            acck_ref[j] += dot(low, qm_ref[i])
            accq_ref[...] += dot(kxt_ref[j], low)
            posg_ref[i - j] += sum(ds[:, h * TILE : (h + 1) * TILE] for h in range(heads))
            return 0

        lax.fori_loop(first_ref[i], i + 1, cols, 0)
        dq = jnp.concatenate(
            [
                accq_ref[
                    NTB + h * HEAD_DIM : NTB + (h + 1) * HEAD_DIM, h * TILE : (h + 1) * TILE
                ]
                for h in range(heads)
            ],
            axis=0,
        )
        tp = sum(accq_ref[:NTB, h * TILE : (h + 1) * TILE] for h in range(heads))
        high = tp.astype(bf16)
        rest = (tp - high.astype(f32)).astype(bf16)
        onehot = kx_ref[i, :, :NTB]
        m2_ref[...] += dot(high, onehot) + dot(rest, onehot)
        gp_ref[i, :width] = gu_ref[i]
        gp_ref[i, 2 * width : 3 * width] = (dq * factor * d_ref[i, 2 * width : 3 * width]).astype(bf16)
        return 0

    lax.fori_loop(0, nb, rows, 0)
    for copy in copies:
        copy.wait()
    acc_ref[...] = jnp.zeros_like(acc_ref)

    def tail(i, _):
        gp_ref[i, width : 2 * width] = (flip(accv_ref[i]) * d_ref[i, width : 2 * width]).astype(bf16)
        gp_ref[i, 3 * width :] = (flip(acck_ref[i]) * factor * d_ref[i, 3 * width :]).astype(bf16)
        gp = gp_ref[i]
        acc_ref[...] += dot(gp[width:], x_ref[i // per, lanes(i % per), :])
        gn_ref[pl.ds(pl.multiple_of(i * TILE, TILE), TILE), :] = dot(
            flip(gp).astype(bf16), wt_ref[: 4 * width]
        ).astype(bf16)
        return 0

    lax.fori_loop(0, nb, tail, 0)
    wg_ref[...] = flip(acc_ref[...]).astype(bf16)
    pg_ref[...] = jnp.zeros_like(pg_ref)
    for d in range(nb):
        g = diagonals(posg_ref[d])
        pg_ref[:, d * TILE : (d + 1) * TILE] += g[:, :TILE]
        if d > 0:
            pg_ref[:, (d - 1) * TILE : d * TILE] += g[:, TILE:]
    m2 = m2_ref[...]
    g = diagonals(m2 + jnp.transpose(m2))[:, :NTB]
    zero = lax.broadcasted_iota(jnp.int32, (1, NTB), 1) == 0
    tg_ref[...] = jnp.where(zero, 0.5 * g, g)


def call(kernel, name, in_specs, outs, scratch):
    return pl.pallas_call(
        kernel,
        out_shape=[jax.ShapeDtypeStruct(shape, dtype) for shape, dtype in outs],
        in_specs=in_specs,
        out_specs=[VMEM] * len(outs),
        scratch_shapes=scratch,
        compiler_params=pltpu.CompilerParams(vmem_limit_bytes=60 * 2**20),
        name=name,
    )


def shards(
    tokens,
    cotangent,
    seq_start,
    time_bucket,
    proj_weight,
    out_weight,
    small_params,
    proj_mean,
    proj_square,
    out_mean,
    out_square,
    small_mean,
    small_square,
):
    n_head = lax.axis_size("head")
    n_dp = lax.axis_size("dp")
    me_head, me_dp = lax.axis_index("head"), lax.axis_index("dp")
    here = tokens.shape[0]
    group = here * n_head
    nb = group // TILE
    rows_here, _, width = proj_weight.shape
    heads = width // HEAD_DIM
    me = jnp.stack([me_head, me_dp]).astype(jnp.int32)

    inputs = tokens.astype(f32)
    centred = inputs - jnp.mean(inputs, -1, keepdims=True)
    scale_in = lax.rsqrt(jnp.mean(centred * centred, -1, keepdims=True) + norm_epsilon)
    normed = centred * scale_in
    weights = jnp.concatenate(
        [proj_weight.reshape(rows_here, 4 * width).astype(bf16), out_weight.T.astype(bf16)], axis=1
    )
    x_pieces = gather_head(normed.astype(bf16))
    w_pieces, offsets = gather_dp(weights)
    cot_pieces = gather_head(cotangent)
    first = seq_start[::TILE] // TILE
    starts = seq_start.reshape(1, group)

    big = [pltpu.VMEM((n_head, here, D), bf16)]
    sems = [pltpu.SemaphoreType.DMA((n_head,))]
    attn, dsilu, gate, grad_gated, stat, kx, kxt, qxt, v, qm, pos, wt = call(
        functools.partial(forward_kernel, heads, n_head, offsets),
        "forward",
        [SMEM] * 2 + [ANY] * (2 * n_head + len(w_pieces)) + [VMEM] * 3,
        [
            ((nb, width, TILE), f32),
            ((nb, 4 * width, TILE), f32),
            ((nb, width, TILE), f32),
            ((nb, width, TILE), f32),
            ((nb, 4, TILE), f32),
            ((nb, TILE, NTB + width), bf16),
            ((nb, NTB + width, TILE), bf16),
            ((nb, NTB + width, heads * TILE), bf16),
            ((nb, TILE, width), bf16),
            ((nb, heads * TILE, width), bf16),
            ((nb, TILE, TILE), f32),
            ((5 * width, D), bf16),
        ],
        big
        + big
        + [
            pltpu.VMEM((D, 5 * width), bf16),
            pltpu.VMEM((nb, width, TILE), bf16),
            pltpu.VMEM((width, heads * TILE), f32),
        ]
        + sems
        + sems
        + [pltpu.SemaphoreType.DMA((n_dp,))],
    )(
        me, first, *x_pieces, *cot_pieces, *w_pieces,
        time_bucket.reshape(1, group), starts, small_params.reshape(1, -1),
    )
    stats = [stat] + [swap(stat, "head", k) for k in range(1, n_head)]
    grad_attn, grad_u, branch, wg_early = call(
        functools.partial(middle_kernel, heads, n_head),
        "middle",
        [SMEM] + [ANY] * (2 * n_head) + [VMEM] * (n_head + 5),
        [
            ((nb, width, TILE), f32),
            ((nb, width, TILE), bf16),
            ((group, D), bf16),
            ((D, 2 * width), bf16),
        ],
        big + big + [pltpu.VMEM((width, D), bf16), pltpu.VMEM((2 * width, D), f32)] + sems + sems,
    )(
        me, *x_pieces, *cot_pieces, *stats, attn, dsilu[:, :width], gate, grad_gated, wt,
    )
    mixed = (scatter_head(branch) + small_params[:D] + inputs).astype(bf16)
    early = scatter_dp(wg_early.reshape(n_dp, rows_here, 2 * width))
    wg_late, grad_rows, pos_grad, time_grad = call(
        functools.partial(backward_kernel, heads, n_head),
        "backward",
        [SMEM] * 2 + [ANY] * n_head + [VMEM] * 11,
        [
            ((D, 3 * width), bf16),
            ((group, D), bf16),
            ((1, group), f32),
            ((1, NTB), f32),
        ],
        big
        + [
            pltpu.VMEM((heads * TILE, width), bf16),
            pltpu.VMEM((width, heads * TILE), bf16),
            pltpu.VMEM((nb, TILE, width), f32),
            pltpu.VMEM((nb, TILE, width), f32),
            pltpu.VMEM((NTB + width, heads * TILE), f32),
            pltpu.VMEM((nb, TILE, TILE), f32),
            pltpu.VMEM((NTB, NTB), f32),
            pltpu.VMEM((nb, 4 * width, TILE), bf16),
            pltpu.VMEM((3 * width, D), f32),
        ]
        + sems,
    )(me, first, *x_pieces, wt, dsilu, kx, kxt, qxt, v, qm, pos, grad_attn, grad_u, starts)

    grad_result = cotangent.astype(f32)
    late = scatter_dp(wg_late.reshape(n_dp, rows_here, 3 * width))
    small_local = jnp.concatenate([jnp.sum(grad_result, 0), pos_grad[0], time_grad[0]])
    small_sum = sum_all(small_local)
    grad_small = jnp.concatenate(
        [small_sum[: D + group], jnp.zeros((POS - group,), f32), small_sum[D + group :]]
    )
    normed_grad = scatter_head(grad_rows)
    input_grad = grad_result + scale_in * (
        normed_grad
        - jnp.mean(normed_grad, -1, keepdims=True)
        - normed * jnp.mean(normed_grad * normed, -1, keepdims=True)
    )
    grad_out = early[:, width:].T
    grad_proj = jnp.concatenate([early[:, :width], late], axis=1).reshape(rows_here, 4, width)
    squares = jnp.sum(early * early) + jnp.sum(late * late)
    total = sum_all(squares) + jnp.sum(small_sum * small_sum)
    grad_norm = jnp.sqrt(total)
    factor = jnp.minimum(1.0, clip_norm / (grad_norm + 1e-06))
    new_proj, mean_proj, square_proj = adam_step(
        proj_weight, grad_proj, proj_mean, proj_square, factor, rate_matrix, decay_matrix
    )
    new_out, mean_out, square_out = adam_step(
        out_weight, grad_out, out_mean, out_square, factor, rate_matrix, decay_matrix
    )
    new_small, mean_small, square_small = adam_step(
        small_params, grad_small, small_mean, small_square, factor, rate_small, 0.0
    )
    return (
        mixed,
        input_grad,
        grad_proj,
        grad_out,
        grad_small,
        grad_norm,
        new_proj,
        mean_proj,
        square_proj,
        new_out,
        mean_out,
        square_out,
        new_small,
        mean_small,
        square_small,
    )


def solution(mesh):
    in_specs = (
        P(("dp", "head"), None),
        P(("dp", "head"), None),
        P("dp"),
        P("dp"),
        P("dp", None, "head"),
        P("head", "dp"),
        P(),
        P("dp", None, "head"),
        P("dp", None, "head"),
        P("head", "dp"),
        P("head", "dp"),
        P(),
        P(),
    )
    out_specs = (
        P(("dp", "head"), None),
        P(("dp", "head"), None),
        P("dp", None, "head"),
        P("head", "dp"),
        P(),
        P(),
        P("dp", None, "head"),
        P("dp", None, "head"),
        P("dp", None, "head"),
        P("head", "dp"),
        P("head", "dp"),
        P("head", "dp"),
        P(),
        P(),
        P(),
    )
    return jax.shard_map(shards, mesh=mesh, in_specs=in_specs, out_specs=out_specs, check_vma=False)
```

```python
import functools
import math

import jax
import jax.numpy as jnp
from jax import lax
from jax.experimental import pallas as pl
from jax.experimental.pallas import tpu as pltpu
from jax.sharding import PartitionSpec as P

D = 512
HEAD_DIM = 64
HD = 512
POS = 8192
NTB = 128
STEP = 10
TILE = 256
NEG = -1e9

norm_epsilon = 1e-06
adam_epsilon = 1e-08
beta_one = 0.9
beta_two = 0.999
clip_norm = 1.0
rate_matrix = 0.05
rate_small = 0.3
decay_matrix = 0.1

f32 = jnp.float32
bf16 = jnp.bfloat16
VMEM = pl.BlockSpec(memory_space=pltpu.VMEM)
SMEM = pl.BlockSpec(memory_space=pltpu.SMEM)
ANY = pl.BlockSpec(memory_space=pl.ANY)


def adam_step(weight, grad, first, second, factor, rate, decay):
    clipped = grad * factor
    first_new = beta_one * first + (1.0 - beta_one) * clipped
    second_new = beta_two * second + (1.0 - beta_two) * clipped * clipped
    update = (
        first_new
        / (1.0 - beta_one**STEP)
        / (jnp.sqrt(second_new / (1.0 - beta_two**STEP)) + adam_epsilon)
    )
    return (weight - rate * (update + decay * weight), first_new, second_new)


def swap(x, axis, k):
    n = lax.axis_size(axis)
    return lax.ppermute(x, axis, [(i, i ^ k) for i in range(n)])


def gather_head(x):
    n = lax.axis_size("head")
    pieces = [None] * n
    pieces[0] = x
    for k in range(2, n, 2):
        pieces[k] = swap(x, "head", k)
    pieces[1] = swap(x, "head", 1)
    for k in range(2, n, 2):
        pieces[k + 1] = swap(pieces[k], "head", 1)
    return pieces


def gather_dp(x):
    n = lax.axis_size("dp")
    arrays, offsets = [x], [[0]]
    k = n // 2
    while k:
        arrays.append(swap(jnp.concatenate(arrays, 0) if len(arrays) > 1 else x, "dp", k))
        offsets.append([o ^ k for group in offsets for o in group])
        k //= 2
    return arrays, offsets


def split_dp(n):
    low = 2 ** ((n.bit_length() - 1) // 2)
    return n // low, low


def scatter_dp(parts):
    n = lax.axis_size("dp")
    high, low = split_dp(n)
    row = lax.axis_index("dp") // low
    total = parts[0].astype(f32)
    for k in range(1, low):
        total = total + swap(parts[k], "dp", k).astype(f32)
    narrow = total.astype(bf16)
    mine = lax.dynamic_index_in_dim(total, row, 0, False)
    for k in range(1, high):
        sent = lax.dynamic_index_in_dim(narrow, row ^ k, 0, False)
        mine = mine + swap(sent, "dp", k * low).astype(f32)
    return mine


def scatter_head(keep, send):
    n = lax.axis_size("head")
    chip = lax.axis_index("head") // 2
    total = keep.astype(f32) + swap(send, "head", 1).astype(f32)
    narrow = total.astype(bf16)
    mine = lax.dynamic_index_in_dim(total, chip, 0, False)
    for k in range(1, n // 2):
        sent = lax.dynamic_index_in_dim(narrow, chip ^ k, 0, False)
        mine = mine + swap(sent, "head", 2 * k).astype(f32)
    return mine


def dot(a, b):
    return lax.dot_general(a, b, (((1,), (0,)), ((), ())), preferred_element_type=f32)


def dot_nt(a, b):
    return lax.dot_general(a, b, (((1,), (1,)), ((), ())), preferred_element_type=f32)


def flip(a):
    return jnp.transpose(a.astype(f32))


def lanes(i):
    return pl.ds(pl.multiple_of(i * TILE, TILE), TILE)


def by_head(block, heads):
    zero = jnp.zeros((HEAD_DIM, block.shape[1]), block.dtype)
    return jnp.concatenate(
        [
            jnp.concatenate(
                [block[g * HEAD_DIM : (g + 1) * HEAD_DIM] if g == h else zero for g in range(heads)], axis=0
            )
            for h in range(heads)
        ],
        axis=1,
    )


def own_rows(block, heads):
    return jnp.concatenate(
        [block[h * HEAD_DIM : (h + 1) * HEAD_DIM, h * TILE : (h + 1) * TILE] for h in range(heads)], axis=0
    )


def own_lanes(block, heads):
    lane = lax.broadcasted_iota(jnp.int32, block.shape, 1) // HEAD_DIM
    return jnp.concatenate([jnp.where(lane == h, block, jnp.zeros_like(block)) for h in range(heads)], axis=0)


def diagonals(x):
    rows, cols = x.shape
    z = jnp.concatenate([x, jnp.zeros((rows, cols), f32)], axis=1)
    total = z[:8]
    for q in range(1, rows // 8):
        total = total + pltpu.roll(z[8 * q : 8 * q + 8], 2 * cols - 8 * q, 1)
    g = total[0:1]
    for r in range(1, 8):
        g = g + pltpu.roll(total, 2 * cols - r, 1)[r : r + 1]
    return g


def start_all(copies):
    for copy in copies:
        copy.start()
    return copies


def wait_all(copies):
    for copy in copies:
        copy.wait()


def piece_copies(pieces, target, sems, me):
    return [pltpu.make_async_copy(piece, target.at[me ^ k], sems.at[k]) for k, piece in enumerate(pieces)]


def row_copies(pieces, offsets, target, sems, me):
    copies = []
    for piece, group in zip(pieces, offsets):
        rows = piece.shape[0] // len(group)
        for at, offset in enumerate(group):
            start = pl.multiple_of((me ^ offset) * rows, 16)
            copies.append(
                pltpu.make_async_copy(
                    piece.at[pl.ds(at * rows, rows)], target.at[pl.ds(start, rows)], sems.at[len(copies)]
                )
            )
    return copies


def prepare_kernel(tb_ref, small_ref, pos_ref, oh_ref, oht_ref, trow_ref):
    nb = pos_ref.shape[0]
    for d in range(nb):
        here = small_ref[:, D + d * TILE : D + (d + 1) * TILE]
        before = here if d == 0 else small_ref[:, D + (d - 1) * TILE : D + d * TILE]
        row = jnp.concatenate([here, before], axis=1) * 0.5
        tile = pltpu.roll(
            jnp.broadcast_to(row, (TILE, 2 * TILE)), 0, 1, stride=1, stride_axis=0
        )[:, :TILE]
        if d == 0:
            b = lax.broadcasted_iota(jnp.int32, (TILE, TILE), 0)
            a = lax.broadcasted_iota(jnp.int32, (TILE, TILE), 1)
            tile = jnp.where(b <= a, tile, NEG)
        pos_ref[d] = tile
    table = small_ref[:, D + POS : D + POS + NTB]
    row = jnp.concatenate([table, table], axis=1)
    upper = pltpu.roll(jnp.broadcast_to(row, (NTB, 2 * NTB)), 0, 1, stride=1, stride_axis=0)[:, :NTB]
    a = lax.broadcasted_iota(jnp.int32, (NTB, NTB), 0)
    b = lax.broadcasted_iota(jnp.int32, (NTB, NTB), 1)
    upper = jnp.where(b >= a, upper, 0.0)
    square = (jnp.where(b > a, upper, jnp.transpose(upper)) * 0.5).astype(bf16)

    def block(i, _):
        onehot = (lax.broadcasted_iota(jnp.int32, (NTB, TILE), 0) == tb_ref[:, lanes(i)]).astype(f32)
        low = onehot.astype(bf16)
        oht_ref[i] = low
        oh_ref[i] = flip(onehot).astype(bf16)
        trow_ref[i] = dot(square, low).astype(bf16)
        return 0

    lax.fori_loop(0, nb, block, 0)


def forward_kernel(heads, n_head, offsets, me_ref, first_ref, *refs):
    refs = list(refs)
    take = lambda count: [refs.pop(0) for _ in range(count)]
    x_pieces, w_pieces = take(n_head), take(len(offsets))
    oh_in, oht_in, trow_in, pos_in, ss_ref = take(5)
    attn_ref = refs.pop(0)
    outs = take(8)
    staged = take(8)
    xn_ref, d_ref, kx_ref, kxt_ref, qxt_ref, v_ref, qm_ref, wt_ref = staged
    x_ref, w_ref, vt_ref, pos_ref, acc_ref, x_sem, w_sem, t_sem, out_sem = refs
    nb, width = attn_ref.shape[0], attn_ref.shape[1]
    per = x_ref.shape[1] // TILE
    needed = start_all(
        row_copies(w_pieces, offsets, w_ref, w_sem, me_ref[1]) + piece_copies(x_pieces, x_ref, x_sem, me_ref[0])
    )
    tables = start_all(
        [
            pltpu.make_async_copy(oh_in, kx_ref.at[:, :, :NTB], t_sem.at[0]),
            pltpu.make_async_copy(oht_in, kxt_ref.at[:, :NTB], t_sem.at[1]),
            pltpu.make_async_copy(pos_in, pos_ref, t_sem.at[2]),
        ]
        + [
            pltpu.make_async_copy(trow_in, qxt_ref.at[:, :NTB, h * TILE : (h + 1) * TILE], t_sem.at[3 + h])
            for h in range(heads)
        ]
    )
    wait_all(needed)
    wt_ref[...] = flip(w_ref[...]).astype(bf16)

    def project(i, _):
        x = x_ref[i // per, lanes(i % per), :].astype(f32)
        x = x - jnp.sum(x, axis=1, keepdims=True) / D
        x = (x * lax.rsqrt(jnp.sum(x * x, axis=1, keepdims=True) / D + norm_epsilon)).astype(bf16)
        xn_ref[i] = x
        p = dot_nt(wt_ref[...], x)
        sg = 0.5 + 0.5 * jnp.tanh(0.5 * p)
        act = p * sg
        d_ref[i] = sg + act * (1.0 - sg)
        vt = act[:width]
        vt_ref[i] = vt.astype(bf16)
        v_ref[i] = flip(vt).astype(bf16)
        qt = act[width : 2 * width].astype(bf16)
        kt = act[2 * width :]
        kxt_ref[i, NTB:] = kt.astype(bf16)
        kx_ref[i, :, NTB:] = flip(kt).astype(bf16)
        qs = (qt.astype(f32) * (0.5 / math.sqrt(HEAD_DIM))).astype(bf16)
        qxt_ref[i, NTB:] = by_head(qs, heads)
        qm_ref[i] = own_lanes(flip(qt).astype(bf16), heads)
        return 0

    lax.fori_loop(0, nb, project, 0)
    wait_all(tables)
    leaving = start_all(
        [pltpu.make_async_copy(a, b, out_sem.at[k]) for k, (a, b) in enumerate(zip(staged, outs))]
    )
    key_index = lax.broadcasted_iota(jnp.int32, (TILE, TILE), 0)

    def rows(i, _):
        acc_ref[...] = jnp.zeros_like(acc_ref)
        start = ss_ref[:, lanes(i)]

        def cols(j, _):
            s = dot(kx_ref[j], qxt_ref[i]) + jnp.concatenate([pos_ref[i - j]] * heads, axis=1)
            seen = (key_index + j * TILE) >= start
            s = jnp.where(jnp.concatenate([seen] * heads, axis=1), s, NEG)
            w = (s + s * jnp.tanh(s)).astype(bf16)
            acc_ref[...] += dot(vt_ref[j], w)
            return 0

        lax.fori_loop(first_ref[i], i + 1, cols, 0)
        attn_ref[i] = own_rows(acc_ref[...], heads)
        return 0

    lax.fori_loop(0, nb, rows, 0)
    wait_all(leaving)


def gate_kernel(n_head, offsets, per, me_ref, *refs):
    refs = list(refs)
    take = lambda count: [refs.pop(0) for _ in range(count)]
    cot_pieces, w_pieces = take(n_head), take(len(offsets))
    attn_ref, xn_ref = take(2)
    gate_ref, ga_ref, gd_ref, stat_ref, cot_out, wt_ref, gb_ref = take(7)
    cot_ref, w_ref, cot_sem, w_sem = refs
    i = pl.program_id(0)
    width = attn_ref.shape[1]

    @pl.when(i == 0)
    def _():
        needed = start_all(row_copies(w_pieces, offsets, w_ref, w_sem, me_ref[1]))
        copies = start_all(piece_copies(cot_pieces, cot_ref, cot_sem, me_ref[0]))
        wait_all(needed)
        wt_ref[...] = flip(w_ref[...]).astype(bf16)
        wait_all(copies)
        gb_ref[...] = jnp.sum(cot_ref[me_ref[0]].astype(f32), axis=0, keepdims=True)

    cot = cot_ref[i // per, lanes(i % per), :]
    cot_out[0] = cot
    p = dot_nt(wt_ref[:width], xn_ref[0])
    sg = 0.5 + 0.5 * jnp.tanh(0.5 * p)
    gate = p * sg
    gg = dot_nt(wt_ref[width:], cot)
    grad = gg * gate
    gate_ref[0] = gate
    ga_ref[0] = grad
    gd_ref[0] = gg * (sg + gate * (1.0 - sg))
    at = attn_ref[0]
    mean = jnp.sum(at, axis=0, keepdims=True) / width
    centred = at - mean
    stat_ref[0] = jnp.concatenate(
        [
            mean,
            jnp.sum(centred * centred, axis=0, keepdims=True),
            jnp.sum(grad, axis=0, keepdims=True),
            jnp.sum(grad * centred, axis=0, keepdims=True),
        ],
        axis=0,
    )


def send_rows(i, per, me, block_ref, keep, send, sem):
    device = i // per
    rows = lanes(i % per)
    mine = device % 2 == me % 2

    @pl.when(mine)
    def _():
        pltpu.make_async_copy(block_ref, keep.at[device // 2, rows], sem).start()

    @pl.when(jnp.logical_not(mine))
    def _():
        pltpu.make_async_copy(block_ref, send.at[device // 2, rows], sem).start()


def middle_kernel(heads, n_head, per, me_ref, *refs):
    refs = list(refs)
    take = lambda count: [refs.pop(0) for _ in range(count)]
    stats = take(n_head)
    attn_ref, gate_ref, ga_ref, gd_ref, xn_ref, cot_ref, wt_ref = take(7)
    dax_ref, daxt_ref, gun_ref, keep, send = take(5)
    parts = take(split_dp_count(refs))
    branch_ref, acc_ref, wg_ref, sem, part_sem = refs
    i = pl.program_id(0)
    nb = branch_ref.shape[0]
    width = attn_ref.shape[1]

    @pl.when(i == 0)
    def _():
        acc_ref[...] = jnp.zeros_like(acc_ref)

    st = [s[0] for s in stats]
    mean = sum(p[0:1] for p in st) / n_head
    spread = sum(p[1:2] + width * (p[0:1] - mean) * (p[0:1] - mean) for p in st)
    scale = lax.rsqrt(spread / HD + norm_epsilon)
    first = sum(p[2:3] for p in st) / HD
    second = scale * sum(p[3:4] + (p[0:1] - mean) * p[2:3] for p in st) / HD
    normed = (attn_ref[0] - mean) * scale
    gated = (normed * gate_ref[0]).astype(bf16)
    grad = scale * (ga_ref[0] - first - normed * second)
    dax_ref[0] = own_lanes(flip(grad).astype(bf16), heads)
    daxt_ref[0] = by_head((grad * 0.5).astype(bf16), heads)
    gu = (gd_ref[0] * normed).astype(bf16)
    gun_ref[0] = flip(gu).astype(bf16)
    branch_ref[i] = dot(flip(gated).astype(bf16), wt_ref[width:]).astype(bf16)
    send_rows(i, per, me_ref[0], branch_ref.at[i], keep, send, sem.at[i])
    acc_ref[:width] += dot(gu, xn_ref[0])
    acc_ref[width:] += dot(gated, cot_ref[0])

    @pl.when(i == nb - 1)
    def _():
        wg_ref[...] = flip(acc_ref[...]).astype(bf16)
        send_parts(wg_ref, parts, part_sem, me_ref[1])
        for k in range(nb):
            pltpu.make_async_copy(branch_ref.at[k], keep.at[0, pl.ds(0, TILE)], sem.at[k]).wait()


def split_dp_count(refs):
    return len(refs) - 5


def send_parts(wg_ref, parts, sem, me):
    low = len(parts)
    high = parts[0].shape[0]
    rows = parts[0].shape[1]
    for p in range(high * low):
        block = wg_ref.at[pl.ds(p * rows, rows)]
        for k in range(low):

            @pl.when((p % low) ^ (me % low) == k)
            def _():
                pltpu.make_async_copy(block, parts[k].at[p // low], sem.at[p]).start()

    for p in range(high * low):
        pltpu.make_async_copy(wg_ref.at[pl.ds(p * rows, rows)], parts[0].at[p // low], sem.at[p]).wait()


def backward_kernel(heads, n_dp, extra, me_ref, first_ref, *refs):
    refs = list(refs)
    take = lambda count: [refs.pop(0) for _ in range(count)]
    ins = take(8)
    d_in, xn_in, ss_ref, gb_ref = take(4)
    gp_out = refs.pop(0)
    parts = take(split_dp(n_dp)[1])
    held = take(8)
    kx_ref, kxt_ref, qxt_ref, v_ref, qm_ref, dax_ref, daxt_ref, pos_ref = held
    d_ref, xn_ref = take(2)
    accv_ref, acck_ref, accq_ref, posg_ref, m2_ref, gpq_ref, acc_ref, wg_ref, small_ref = take(9)
    in_sem, late_sem, part_sem = refs
    nb, width = v_ref.shape[0], v_ref.shape[2]
    for i in range(nb):
        for k in range(8):
            pltpu.make_async_copy(ins[k].at[i], held[k].at[i], in_sem.at[k, i]).start()
    late = start_all(
        [
            pltpu.make_async_copy(d_in, d_ref, late_sem.at[0]),
            pltpu.make_async_copy(xn_in, xn_ref, late_sem.at[1]),
        ]
    )
    accv_ref[...] = jnp.zeros_like(accv_ref)
    acck_ref[...] = jnp.zeros_like(acck_ref)
    posg_ref[...] = jnp.zeros_like(posg_ref)
    m2_ref[...] = jnp.zeros_like(m2_ref)
    key_index = lax.broadcasted_iota(jnp.int32, (TILE, TILE), 0)
    factor = 1.0 / math.sqrt(HEAD_DIM)

    def rows(i, _):
        for k in range(8):
            pltpu.make_async_copy(ins[k].at[i], held[k].at[i], in_sem.at[k, i]).wait()
        accq_ref[...] = jnp.zeros_like(accq_ref)
        start = ss_ref[:, lanes(i)]

        def cols(j, _):
            s = dot(kx_ref[j], qxt_ref[i]) + jnp.concatenate([pos_ref[i - j]] * heads, axis=1)
            seen = (key_index + j * TILE) >= start
            s = jnp.where(jnp.concatenate([seen] * heads, axis=1), s, NEG)
            t = jnp.tanh(s)
            u = 1.0 + t
            w = s * u
            ds = dot(v_ref[j], daxt_ref[i]) * (u + w * (1.0 - t))
            low = ds.astype(bf16)
            accv_ref[j] += dot(w.astype(bf16), dax_ref[i])
            acck_ref[j] += dot(low, qm_ref[i])
            accq_ref[...] += dot(kxt_ref[j], low)
            posg_ref[i - j] += sum(ds[:, h * TILE : (h + 1) * TILE] for h in range(heads))
            return 0

        lax.fori_loop(first_ref[i], i + 1, cols, 0)
        gpq_ref[i] = own_rows(accq_ref[NTB:], heads)
        tp = sum(accq_ref[:NTB, h * TILE : (h + 1) * TILE] for h in range(heads))
        high = tp.astype(bf16)
        rest = (tp - high.astype(f32)).astype(bf16)
        onehot = kx_ref[i, :, :NTB]
        m2_ref[...] += dot(high, onehot) + dot(rest, onehot)
        return 0

    lax.fori_loop(0, nb, rows, 0)
    wait_all(late)
    acc_ref[...] = jnp.zeros_like(acc_ref)

    def tail(i, _):
        gp = jnp.concatenate([flip(accv_ref[i]), gpq_ref[i] * factor, flip(acck_ref[i]) * factor], axis=0)
        gp = (gp * d_ref[i]).astype(bf16)
        gp_out[i] = flip(gp).astype(bf16)
        acc_ref[...] += dot(gp, xn_ref[i])
        return 0

    lax.fori_loop(0, nb, tail, 0)
    small_ref[...] = jnp.zeros_like(small_ref)
    small_ref[:, :D] = gb_ref[...]
    for d in range(nb):
        g = diagonals(posg_ref[d])
        small_ref[:, D + d * TILE : D + (d + 1) * TILE] += g[:, :TILE]
        if d > 0:
            small_ref[:, D + (d - 1) * TILE : D + d * TILE] += g[:, TILE:]
    m2 = m2_ref[...]
    g = diagonals(m2 + jnp.transpose(m2))[:, :NTB]
    zero = lax.broadcasted_iota(jnp.int32, (1, NTB), 1) == 0
    at = D + nb * TILE
    small_ref[:, at : at + NTB] = jnp.where(zero, 0.5 * g, g)
    step = D // n_dp
    grads = flip(acc_ref[...])
    for p in range(n_dp):
        here = jnp.concatenate(
            [small_ref[:, (p * extra + r) * 128 : (p * extra + r + 1) * 128] for r in range(extra)], axis=0
        )
        high = here.astype(bf16).astype(f32)
        block = jnp.concatenate([high, here - high, jnp.zeros((16 - 2 * extra, 128), f32)], axis=0)
        wg_ref[p * (step + 16) : p * (step + 16) + step] = grads[p * step : (p + 1) * step].astype(bf16)
        wg_ref[p * (step + 16) + step : (p + 1) * (step + 16)] = jnp.concatenate(
            [block, jnp.zeros((16, 3 * width - 128), f32)], axis=1
        ).astype(bf16)
    send_parts(wg_ref, parts, part_sem, me_ref[1])


def input_kernel(per, me_ref, gp_ref, gun_ref, wt_ref, wtu_ref, keep, send, rows_ref, sem):
    i = pl.program_id(0)
    nb = rows_ref.shape[0]
    width = gun_ref.shape[2]
    rows_ref[i] = (dot(gp_ref[0], wt_ref[...]) + dot(gun_ref[0], wtu_ref[:width])).astype(bf16)
    send_rows(i, per, me_ref[0], rows_ref.at[i], keep, send, sem.at[i])

    @pl.when(i == nb - 1)
    def _():
        for k in range(nb):
            pltpu.make_async_copy(rows_ref.at[k], keep.at[0, pl.ds(0, TILE)], sem.at[k]).wait()


def call(kernel, name, in_specs, outs, scratch, us, **more):
    return pl.pallas_call(
        kernel,
        out_shape=[jax.ShapeDtypeStruct(shape, dtype) for shape, dtype, _ in outs],
        in_specs=in_specs,
        out_specs=[spec for _, _, spec in outs],
        scratch_shapes=scratch,
        compiler_params=pltpu.CompilerParams(vmem_limit_bytes=60 * 2**20),
        cost_estimate=pl.CostEstimate(flops=int(us * 1e9), bytes_accessed=int(us * 3e6), transcendentals=0),
        name=name,
        **more,
    )


def block(shape):
    return pl.BlockSpec((1,) + tuple(shape[1:]), lambda i: (i,) + (0,) * (len(shape) - 1))


def shards(
    tokens,
    cotangent,
    seq_start,
    time_bucket,
    proj_weight,
    out_weight,
    small_params,
    proj_mean,
    proj_square,
    out_mean,
    out_square,
    small_mean,
    small_square,
):
    n_head = lax.axis_size("head")
    n_dp = lax.axis_size("dp")
    me_head, me_dp = lax.axis_index("head"), lax.axis_index("dp")
    here = tokens.shape[0]
    group = here * n_head
    nb = group // TILE
    per = here // TILE
    rows_here, _, width = proj_weight.shape
    heads = width // HEAD_DIM
    high, low = split_dp(n_dp)
    me = jnp.stack([me_head, me_dp]).astype(jnp.int32)
    dma = pltpu.SemaphoreType.DMA

    flat = proj_weight.reshape(rows_here, 4 * width)
    x_pieces = gather_head(tokens)
    w_pieces, offsets = gather_dp(flat[:, width:].astype(bf16))
    u_pieces, _ = gather_dp(
        jnp.concatenate([flat[:, :width].astype(bf16), out_weight.T.astype(bf16)], axis=1)
    )
    cot_pieces = gather_head(cotangent)
    first = seq_start[::TILE] // TILE
    starts = seq_start.reshape(1, group)

    pos, oh, oht, trow = call(
        prepare_kernel,
        "prepare",
        [VMEM] * 2,
        [
            ((nb, TILE, TILE), f32, VMEM),
            ((nb, TILE, NTB), bf16, VMEM),
            ((nb, NTB, TILE), bf16, VMEM),
            ((nb, NTB, TILE), bf16, VMEM),
        ],
        [],
        5,
    )(time_bucket.reshape(1, group), small_params.reshape(1, -1))

    shapes = [
        ((nb, TILE, D), bf16),
        ((nb, 3 * width, TILE), f32),
        ((nb, TILE, NTB + width), bf16),
        ((nb, NTB + width, TILE), bf16),
        ((nb, NTB + width, heads * TILE), bf16),
        ((nb, TILE, width), bf16),
        ((nb, heads * TILE, width), bf16),
        ((3 * width, D), bf16),
    ]
    attn, xn, dsilu, kx, kxt, qxt, v, qm, wt = call(
        functools.partial(forward_kernel, heads, n_head, offsets),
        "forward",
        [SMEM] * 2 + [ANY] * (n_head + len(w_pieces) + 4) + [VMEM],
        [((nb, width, TILE), f32, VMEM)] + [(shape, dtype, ANY) for shape, dtype in shapes],
        [pltpu.VMEM(shape, dtype) for shape, dtype in shapes]
        + [
            pltpu.VMEM((n_head, here, D), bf16),
            pltpu.VMEM((D, 3 * width), bf16),
            pltpu.VMEM((nb, width, TILE), bf16),
            pltpu.VMEM((nb, TILE, TILE), f32),
            pltpu.VMEM((width, heads * TILE), f32),
            dma((n_head,)),
            dma((n_dp,)),
            dma((3 + heads,)),
            dma((8,)),
        ],
        30,
    )(me, first, *x_pieces, *w_pieces, oh, oht, trow, pos, starts)

    column = ((nb, width, TILE), f32, block((nb, width, TILE)))
    stat_block = block((nb, 4, TILE))
    row_block = block((nb, TILE, D))
    whole = pl.BlockSpec((2 * width, D), lambda i: (0, 0))
    gate, ga, gd, stat, cot, wtu, gb = call(
        functools.partial(gate_kernel, n_head, offsets, per),
        "gate",
        [SMEM] + [ANY] * (n_head + len(u_pieces)) + [column[2], row_block],
        [
            column,
            column,
            column,
            ((nb, 4, TILE), f32, stat_block),
            ((nb, TILE, D), bf16, row_block),
            ((2 * width, D), bf16, whole),
            ((1, D), f32, pl.BlockSpec((1, D), lambda i: (0, 0))),
        ],
        [pltpu.VMEM((n_head, here, D), bf16), pltpu.VMEM((D, 2 * width), bf16), dma((n_head,)), dma((n_dp,))],
        5,
        grid=(nb,),
    )(me, *cot_pieces, *u_pieces, attn, xn)

    stats = [stat] + [swap(stat, "head", k) for k in range(1, n_head)]
    dax, daxt, gun, keep, send, *early_parts = call(
        functools.partial(middle_kernel, heads, n_head, per),
        "middle",
        [SMEM] + [stat_block] * n_head + [column[2]] * 4 + [row_block] * 2 + [whole],
        [
            ((nb, heads * TILE, width), bf16, block((nb, heads * TILE, width))),
            ((nb, width, heads * TILE), bf16, block((nb, width, heads * TILE))),
            ((nb, TILE, width), bf16, block((nb, TILE, width))),
            ((n_head // 2, here, D), bf16, ANY),
            ((n_head // 2, here, D), bf16, ANY),
        ]
        + [((high, rows_here, 2 * width), bf16, ANY)] * low,
        [
            pltpu.VMEM((nb, TILE, D), bf16),
            pltpu.VMEM((2 * width, D), f32),
            pltpu.VMEM((D, 2 * width), bf16),
            dma((nb,)),
            dma((n_dp,)),
        ],
        6,
        grid=(nb,),
    )(me, *stats, attn, gate, ga, gd, xn, cot, wtu)
    branch = scatter_head(keep, send)
    early = scatter_dp(early_parts)

    length = D + group + NTB
    extra = -(-length // (128 * n_dp))
    loaded = [shapes[2], shapes[3], shapes[4], shapes[5], shapes[6]] + [
        ((nb, heads * TILE, width), bf16),
        ((nb, width, heads * TILE), bf16),
        ((nb, TILE, TILE), f32),
    ]
    gp, *late_parts = call(
        functools.partial(backward_kernel, heads, n_dp, extra),
        "backward",
        [SMEM] * 2 + [ANY] * 10 + [VMEM] * 2,
        [((nb, TILE, 3 * width), bf16, VMEM)] + [((high, rows_here + 16, 3 * width), bf16, ANY)] * low,
        [pltpu.VMEM(shape, dtype) for shape, dtype in loaded]
        + [
            pltpu.VMEM(*shapes[1]),
            pltpu.VMEM(*shapes[0]),
            pltpu.VMEM((nb, TILE, width), f32),
            pltpu.VMEM((nb, TILE, width), f32),
            pltpu.VMEM((NTB + width, heads * TILE), f32),
            pltpu.VMEM((nb, TILE, TILE), f32),
            pltpu.VMEM((NTB, NTB), f32),
            pltpu.VMEM((nb, width, TILE), f32),
            pltpu.VMEM((3 * width, D), f32),
            pltpu.VMEM((n_dp * (rows_here + 16), 3 * width), bf16),
            pltpu.VMEM((1, extra * n_dp * 128), f32),
            dma((8, nb)),
            dma((2,)),
            dma((n_dp,)),
        ],
        35,
    )(me, first, kx, kxt, qxt, v, qm, dax, daxt, pos, dsilu, xn, starts, gb)

    keep, send = call(
        functools.partial(input_kernel, per),
        "input_rows",
        [
            SMEM,
            block((nb, TILE, 3 * width)),
            block((nb, TILE, width)),
            pl.BlockSpec((3 * width, D), lambda i: (0, 0)),
            whole,
        ],
        [((n_head // 2, here, D), bf16, ANY)] * 2,
        [pltpu.VMEM((nb, TILE, D), bf16), dma((nb,))],
        4,
        grid=(nb,),
    )(me, gp, gun, wt, wtu)
    late = scatter_dp(late_parts)
    normed_grad = scatter_head(keep, send)

    inputs = tokens.astype(f32)
    centred = inputs - jnp.mean(inputs, -1, keepdims=True)
    scale_in = lax.rsqrt(jnp.mean(centred * centred, -1, keepdims=True) + norm_epsilon)
    normed = centred * scale_in
    mixed = (branch + small_params[:D] + inputs).astype(bf16)
    input_grad = cotangent.astype(f32) + scale_in * (
        normed_grad
        - jnp.mean(normed_grad, -1, keepdims=True)
        - normed * jnp.mean(normed_grad * normed, -1, keepdims=True)
    )

    small_here = late[rows_here : rows_here + extra, :128] + late[rows_here + extra : rows_here + 2 * extra, :128]
    late = late[:rows_here]
    squares = jnp.sum(early * early) + jnp.sum(late * late)
    message = jnp.concatenate(
        [small_here, jnp.zeros((7 - extra, 128), f32), jnp.broadcast_to(squares, (1, 128))], axis=0
    )
    n_all = n_dp * n_head
    heard = lax.all_to_all(jnp.broadcast_to(message, (n_all, 8, 128)), ("dp", "head"), 0, 0, tiled=True)
    heard = heard.reshape(n_dp, n_head, 8, 128)
    small_sum = jnp.sum(heard[:, :, :extra], axis=1).reshape(-1)[:length]
    grad_small = jnp.concatenate(
        [small_sum[: D + group], jnp.zeros((POS - group,), f32), small_sum[D + group :]]
    )
    total = jnp.sum(heard[:, :, 7, 0]) + jnp.sum(small_sum * small_sum)
    grad_norm = jnp.sqrt(total)
    factor = jnp.minimum(1.0, clip_norm / (grad_norm + 1e-06))
    grad_out = early[:, width:].T
    grad_proj = jnp.concatenate([early[:, :width], late], axis=1).reshape(rows_here, 4, width)
    new_proj, mean_proj, square_proj = adam_step(
        proj_weight, grad_proj, proj_mean, proj_square, factor, rate_matrix, decay_matrix
    )
    new_out, mean_out, square_out = adam_step(
        out_weight, grad_out, out_mean, out_square, factor, rate_matrix, decay_matrix
    )
    new_small, mean_small, square_small = adam_step(
        small_params, grad_small, small_mean, small_square, factor, rate_small, 0.0
    )
    return (
        mixed,
        input_grad,
        grad_proj,
        grad_out,
        grad_small,
        grad_norm,
        new_proj,
        mean_proj,
        square_proj,
        new_out,
        mean_out,
        square_out,
        new_small,
        mean_small,
        square_small,
    )


def solution(mesh):
    in_specs = (
        P(("dp", "head"), None),
        P(("dp", "head"), None),
        P("dp"),
        P("dp"),
        P("dp", None, "head"),
        P("head", "dp"),
        P(),
        P("dp", None, "head"),
        P("dp", None, "head"),
        P("head", "dp"),
        P("head", "dp"),
        P(),
        P(),
    )
    out_specs = (
        P(("dp", "head"), None),
        P(("dp", "head"), None),
        P("dp", None, "head"),
        P("head", "dp"),
        P(),
        P(),
        P("dp", None, "head"),
        P("dp", None, "head"),
        P("dp", None, "head"),
        P("head", "dp"),
        P("head", "dp"),
        P("head", "dp"),
        P(),
        P(),
        P(),
    )
    return jax.shard_map(shards, mesh=mesh, in_specs=in_specs, out_specs=out_specs, check_vma=False)
```

```python
import functools
import math

import jax
import jax.numpy as jnp
from jax import lax
from jax.experimental import pallas as pl
from jax.experimental.pallas import tpu as pltpu
from jax.sharding import PartitionSpec as P

D = 512
HEAD_DIM = 64
HD = 512
POS = 8192
NTB = 128
STEP = 10
TILE = 256
NEG = -1e9

norm_epsilon = 1e-06
adam_epsilon = 1e-08
beta_one = 0.9
beta_two = 0.999
clip_norm = 1.0
rate_matrix = 0.05
rate_small = 0.3
decay_matrix = 0.1

f32 = jnp.float32
bf16 = jnp.bfloat16
VMEM = pl.BlockSpec(memory_space=pltpu.VMEM)
SMEM = pl.BlockSpec(memory_space=pltpu.SMEM)


def adam_step(weight, grad, first, second, factor, rate, decay):
    clipped = grad * factor
    first_new = beta_one * first + (1.0 - beta_one) * clipped
    second_new = beta_two * second + (1.0 - beta_two) * clipped * clipped
    update = (
        first_new
        / (1.0 - beta_one**STEP)
        / (jnp.sqrt(second_new / (1.0 - beta_two**STEP)) + adam_epsilon)
    )
    return (weight - rate * (update + decay * weight), first_new, second_new)


def swap(x, axis, k):
    n = lax.axis_size(axis)
    return lax.ppermute(x, axis, [(i, i ^ k) for i in range(n)])


def gather_head(x):
    n = lax.axis_size("head")
    pieces = [x] + [None] * (n - 1)
    for k in range(2, n, 2):
        pieces[k] = swap(x, "head", k)
    pieces[1] = swap(x, "head", 1)
    for k in range(2, n, 2):
        pieces[k + 1] = swap(pieces[k], "head", 1)
    return pieces


def gather_direct(x):
    return [x] + [swap(x, "head", k) for k in range(1, lax.axis_size("head"))]


def after_all(arrays, other):
    return lax.optimization_barrier((*arrays, other))[:-1]


def after(x, *others):
    return lax.optimization_barrier((x,) + others)[0]


def gather_dp(x):
    n = lax.axis_size("dp")
    arrays, offsets, operands = [x], [[0]], []
    k = n // 2
    while k:
        operand = jnp.concatenate(arrays, 0) if len(arrays) > 1 else x
        operands.append(operand)
        arrays.append(swap(operand, "dp", k))
        offsets.append([o ^ k for group in offsets for o in group])
        k //= 2
    return arrays, offsets, operands


def split_dp(n):
    low = 2 ** ((n.bit_length() - 1) // 2)
    return n // low, low


def add_parts(own, received):
    total = own.astype(f32)
    for part in received:
        total = total + part.astype(f32)
    return total


def send_high(total):
    high, low = split_dp(lax.axis_size("dp"))
    row = lax.axis_index("dp") // low
    narrow = total.astype(bf16)
    blocks = [lax.dynamic_index_in_dim(total, row, 0, False)]
    for k in range(1, high):
        sent = lax.dynamic_index_in_dim(narrow, row ^ k, 0, False)
        blocks.append(swap(sent, "dp", k * low))
    return blocks


def scatter_core(keep, send, behind):
    return keep.astype(f32) + after(swap(send, "head", 1), behind).astype(f32)


def scatter_chip(total):
    n = lax.axis_size("head")
    chip = lax.axis_index("head") // 2
    narrow = total.astype(bf16)
    mine = lax.dynamic_index_in_dim(total, chip, 0, False)
    for k in range(1, n // 2):
        sent = lax.dynamic_index_in_dim(narrow, chip ^ k, 0, False)
        mine = mine + swap(sent, "head", 2 * k).astype(f32)
    return mine


def dot(a, b):
    return lax.dot_general(a, b, (((1,), (0,)), ((), ())), preferred_element_type=f32)


def dot_nt(a, b):
    return lax.dot_general(a, b, (((1,), (1,)), ((), ())), preferred_element_type=f32)


def flip(a):
    return jnp.transpose(a.astype(f32))


def lanes(i):
    return pl.ds(pl.multiple_of(i * TILE, TILE), TILE)


def by_head(block, heads):
    zero = jnp.zeros((HEAD_DIM, block.shape[1]), block.dtype)
    return jnp.concatenate(
        [
            jnp.concatenate(
                [block[g * HEAD_DIM : (g + 1) * HEAD_DIM] if g == h else zero for g in range(heads)], axis=0
            )
            for h in range(heads)
        ],
        axis=1,
    )


def own_rows(block, heads):
    return jnp.concatenate(
        [block[h * HEAD_DIM : (h + 1) * HEAD_DIM, h * TILE : (h + 1) * TILE] for h in range(heads)], axis=0
    )


def own_lanes(block, heads):
    lane = lax.broadcasted_iota(jnp.int32, block.shape, 1) // HEAD_DIM
    return jnp.concatenate([jnp.where(lane == h, block, jnp.zeros_like(block)) for h in range(heads)], axis=0)


def diagonals(x):
    rows, cols = x.shape
    z = jnp.concatenate([x, jnp.zeros((rows, cols), f32)], axis=1)
    total = z[:8]
    for q in range(1, rows // 8):
        total = total + pltpu.roll(z[8 * q : 8 * q + 8], 2 * cols - 8 * q, 1)
    g = total[0:1]
    for r in range(1, 8):
        g = g + pltpu.roll(total, 2 * cols - r, 1)[r : r + 1]
    return g


def cast_kernel(w_ref, o_ref, low_ref):
    width = o_ref.shape[1]
    for c in range(4):
        low_ref[:, c * width : (c + 1) * width] = w_ref[:, c, :].astype(bf16)
    low_ref[:, 4 * width :] = o_ref[...].astype(bf16)


def row_lanes(ref, first, count):
    return jnp.concatenate([ref[first + k : first + k + 1, :] for k in range(count)], axis=1)


def prepare_kernel(tb_ref, small_ref, pos_ref, oh_ref, oht_ref, trow_ref):
    nb = pos_ref.shape[0]
    for d in range(nb):
        here = row_lanes(small_ref, D // 128 + d * TILE // 128, TILE // 128)
        before = here if d == 0 else row_lanes(small_ref, D // 128 + (d - 1) * TILE // 128, TILE // 128)
        row = jnp.concatenate([here, before], axis=1) * 0.5
        tile = pltpu.roll(
            jnp.broadcast_to(row, (TILE, 2 * TILE)), 0, 1, stride=1, stride_axis=0
        )[:, :TILE]
        if d == 0:
            b = lax.broadcasted_iota(jnp.int32, (TILE, TILE), 0)
            a = lax.broadcasted_iota(jnp.int32, (TILE, TILE), 1)
            tile = jnp.where(b <= a, tile, NEG)
        pos_ref[d] = tile
    table = row_lanes(small_ref, (D + POS) // 128, NTB // 128)
    row = jnp.concatenate([table, table], axis=1)
    upper = pltpu.roll(jnp.broadcast_to(row, (NTB, 2 * NTB)), 0, 1, stride=1, stride_axis=0)[:, :NTB]
    a = lax.broadcasted_iota(jnp.int32, (NTB, NTB), 0)
    b = lax.broadcasted_iota(jnp.int32, (NTB, NTB), 1)
    upper = jnp.where(b >= a, upper, 0.0)
    square = (jnp.where(b > a, upper, jnp.transpose(upper)) * 0.5).astype(bf16)

    def block(i, _):
        onehot = (lax.broadcasted_iota(jnp.int32, (NTB, TILE), 0) == tb_ref[:, lanes(i)]).astype(f32)
        low = onehot.astype(bf16)
        oht_ref[i] = low
        oh_ref[i] = flip(onehot).astype(bf16)
        trow_ref[i] = dot(square, low).astype(bf16)
        return 0

    lax.fori_loop(0, nb, block, 0)


def forward_kernel(heads, n_head, offsets, first_ref, *refs):
    refs = list(refs)
    take = lambda count: [refs.pop(0) for _ in range(count)]
    x_pieces, w_pieces = take(n_head), take(len(offsets))
    oh_ref, oht_ref, trow_ref, pos_ref, ss_ref = take(5)
    attn_ref, xn_ref, d_ref, kx_ref, kxt_ref, qxt_ref, v_ref, qm_ref, wt_ref = take(9)
    w_ref, vt_ref, acc_ref = refs
    nb, width = attn_ref.shape[0], attn_ref.shape[1]
    per = x_pieces[0].shape[0] // TILE
    for piece, group in zip(w_pieces, offsets):
        rows = piece.shape[0] // len(group)
        for at, offset in enumerate(group):
            start = pl.multiple_of((lax.axis_index("dp") ^ offset) * rows, 16)
            w_ref[pl.ds(start, rows), :] = piece[at * rows : (at + 1) * rows, :]
    wt_ref[...] = flip(w_ref[...]).astype(bf16)

    def project(i, x):
        x = x.astype(f32)
        x = x - jnp.sum(x, axis=1, keepdims=True) / D
        x = (x * lax.rsqrt(jnp.sum(x * x, axis=1, keepdims=True) / D + norm_epsilon)).astype(bf16)
        xn_ref[i] = x
        p = dot_nt(wt_ref[width : 4 * width], x)
        sg = 0.5 + 0.5 * jnp.tanh(0.5 * p)
        act = p * sg
        d_ref[i] = sg + act * (1.0 - sg)
        vt = act[:width]
        vt_ref[i] = vt.astype(bf16)
        v_ref[i] = flip(vt).astype(bf16)
        qt = act[width : 2 * width].astype(bf16)
        kt = act[2 * width :]
        kxt_ref[i, :NTB] = oht_ref[i]
        kxt_ref[i, NTB:] = kt.astype(bf16)
        kx_ref[i, :, :NTB] = oh_ref[i]
        kx_ref[i, :, NTB:] = flip(kt).astype(bf16)
        qs = (qt.astype(f32) * (0.5 / math.sqrt(HEAD_DIM))).astype(bf16)
        qxt_ref[i, :NTB] = jnp.concatenate([trow_ref[i]] * heads, axis=1)
        qxt_ref[i, NTB:] = by_head(qs, heads)
        qm_ref[i] = own_lanes(flip(qt).astype(bf16), heads)

    for k, piece in enumerate(x_pieces):
        for r in range(per):
            project((lax.axis_index("head") ^ k) * per + r, piece[r * TILE : (r + 1) * TILE, :])
    key_index = lax.broadcasted_iota(jnp.int32, (TILE, TILE), 0)

    def rows(i, _):
        acc_ref[...] = jnp.zeros_like(acc_ref)
        start = ss_ref[:, lanes(i)]

        def cols(j, _):
            s = dot(kx_ref[j], qxt_ref[i]) + jnp.concatenate([pos_ref[i - j]] * heads, axis=1)
            seen = (key_index + j * TILE) >= start
            s = jnp.where(jnp.concatenate([seen] * heads, axis=1), s, NEG)
            w = (s + s * jnp.tanh(s)).astype(bf16)
            acc_ref[...] += dot(vt_ref[j], w)
            return 0

        lax.fori_loop(first_ref[i * TILE] // TILE, i + 1, cols, 0)
        attn_ref[i] = own_rows(acc_ref[...], heads)
        return 0

    lax.fori_loop(0, nb, rows, 0)


def gate_kernel(n_head, *refs):
    refs = list(refs)
    take = lambda count: [refs.pop(0) for _ in range(count)]
    cot_pieces = take(n_head)
    attn_ref, xn_ref, wt_ref = take(3)
    p_ref, gg_ref, stat_ref, gb_ref = refs
    width = attn_ref.shape[1]
    per = cot_pieces[0].shape[0] // TILE
    gb_ref[...] = jnp.sum(cot_pieces[0][...].astype(f32), axis=0, keepdims=True)
    for k, piece in enumerate(cot_pieces):
        for r in range(per):
            i = (lax.axis_index("head") ^ k) * per + r
            p = dot_nt(wt_ref[:width], xn_ref[i])
            gate = p * (0.5 + 0.5 * jnp.tanh(0.5 * p))
            gg = dot_nt(wt_ref[4 * width :], piece[r * TILE : (r + 1) * TILE, :])
            grad = gg * gate
            p_ref[i] = p
            gg_ref[i] = gg
            at = attn_ref[i]
            mean = jnp.sum(at, axis=0, keepdims=True) / width
            centred = at - mean
            stat_ref[i] = jnp.concatenate(
                [
                    mean,
                    jnp.sum(centred * centred, axis=0, keepdims=True),
                    jnp.sum(grad, axis=0, keepdims=True),
                    jnp.sum(grad * centred, axis=0, keepdims=True),
                ],
                axis=0,
            )


def middle_kernel(heads, n_head, *refs):
    refs = list(refs)
    take = lambda count: [refs.pop(0) for _ in range(count)]
    stats = take(n_head)
    cot_pieces = take(n_head)
    attn_ref, p_ref, gg_ref, xn_ref, wt_ref = take(5)
    branches = take(n_head)
    dax_ref, daxt_ref, gun_ref = take(3)
    parts, acc_ref, wg_ref = refs[:-2], refs[-2], refs[-1]
    width = attn_ref.shape[1]
    per = cot_pieces[0].shape[0] // TILE
    for k, piece in enumerate(cot_pieces):
        for r in range(per):
            i = (lax.axis_index("head") ^ k) * per + r
            at = slice(r * TILE, (r + 1) * TILE)
            st = [s[i] for s in stats]
            mean = sum(p[0:1] for p in st) / n_head
            spread = sum(p[1:2] + width * (p[0:1] - mean) * (p[0:1] - mean) for p in st)
            scale = lax.rsqrt(spread / HD + norm_epsilon)
            first = sum(p[2:3] for p in st) / HD
            second = scale * sum(p[3:4] + (p[0:1] - mean) * p[2:3] for p in st) / HD
            normed = (attn_ref[i] - mean) * scale
            p = p_ref[i]
            sg = 0.5 + 0.5 * jnp.tanh(0.5 * p)
            gate = p * sg
            gg = gg_ref[i]
            gated = (normed * gate).astype(bf16)
            grad = scale * (gg * gate - first - normed * second)
            dax_ref[i] = own_lanes(flip(grad).astype(bf16), heads)
            daxt_ref[i] = by_head((grad * 0.5).astype(bf16), heads)
            gu = (gg * normed * (sg + gate * (1.0 - sg))).astype(bf16)
            gun_ref[i] = flip(gu).astype(bf16)
            branches[k][at, :] = dot(flip(gated).astype(bf16), wt_ref[4 * width :]).astype(bf16)
            add_gate, add_out = dot(gu, xn_ref[i]), dot(gated, piece[at, :])
            if k + r == 0:
                acc_ref[:width] = add_gate
                acc_ref[width:] = add_out
            else:
                acc_ref[:width] += add_gate
                acc_ref[width:] += add_out
    wg_ref[...] = flip(acc_ref[...])
    send_parts(wg_ref, parts)


def send_parts(wg_ref, parts):
    low = len(parts)
    high, rows = parts[0].shape[0], parts[0].shape[1]
    me = lax.axis_index("dp") % low
    for k in range(low):
        for p in range(high):
            start = pl.multiple_of((p * low + (me ^ k)) * rows, 16)
            parts[k][p] = wg_ref[pl.ds(start, rows), :].astype(bf16)


def backward_kernel(heads, n_dp, extra, first_ref, *refs):
    refs = list(refs)
    take = lambda count: [refs.pop(0) for _ in range(count)]
    kx_ref, kxt_ref, qxt_ref, v_ref, qm_ref, dax_ref, daxt_ref, pos_ref = take(8)
    d_ref, xn_ref, ss_ref, gb_ref = take(4)
    gp_ref = refs.pop(0)
    parts = take(split_dp(n_dp)[1])
    accv_ref, acck_ref, accq_ref, posg_ref, m2_ref, gpq_ref, acc_ref, wg_ref, small_ref = refs
    nb, width = v_ref.shape[0], v_ref.shape[2]
    accv_ref[...] = jnp.zeros_like(accv_ref)
    acck_ref[...] = jnp.zeros_like(acck_ref)
    posg_ref[...] = jnp.zeros_like(posg_ref)
    m2_ref[...] = jnp.zeros_like(m2_ref)
    key_index = lax.broadcasted_iota(jnp.int32, (TILE, TILE), 0)
    factor = 1.0 / math.sqrt(HEAD_DIM)

    def rows(i, _):
        accq_ref[...] = jnp.zeros_like(accq_ref)
        start = ss_ref[:, lanes(i)]

        def cols(j, _):
            s = dot(kx_ref[j], qxt_ref[i]) + jnp.concatenate([pos_ref[i - j]] * heads, axis=1)
            seen = (key_index + j * TILE) >= start
            s = jnp.where(jnp.concatenate([seen] * heads, axis=1), s, NEG)
            t = jnp.tanh(s)
            u = 1.0 + t
            w = s * u
            ds = dot(v_ref[j], daxt_ref[i]) * (u + w * (1.0 - t))
            low = ds.astype(bf16)
            accv_ref[j] += dot(w.astype(bf16), dax_ref[i])
            acck_ref[j] += dot(low, qm_ref[i])
            accq_ref[...] += dot(kxt_ref[j], low)
            posg_ref[i - j] += sum(ds[:, h * TILE : (h + 1) * TILE] for h in range(heads))
            return 0

        lax.fori_loop(first_ref[i * TILE] // TILE, i + 1, cols, 0)
        gpq_ref[i] = own_rows(accq_ref[NTB:], heads)
        tp = sum(accq_ref[:NTB, h * TILE : (h + 1) * TILE] for h in range(heads))
        high = tp.astype(bf16)
        rest = (tp - high.astype(f32)).astype(bf16)
        onehot = kx_ref[i, :, :NTB]
        m2_ref[...] += dot(high, onehot) + dot(rest, onehot)
        return 0

    lax.fori_loop(0, nb, rows, 0)
    acc_ref[...] = jnp.zeros_like(acc_ref)

    def tail(i, _):
        gp = jnp.concatenate([flip(accv_ref[i]), gpq_ref[i] * factor, flip(acck_ref[i]) * factor], axis=0)
        gp = (gp * d_ref[i]).astype(bf16)
        gp_ref[i] = flip(gp).astype(bf16)
        acc_ref[...] += dot(gp, xn_ref[i])
        return 0

    lax.fori_loop(0, nb, tail, 0)
    small_ref[...] = jnp.zeros_like(small_ref)
    small_ref[:, :D] = gb_ref[...]
    for d in range(nb):
        g = diagonals(posg_ref[d])
        small_ref[:, D + d * TILE : D + (d + 1) * TILE] += g[:, :TILE]
        if d > 0:
            small_ref[:, D + (d - 1) * TILE : D + d * TILE] += g[:, TILE:]
    m2 = m2_ref[...]
    g = diagonals(m2 + jnp.transpose(m2))[:, :NTB]
    zero = lax.broadcasted_iota(jnp.int32, (1, NTB), 1) == 0
    at = D + nb * TILE
    small_ref[:, at : at + NTB] = jnp.where(zero, 0.5 * g, g)
    step = D // n_dp
    grads = flip(acc_ref[...])
    for p in range(n_dp):
        here = jnp.concatenate(
            [small_ref[:, (p * extra + r) * 128 : (p * extra + r + 1) * 128] for r in range(extra)], axis=0
        )
        high = here.astype(bf16).astype(f32)
        block = jnp.concatenate([high, here - high, jnp.zeros((16 - 2 * extra, 128), f32)], axis=0)
        wg_ref[p * (step + 16) : p * (step + 16) + step] = grads[p * step : (p + 1) * step]
        wg_ref[p * (step + 16) + step : (p + 1) * (step + 16)] = jnp.concatenate(
            [block, jnp.zeros((16, 3 * width - 128), f32)], axis=1
        )
    send_parts(wg_ref, parts)


def input_kernel(n_head, gp_ref, gun_ref, wt_ref, keep, send):
    width = gun_ref.shape[2]
    per = keep.shape[1] // TILE
    for k in range(n_head):
        device = lax.axis_index("head") ^ k
        target = (keep, send)[k % 2]
        for r in range(per):
            i = device * per + r
            rows = dot(gp_ref[i], wt_ref[width : 4 * width]) + dot(gun_ref[i], wt_ref[:width])
            target[device // 2, r * TILE : (r + 1) * TILE] = rows.astype(bf16)


def collect_kernel(high, extra, *refs):
    blocks, (grads_ref, message_ref) = refs[:high], refs[high:]
    total = blocks[0][...]
    for k in range(1, high):
        total = total + blocks[k][...].astype(f32)
    rows = grads_ref.shape[0]
    grads = total[:rows]
    grads_ref[...] = grads
    squares = jnp.sum(jnp.sum(grads * grads, axis=0, keepdims=True), axis=1, keepdims=True)
    message = jnp.concatenate(
        [
            total[rows : rows + extra, :128] + total[rows + extra : rows + 2 * extra, :128],
            jnp.zeros((7 - extra, 128), f32),
            jnp.broadcast_to(squares, (1, 128)),
        ],
        axis=0,
    )
    for k in range(message_ref.shape[0]):
        message_ref[k] = message


def update_kernel(n_head, extra, group, heard_ref, grads_ref, *refs):
    state, outs = refs[:9], refs[9:]
    grad_proj_ref, grad_out_ref, grad_small_ref, norm_ref = outs[:4]
    n_all = heard_ref.shape[0]
    width = grad_out_ref.shape[1]
    lead, pos_rows, used = D // 128, POS // 128, (D + group) // 128
    grad_small_ref[...] = jnp.zeros_like(grad_small_ref)
    squares = heard_ref[0, 7:8, :]
    for k in range(1, n_all):
        squares = squares + heard_ref[k, 7:8, :]
    for p in range(n_all // n_head):
        rows = heard_ref[p * n_head, :extra, :]
        for h in range(1, n_head):
            rows = rows + heard_ref[p * n_head + h, :extra, :]
        for r in range(extra):
            at = p * extra + r
            if at < used:
                grad_small_ref[at : at + 1, :] = rows[r : r + 1]
            elif at == used:
                grad_small_ref[lead + pos_rows : lead + pos_rows + 1, :] = rows[r : r + 1]
    small = grad_small_ref[...]
    total = jnp.sum(jnp.sum(small * small, axis=0, keepdims=True), axis=1, keepdims=True) + squares[:, :1]
    norm = jnp.sqrt(total)
    norm_ref[...] = norm
    factor = jnp.minimum(1.0, clip_norm / (norm + 1e-06))

    def update(get, put, grad, rate, decay):
        for k, value in enumerate(adam_step(get(0), grad, get(1), get(2), factor, rate, decay)):
            put(k, value)

    for c in range(4):
        grad = grads_ref[:, 3 * width : 4 * width] if c == 0 else grads_ref[:, (c - 1) * width : c * width]
        grad_proj_ref[:, c, :] = grad

        def put(k, value):
            outs[4 + k][:, c, :] = value

        update(lambda k: state[k][:, c, :], put, grad, rate_matrix, decay_matrix)
    grad = grads_ref[:, 4 * width :]
    grad_out_ref[...] = grad

    def put_out(k, value):
        outs[7 + k][...] = value

    update(lambda k: state[3 + k][...], put_out, grad, rate_matrix, decay_matrix)

    def put_small(k, value):
        outs[10 + k][...] = value

    update(lambda k: state[6 + k][...], put_small, small, rate_small, 0.0)


def call(kernel, name, in_specs, outs, scratch, us, room=20):
    return pl.pallas_call(
        kernel,
        out_shape=[jax.ShapeDtypeStruct(shape, dtype) for shape, dtype, _ in outs],
        in_specs=in_specs,
        out_specs=[spec for _, _, spec in outs],
        scratch_shapes=scratch,
        compiler_params=pltpu.CompilerParams(vmem_limit_bytes=room * 2**20),
        cost_estimate=pl.CostEstimate(flops=int(us * 1e9), bytes_accessed=int(us * 3e6), transcendentals=0),
        name=name,
    )


def block(shape):
    return pl.BlockSpec((1,) + tuple(shape[1:]), lambda i: (i,) + (0,) * (len(shape) - 1))


def shards(
    tokens,
    cotangent,
    seq_start,
    time_bucket,
    proj_weight,
    out_weight,
    small_params,
    proj_mean,
    proj_square,
    out_mean,
    out_square,
    small_mean,
    small_square,
):
    n_head = lax.axis_size("head")
    n_dp = lax.axis_size("dp")
    here = tokens.shape[0]
    group = here * n_head
    nb = group // TILE
    per = here // TILE
    rows_here, _, width = proj_weight.shape
    heads = width // HEAD_DIM
    high, low = split_dp(n_dp)

    (weights,) = call(
        cast_kernel, "cast", [VMEM] * 2, [((rows_here, 5 * width), bf16, VMEM)], [], 1
    )(proj_weight, out_weight.T)
    x_pieces = gather_head(tokens)
    w_pieces, offsets, operands = gather_dp(weights)
    cot_pieces = gather_direct(after(cotangent, operands[-1]))
    starts = seq_start.reshape(1, group)
    small_rows = small_params.reshape(-1, 128)
    times = time_bucket.reshape(1, group)

    pos, oh, oht, trow = call(
        prepare_kernel,
        "prepare",
        [VMEM] * 2,
        [
            ((nb, TILE, TILE), f32, VMEM),
            ((nb, TILE, NTB), bf16, VMEM),
            ((nb, NTB, TILE), bf16, VMEM),
            ((nb, NTB, TILE), bf16, VMEM),
        ],
        [],
        5,
    )(after(times, operands[1]), small_rows)

    items = [
        ((nb, width, TILE), f32),
        ((nb, TILE, D), bf16),
        ((nb, 3 * width, TILE), f32),
        ((nb, TILE, NTB + width), bf16),
        ((nb, NTB + width, TILE), bf16),
        ((nb, NTB + width, heads * TILE), bf16),
        ((nb, TILE, width), bf16),
        ((nb, heads * TILE, width), bf16),
        ((5 * width, D), bf16),
    ]
    attn, xn, dsilu, kx, kxt, qxt, v, qm, wt = call(
        functools.partial(forward_kernel, heads, n_head, offsets),
        "forward",
        [SMEM] + [VMEM] * (n_head + len(w_pieces) + 5),
        [item + (VMEM,) for item in items],
        [
            pltpu.VMEM((D, 5 * width), bf16),
            pltpu.VMEM((nb, width, TILE), bf16),
            pltpu.VMEM((width, heads * TILE), f32),
        ],
        30,
    )(seq_start, *x_pieces, *w_pieces, oh, oht, trow, pos, starts)

    column = ((nb, width, TILE), f32, VMEM)
    p_gate, gg, stat, gb = call(
        functools.partial(gate_kernel, n_head),
        "gate",
        [VMEM] * (n_head + 3),
        [column, column, ((nb, 4, TILE), f32, VMEM), ((1, D), f32, VMEM)],
        [],
        5,
    )(*cot_pieces, attn, xn, wt)

    stats = [stat] + [swap(stat, "head", k) for k in range(1, n_head)]
    out = call(
        functools.partial(middle_kernel, heads, n_head),
        "middle",
        [VMEM] * (2 * n_head + 5),
        [((here, D), bf16, VMEM)] * n_head
        + [
            ((nb, heads * TILE, width), bf16, VMEM),
            ((nb, width, heads * TILE), bf16, VMEM),
            ((nb, TILE, width), bf16, VMEM),
        ]
        + [((high, rows_here, 2 * width), bf16, VMEM)] * low,
        [pltpu.VMEM((2 * width, D), f32), pltpu.VMEM((D, 2 * width), f32)],
        6,
    )(*stats, *cot_pieces, attn, p_gate, gg, xn, wt)
    branches, (dax, daxt, gun), early_parts = out[:n_head], out[n_head : n_head + 3], out[n_head + 3 :]
    received = [swap(branches[k], "head", k) for k in range(1, n_head)]
    early_received = [swap(early_parts[k], "dp", k) for k in range(1, low)]

    length = D + group + NTB
    extra = -(-length // (128 * n_dp))
    gp, *late_parts = call(
        functools.partial(backward_kernel, heads, n_dp, extra),
        "backward",
        [SMEM] + [VMEM] * 12,
        [((nb, TILE, 3 * width), bf16, VMEM)] + [((high, rows_here + 16, 3 * width), bf16, VMEM)] * low,
        [
            pltpu.VMEM((nb, TILE, width), f32),
            pltpu.VMEM((nb, TILE, width), f32),
            pltpu.VMEM((NTB + width, heads * TILE), f32),
            pltpu.VMEM((nb, TILE, TILE), f32),
            pltpu.VMEM((NTB, NTB), f32),
            pltpu.VMEM((nb, width, TILE), f32),
            pltpu.VMEM((3 * width, D), f32),
            pltpu.VMEM((n_dp * (rows_here + 16), 3 * width), f32),
            pltpu.VMEM((1, extra * n_dp * 128), f32),
        ],
        35,
        24,
    )(seq_start, kx, kxt, qxt, v, qm, dax, daxt, pos, dsilu, xn, starts, gb)

    tied = lax.optimization_barrier((gp, *late_parts, *received, *early_received))
    gp, late_parts = tied[0], tied[1 : 1 + low]
    received, early_received = tied[1 + low : low + n_head], tied[low + n_head :]
    late_received = [swap(late_parts[k], "dp", k) for k in range(1, low)]
    early = add_parts(early_parts[0], early_received)
    keep, send = call(
        functools.partial(input_kernel, n_head),
        "input_rows",
        [VMEM] * 3,
        [((n_head // 2, here, D), bf16, VMEM)] * 2,
        [],
        4,
    )(gp, gun, wt)
    late_received = after_all(late_received, send)
    late = add_parts(late_parts[0], late_received)
    both = jnp.concatenate([late, jnp.pad(early, ((0, 0), (0, 16), (0, 0)))], axis=2)
    blocks = send_high(both)
    rows_total = scatter_core(keep, send, both)
    blocks[0] = after(blocks[0], rows_total)
    n_all = n_dp * n_head
    grads_shape = ((rows_here, 5 * width), f32)
    grads, message = call(
        functools.partial(collect_kernel, high, extra),
        "collect",
        [VMEM] * high,
        [grads_shape + (VMEM,), ((n_all, 8, 128), f32, VMEM)],
        [],
        0.1,
    )(*blocks)
    message, rows_total = lax.optimization_barrier((message, rows_total))
    heard = lax.all_to_all(message, ("dp", "head"), 0, 0, tiled=True)
    normed_grad = scatter_chip(rows_total)
    mixed = (add_parts(branches[0], after_all(received, message)) + small_params[:D] + tokens.astype(f32)).astype(bf16)

    inputs = tokens.astype(f32)
    centred = inputs - jnp.mean(inputs, -1, keepdims=True)
    scale_in = lax.rsqrt(jnp.mean(centred * centred, -1, keepdims=True) + norm_epsilon)
    normed = centred * scale_in
    input_grad = cotangent.astype(f32) + scale_in * (
        normed_grad
        - jnp.mean(normed_grad, -1, keepdims=True)
        - normed * jnp.mean(normed_grad * normed, -1, keepdims=True)
    )

    state = [proj_weight, proj_mean, proj_square, out_weight.T, out_mean.T, out_square.T]
    state += [x.reshape(-1, 128) for x in (small_params, small_mean, small_square)]
    proj_shape, out_shape, small_shape = proj_weight.shape, (rows_here, width), small_rows.shape
    shapes = [proj_shape, out_shape, small_shape, (1, 1)] + [proj_shape] * 3 + [out_shape] * 3 + [small_shape] * 3
    results = call(
        functools.partial(update_kernel, n_head, extra, group),
        "update",
        [VMEM] * (2 + len(state)),
        [(shape, f32, VMEM) for shape in shapes],
        [],
        0.1,
    )(heard, grads, *state)
    grad_proj, grad_out, grad_small, grad_norm = results[:4]
    grad_out, grad_small, grad_norm = grad_out.T, grad_small.reshape(-1), grad_norm.reshape(())
    new_proj, mean_proj, square_proj = results[4:7]
    new_out, mean_out, square_out = [x.T for x in results[7:10]]
    new_small, mean_small, square_small = [x.reshape(-1) for x in results[10:13]]
    return (
        mixed,
        input_grad,
        grad_proj,
        grad_out,
        grad_small,
        grad_norm,
        new_proj,
        mean_proj,
        square_proj,
        new_out,
        mean_out,
        square_out,
        new_small,
        mean_small,
        square_small,
    )


def solution(mesh):
    in_specs = (
        P(("dp", "head"), None),
        P(("dp", "head"), None),
        P("dp"),
        P("dp"),
        P("dp", None, "head"),
        P("head", "dp"),
        P(),
        P("dp", None, "head"),
        P("dp", None, "head"),
        P("head", "dp"),
        P("head", "dp"),
        P(),
        P(),
    )
    out_specs = (
        P(("dp", "head"), None),
        P(("dp", "head"), None),
        P("dp", None, "head"),
        P("head", "dp"),
        P(),
        P(),
        P("dp", None, "head"),
        P("dp", None, "head"),
        P("dp", None, "head"),
        P("head", "dp"),
        P("head", "dp"),
        P("head", "dp"),
        P(),
        P(),
        P(),
    )
    return jax.shard_map(shards, mesh=mesh, in_specs=in_specs, out_specs=out_specs, check_vma=False)
```

```python
import functools
import math

import jax
import jax.numpy as jnp
from jax import lax
from jax.experimental import pallas as pl
from jax.experimental.pallas import tpu as pltpu
from jax.sharding import PartitionSpec as P

D = 512
HEAD_DIM = 64
HD = 512
POS = 8192
NTB = 128
STEP = 10
TILE = 256
NEG = -1e9
ROOM = 24

norm_epsilon = 1e-06
adam_epsilon = 1e-08
beta_one = 0.9
beta_two = 0.999
clip_norm = 1.0
rate_matrix = 0.05
rate_small = 0.3
decay_matrix = 0.1

f32 = jnp.float32
bf16 = jnp.bfloat16
VMEM = pl.BlockSpec(memory_space=pltpu.VMEM)


def adam_step(weight, grad, first, second, factor, rate, decay):
    clipped = grad * factor
    first_new = beta_one * first + (1.0 - beta_one) * clipped
    second_new = beta_two * second + (1.0 - beta_two) * clipped * clipped
    update = (
        first_new
        / (1.0 - beta_one**STEP)
        / (jnp.sqrt(second_new / (1.0 - beta_two**STEP)) + adam_epsilon)
    )
    return (weight - rate * (update + decay * weight), first_new, second_new)


def swap(x, axis, k):
    n = lax.axis_size(axis)
    return lax.ppermute(x, axis, [(i, i ^ k) for i in range(n)])


def gather_chips(x):
    return [swap(x, "head", k) for k in range(2, lax.axis_size("head"), 2)]


def gather_cores(x, others):
    pieces = [x, swap(x, "head", 1)]
    for other in others:
        pieces += [other, swap(other, "head", 1)]
    return pieces


def after_all(arrays, *others):
    arrays = tuple(arrays)
    return lax.optimization_barrier(arrays + others)[: len(arrays)]


def after(x, *others):
    return lax.optimization_barrier((x,) + others)[0]


def gather_dp(x):
    n = lax.axis_size("dp")
    arrays, offsets, operands = [x], [[0]], []
    k = n // 2
    while k:
        operand = jnp.concatenate(arrays, 0) if len(arrays) > 1 else x
        operands.append(operand)
        arrays.append(swap(operand, "dp", k))
        offsets.append([o ^ k for group in offsets for o in group])
        k //= 2
    return arrays, offsets, operands


def split_dp(n):
    low = 2 ** ((n.bit_length() - 1) // 2)
    return n // low, low


def scatter_high(own, received, us):
    high, rows, columns = own.shape
    low = 1 + len(received)
    mine, *leaving = call(
        fold_kernel,
        "fold",
        [VMEM] * low,
        [((rows, columns), f32, VMEM)] + [((rows, columns), bf16, VMEM)] * (high - 1),
        [],
        us,
    )(own, *received)
    return [mine] + [swap(sent, "dp", (k + 1) * low) for k, sent in enumerate(leaving)]


def dot(a, b):
    return lax.dot_general(a, b, (((1,), (0,)), ((), ())), preferred_element_type=f32)


def dot_nt(a, b):
    return lax.dot_general(a, b, (((1,), (1,)), ((), ())), preferred_element_type=f32)


def flip(a):
    return jnp.transpose(a.astype(f32))


def lanes(i):
    return pl.ds(pl.multiple_of(i * TILE, TILE), TILE)


def by_head(block, heads):
    zero = jnp.zeros((HEAD_DIM, block.shape[1]), block.dtype)
    return jnp.concatenate(
        [
            jnp.concatenate(
                [block[g * HEAD_DIM : (g + 1) * HEAD_DIM] if g == h else zero for g in range(heads)], axis=0
            )
            for h in range(heads)
        ],
        axis=1,
    )


def query_columns(qs, trow, heads):
    return jnp.concatenate([jnp.concatenate([trow] * heads, axis=1), by_head(qs, heads)], axis=0)


def own_rows(block, heads):
    return jnp.concatenate(
        [block[h * HEAD_DIM : (h + 1) * HEAD_DIM, h * TILE : (h + 1) * TILE] for h in range(heads)], axis=0
    )


def own_lanes(block, heads):
    lane = lax.broadcasted_iota(jnp.int32, block.shape, 1) // HEAD_DIM
    return jnp.concatenate([jnp.where(lane == h, block, jnp.zeros_like(block)) for h in range(heads)], axis=0)


def masked(product, bias, start, j, heads):
    key = j * TILE + lax.broadcasted_iota(jnp.int32, (TILE, TILE), 0)
    seen = key >= start
    return jnp.where(
        jnp.concatenate([seen] * heads, axis=1), product + jnp.concatenate([bias] * heads, axis=1), NEG
    )


def diagonals(x):
    rows, cols = x.shape
    z = jnp.concatenate([x, jnp.zeros((rows, cols), f32)], axis=1)
    total = z[:8]
    for q in range(1, rows // 8):
        total = total + pltpu.roll(z[8 * q : 8 * q + 8], 2 * cols - 8 * q, 1)
    g = total[0:1]
    for r in range(1, 8):
        g = g + pltpu.roll(total, 2 * cols - r, 1)[r : r + 1]
    return g


def cast_kernel(w_ref, o_ref, low_ref):
    width = o_ref.shape[1]
    for c in range(4):
        low_ref[:, c * width : (c + 1) * width] = w_ref[:, c, :].astype(bf16)
    low_ref[:, 4 * width :] = o_ref[...].astype(bf16)


def row_lanes(ref, first, count):
    return jnp.concatenate([ref[first + k : first + k + 1, :] for k in range(count)], axis=1)


def prepare_kernel(tb_ref, small_ref, pos_ref, oh_ref, oht_ref, trow_ref):
    nb = pos_ref.shape[0]
    for d in range(nb):
        here = row_lanes(small_ref, D // 128 + d * TILE // 128, TILE // 128)
        before = here if d == 0 else row_lanes(small_ref, D // 128 + (d - 1) * TILE // 128, TILE // 128)
        row = jnp.concatenate([here, before], axis=1) * 0.5
        tile = pltpu.roll(
            jnp.broadcast_to(row, (TILE, 2 * TILE)), 0, 1, stride=1, stride_axis=0
        )[:, :TILE]
        if d == 0:
            b = lax.broadcasted_iota(jnp.int32, (TILE, TILE), 0)
            a = lax.broadcasted_iota(jnp.int32, (TILE, TILE), 1)
            tile = jnp.where(b <= a, tile, NEG)
        pos_ref[d] = tile
    table = row_lanes(small_ref, (D + POS) // 128, NTB // 128)
    row = jnp.concatenate([table, table], axis=1)
    upper = pltpu.roll(jnp.broadcast_to(row, (NTB, 2 * NTB)), 0, 1, stride=1, stride_axis=0)[:, :NTB]
    a = lax.broadcasted_iota(jnp.int32, (NTB, NTB), 0)
    b = lax.broadcasted_iota(jnp.int32, (NTB, NTB), 1)
    upper = jnp.where(b >= a, upper, 0.0)
    square = (jnp.where(b > a, upper, jnp.transpose(upper)) * 0.5).astype(bf16)

    def block(i, _):
        onehot = (lax.broadcasted_iota(jnp.int32, (NTB, TILE), 0) == tb_ref[:, lanes(i)]).astype(f32)
        low = onehot.astype(bf16)
        oht_ref[i] = low
        oh_ref[i] = flip(onehot).astype(bf16)
        trow_ref[i] = dot(square, low).astype(bf16)
        return 0

    lax.fori_loop(0, nb, block, 0)


def normalize_kernel(*refs):
    x_pieces, xn_ref = refs[:-1], refs[-1]
    per = x_pieces[0].shape[0] // TILE
    for k, piece in enumerate(x_pieces):
        for r in range(per):
            x = piece[r * TILE : (r + 1) * TILE, :].astype(f32)
            x = x - jnp.sum(x, axis=1, keepdims=True) / D
            x = x * lax.rsqrt(jnp.sum(x * x, axis=1, keepdims=True) / D + norm_epsilon)
            xn_ref[(lax.axis_index("head") ^ k) * per + r] = x.astype(bf16)


def assemble_kernel(offsets, *refs):
    w_pieces, (wt_ref, w_ref) = refs[:-2], refs[-2:]
    for piece, group in zip(w_pieces, offsets):
        rows = piece.shape[0] // len(group)
        for at, offset in enumerate(group):
            start = pl.multiple_of((lax.axis_index("dp") ^ offset) * rows, 16)
            w_ref[pl.ds(start, rows), :] = piece[at * rows : (at + 1) * rows, :]
    wt_ref[...] = flip(w_ref[...]).astype(bf16)


def project_kernel(heads, *refs):
    refs = list(refs)
    take = lambda count: [refs.pop(0) for _ in range(count)]
    xn_ref, wt_ref, oh_ref, oht_ref = take(4)
    d_ref, kx_ref, kxt_ref, qs_ref, q_ref, v_ref, vt_ref = refs
    width = v_ref.shape[2]

    def project(i):
        x = xn_ref[i]
        p = dot_nt(wt_ref[width : 4 * width], x)
        sg = 0.5 + 0.5 * jnp.tanh(0.5 * p)
        act = p * sg
        d_ref[i] = (sg + act * (1.0 - sg)).astype(bf16)
        vt = act[:width]
        vt_ref[i] = vt.astype(bf16)
        v_ref[i] = flip(vt).astype(bf16)
        qt = act[width : 2 * width].astype(bf16)
        kt = act[2 * width :]
        kxt_ref[i, :NTB] = oht_ref[i]
        kxt_ref[i, NTB:] = kt.astype(bf16)
        kx_ref[i, :, :NTB] = oh_ref[i]
        kx_ref[i, :, NTB:] = flip(kt).astype(bf16)
        qs = (qt.astype(f32) * (0.5 / math.sqrt(HEAD_DIM))).astype(bf16)
        qs_ref[i] = qs
        q_ref[i] = flip(qt).astype(bf16)

    for i in range(xn_ref.shape[0]):
        project(i)

def attend_kernel(heads, first, last, *refs):
    if first:
        before_ref, refs = refs[0], refs[1:]
    kx_ref, qs_ref, trow_ref, vt_ref, pos_ref, ss_ref, attn_ref = refs
    if first:
        attn_ref[:first] = before_ref[...]
    for i in range(first, last):
        queries = query_columns(qs_ref[i], trow_ref[i], heads)
        scores = [dot(kx_ref[j], queries) for j in range(i + 1)]
        weights = []
        for j in range(i + 1):
            h = masked(scores[j], pos_ref[i - j], ss_ref[:, i * TILE : (i + 1) * TILE], j, heads)
            weights.append((h + h * jnp.tanh(h)).astype(bf16))
        total = dot(vt_ref[0], weights[0])
        for j in range(1, i + 1):
            total = total + dot(vt_ref[j], weights[j])
        attn_ref[i] = own_rows(total, heads)


def gate_kernel(n_head, *refs):
    refs = list(refs)
    take = lambda count: [refs.pop(0) for _ in range(count)]
    cot_pieces = take(n_head)
    attn_ref, xn_ref, wt_ref = take(3)
    p_ref, gg_ref, stat_ref, gb_ref = refs
    width = attn_ref.shape[1]
    per = cot_pieces[0].shape[0] // TILE
    gb_ref[...] = jnp.sum(cot_pieces[0][...].astype(f32), axis=0, keepdims=True)
    for k, piece in enumerate(cot_pieces):
        for r in range(per):
            i = (lax.axis_index("head") ^ k) * per + r
            p = dot_nt(wt_ref[:width], xn_ref[i])
            gate = p * (0.5 + 0.5 * jnp.tanh(0.5 * p))
            gg = dot_nt(wt_ref[4 * width :], piece[r * TILE : (r + 1) * TILE, :])
            grad = gg * gate
            p_ref[i] = p
            gg_ref[i] = gg
            at = attn_ref[i]
            mean = jnp.sum(at, axis=0, keepdims=True) / width
            centred = at - mean
            stat_ref[i] = jnp.concatenate(
                [
                    mean,
                    jnp.sum(centred * centred, axis=0, keepdims=True),
                    jnp.sum(grad, axis=0, keepdims=True),
                    jnp.sum(grad * centred, axis=0, keepdims=True),
                ],
                axis=0,
            )


def middle_kernel(n_head, *refs):
    refs = list(refs)
    take = lambda count: [refs.pop(0) for _ in range(count)]
    stats = take(n_head)
    cot_pieces = take(n_head)
    attn_ref, p_ref, gg_ref, xn_ref, wt_ref = take(5)
    branches = take(n_head)
    da_ref, dat_ref, gun_ref = take(3)
    parts, acc_ref, wg_ref = refs[:-2], refs[-2], refs[-1]
    width = attn_ref.shape[1]
    per = cot_pieces[0].shape[0] // TILE
    for k, piece in enumerate(cot_pieces):
        for r in range(per):
            i = (lax.axis_index("head") ^ k) * per + r
            at = slice(r * TILE, (r + 1) * TILE)
            st = [s[i] for s in stats]
            mean = sum(p[0:1] for p in st) / n_head
            spread = sum(p[1:2] + width * (p[0:1] - mean) * (p[0:1] - mean) for p in st)
            scale = lax.rsqrt(spread / HD + norm_epsilon)
            first = sum(p[2:3] for p in st) / HD
            second = scale * sum(p[3:4] + (p[0:1] - mean) * p[2:3] for p in st) / HD
            normed = (attn_ref[i] - mean) * scale
            p = p_ref[i]
            sg = 0.5 + 0.5 * jnp.tanh(0.5 * p)
            gate = p * sg
            gg = gg_ref[i]
            gated = (normed * gate).astype(bf16)
            grad = scale * (gg * gate - first - normed * second)
            da_ref[i] = flip(grad).astype(bf16)
            dat_ref[i] = (grad * 0.5).astype(bf16)
            gu = (gg * normed * (sg + gate * (1.0 - sg))).astype(bf16)
            gun_ref[i] = flip(gu).astype(bf16)
            branches[k][at, :] = dot(flip(gated).astype(bf16), wt_ref[4 * width :]).astype(bf16)
            add_gate, add_out = dot(gu, xn_ref[i]), dot(gated, piece[at, :])
            if k + r == 0:
                acc_ref[:width] = add_gate
                acc_ref[width:] = add_out
            else:
                acc_ref[:width] += add_gate
                acc_ref[width:] += add_out
    wg_ref[...] = flip(acc_ref[...])
    send_parts(wg_ref, parts)


def send_parts(wg_ref, parts):
    low = len(parts)
    high, rows = parts[0].shape[0], parts[0].shape[1]
    me = lax.axis_index("dp") % low
    for k in range(low):
        for p in range(high):
            start = pl.multiple_of((p * low + (me ^ k)) * rows, 16)
            parts[k][p] = wg_ref[pl.ds(start, rows), :].astype(bf16)


def backward_kernel(heads, n_dp, extra, *refs):
    refs = list(refs)
    take = lambda count: [refs.pop(0) for _ in range(count)]
    kx_ref, kxt_ref, qs_ref, trow_ref, q_ref, v_ref, da_ref, dat_ref, pos_ref = take(9)
    d_ref, xn_ref, ss_ref, gb_ref = take(4)
    gp_ref = refs.pop(0)
    parts = take(split_dp(n_dp)[1])
    accv_ref, acck_ref, posg_ref, gpq_ref, acc_ref, wg_ref, small_ref = refs
    nb, width = v_ref.shape[0], v_ref.shape[2]
    factor = 1.0 / math.sqrt(HEAD_DIM)
    tiles = [(i, j) for i in range(nb) for j in range(i + 1)]
    products, weights, grads = {}, {}, {}
    dq = None

    def add(ref, at, value, first):
        ref[at] = value if first else ref[at] + value

    for t in range(len(tiles) + 2):
        if t < len(tiles):
            i, j = tiles[t]
            if j == 0:
                queries = query_columns(qs_ref[i], trow_ref[i], heads)
                backs = by_head(dat_ref[i], heads)
            products[t] = dot(kx_ref[j], queries), dot(v_ref[j], backs)
        if 0 <= t - 1 < len(tiles):
            i, j = tiles[t - 1]
            product, back = products.pop(t - 1)
            h = masked(product, pos_ref[i - j], ss_ref[:, i * TILE : (i + 1) * TILE], j, heads)
            th = jnp.tanh(h)
            u = 1.0 + th
            w = h * u
            ds = back * (u + w * (1.0 - th))
            weights[t - 1], grads[t - 1] = w.astype(bf16), ds.astype(bf16)
            add(posg_ref, i - j, sum(ds[:, g * TILE : (g + 1) * TILE] for g in range(heads)), j == 0)
        if t >= 2:
            i, j = tiles[t - 2]
            low = grads.pop(t - 2)
            if j == 0:
                da = own_lanes(da_ref[i], heads)
                times = jnp.concatenate([kx_ref[i, :, :NTB]] * heads, axis=0)
                q = jnp.concatenate([times, own_lanes(q_ref[i], heads)], axis=1)
            add(accv_ref, j, dot(weights.pop(t - 2), da), i == j)
            add(acck_ref, j, dot(low, q), i == j)
            more = dot(kxt_ref[j, NTB:], low)
            dq = more if j == 0 else dq + more
            if i == j:
                gpq_ref[i] = own_rows(dq, heads)
    m2 = None
    for j in range(nb):
        part = acck_ref[j, :, :NTB]
        high = part.astype(bf16)
        rest = (part - high.astype(f32)).astype(bf16)
        onehot = kxt_ref[j, :NTB]
        part = dot(onehot, high) + dot(onehot, rest)
        m2 = part if j == 0 else m2 + part
    acc_ref[...] = jnp.zeros_like(acc_ref)

    def tail(i, _):
        gp = jnp.concatenate([flip(accv_ref[i]), gpq_ref[i] * factor, flip(acck_ref[i, :, NTB:]) * factor], axis=0)
        gp = (gp * d_ref[i]).astype(bf16)
        gp_ref[i] = flip(gp).astype(bf16)
        acc_ref[...] += dot(gp, xn_ref[i])
        return 0

    lax.fori_loop(0, nb, tail, 0)
    small_ref[...] = jnp.zeros_like(small_ref)
    small_ref[:, :D] = gb_ref[...]
    for d in range(nb):
        g = diagonals(posg_ref[d])
        small_ref[:, D + d * TILE : D + (d + 1) * TILE] += g[:, :TILE]
        if d > 0:
            small_ref[:, D + (d - 1) * TILE : D + d * TILE] += g[:, TILE:]
    g = diagonals(m2 + jnp.transpose(m2))[:, :NTB]
    zero = lax.broadcasted_iota(jnp.int32, (1, NTB), 1) == 0
    at = D + nb * TILE
    small_ref[:, at : at + NTB] = jnp.where(zero, 0.5 * g, g)
    step = D // n_dp
    grads = flip(acc_ref[...])
    for p in range(n_dp):
        here = jnp.concatenate(
            [small_ref[:, (p * extra + r) * 128 : (p * extra + r + 1) * 128] for r in range(extra)], axis=0
        )
        high = here.astype(bf16).astype(f32)
        block = jnp.concatenate([high, here - high, jnp.zeros((16 - 2 * extra, 128), f32)], axis=0)
        wg_ref[p * (step + 16) : p * (step + 16) + step] = grads[p * step : (p + 1) * step]
        wg_ref[p * (step + 16) + step : (p + 1) * (step + 16)] = jnp.concatenate(
            [block, jnp.zeros((16, 3 * width - 128), f32)], axis=1
        )
    send_parts(wg_ref, parts)


def input_kernel(n_head, gp_ref, gun_ref, wt_ref, keep, send):
    width = gun_ref.shape[2]
    per = keep.shape[1] // TILE
    for k in range(n_head):
        device = lax.axis_index("head") ^ k
        target = (keep, send)[k % 2]
        for r in range(per):
            i = device * per + r
            rows = dot(gp_ref[i], wt_ref[width : 4 * width]) + dot(gun_ref[i], wt_ref[:width])
            target[device // 2, r * TILE : (r + 1) * TILE] = rows.astype(bf16)


def fold_kernel(*refs):
    low = sum(len(ref.shape) == 3 for ref in refs)
    row = lax.axis_index("dp") // low
    for k, out in enumerate(refs[low:]):
        total = refs[0][row ^ k].astype(f32)
        for ref in refs[1:low]:
            total = total + ref[row ^ k].astype(f32)
        out[...] = total.astype(out.dtype)


def mix_kernel(tokens_ref, bias_ref, *refs):
    total = tokens_ref[...].astype(f32) + row_lanes(bias_ref, 0, D // 128)
    for ref in refs[:-1]:
        total = total + ref[...].astype(f32)
    refs[-1][...] = total.astype(bf16)


def finish_kernel(tokens_ref, cot_ref, mine_ref, *refs):
    x = tokens_ref[...].astype(f32)
    x = x - jnp.sum(x, axis=1, keepdims=True) / D
    scale = lax.rsqrt(jnp.sum(x * x, axis=1, keepdims=True) / D + norm_epsilon)
    x = x * scale
    grad = mine_ref[...]
    for ref in refs[:-1]:
        grad = grad + ref[...].astype(f32)
    mean = jnp.sum(grad, axis=1, keepdims=True) / D
    along = jnp.sum(grad * x, axis=1, keepdims=True) / D
    refs[-1][...] = cot_ref[...].astype(f32) + scale * (grad - mean - x * along)


def rows_kernel(chips, keep_ref, crossed_ref, mine_ref, *leaving):
    chip = lax.axis_index("head") // 2
    for k in range(chips):
        total = keep_ref[chip ^ k].astype(f32) + crossed_ref[chip ^ k].astype(f32)
        if k == 0:
            mine_ref[...] = total
        else:
            leaving[k - 1][...] = total.astype(bf16)


def collect_kernel(high, extra, *refs):
    late_blocks, early_blocks, (grads_ref, message_ref) = refs[:high], refs[high : 2 * high], refs[2 * high :]
    rows = grads_ref.shape[0]
    total, early = late_blocks[0][...], early_blocks[0][...]
    for k in range(1, high):
        total = total + late_blocks[k][...].astype(f32)
        early = early + early_blocks[k][...].astype(f32)
    grads = jnp.concatenate([total[:rows], early], axis=1)
    grads_ref[...] = grads
    squares = jnp.sum(jnp.sum(grads * grads, axis=0, keepdims=True), axis=1, keepdims=True)
    message = jnp.concatenate(
        [
            total[rows : rows + extra, :128] + total[rows + extra : rows + 2 * extra, :128],
            jnp.zeros((7 - extra, 128), f32),
            jnp.broadcast_to(squares, (1, 128)),
        ],
        axis=0,
    )
    for k in range(message_ref.shape[0]):
        message_ref[k] = message


def update_kernel(n_head, extra, group, heard_ref, grads_ref, *refs):
    state, outs = refs[:9], refs[9:]
    grad_proj_ref, grad_out_ref, grad_small_ref, norm_ref = outs[:4]
    n_all = heard_ref.shape[0]
    width = grad_out_ref.shape[1]
    lead, pos_rows, used = D // 128, POS // 128, (D + group) // 128
    grad_small_ref[...] = jnp.zeros_like(grad_small_ref)
    squares = heard_ref[0, 7:8, :]
    for k in range(1, n_all):
        squares = squares + heard_ref[k, 7:8, :]
    for p in range(n_all // n_head):
        rows = heard_ref[p * n_head, :extra, :]
        for h in range(1, n_head):
            rows = rows + heard_ref[p * n_head + h, :extra, :]
        for r in range(extra):
            at = p * extra + r
            if at < used:
                grad_small_ref[at : at + 1, :] = rows[r : r + 1]
            elif at == used:
                grad_small_ref[lead + pos_rows : lead + pos_rows + 1, :] = rows[r : r + 1]
    small = grad_small_ref[...]
    total = jnp.sum(jnp.sum(small * small, axis=0, keepdims=True), axis=1, keepdims=True) + squares[:, :1]
    norm = jnp.sqrt(total)
    norm_ref[...] = norm
    factor = jnp.minimum(1.0, clip_norm / (norm + 1e-06))

    def update(get, put, grad, rate, decay):
        for k, value in enumerate(adam_step(get(0), grad, get(1), get(2), factor, rate, decay)):
            put(k, value)

    for c in range(4):
        grad = grads_ref[:, 3 * width : 4 * width] if c == 0 else grads_ref[:, (c - 1) * width : c * width]
        grad_proj_ref[:, c, :] = grad

        def put(k, value):
            outs[4 + k][:, c, :] = value

        update(lambda k: state[k][:, c, :], put, grad, rate_matrix, decay_matrix)
    grad = grads_ref[:, 4 * width :]
    grad_out_ref[...] = grad

    def put_out(k, value):
        outs[7 + k][...] = value

    update(lambda k: state[3 + k][...], put_out, grad, rate_matrix, decay_matrix)

    def put_small(k, value):
        outs[10 + k][...] = value

    update(lambda k: state[6 + k][...], put_small, small, rate_small, 0.0)


def call(kernel, name, in_specs, outs, scratch, us, room=20):
    return pl.pallas_call(
        kernel,
        out_shape=[jax.ShapeDtypeStruct(shape, dtype) for shape, dtype, _ in outs],
        in_specs=in_specs,
        out_specs=[spec for _, _, spec in outs],
        scratch_shapes=scratch,
        compiler_params=pltpu.CompilerParams(vmem_limit_bytes=room * 2**20),
        cost_estimate=pl.CostEstimate(flops=int(us * 1e9), bytes_accessed=int(us * 3e6), transcendentals=0),
        name=name,
    )


def block(shape):
    return pl.BlockSpec((1,) + tuple(shape[1:]), lambda i: (i,) + (0,) * (len(shape) - 1))


def shards(
    tokens,
    cotangent,
    seq_start,
    time_bucket,
    proj_weight,
    out_weight,
    small_params,
    proj_mean,
    proj_square,
    out_mean,
    out_square,
    small_mean,
    small_square,
):
    n_head = lax.axis_size("head")
    n_dp = lax.axis_size("dp")
    here = tokens.shape[0]
    group = here * n_head
    nb = group // TILE
    per = here // TILE
    rows_here, _, width = proj_weight.shape
    heads = width // HEAD_DIM
    high, low = split_dp(n_dp)

    (weights,) = call(
        cast_kernel, "cast", [VMEM] * 2, [((rows_here, 5 * width), bf16, VMEM)], [], 1
    )(proj_weight, out_weight.T)
    x_pieces = gather_cores(tokens, gather_chips(after(tokens, weights)))
    w_pieces, offsets, operands = gather_dp(weights)
    cot_chips = gather_chips(after(cotangent, weights))
    starts = seq_start.reshape(1, group)
    small_rows = small_params.reshape(-1, 128)
    times = time_bucket.reshape(1, group)

    pos, oh, oht, trow = call(
        prepare_kernel,
        "prepare",
        [VMEM] * 2,
        [
            ((nb, TILE, TILE), f32, VMEM),
            ((nb, TILE, NTB), bf16, VMEM),
            ((nb, NTB, TILE), bf16, VMEM),
            ((nb, NTB, TILE), bf16, VMEM),
        ],
        [],
        5,
    )(after(times, operands[1]), small_rows)

    items = [
        ((nb, 3 * width, TILE), bf16),
        ((nb, TILE, NTB + width), bf16),
        ((nb, NTB + width, TILE), bf16),
        ((nb, width, TILE), bf16),
        ((nb, TILE, width), bf16),
        ((nb, TILE, width), bf16),
        ((nb, width, TILE), bf16),
    ]
    (xn,) = call(normalize_kernel, "normalize", [VMEM] * n_head, [((nb, TILE, D), bf16, VMEM)], [], 1)(*x_pieces)
    (wt,) = call(
        functools.partial(assemble_kernel, offsets),
        "assemble",
        [VMEM] * len(w_pieces),
        [((5 * width, D), bf16, VMEM)],
        [pltpu.VMEM((D, 5 * width), bf16)],
        5,
    )(*w_pieces)
    dsilu, kx, kxt, qs, q, v, vt = call(
        functools.partial(project_kernel, heads),
        "project",
        [VMEM] * 4,
        [item + (VMEM,) for item in items],
        [],
        5,
    )(xn, wt, oh, oht)

    def attend(first, last, *before):
        (attn,) = call(
            functools.partial(attend_kernel, heads, first, last),
            "attend",
            [VMEM] * (len(before) + 6),
            [((last, width, TILE), f32, VMEM)],
            [],
            8,
        )(*before, kx, qs, trow, vt, pos, starts)
        return attn

    split = nb - nb // 4
    attn = attend(0, split)
    cot_chips = after_all(cot_chips, attn)
    attn = attend(split, nb, after(attn, *cot_chips))
    cot_pieces = gather_cores(cotangent, cot_chips)

    column = ((nb, width, TILE), f32, VMEM)
    p_gate, gg, stat, gb = call(
        functools.partial(gate_kernel, n_head),
        "gate",
        [VMEM] * (n_head + 3),
        [column, column, ((nb, 4, TILE), f32, VMEM), ((1, D), f32, VMEM)],
        [],
        5,
    )(*cot_pieces, attn, xn, wt)

    stats = [stat] + [swap(stat, "head", k) for k in range(1, n_head)]
    out = call(
        functools.partial(middle_kernel, n_head),
        "middle",
        [VMEM] * (2 * n_head + 5),
        [((here, D), bf16, VMEM)] * n_head
        + [
            ((nb, TILE, width), bf16, VMEM),
            ((nb, width, TILE), bf16, VMEM),
            ((nb, TILE, width), bf16, VMEM),
        ]
        + [((high, rows_here, 2 * width), bf16, VMEM)] * low,
        [pltpu.VMEM((2 * width, D), f32), pltpu.VMEM((D, 2 * width), f32)],
        6,
    )(*stats, *cot_pieces, attn, p_gate, gg, xn, wt)
    branches, (da, dat, gun), early_parts = out[:n_head], out[n_head : n_head + 3], out[n_head + 3 :]
    received = [swap(branches[k], "head", k) for k in range(1, n_head)]
    early_received = [swap(early_parts[k], "dp", k) for k in range(1, low)]

    length = D + group + NTB
    extra = -(-length // (128 * n_dp))
    gp, *late_parts = call(
        functools.partial(backward_kernel, heads, n_dp, extra),
        "backward",
        [VMEM] * 13,
        [((nb, TILE, 3 * width), bf16, VMEM)] + [((high, rows_here + 16, 3 * width), bf16, VMEM)] * low,
        [
            pltpu.VMEM((nb, TILE, width), f32),
            pltpu.VMEM((nb, TILE, NTB + width), f32),
            pltpu.VMEM((nb, TILE, TILE), f32),
            pltpu.VMEM((nb, width, TILE), f32),
            pltpu.VMEM((3 * width, D), f32),
            pltpu.VMEM((n_dp * (rows_here + 16), 3 * width), f32),
            pltpu.VMEM((1, extra * n_dp * 128), f32),
        ],
        35,
        ROOM,
    )(kx, kxt, qs, trow, q, v, da, dat, pos, dsilu, xn, starts, gb)

    tied = lax.optimization_barrier((gp, *late_parts, *received, *early_received))
    gp, late_parts = tied[0], tied[1 : 1 + low]
    received, early_received = tied[1 + low : low + n_head], tied[low + n_head :]
    late_received = [swap(late_parts[k], "dp", k) for k in range(1, low)]
    keep, send = call(
        functools.partial(input_kernel, n_head),
        "input_rows",
        [VMEM] * 3,
        [((n_head // 2, here, D), bf16, VMEM)] * 2,
        [],
        4,
    )(gp, gun, wt)
    early_blocks = scatter_high(after(early_parts[0], send), early_received, 1)
    late_received = after_all(late_received, send)
    late_blocks = scatter_high(late_parts[0], late_received, 6)
    late_blocks[0] = after(late_blocks[0], *early_blocks)
    chips = n_head // 2
    crossed = swap(after(send, late_blocks[0]), "head", 1)
    mine, *leaving = call(
        functools.partial(rows_kernel, chips),
        "rows",
        [VMEM] * 2,
        [((here, D), f32, VMEM)] + [((here, D), bf16, VMEM)] * (chips - 1),
        [],
        0.1,
    )(keep, crossed)
    arrived = [swap(leaving[k - 1], "head", 2 * k) for k in range(1, chips)]
    n_all = n_dp * n_head
    grads_shape = ((rows_here, 5 * width), f32)
    grads, message = call(
        functools.partial(collect_kernel, high, extra),
        "collect",
        [VMEM] * (2 * high),
        [grads_shape + (VMEM,), ((n_all, 8, 128), f32, VMEM)],
        [],
        10,
    )(*late_blocks, *early_blocks)
    message = after(message, *leaving)
    heard = lax.all_to_all(message, ("dp", "head"), 0, 0, tiled=True)
    (mixed,) = call(
        mix_kernel, "mix", [VMEM] * (2 + n_head), [((here, D), bf16, VMEM)], [], 1
    )(after(tokens, message), small_rows, branches[0], *received)
    (input_grad,) = call(
        finish_kernel, "finish", [VMEM] * (2 + chips), [((here, D), f32, VMEM)], [], 1
    )(after(tokens, mixed), cotangent, mine, *arrived)
    heard = after(heard, input_grad)
    state = [proj_weight, proj_mean, proj_square, out_weight.T, out_mean.T, out_square.T]
    state += [x.reshape(-1, 128) for x in (small_params, small_mean, small_square)]
    proj_shape, out_shape, small_shape = proj_weight.shape, (rows_here, width), small_rows.shape
    shapes = [proj_shape, out_shape, small_shape, (1, 1)] + [proj_shape] * 3 + [out_shape] * 3 + [small_shape] * 3
    results = call(
        functools.partial(update_kernel, n_head, extra, group),
        "update",
        [VMEM] * (2 + len(state)),
        [(shape, f32, VMEM) for shape in shapes],
        [],
        0.1,
    )(heard, grads, *state)
    grad_proj, grad_out, grad_small, grad_norm = results[:4]
    grad_out, grad_small, grad_norm = grad_out.T, grad_small.reshape(-1), grad_norm.reshape(())
    new_proj, mean_proj, square_proj = results[4:7]
    new_out, mean_out, square_out = [x.T for x in results[7:10]]
    new_small, mean_small, square_small = [x.reshape(-1) for x in results[10:13]]
    return (
        mixed,
        input_grad,
        grad_proj,
        grad_out,
        grad_small,
        grad_norm,
        new_proj,
        mean_proj,
        square_proj,
        new_out,
        mean_out,
        square_out,
        new_small,
        mean_small,
        square_small,
    )


def solution(mesh):
    in_specs = (
        P(("dp", "head"), None),
        P(("dp", "head"), None),
        P("dp"),
        P("dp"),
        P("dp", None, "head"),
        P("head", "dp"),
        P(),
        P("dp", None, "head"),
        P("dp", None, "head"),
        P("head", "dp"),
        P("head", "dp"),
        P(),
        P(),
    )
    out_specs = (
        P(("dp", "head"), None),
        P(("dp", "head"), None),
        P("dp", None, "head"),
        P("head", "dp"),
        P(),
        P(),
        P("dp", None, "head"),
        P("dp", None, "head"),
        P("dp", None, "head"),
        P("head", "dp"),
        P("head", "dp"),
        P("head", "dp"),
        P(),
        P(),
        P(),
    )
    return jax.shard_map(shards, mesh=mesh, in_specs=in_specs, out_specs=out_specs, check_vma=False)
```

```python
import functools
import math

import jax
import jax.numpy as jnp
from jax import lax
from jax.experimental import pallas as pl
from jax.experimental.pallas import tpu as pltpu
from jax.sharding import PartitionSpec as P

D = 512
HEAD_DIM = 64
HD = 512
POS = 8192
NTB = 128
STEP = 10
TILE = 256
NEG = -1e9
ROOM = 24

norm_epsilon = 1e-06
adam_epsilon = 1e-08
beta_one = 0.9
beta_two = 0.999
clip_norm = 1.0
rate_matrix = 0.05
rate_small = 0.3
decay_matrix = 0.1

f32 = jnp.float32
bf16 = jnp.bfloat16
VMEM = pl.BlockSpec(memory_space=pltpu.VMEM)


def adam_step(weight, grad, first, second, factor, rate, decay):
    clipped = grad * factor
    first_new = beta_one * first + (1.0 - beta_one) * clipped
    second_new = beta_two * second + (1.0 - beta_two) * clipped * clipped
    update = (
        first_new
        / (1.0 - beta_one**STEP)
        / (jnp.sqrt(second_new / (1.0 - beta_two**STEP)) + adam_epsilon)
    )
    return (weight - rate * (update + decay * weight), first_new, second_new)


def swap(x, axis, k):
    n = lax.axis_size(axis)
    return lax.ppermute(x, axis, [(i, i ^ k) for i in range(n)])


def gather_chips(x):
    return [swap(x, "head", k) for k in range(2, lax.axis_size("head"), 2)]


def gather_cores(x, others):
    pieces = [x, swap(x, "head", 1)]
    for other in others:
        pieces += [other, swap(other, "head", 1)]
    return pieces


def after_all(arrays, *others):
    arrays = tuple(arrays)
    return lax.optimization_barrier(arrays + others)[: len(arrays)]


def after(x, *others):
    return lax.optimization_barrier((x,) + others)[0]


def gather_dp(x):
    n = lax.axis_size("dp")
    arrays, offsets, operands = [x], [[0]], []
    k = n // 2
    while k:
        operand = join(arrays) if len(arrays) > 1 else x
        operands.append(operand)
        arrays.append(swap(operand, "dp", k))
        offsets.append([o ^ k for group in offsets for o in group])
        k //= 2
    return arrays, offsets, operands


def join(arrays, us=2):
    shape = (sum(x.shape[0] for x in arrays), arrays[0].shape[1])
    return call(join_kernel, "join", [VMEM] * len(arrays), [(shape, arrays[0].dtype, VMEM)], [], us)(*arrays)[0]


def split_dp(n):
    low = 2 ** ((n.bit_length() - 1) // 2)
    return n // low, low


def scatter_high(own, received, us):
    high, rows, columns = own.shape
    low = 1 + len(received)
    mine, *leaving = call(
        fold_kernel,
        "fold",
        [VMEM] * low,
        [((rows, columns), f32, VMEM)] + [((rows, columns), bf16, VMEM)] * (high - 1),
        [],
        us,
    )(own, *received)
    return [mine] + [swap(sent, "dp", (k + 1) * low) for k, sent in enumerate(leaving)]


def fold_cores(keep, crossed):
    chips, rows, columns = keep.shape
    return call(
        functools.partial(rows_kernel, chips),
        "rows",
        [VMEM] * 2,
        [((rows, columns), f32, VMEM)] + [((rows, columns), bf16, VMEM)] * (chips - 1),
        [],
        0.1,
    )(keep, crossed)


def dot(a, b):
    return lax.dot_general(a, b, (((1,), (0,)), ((), ())), preferred_element_type=f32)


def dot_nt(a, b):
    return lax.dot_general(a, b, (((1,), (1,)), ((), ())), preferred_element_type=f32)


def flip(a):
    return jnp.transpose(a.astype(f32))


def lanes(i):
    return pl.ds(pl.multiple_of(i * TILE, TILE), TILE)


def by_head(block, heads):
    zero = jnp.zeros((HEAD_DIM, block.shape[1]), block.dtype)
    return jnp.concatenate(
        [
            jnp.concatenate(
                [block[g * HEAD_DIM : (g + 1) * HEAD_DIM] if g == h else zero for g in range(heads)], axis=0
            )
            for h in range(heads)
        ],
        axis=1,
    )


def query_columns(qs, trow, heads):
    return jnp.concatenate([jnp.concatenate([trow] * heads, axis=1), by_head(qs, heads)], axis=0)


def own_rows(block, heads):
    return jnp.concatenate(
        [block[h * HEAD_DIM : (h + 1) * HEAD_DIM, h * TILE : (h + 1) * TILE] for h in range(heads)], axis=0
    )


def own_lanes(block, heads):
    lane = lax.broadcasted_iota(jnp.int32, block.shape, 1) // HEAD_DIM
    return jnp.concatenate([jnp.where(lane == h, block, jnp.zeros_like(block)) for h in range(heads)], axis=0)


def masked(product, bias, start, j, heads):
    key = j * TILE + lax.broadcasted_iota(jnp.int32, (TILE, TILE), 0)
    seen = key >= start
    return jnp.where(
        jnp.concatenate([seen] * heads, axis=1), product + jnp.concatenate([bias] * heads, axis=1), NEG
    )


def diagonals(x):
    rows, cols = x.shape
    z = jnp.concatenate([x, jnp.zeros((rows, cols), f32)], axis=1)
    total = z[:8]
    for q in range(1, rows // 8):
        total = total + pltpu.roll(z[8 * q : 8 * q + 8], 2 * cols - 8 * q, 1)
    g = total[0:1]
    for r in range(1, 8):
        g = g + pltpu.roll(total, 2 * cols - r, 1)[r : r + 1]
    return g


def cast_kernel(w_in, o_in, low_ref, w_ref, o_ref, sems):
    copies = [pltpu.make_async_copy(w_in, w_ref, sems.at[0]), pltpu.make_async_copy(o_in, o_ref, sems.at[1])]
    for copy in copies:
        copy.start()
    for copy in copies:
        copy.wait()
    width = o_ref.shape[1]
    for c in range(4):
        low_ref[:, c * width : (c + 1) * width] = w_ref[:, c, :].astype(bf16)
    low_ref[:, 4 * width :] = o_ref[...].astype(bf16)


def row_lanes(ref, first, count):
    return jnp.concatenate([ref[pl.ds(first + k, 1), :] for k in range(count)], axis=1)


def prepare_kernel(tb_ref, small_ref, pos_ref, oh_ref, oht_ref, trow_ref):
    nb = pos_ref.shape[0]
    step = TILE // 128

    def tile(d, _):
        first = D // 128 + d * step
        row = jnp.concatenate([row_lanes(small_ref, first, step), row_lanes(small_ref, first - step, step)], axis=1)
        pos_ref[d] = pltpu.roll(
            jnp.broadcast_to(row * 0.5, (TILE, 2 * TILE)), 0, 1, stride=1, stride_axis=0
        )[:, :TILE]
        return 0

    lax.fori_loop(0, nb, tile, 0)
    b = lax.broadcasted_iota(jnp.int32, (TILE, TILE), 0)
    a = lax.broadcasted_iota(jnp.int32, (TILE, TILE), 1)
    pos_ref[0] = jnp.where(b <= a, pos_ref[0], NEG)
    table = row_lanes(small_ref, (D + POS) // 128, NTB // 128)
    row = jnp.concatenate([table, table], axis=1)
    upper = pltpu.roll(jnp.broadcast_to(row, (NTB, 2 * NTB)), 0, 1, stride=1, stride_axis=0)[:, :NTB]
    a = lax.broadcasted_iota(jnp.int32, (NTB, NTB), 0)
    b = lax.broadcasted_iota(jnp.int32, (NTB, NTB), 1)
    upper = jnp.where(b >= a, upper, 0.0)
    square = (jnp.where(b > a, upper, jnp.transpose(upper)) * 0.5).astype(bf16)

    def block(i, _):
        onehot = (lax.broadcasted_iota(jnp.int32, (NTB, TILE), 0) == tb_ref[:, lanes(i)]).astype(f32)
        low = onehot.astype(bf16)
        oht_ref[i] = low
        oh_ref[i] = flip(onehot).astype(bf16)
        trow_ref[i] = dot(square, low).astype(bf16)
        return 0

    lax.fori_loop(0, nb, block, 0)


def join_kernel(*refs):
    at = 0
    for ref in refs[:-1]:
        refs[-1][at : at + ref.shape[0]] = ref[...]
        at += ref.shape[0]


def normalize_kernel(*refs):
    x_pieces, xn_ref = refs[:-1], refs[-1]
    per = x_pieces[0].shape[0] // TILE
    for k, piece in enumerate(x_pieces):
        for r in range(per):
            x = piece[r * TILE : (r + 1) * TILE, :].astype(f32)
            x = x - jnp.sum(x, axis=1, keepdims=True) / D
            x = x * lax.rsqrt(jnp.sum(x * x, axis=1, keepdims=True) / D + norm_epsilon)
            xn_ref[(lax.axis_index("head") ^ k) * per + r] = x.astype(bf16)


def assemble_kernel(offsets, *refs):
    w_pieces, (wt_ref, w_ref) = refs[:-2], refs[-2:]
    for piece, group in zip(w_pieces, offsets):
        rows = piece.shape[0] // len(group)
        for at, offset in enumerate(group):
            start = pl.multiple_of((lax.axis_index("dp") ^ offset) * rows, 16)
            w_ref[pl.ds(start, rows), :] = piece[at * rows : (at + 1) * rows, :]
    wt_ref[...] = flip(w_ref[...]).astype(bf16)


def project_kernel(heads, *refs):
    refs = list(refs)
    take = lambda count: [refs.pop(0) for _ in range(count)]
    xn_ref, wt_ref, oh_ref, oht_ref = take(4)
    d_ref, kx_ref, kxt_ref, qs_ref, q_ref, v_ref, vt_ref = refs
    width = v_ref.shape[2]

    def project(i):
        x = xn_ref[i]
        p = dot_nt(wt_ref[width : 4 * width], x)
        sg = 0.5 + 0.5 * jnp.tanh(0.5 * p)
        act = p * sg
        d_ref[i] = (sg + act * (1.0 - sg)).astype(bf16)
        vt = act[:width]
        vt_ref[i] = vt.astype(bf16)
        v_ref[i] = flip(vt).astype(bf16)
        qt = act[width : 2 * width].astype(bf16)
        kt = act[2 * width :]
        kxt_ref[i, :NTB] = oht_ref[i]
        kxt_ref[i, NTB:] = kt.astype(bf16)
        kx_ref[i, :, :NTB] = oh_ref[i]
        kx_ref[i, :, NTB:] = flip(kt).astype(bf16)
        qs = (qt.astype(f32) * (0.5 / math.sqrt(HEAD_DIM))).astype(bf16)
        qs_ref[i] = qs
        q_ref[i] = flip(qt).astype(bf16)

    for i in range(xn_ref.shape[0]):
        project(i)

def attend_kernel(heads, first, last, *refs):
    if first:
        before_ref, refs = refs[0], refs[1:]
    kx_ref, qs_ref, trow_ref, vt_ref, pos_ref, ss_ref, attn_ref = refs
    if first:
        attn_ref[:first] = before_ref[...]
    for i in range(first, last):
        queries = query_columns(qs_ref[i], trow_ref[i], heads)
        scores = [dot(kx_ref[j], queries) for j in range(i + 1)]
        weights = []
        for j in range(i + 1):
            h = masked(scores[j], pos_ref[i - j], ss_ref[:, i * TILE : (i + 1) * TILE], j, heads)
            weights.append((h + h * jnp.tanh(h)).astype(bf16))
        total = dot(vt_ref[0], weights[0])
        for j in range(1, i + 1):
            total = total + dot(vt_ref[j], weights[j])
        attn_ref[i] = own_rows(total, heads)


def gate_kernel(n_head, *refs):
    refs = list(refs)
    take = lambda count: [refs.pop(0) for _ in range(count)]
    cot_pieces = take(n_head)
    attn_ref, xn_ref, wt_ref = take(3)
    p_ref, gg_ref, stat_ref, gb_ref = refs
    width = attn_ref.shape[1]
    per = cot_pieces[0].shape[0] // TILE
    gb_ref[...] = jnp.sum(cot_pieces[0][...].astype(f32), axis=0, keepdims=True)
    for k, piece in enumerate(cot_pieces):
        for r in range(per):
            i = (lax.axis_index("head") ^ k) * per + r
            p = dot_nt(wt_ref[:width], xn_ref[i])
            gate = p * (0.5 + 0.5 * jnp.tanh(0.5 * p))
            gg = dot_nt(wt_ref[4 * width :], piece[r * TILE : (r + 1) * TILE, :])
            grad = gg * gate
            p_ref[i] = p
            gg_ref[i] = gg
            at = attn_ref[i]
            mean = jnp.sum(at, axis=0, keepdims=True) / width
            centred = at - mean
            stat_ref[i] = jnp.concatenate(
                [
                    mean,
                    jnp.sum(centred * centred, axis=0, keepdims=True),
                    jnp.sum(grad, axis=0, keepdims=True),
                    jnp.sum(grad * centred, axis=0, keepdims=True),
                ],
                axis=0,
            )


def standardized(i, n_head, stats, attn_ref):
    width = attn_ref.shape[1]
    st = [s[i] for s in stats]
    mean = sum(p[0:1] for p in st) / n_head
    spread = sum(p[1:2] + width * (p[0:1] - mean) * (p[0:1] - mean) for p in st)
    scale = lax.rsqrt(spread / HD + norm_epsilon)
    first = sum(p[2:3] for p in st) / HD
    second = scale * sum(p[3:4] + (p[0:1] - mean) * p[2:3] for p in st) / HD
    return (attn_ref[i] - mean) * scale, scale, first, second


def branch_kernel(n_head, *refs):
    stats, (attn_ref, p_ref, wt_ref, keep, send) = refs[:n_head], refs[n_head:]
    width = attn_ref.shape[1]
    per = keep.shape[1] // TILE
    for k in range(n_head):
        device = lax.axis_index("head") ^ k
        for r in range(per):
            i = device * per + r
            normed = standardized(i, n_head, stats, attn_ref)[0]
            p = p_ref[i]
            gated = (normed * (p * (0.5 + 0.5 * jnp.tanh(0.5 * p)))).astype(bf16)
            (keep, send)[k % 2][device // 2, r * TILE : (r + 1) * TILE] = dot(
                flip(gated).astype(bf16), wt_ref[4 * width :]
            ).astype(bf16)


def middle_kernel(n_head, *refs):
    refs = list(refs)
    take = lambda count: [refs.pop(0) for _ in range(count)]
    stats = take(n_head)
    cot_pieces = take(n_head)
    attn_ref, p_ref, gg_ref, xn_ref = take(4)
    da_ref, dat_ref, gun_ref = take(3)
    parts, acc_ref, wg_ref = refs[:-2], refs[-2], refs[-1]
    width = attn_ref.shape[1]
    per = cot_pieces[0].shape[0] // TILE
    for k, piece in enumerate(cot_pieces):
        for r in range(per):
            i = (lax.axis_index("head") ^ k) * per + r
            normed, scale, first, second = standardized(i, n_head, stats, attn_ref)
            p = p_ref[i]
            sg = 0.5 + 0.5 * jnp.tanh(0.5 * p)
            gate = p * sg
            gg = gg_ref[i]
            gated = (normed * gate).astype(bf16)
            grad = scale * (gg * gate - first - normed * second)
            da_ref[i] = flip(grad).astype(bf16)
            dat_ref[i] = (grad * 0.5).astype(bf16)
            gu = (gg * normed * (sg + gate * (1.0 - sg))).astype(bf16)
            gun_ref[i] = flip(gu).astype(bf16)
            add_gate, add_out = dot(gu, xn_ref[i]), dot(gated, piece[r * TILE : (r + 1) * TILE, :])
            if k + r == 0:
                acc_ref[:width] = add_gate
                acc_ref[width:] = add_out
            else:
                acc_ref[:width] += add_gate
                acc_ref[width:] += add_out
    wg_ref[...] = flip(acc_ref[...])
    send_parts(wg_ref, parts)


def send_parts(wg_ref, parts):
    low = len(parts)
    high, rows = parts[0].shape[0], parts[0].shape[1]
    me = lax.axis_index("dp") % low
    for k in range(low):
        for p in range(high):
            start = pl.multiple_of((p * low + (me ^ k)) * rows, 16)
            parts[k][p] = wg_ref[pl.ds(start, rows), :].astype(bf16)


def backward_kernel(heads, n_dp, extra, *refs):
    refs = list(refs)
    take = lambda count: [refs.pop(0) for _ in range(count)]
    kx_ref, kxt_ref, qs_ref, trow_ref, q_ref, v_ref, da_ref, dat_ref, pos_ref = take(9)
    d_ref, xn_ref, ss_ref, gb_ref = take(4)
    gp_ref = refs.pop(0)
    parts = take(split_dp(n_dp)[1])
    accv_ref, acck_ref, posg_ref, acc_ref, wg_ref, small_ref = refs
    nb, width = v_ref.shape[0], v_ref.shape[2]
    factor = 1.0 / math.sqrt(HEAD_DIM)
    tiles = [(i, j) for i in reversed(range(nb)) for j in range(i + 1)]
    products, weights, grads = {}, {}, {}
    dq = m2 = None
    small_ref[...] = jnp.zeros_like(small_ref)
    small_ref[:, :D] = gb_ref[...]

    def add(ref, at, value, first):
        ref[at] = value if first else ref[at] + value

    for t in range(len(tiles) + 2):
        if t < len(tiles):
            i, j = tiles[t]
            if j == 0:
                queries = query_columns(qs_ref[i], trow_ref[i], heads)
                backs = by_head(dat_ref[i], heads)
            products[t] = dot(kx_ref[j], queries), dot(v_ref[j], backs)
        if 0 <= t - 1 < len(tiles):
            i, j = tiles[t - 1]
            product, back = products.pop(t - 1)
            h = masked(product, pos_ref[i - j], ss_ref[:, i * TILE : (i + 1) * TILE], j, heads)
            th = jnp.tanh(h)
            u = 1.0 + th
            w = h * u
            ds = back * (u + w * (1.0 - th))
            weights[t - 1], grads[t - 1] = w.astype(bf16), ds.astype(bf16)
            add(posg_ref, i - j, sum(ds[:, g * TILE : (g + 1) * TILE] for g in range(heads)), i == nb - 1)
        if t >= 2:
            i, j = tiles[t - 2]
            low = grads.pop(t - 2)
            if j == 0:
                da = own_lanes(da_ref[i], heads)
                times = jnp.concatenate([kx_ref[i, :, :NTB]] * heads, axis=0)
                q = jnp.concatenate([times, own_lanes(q_ref[i], heads)], axis=1)
            add(accv_ref, j, dot(weights.pop(t - 2), da), i == nb - 1)
            add(acck_ref, j, dot(low, q), i == nb - 1)
            more = dot(kxt_ref[j, NTB:], low)
            dq = more if j == 0 else dq + more
            if i == j:
                gp = jnp.concatenate(
                    [flip(accv_ref[i]), own_rows(dq, heads) * factor, flip(acck_ref[i, :, NTB:]) * factor], axis=0
                )
                gp = (gp * d_ref[i]).astype(bf16)
                gp_ref[i] = flip(gp).astype(bf16)
                more = dot(gp, xn_ref[i])
                acc_ref[...] = more if i == nb - 1 else acc_ref[...] + more
                part = acck_ref[i, :, :NTB]
                high = part.astype(bf16)
                rest = (part - high.astype(f32)).astype(bf16)
                onehot = kxt_ref[i, :NTB]
                part = dot(onehot, high) + dot(onehot, rest)
                m2 = part if i == nb - 1 else m2 + part
                g = diagonals(posg_ref[i])
                small_ref[:, D + i * TILE : D + (i + 1) * TILE] += g[:, :TILE]
                if i > 0:
                    small_ref[:, D + (i - 1) * TILE : D + i * TILE] += g[:, TILE:]
    g = diagonals(m2 + jnp.transpose(m2))[:, :NTB]
    zero = lax.broadcasted_iota(jnp.int32, (1, NTB), 1) == 0
    at = D + nb * TILE
    small_ref[:, at : at + NTB] = jnp.where(zero, 0.5 * g, g)
    step = D // n_dp
    grads = flip(acc_ref[...])
    for p in range(n_dp):
        here = jnp.concatenate(
            [small_ref[:, (p * extra + r) * 128 : (p * extra + r + 1) * 128] for r in range(extra)], axis=0
        )
        high = here.astype(bf16).astype(f32)
        block = jnp.concatenate([high, here - high, jnp.zeros((16 - 2 * extra, 128), f32)], axis=0)
        wg_ref[p * (step + 16) : p * (step + 16) + step] = grads[p * step : (p + 1) * step]
        wg_ref[p * (step + 16) + step : (p + 1) * (step + 16)] = jnp.concatenate(
            [block, jnp.zeros((16, 3 * width - 128), f32)], axis=1
        )
    send_parts(wg_ref, parts)


def input_kernel(n_head, gp_ref, gun_ref, wt_ref, keep, send):
    width = gun_ref.shape[2]
    per = keep.shape[1] // TILE
    for k in range(n_head):
        device = lax.axis_index("head") ^ k
        target = (keep, send)[k % 2]
        for r in range(per):
            i = device * per + r
            rows = dot(gp_ref[i], wt_ref[width : 4 * width]) + dot(gun_ref[i], wt_ref[:width])
            target[device // 2, r * TILE : (r + 1) * TILE] = rows.astype(bf16)


def fold_kernel(*refs):
    low = sum(len(ref.shape) == 3 for ref in refs)
    row = lax.axis_index("dp") // low
    for k, out in enumerate(refs[low:]):
        total = refs[0][row ^ k].astype(f32)
        for ref in refs[1:low]:
            total = total + ref[row ^ k].astype(f32)
        out[...] = total.astype(out.dtype)


def sum_kernel(*refs):
    total = refs[0][...]
    for ref in refs[1:-1]:
        total = total + ref[...].astype(f32)
    refs[-1][...] = total


def mix_kernel(tokens_ref, bias_ref, *refs):
    total = tokens_ref[...].astype(f32) + row_lanes(bias_ref, 0, D // 128)
    for ref in refs[:-1]:
        total = total + ref[...].astype(f32)
    refs[-1][...] = total.astype(bf16)


def finish_kernel(tokens_ref, cot_ref, mine_ref, *refs):
    x = tokens_ref[...].astype(f32)
    x = x - jnp.sum(x, axis=1, keepdims=True) / D
    scale = lax.rsqrt(jnp.sum(x * x, axis=1, keepdims=True) / D + norm_epsilon)
    x = x * scale
    grad = mine_ref[...]
    for ref in refs[:-1]:
        grad = grad + ref[...].astype(f32)
    mean = jnp.sum(grad, axis=1, keepdims=True) / D
    along = jnp.sum(grad * x, axis=1, keepdims=True) / D
    refs[-1][...] = cot_ref[...].astype(f32) + scale * (grad - mean - x * along)


def rows_kernel(chips, keep_ref, crossed_ref, mine_ref, *leaving):
    chip = lax.axis_index("head") // 2
    for k in range(chips):
        total = keep_ref[chip ^ k].astype(f32) + crossed_ref[chip ^ k].astype(f32)
        if k == 0:
            mine_ref[...] = total
        else:
            leaving[k - 1][...] = total.astype(bf16)


def collect_kernel(high, extra, *refs):
    late_blocks, (early_ref, grads_ref, message_ref) = refs[:high], refs[high:]
    rows = grads_ref.shape[0]
    total, early = late_blocks[0][...], early_ref[...]
    for k in range(1, high):
        total = total + late_blocks[k][...].astype(f32)
    grads = jnp.concatenate([total[:rows], early], axis=1)
    grads_ref[...] = grads
    squares = jnp.sum(jnp.sum(grads * grads, axis=0, keepdims=True), axis=1, keepdims=True)
    message = jnp.concatenate(
        [
            total[rows : rows + extra, :128] + total[rows + extra : rows + 2 * extra, :128],
            jnp.zeros((7 - extra, 128), f32),
            jnp.broadcast_to(squares, (1, 128)),
        ],
        axis=0,
    )
    for k in range(message_ref.shape[0]):
        message_ref[k] = message


def update_kernel(n_head, extra, group, heard_ref, grads_ref, *refs):
    state, outs = refs[:9], refs[9:]
    grad_proj_ref, grad_out_ref, grad_small_ref, norm_ref = outs[:4]
    n_all = heard_ref.shape[0]
    width = grad_out_ref.shape[1]
    lead, pos_rows, used = D // 128, POS // 128, (D + group) // 128
    grad_small_ref[...] = jnp.zeros_like(grad_small_ref)
    squares = heard_ref[0, 7:8, :]
    for k in range(1, n_all):
        squares = squares + heard_ref[k, 7:8, :]
    for p in range(n_all // n_head):
        rows = heard_ref[p * n_head, :extra, :]
        for h in range(1, n_head):
            rows = rows + heard_ref[p * n_head + h, :extra, :]
        for r in range(extra):
            at = p * extra + r
            if at < used:
                grad_small_ref[at : at + 1, :] = rows[r : r + 1]
            elif at == used:
                grad_small_ref[lead + pos_rows : lead + pos_rows + 1, :] = rows[r : r + 1]
    small = grad_small_ref[...]
    total = jnp.sum(jnp.sum(small * small, axis=0, keepdims=True), axis=1, keepdims=True) + squares[:, :1]
    norm = jnp.sqrt(total)
    norm_ref[...] = norm
    factor = jnp.minimum(1.0, clip_norm / (norm + 1e-06))

    def update(get, put, grad, rate, decay):
        for k, value in enumerate(adam_step(get(0), grad, get(1), get(2), factor, rate, decay)):
            put(k, value)

    for c in range(4):
        grad = grads_ref[:, 3 * width : 4 * width] if c == 0 else grads_ref[:, (c - 1) * width : c * width]
        grad_proj_ref[:, c, :] = grad

        def put(k, value):
            outs[4 + k][:, c, :] = value

        update(lambda k: state[k][:, c, :], put, grad, rate_matrix, decay_matrix)
    grad = grads_ref[:, 4 * width :]
    grad_out_ref[...] = grad

    def put_out(k, value):
        outs[7 + k][...] = value

    update(lambda k: state[3 + k][...], put_out, grad, rate_matrix, decay_matrix)

    def put_small(k, value):
        outs[10 + k][...] = value

    update(lambda k: state[6 + k][...], put_small, small, rate_small, 0.0)


def call(kernel, name, in_specs, outs, scratch, us, room=20):
    return pl.pallas_call(
        kernel,
        out_shape=[jax.ShapeDtypeStruct(shape, dtype) for shape, dtype, _ in outs],
        in_specs=in_specs,
        out_specs=[spec for _, _, spec in outs],
        scratch_shapes=scratch,
        compiler_params=pltpu.CompilerParams(vmem_limit_bytes=room * 2**20),
        cost_estimate=pl.CostEstimate(flops=int(us * 1e9), bytes_accessed=int(us * 3e6), transcendentals=0),
        name=name,
    )


def block(shape):
    return pl.BlockSpec((1,) + tuple(shape[1:]), lambda i: (i,) + (0,) * (len(shape) - 1))


def shards(
    tokens,
    cotangent,
    seq_start,
    time_bucket,
    proj_weight,
    out_weight,
    small_params,
    proj_mean,
    proj_square,
    out_mean,
    out_square,
    small_mean,
    small_square,
):
    n_head = lax.axis_size("head")
    n_dp = lax.axis_size("dp")
    here = tokens.shape[0]
    group = here * n_head
    nb = group // TILE
    per = here // TILE
    rows_here, _, width = proj_weight.shape
    heads = width // HEAD_DIM
    high, low = split_dp(n_dp)

    (weights,) = call(
        cast_kernel,
        "cast",
        [pl.BlockSpec(memory_space=pl.ANY)] * 2,
        [((rows_here, 5 * width), bf16, VMEM)],
        [
            pltpu.VMEM(proj_weight.shape, f32),
            pltpu.VMEM((rows_here, width), f32),
            pltpu.SemaphoreType.DMA((2,)),
        ],
        1,
    )(proj_weight, out_weight.T)
    x_pieces = gather_cores(tokens, gather_chips(after(tokens, weights)))
    w_pieces, offsets, operands = gather_dp(weights)
    cot_chips = gather_chips(after(cotangent, weights))
    starts = seq_start.reshape(1, group)
    small_rows = small_params.reshape(-1, 128)
    times = time_bucket.reshape(1, group)

    pos, oh, oht, trow = call(
        prepare_kernel,
        "prepare",
        [VMEM] * 2,
        [
            ((nb, TILE, TILE), f32, VMEM),
            ((nb, TILE, NTB), bf16, VMEM),
            ((nb, NTB, TILE), bf16, VMEM),
            ((nb, NTB, TILE), bf16, VMEM),
        ],
        [],
        5,
    )(after(times, operands[1]), small_rows)

    items = [
        ((nb, 3 * width, TILE), bf16),
        ((nb, TILE, NTB + width), bf16),
        ((nb, NTB + width, TILE), bf16),
        ((nb, width, TILE), bf16),
        ((nb, TILE, width), bf16),
        ((nb, TILE, width), bf16),
        ((nb, width, TILE), bf16),
    ]
    (xn,) = call(normalize_kernel, "normalize", [VMEM] * n_head, [((nb, TILE, D), bf16, VMEM)], [], 1)(*x_pieces)
    w_pieces[-1] = after(join(w_pieces[-1:], 4), xn)
    (wt,) = call(
        functools.partial(assemble_kernel, offsets),
        "assemble",
        [VMEM] * len(w_pieces),
        [((5 * width, D), bf16, VMEM)],
        [pltpu.VMEM((D, 5 * width), bf16)],
        5,
    )(*w_pieces)
    dsilu, kx, kxt, qs, q, v, vt = call(
        functools.partial(project_kernel, heads),
        "project",
        [VMEM] * 4,
        [item + (VMEM,) for item in items],
        [],
        5,
    )(xn, wt, oh, oht)

    def attend(first, last, *before):
        (attn,) = call(
            functools.partial(attend_kernel, heads, first, last),
            "attend",
            [VMEM] * (len(before) + 6),
            [((last, width, TILE), f32, VMEM)],
            [],
            8,
        )(*before, kx, qs, trow, vt, pos, starts)
        return attn

    split = nb - nb // 4
    attn = attend(0, split)
    cot_chips = after_all(cot_chips, attn)
    attn = attend(split, nb, after(attn, *cot_chips))
    cot_pieces = gather_cores(cotangent, cot_chips)

    column = ((nb, width, TILE), f32, VMEM)
    p_gate, gg, stat, gb = call(
        functools.partial(gate_kernel, n_head),
        "gate",
        [VMEM] * (n_head + 3),
        [column, column, ((nb, 4, TILE), f32, VMEM), ((1, D), f32, VMEM)],
        [],
        5,
    )(*cot_pieces, attn, xn, wt)

    stats = [stat] + [swap(stat, "head", k) for k in range(1, n_head)]
    chips = n_head // 2
    split_shape = ((chips, here, D), bf16, VMEM)
    keep, send = call(
        functools.partial(branch_kernel, n_head), "branch", [VMEM] * (n_head + 3), [split_shape] * 2, [], 1
    )(*stats, attn, p_gate, wt)
    crossed = swap(send, "head", 1)
    da, dat, gun, *early_parts = call(
        functools.partial(middle_kernel, n_head),
        "middle",
        [VMEM] * (2 * n_head + 4),
        [
            ((nb, TILE, width), bf16, VMEM),
            ((nb, width, TILE), bf16, VMEM),
            ((nb, TILE, width), bf16, VMEM),
        ]
        + [((high, rows_here, 2 * width), bf16, VMEM)] * low,
        [pltpu.VMEM((2 * width, D), f32), pltpu.VMEM((D, 2 * width), f32)],
        6,
    )(*stats, *cot_pieces, attn, p_gate, gg, xn)
    branch, *leaving = fold_cores(keep, crossed)
    received = [swap(sent, "head", 2 * (k + 1)) for k, sent in enumerate(leaving)]
    early_received = [swap(early_parts[k], "dp", k) for k in range(1, low)]

    length = D + group + NTB
    extra = -(-length // (128 * n_dp))
    gp, *late_parts = call(
        functools.partial(backward_kernel, heads, n_dp, extra),
        "backward",
        [VMEM] * 13,
        [((nb, TILE, 3 * width), bf16, VMEM)] + [((high, rows_here + 16, 3 * width), bf16, VMEM)] * low,
        [
            pltpu.VMEM((nb, TILE, width), f32),
            pltpu.VMEM((nb, TILE, NTB + width), f32),
            pltpu.VMEM((nb, TILE, TILE), f32),
            pltpu.VMEM((3 * width, D), f32),
            pltpu.VMEM((n_dp * (rows_here + 16), 3 * width), f32),
            pltpu.VMEM((1, extra * n_dp * 128), f32),
        ],
        35,
        ROOM,
    )(kx, kxt, qs, trow, q, v, da, dat, pos, dsilu, xn, starts, gb)

    tied = lax.optimization_barrier((gp, *late_parts, *early_received, *received))
    gp, late_parts = tied[0], tied[1 : 1 + low]
    early_received, received = tied[1 + low : 2 * low], tied[2 * low :]
    late_received = [swap(late_parts[k], "dp", k) for k in range(1, low)]
    keep, send = call(
        functools.partial(input_kernel, n_head),
        "input_rows",
        [VMEM] * 3,
        [((n_head // 2, here, D), bf16, VMEM)] * 2,
        [],
        4,
    )(gp, gun, wt)
    early_blocks = scatter_high(after(early_parts[0], send), early_received, 1)
    crossed = swap(send, "head", 1)
    late_received = after_all(late_received, send, crossed)
    late_blocks = scatter_high(late_parts[0], late_received, 0.1)
    (early,) = call(
        sum_kernel, "sum", [VMEM] * high, [((rows_here, 2 * width), f32, VMEM)], [], 14
    )(*early_blocks)
    mine, *leaving = fold_cores(keep, after(crossed, late_blocks[0]))
    arrived = [swap(leaving[k - 1], "head", 2 * k) for k in range(1, chips)]
    n_all = n_dp * n_head
    grads_shape = ((rows_here, 5 * width), f32)
    grads, message = call(
        functools.partial(collect_kernel, high, extra),
        "collect",
        [VMEM] * (high + 1),
        [grads_shape + (VMEM,), ((n_all, 8, 128), f32, VMEM)],
        [],
        10,
    )(*late_blocks, early)
    message = after(message, *leaving)
    heard = lax.all_to_all(message, ("dp", "head"), 0, 0, tiled=True)
    (mixed,) = call(
        mix_kernel, "mix", [VMEM] * (2 + chips), [((here, D), bf16, VMEM)], [], 1
    )(after(tokens, message), small_rows, branch, *received)
    (input_grad,) = call(
        finish_kernel, "finish", [VMEM] * (2 + chips), [((here, D), f32, VMEM)], [], 1
    )(after(tokens, mixed), cotangent, mine, *arrived)
    heard = after(heard, input_grad)
    state = [proj_weight, proj_mean, proj_square, out_weight.T, out_mean.T, out_square.T]
    state += [x.reshape(-1, 128) for x in (small_params, small_mean, small_square)]
    proj_shape, out_shape, small_shape = proj_weight.shape, (rows_here, width), small_rows.shape
    shapes = [proj_shape, out_shape, small_shape, (1, 1)] + [proj_shape] * 3 + [out_shape] * 3 + [small_shape] * 3
    results = call(
        functools.partial(update_kernel, n_head, extra, group),
        "update",
        [VMEM] * (2 + len(state)),
        [(shape, f32, VMEM) for shape in shapes],
        [],
        0.1,
    )(heard, grads, *state)
    grad_proj, grad_out, grad_small, grad_norm = results[:4]
    grad_out, grad_small, grad_norm = grad_out.T, grad_small.reshape(-1), grad_norm.reshape(())
    new_proj, mean_proj, square_proj = results[4:7]
    new_out, mean_out, square_out = [x.T for x in results[7:10]]
    new_small, mean_small, square_small = [x.reshape(-1) for x in results[10:13]]
    return (
        mixed,
        input_grad,
        grad_proj,
        grad_out,
        grad_small,
        grad_norm,
        new_proj,
        mean_proj,
        square_proj,
        new_out,
        mean_out,
        square_out,
        new_small,
        mean_small,
        square_small,
    )


def solution(mesh):
    in_specs = (
        P(("dp", "head"), None),
        P(("dp", "head"), None),
        P("dp"),
        P("dp"),
        P("dp", None, "head"),
        P("head", "dp"),
        P(),
        P("dp", None, "head"),
        P("dp", None, "head"),
        P("head", "dp"),
        P("head", "dp"),
        P(),
        P(),
    )
    out_specs = (
        P(("dp", "head"), None),
        P(("dp", "head"), None),
        P("dp", None, "head"),
        P("head", "dp"),
        P(),
        P(),
        P("dp", None, "head"),
        P("dp", None, "head"),
        P("dp", None, "head"),
        P("head", "dp"),
        P("head", "dp"),
        P("head", "dp"),
        P(),
        P(),
        P(),
    )
    return jax.shard_map(shards, mesh=mesh, in_specs=in_specs, out_specs=out_specs, check_vma=False)
```

```python
import functools
import math

import jax
import jax.numpy as jnp
from jax import lax
from jax.experimental import pallas as pl
from jax.experimental.pallas import tpu as pltpu
from jax.sharding import PartitionSpec as P

D = 512
HEAD_DIM = 64
HD = 512
POS = 8192
NTB = 128
STEP = 10
TILE = 256
NEG = -1e9
ROOM = 16
KEPT_TILES = 72
VALUES = 12
BACKWARD = 2

norm_epsilon = 1e-06
adam_epsilon = 1e-08
beta_one = 0.9
beta_two = 0.999
clip_norm = 1.0
rate_matrix = 0.05
rate_small = 0.3
decay_matrix = 0.1

f32 = jnp.float32
bf16 = jnp.bfloat16
VMEM = pl.BlockSpec(memory_space=pltpu.VMEM)


def adam_step(weight, grad, first, second, factor, rate, decay):
    clipped = grad * factor
    first_new = beta_one * first + (1.0 - beta_one) * clipped
    second_new = beta_two * second + (1.0 - beta_two) * clipped * clipped
    update = (
        first_new
        / (1.0 - beta_one**STEP)
        / (jnp.sqrt(second_new / (1.0 - beta_two**STEP)) + adam_epsilon)
    )
    return (weight - rate * (update + decay * weight), first_new, second_new)


def swap(x, axis, k):
    n = lax.axis_size(axis)
    return lax.ppermute(x, axis, [(i, i ^ k) for i in range(n)])


def gather_chips(x):
    return [swap(x, "head", k) for k in range(2, lax.axis_size("head"), 2)]


def gather_cores(x, others):
    pieces = [x, swap(x, "head", 1)]
    for other in others:
        pieces += [other, swap(other, "head", 1)]
    return pieces


def after_all(arrays, *others):
    arrays = tuple(arrays)
    return lax.optimization_barrier(arrays + others)[: len(arrays)]


def after(x, *others):
    return lax.optimization_barrier((x,) + others)[0]


def gather_dp(x):
    n = lax.axis_size("dp")
    arrays, offsets, operands = [x], [[0]], []
    k = n // 2
    while k:
        operand = join(arrays) if len(arrays) > 1 else x
        operands.append(operand)
        arrays.append(swap(operand, "dp", k))
        offsets.append([o ^ k for group in offsets for o in group])
        k //= 2
    return arrays, offsets, operands


def join(arrays, us=2):
    shape = (sum(x.shape[0] for x in arrays), arrays[0].shape[1])
    return call(join_kernel, "join", [VMEM] * len(arrays), [(shape, arrays[0].dtype, VMEM)], [], us)(*arrays)[0]


def split_dp(n):
    low = 2 ** ((n.bit_length() - 1) // 2)
    return n // low, low


def scatter_high(own, received, us, *behind):
    high, rows, columns = own.shape
    low = 1 + len(received)
    mine, *leaving = call(
        fold_kernel,
        "fold",
        [VMEM] * low,
        [((rows, columns), f32, VMEM)] + [((rows, columns), bf16, VMEM)] * (high - 1),
        [],
        us,
    )(own, *received)
    leaving = after_all(leaving, *behind)
    order = sorted(range(1, high), key=lambda k: k != high // 2)
    return [mine] + [swap(leaving[k - 1], "dp", k * low) for k in order]


def fold_cores(keep, crossed):
    chips, rows, columns = keep.shape
    return call(
        functools.partial(rows_kernel, chips),
        "rows",
        [VMEM] * 2,
        [((rows, columns), f32, VMEM)] + [((rows, columns), bf16, VMEM)] * (chips - 1),
        [],
        0.1,
    )(keep, crossed)


def dot(a, b):
    return lax.dot_general(a, b, (((1,), (0,)), ((), ())), preferred_element_type=f32)


def dot_nt(a, b):
    return lax.dot_general(a, b, (((1,), (1,)), ((), ())), preferred_element_type=f32)


def flip(a):
    return jnp.transpose(a.astype(f32))


def lanes(i):
    return pl.ds(pl.multiple_of(i * TILE, TILE), TILE)


def by_head(block, heads):
    zero = jnp.zeros((HEAD_DIM, block.shape[1]), block.dtype)
    return jnp.concatenate(
        [
            jnp.concatenate(
                [block[g * HEAD_DIM : (g + 1) * HEAD_DIM] if g == h else zero for g in range(heads)], axis=0
            )
            for h in range(heads)
        ],
        axis=1,
    )


def query_columns(qs, trow, heads):
    return jnp.concatenate([jnp.concatenate([trow] * heads, axis=1), by_head(qs, heads)], axis=0)


def own_rows(block, heads):
    return jnp.concatenate(
        [block[h * HEAD_DIM : (h + 1) * HEAD_DIM, h * TILE : (h + 1) * TILE] for h in range(heads)], axis=0
    )


def own_lanes(block, heads):
    lane = lax.broadcasted_iota(jnp.int32, block.shape, 1) // HEAD_DIM
    return jnp.concatenate([jnp.where(lane == h, block, jnp.zeros_like(block)) for h in range(heads)], axis=0)


def masked(product, bias, start, j, heads):
    key = j * TILE + lax.broadcasted_iota(jnp.int32, (TILE, TILE), 0)
    seen = key >= start
    return jnp.where(
        jnp.concatenate([seen] * heads, axis=1), product + jnp.concatenate([bias] * heads, axis=1), NEG
    )


def diagonals(x):
    rows, cols = x.shape
    z = jnp.concatenate([x, jnp.zeros((rows, cols), f32)], axis=1)
    total = z[:8]
    for q in range(1, rows // 8):
        total = total + pltpu.roll(z[8 * q : 8 * q + 8], 2 * cols - 8 * q, 1)
    g = total[0:1]
    for r in range(1, 8):
        g = g + pltpu.roll(total, 2 * cols - r, 1)[r : r + 1]
    return g


def cast_kernel(w_in, o_in, low_ref, w_ref, o_ref, sems):
    copies = [pltpu.make_async_copy(w_in, w_ref, sems.at[0]), pltpu.make_async_copy(o_in, o_ref, sems.at[1])]
    for copy in copies:
        copy.start()
    for copy in copies:
        copy.wait()
    width = o_ref.shape[1]
    for c in range(4):
        low_ref[:, c * width : (c + 1) * width] = w_ref[:, c, :].astype(bf16)
    low_ref[:, 4 * width :] = o_ref[...].astype(bf16)


def row_lanes(ref, first, count):
    return jnp.concatenate([ref[pl.ds(first + k, 1), :] for k in range(count)], axis=1)


def prepare_kernel(tb_ref, small_ref, pos_ref, oh_ref, oht_ref, trow_ref):
    nb = pos_ref.shape[0]
    step = TILE // 128

    def tile(d, _):
        first = D // 128 + d * step
        row = jnp.concatenate([row_lanes(small_ref, first, step), row_lanes(small_ref, first - step, step)], axis=1)
        pos_ref[d] = pltpu.roll(
            jnp.broadcast_to(row * 0.5, (TILE, 2 * TILE)), 0, 1, stride=1, stride_axis=0
        )[:, :TILE]
        return 0

    lax.fori_loop(0, nb, tile, 0)
    b = lax.broadcasted_iota(jnp.int32, (TILE, TILE), 0)
    a = lax.broadcasted_iota(jnp.int32, (TILE, TILE), 1)
    pos_ref[0] = jnp.where(b <= a, pos_ref[0], NEG)
    table = row_lanes(small_ref, (D + POS) // 128, NTB // 128)
    row = jnp.concatenate([table, table], axis=1)
    upper = pltpu.roll(jnp.broadcast_to(row, (NTB, 2 * NTB)), 0, 1, stride=1, stride_axis=0)[:, :NTB]
    a = lax.broadcasted_iota(jnp.int32, (NTB, NTB), 0)
    b = lax.broadcasted_iota(jnp.int32, (NTB, NTB), 1)
    upper = jnp.where(b >= a, upper, 0.0)
    square = (jnp.where(b > a, upper, jnp.transpose(upper)) * 0.5).astype(bf16)

    def block(i, _):
        onehot = (lax.broadcasted_iota(jnp.int32, (NTB, TILE), 0) == tb_ref[:, lanes(i)]).astype(f32)
        low = onehot.astype(bf16)
        oht_ref[i] = low
        oh_ref[i] = flip(onehot).astype(bf16)
        trow_ref[i] = dot(square, low).astype(bf16)
        return 0

    lax.fori_loop(0, nb, block, 0)


def join_kernel(*refs):
    at = 0
    for ref in refs[:-1]:
        refs[-1][at : at + ref.shape[0]] = ref[...]
        at += ref.shape[0]


def normalize_kernel(*refs):
    x_pieces, xn_ref = refs[:-1], refs[-1]
    per = x_pieces[0].shape[0] // TILE
    for k, piece in enumerate(x_pieces):
        for r in range(per):
            x = piece[r * TILE : (r + 1) * TILE, :].astype(f32)
            x = x - jnp.sum(x, axis=1, keepdims=True) / D
            x = x * lax.rsqrt(jnp.sum(x * x, axis=1, keepdims=True) / D + norm_epsilon)
            xn_ref[(lax.axis_index("head") ^ k) * per + r] = x.astype(bf16)


def assemble_kernel(offsets, *refs):
    w_pieces, (wt_ref, w_ref) = refs[:-2], refs[-2:]
    for piece, group in zip(w_pieces, offsets):
        rows = piece.shape[0] // len(group)
        for at, offset in enumerate(group):
            start = pl.multiple_of((lax.axis_index("dp") ^ offset) * rows, 16)
            w_ref[pl.ds(start, rows), :] = piece[at * rows : (at + 1) * rows, :]
    wt_ref[...] = flip(w_ref[...]).astype(bf16)


def project_kernel(heads, *refs):
    refs = list(refs)
    take = lambda count: [refs.pop(0) for _ in range(count)]
    xn_ref, wt_ref, oh_ref, oht_ref = take(4)
    d_ref, kx_ref, kxt_ref, qs_ref, q_ref, v_ref, vt_ref = refs
    width = v_ref.shape[2]

    def project(i):
        x = xn_ref[i]
        p = dot_nt(wt_ref[width : 4 * width], x)
        sg = 0.5 + 0.5 * jnp.tanh(0.5 * p)
        act = p * sg
        d_ref[i] = (sg + act * (1.0 - sg)).astype(bf16)
        vt = act[:width]
        vt_ref[i] = vt.astype(bf16)
        v_ref[i] = flip(vt).astype(bf16)
        qt = act[width : 2 * width].astype(bf16)
        kt = act[2 * width :]
        kxt_ref[i, :NTB] = oht_ref[i]
        kxt_ref[i, NTB:] = kt.astype(bf16)
        kx_ref[i, :, :NTB] = oh_ref[i]
        kx_ref[i, :, NTB:] = flip(kt).astype(bf16)
        qs = (qt.astype(f32) * (0.5 / math.sqrt(HEAD_DIM))).astype(bf16)
        qs_ref[i] = qs
        q_ref[i] = flip(qt).astype(bf16)

    for i in range(xn_ref.shape[0]):
        project(i)

def tile_at(refs, i, j):
    at = i * (i + 1) // 2 + j
    for ref in refs:
        if at < ref.shape[0]:
            return ref[at]
        at -= ref.shape[0]


def weights_and_slope(h):
    th = jnp.tanh(h)
    u = 1.0 + th
    w = h * u
    return w, u + w * (1.0 - th)


def attend_kernel(heads, first, last, kept, *refs):
    if first:
        before_ref, refs = refs[0], refs[1:]
    kx_ref, qs_ref, trow_ref, vt_ref, pos_ref, ss_ref, attn_ref = refs[:7]
    if first:
        attn_ref[:first] = before_ref[...]
    for i in range(first, last):
        queries = query_columns(qs_ref[i], trow_ref[i], heads)
        scores = [dot(kx_ref[j], queries) for j in range(i + 1)]
        weights = []
        for j in range(i + 1):
            h = masked(scores[j], pos_ref[i - j], ss_ref[:, i * TILE : (i + 1) * TILE], j, heads)
            w, slope = weights_and_slope(h)
            weights.append(w.astype(bf16))
            if kept:
                at = (i * (i + 1) - first * (first + 1)) // 2 + j
                refs[7][at] = weights[j]
                refs[8][at] = slope.astype(bf16)
        total = dot(vt_ref[0], weights[0])
        for j in range(1, i + 1):
            total = total + dot(vt_ref[j], weights[j])
        attn_ref[i] = own_rows(total, heads)


def gate_kernel(n_head, *refs):
    refs = list(refs)
    take = lambda count: [refs.pop(0) for _ in range(count)]
    cot_pieces = take(n_head)
    attn_ref, xn_ref, wt_ref = take(3)
    p_ref, gg_ref, stat_ref, gb_ref = refs
    width = attn_ref.shape[1]
    per = cot_pieces[0].shape[0] // TILE
    gb_ref[...] = jnp.sum(cot_pieces[0][...].astype(f32), axis=0, keepdims=True)
    for k, piece in enumerate(cot_pieces):
        for r in range(per):
            i = (lax.axis_index("head") ^ k) * per + r
            p = dot_nt(wt_ref[:width], xn_ref[i])
            gate = p * (0.5 + 0.5 * jnp.tanh(0.5 * p))
            gg = dot_nt(wt_ref[4 * width :], piece[r * TILE : (r + 1) * TILE, :])
            grad = gg * gate
            p_ref[i] = p
            gg_ref[i] = gg
            at = attn_ref[i]
            mean = jnp.sum(at, axis=0, keepdims=True) / width
            centred = at - mean
            stat_ref[i] = jnp.concatenate(
                [
                    mean,
                    jnp.sum(centred * centred, axis=0, keepdims=True),
                    jnp.sum(grad, axis=0, keepdims=True),
                    jnp.sum(grad * centred, axis=0, keepdims=True),
                ],
                axis=0,
            )


def standardized(i, n_head, stats, attn_ref):
    width = attn_ref.shape[1]
    st = [s[i] for s in stats]
    mean = sum(p[0:1] for p in st) / n_head
    spread = sum(p[1:2] + width * (p[0:1] - mean) * (p[0:1] - mean) for p in st)
    scale = lax.rsqrt(spread / HD + norm_epsilon)
    first = sum(p[2:3] for p in st) / HD
    second = scale * sum(p[3:4] + (p[0:1] - mean) * p[2:3] for p in st) / HD
    return (attn_ref[i] - mean) * scale, scale, first, second


def branch_kernel(n_head, *refs):
    stats, (attn_ref, p_ref, wt_ref, keep, send) = refs[:n_head], refs[n_head:]
    width = attn_ref.shape[1]
    per = keep.shape[1] // TILE
    for k in range(n_head):
        device = lax.axis_index("head") ^ k
        for r in range(per):
            i = device * per + r
            normed = standardized(i, n_head, stats, attn_ref)[0]
            p = p_ref[i]
            gated = (normed * (p * (0.5 + 0.5 * jnp.tanh(0.5 * p)))).astype(bf16)
            (keep, send)[k % 2][device // 2, r * TILE : (r + 1) * TILE] = dot(
                flip(gated).astype(bf16), wt_ref[4 * width :]
            ).astype(bf16)


def middle_kernel(n_head, *refs):
    refs = list(refs)
    take = lambda count: [refs.pop(0) for _ in range(count)]
    stats = take(n_head)
    cot_pieces = take(n_head)
    attn_ref, p_ref, gg_ref, xn_ref = take(4)
    da_ref, dat_ref, gun_ref = take(3)
    (acc_ref,) = refs
    width = attn_ref.shape[1]
    per = cot_pieces[0].shape[0] // TILE
    for k, piece in enumerate(cot_pieces):
        for r in range(per):
            i = (lax.axis_index("head") ^ k) * per + r
            normed, scale, first, second = standardized(i, n_head, stats, attn_ref)
            p = p_ref[i]
            sg = 0.5 + 0.5 * jnp.tanh(0.5 * p)
            gate = p * sg
            gg = gg_ref[i]
            gated = (normed * gate).astype(bf16)
            grad = scale * (gg * gate - first - normed * second)
            da_ref[i] = flip(grad).astype(bf16)
            dat_ref[i] = (grad * 0.5).astype(bf16)
            gu = (gg * normed * (sg + gate * (1.0 - sg))).astype(bf16)
            gun_ref[i] = flip(gu).astype(bf16)
            add_gate, add_out = dot(gu, xn_ref[i]), dot(gated, piece[r * TILE : (r + 1) * TILE, :])
            if k + r == 0:
                acc_ref[:width] = add_gate
                acc_ref[width:] = add_out
            else:
                acc_ref[:width] += add_gate
                acc_ref[width:] += add_out


def send_parts(wg_ref, parts):
    low = len(parts)
    high, rows = parts[0].shape[0], parts[0].shape[1]
    me = lax.axis_index("dp") % low
    for k in range(low):
        for p in range(high):
            start = pl.multiple_of((p * low + (me ^ k)) * rows, 16)
            parts[k][p] = wg_ref[pl.ds(start, rows), :].astype(bf16)


def values_kernel(heads, kept, *refs):
    refs = list(refs)
    take = lambda count: [refs.pop(0) for _ in range(count)]
    held = take(2 if kept else 5)
    da_ref, d_ref, xn_ref, acc_in = take(4)
    gpv_ref = refs.pop(0)
    parts, wg_ref = refs[:-1], refs[-1]
    nb, width = da_ref.shape[0], da_ref.shape[2]
    das = [own_lanes(da_ref[i], heads) for i in range(nb)]
    queries = None if kept else [query_columns(held[1][i], held[2][i], heads) for i in range(nb)]
    acc = None
    for j in range(nb):
        if kept:
            tiles = [tile_at(held, i, j) for i in range(j, nb)]
        else:
            kx_ref, _, _, pos_ref, ss_ref = held
            tiles = [
                weights_and_slope(
                    masked(
                        dot(kx_ref[j], queries[i]), pos_ref[i - j], ss_ref[:, i * TILE : (i + 1) * TILE], j, heads
                    )
                )[0].astype(bf16)
                for i in range(j, nb)
            ]
        total = dot(jnp.concatenate(tiles, axis=1), jnp.concatenate(das[j:], axis=0))
        gv = (flip(total) * d_ref[j, :width]).astype(bf16)
        gpv_ref[j] = flip(gv).astype(bf16)
        more = dot(gv, xn_ref[j])
        acc = more if j == 0 else acc + more
    wg_ref[...] = flip(jnp.concatenate([acc_in[...], acc], axis=0))
    send_parts(wg_ref, parts)


def backward_kernel(heads, n_dp, extra, kept, *refs):
    refs = list(refs)
    take = lambda count: [refs.pop(0) for _ in range(count)]
    held = take(2 if kept else 4)
    kx_ref, kxt_ref, q_ref, v_ref, dat_ref = take(5)
    d_ref, xn_ref, gb_ref = take(3)
    gp_ref = refs.pop(0)
    parts = take(split_dp(n_dp)[1])
    acck_ref, posg_ref, acc_ref, wg_ref, small_ref = refs
    nb, width = v_ref.shape[0], v_ref.shape[2]
    factor = 1.0 / math.sqrt(HEAD_DIM)
    tiles = [(i, j) for i in reversed(range(nb)) for j in range(i + 1)]
    products, grads = {}, {}
    dq = m2 = None
    small_ref[...] = jnp.zeros_like(small_ref)
    small_ref[:, :D] = gb_ref[...]

    def add(ref, at, value, first):
        ref[at] = value if first else ref[at] + value

    for t in range(len(tiles) + 2):
        if t < len(tiles):
            i, j = tiles[t]
            if j == 0:
                backs = by_head(dat_ref[i], heads)
                queries = None if kept else query_columns(held[0][i], held[1][i], heads)
            products[t] = dot(v_ref[j], backs), None if kept else dot(kx_ref[j], queries)
        if 0 <= t - 1 < len(tiles):
            i, j = tiles[t - 1]
            back, product = products.pop(t - 1)
            if kept:
                slope = tile_at(held, i, j).astype(f32)
            else:
                start = held[3][:, i * TILE : (i + 1) * TILE]
                slope = weights_and_slope(masked(product, held[2][i - j], start, j, heads))[1]
            ds = back * slope
            grads[t - 1] = ds.astype(bf16)
            add(posg_ref, i - j, sum(ds[:, g * TILE : (g + 1) * TILE] for g in range(heads)), i == nb - 1)
        if t >= 2:
            i, j = tiles[t - 2]
            low = grads.pop(t - 2)
            if j == 0:
                times = jnp.concatenate([kx_ref[i, :, :NTB]] * heads, axis=0)
                q = jnp.concatenate([times, own_lanes(q_ref[i], heads)], axis=1)
            add(acck_ref, j, dot(low, q), i == nb - 1)
            more = dot(kxt_ref[j, NTB:], low)
            dq = more if j == 0 else dq + more
            if i == j:
                gp = jnp.concatenate([own_rows(dq, heads), flip(acck_ref[i, :, NTB:])], axis=0)
                gp = (gp * factor * d_ref[i, width:]).astype(bf16)
                gp_ref[i] = flip(gp).astype(bf16)
                more = dot(gp, xn_ref[i])
                acc_ref[...] = more if i == nb - 1 else acc_ref[...] + more
                part = acck_ref[i, :, :NTB]
                high = part.astype(bf16)
                rest = (part - high.astype(f32)).astype(bf16)
                onehot = kxt_ref[i, :NTB]
                part = dot(onehot, high) + dot(onehot, rest)
                m2 = part if i == nb - 1 else m2 + part
                g = diagonals(posg_ref[i])
                small_ref[:, D + i * TILE : D + (i + 1) * TILE] += g[:, :TILE]
                if i > 0:
                    small_ref[:, D + (i - 1) * TILE : D + i * TILE] += g[:, TILE:]
    g = diagonals(m2 + jnp.transpose(m2))[:, :NTB]
    zero = lax.broadcasted_iota(jnp.int32, (1, NTB), 1) == 0
    at = D + nb * TILE
    small_ref[:, at : at + NTB] = jnp.where(zero, 0.5 * g, g)
    step = D // n_dp
    grads = flip(acc_ref[...])
    for p in range(n_dp):
        here = jnp.concatenate(
            [small_ref[:, (p * extra + r) * 128 : (p * extra + r + 1) * 128] for r in range(extra)], axis=0
        )
        high = here.astype(bf16).astype(f32)
        block = jnp.concatenate([high, here - high, jnp.zeros((16 - 2 * extra, 128), f32)], axis=0)
        wg_ref[p * (step + 16) : p * (step + 16) + step] = grads[p * step : (p + 1) * step]
        if 2 * width > 128:
            block = jnp.concatenate([block, jnp.zeros((16, 2 * width - 128), f32)], axis=1)
        wg_ref[p * (step + 16) + step : (p + 1) * (step + 16)] = block
    send_parts(wg_ref, parts)


def input_kernel(n_head, gp_ref, gun_ref, gpv_ref, wt_ref, keep, send):
    width = gun_ref.shape[2]
    per = keep.shape[1] // TILE
    for k in range(n_head):
        device = lax.axis_index("head") ^ k
        target = (keep, send)[k % 2]
        for r in range(per):
            i = device * per + r
            rows = dot(jnp.concatenate([gun_ref[i], gpv_ref[i]], axis=1), wt_ref[: 2 * width])
            rows = rows + dot(gp_ref[i], wt_ref[2 * width : 4 * width])
            target[device // 2, r * TILE : (r + 1) * TILE] = rows.astype(bf16)


def fold_kernel(*refs):
    low = sum(len(ref.shape) == 3 for ref in refs)
    row = lax.axis_index("dp") // low
    for k, out in enumerate(refs[low:]):
        total = refs[0][row ^ k].astype(f32)
        for ref in refs[1:low]:
            total = total + ref[row ^ k].astype(f32)
        out[...] = total.astype(out.dtype)


def sum_kernel(*refs):
    total = refs[0][...]
    for ref in refs[1:-1]:
        total = total + ref[...].astype(f32)
    refs[-1][...] = total


def mix_kernel(tokens_ref, bias_ref, *refs):
    total = tokens_ref[...].astype(f32) + row_lanes(bias_ref, 0, D // 128)
    for ref in refs[:-1]:
        total = total + ref[...].astype(f32)
    refs[-1][...] = total.astype(bf16)


def finish_kernel(tokens_ref, cot_ref, mine_ref, *refs):
    x = tokens_ref[...].astype(f32)
    x = x - jnp.sum(x, axis=1, keepdims=True) / D
    scale = lax.rsqrt(jnp.sum(x * x, axis=1, keepdims=True) / D + norm_epsilon)
    x = x * scale
    grad = mine_ref[...]
    for ref in refs[:-1]:
        grad = grad + ref[...].astype(f32)
    mean = jnp.sum(grad, axis=1, keepdims=True) / D
    along = jnp.sum(grad * x, axis=1, keepdims=True) / D
    refs[-1][...] = cot_ref[...].astype(f32) + scale * (grad - mean - x * along)


def rows_kernel(chips, keep_ref, crossed_ref, mine_ref, *leaving):
    chip = lax.axis_index("head") // 2
    for k in range(chips):
        total = keep_ref[chip ^ k].astype(f32) + crossed_ref[chip ^ k].astype(f32)
        if k == 0:
            mine_ref[...] = total
        else:
            leaving[k - 1][...] = total.astype(bf16)


def collect_kernel(high, extra, *refs):
    late_blocks, (early_ref, grads_ref, message_ref) = refs[:high], refs[high:]
    rows = grads_ref.shape[0]
    total, early = late_blocks[0][...], early_ref[...]
    for k in range(1, high):
        total = total + late_blocks[k][...].astype(f32)
    grads = jnp.concatenate([total[:rows], early], axis=1)
    grads_ref[...] = grads
    squares = jnp.sum(jnp.sum(grads * grads, axis=0, keepdims=True), axis=1, keepdims=True)
    message = jnp.concatenate(
        [
            total[rows : rows + extra, :128] + total[rows + extra : rows + 2 * extra, :128],
            jnp.zeros((7 - extra, 128), f32),
            jnp.broadcast_to(squares, (1, 128)),
        ],
        axis=0,
    )
    for k in range(message_ref.shape[0]):
        message_ref[k] = message


def update_kernel(n_head, extra, group, heard_ref, grads_ref, *refs):
    state, outs = refs[:9], refs[9:]
    grad_proj_ref, grad_out_ref, grad_small_ref, norm_ref = outs[:4]
    n_all = heard_ref.shape[0]
    width = grad_out_ref.shape[1]
    lead, pos_rows, used = D // 128, POS // 128, (D + group) // 128
    grad_small_ref[...] = jnp.zeros_like(grad_small_ref)
    squares = heard_ref[0, 7:8, :]
    for k in range(1, n_all):
        squares = squares + heard_ref[k, 7:8, :]
    for p in range(n_all // n_head):
        rows = heard_ref[p * n_head, :extra, :]
        for h in range(1, n_head):
            rows = rows + heard_ref[p * n_head + h, :extra, :]
        for r in range(extra):
            at = p * extra + r
            if at < used:
                grad_small_ref[at : at + 1, :] = rows[r : r + 1]
            elif at == used:
                grad_small_ref[lead + pos_rows : lead + pos_rows + 1, :] = rows[r : r + 1]
    small = grad_small_ref[...]
    total = jnp.sum(jnp.sum(small * small, axis=0, keepdims=True), axis=1, keepdims=True) + squares[:, :1]
    norm = jnp.sqrt(total)
    norm_ref[...] = norm
    factor = jnp.minimum(1.0, clip_norm / (norm + 1e-06))

    def update(get, put, grad, rate, decay):
        for k, value in enumerate(adam_step(get(0), grad, get(1), get(2), factor, rate, decay)):
            put(k, value)

    for c in range(4):
        at = (2, 4, 0, 1)[c] * width
        grad = grads_ref[:, at : at + width]
        grad_proj_ref[:, c, :] = grad

        def put(k, value):
            outs[4 + k][:, c, :] = value

        update(lambda k: state[k][:, c, :], put, grad, rate_matrix, decay_matrix)
    grad = grads_ref[:, 3 * width : 4 * width]
    grad_out_ref[...] = grad

    def put_out(k, value):
        outs[7 + k][...] = value

    update(lambda k: state[3 + k][...], put_out, grad, rate_matrix, decay_matrix)

    def put_small(k, value):
        outs[10 + k][...] = value

    update(lambda k: state[6 + k][...], put_small, small, rate_small, 0.0)


def call(kernel, name, in_specs, outs, scratch, us, room=16):
    return pl.pallas_call(
        kernel,
        out_shape=[jax.ShapeDtypeStruct(shape, dtype) for shape, dtype, _ in outs],
        in_specs=in_specs,
        out_specs=[spec for _, _, spec in outs],
        scratch_shapes=scratch,
        compiler_params=pltpu.CompilerParams(vmem_limit_bytes=room * 2**20 * max(1, lax.axis_size("head") // 4)),
        cost_estimate=pl.CostEstimate(flops=int(us * 1e9), bytes_accessed=int(us * 3e6), transcendentals=0),
        name=name,
    )


def block(shape):
    return pl.BlockSpec((1,) + tuple(shape[1:]), lambda i: (i,) + (0,) * (len(shape) - 1))


def shards(
    tokens,
    cotangent,
    seq_start,
    time_bucket,
    proj_weight,
    out_weight,
    small_params,
    proj_mean,
    proj_square,
    out_mean,
    out_square,
    small_mean,
    small_square,
):
    n_head = lax.axis_size("head")
    n_dp = lax.axis_size("dp")
    here = tokens.shape[0]
    group = here * n_head
    nb = group // TILE
    per = here // TILE
    rows_here, _, width = proj_weight.shape
    heads = width // HEAD_DIM
    high, low = split_dp(n_dp)

    (weights,) = call(
        cast_kernel,
        "cast",
        [pl.BlockSpec(memory_space=pl.ANY)] * 2,
        [((rows_here, 5 * width), bf16, VMEM)],
        [
            pltpu.VMEM(proj_weight.shape, f32),
            pltpu.VMEM((rows_here, width), f32),
            pltpu.SemaphoreType.DMA((2,)),
        ],
        1,
    )(proj_weight, out_weight.T)
    x_pieces = gather_cores(tokens, gather_chips(after(tokens, weights)))
    w_pieces, offsets, operands = gather_dp(weights)
    cot_chips = gather_chips(after(cotangent, weights))
    starts = seq_start.reshape(1, group)
    small_rows = small_params.reshape(-1, 128)
    times = time_bucket.reshape(1, group)

    pos, oh, oht, trow = call(
        prepare_kernel,
        "prepare",
        [VMEM] * 2,
        [
            ((nb, TILE, TILE), f32, VMEM),
            ((nb, TILE, NTB), bf16, VMEM),
            ((nb, NTB, TILE), bf16, VMEM),
            ((nb, NTB, TILE), bf16, VMEM),
        ],
        [],
        5,
    )(after(times, operands[1]), small_rows)

    items = [
        ((nb, 3 * width, TILE), bf16),
        ((nb, TILE, NTB + width), bf16),
        ((nb, NTB + width, TILE), bf16),
        ((nb, width, TILE), bf16),
        ((nb, TILE, width), bf16),
        ((nb, TILE, width), bf16),
        ((nb, width, TILE), bf16),
    ]
    (xn,) = call(normalize_kernel, "normalize", [VMEM] * n_head, [((nb, TILE, D), bf16, VMEM)], [], 1)(*x_pieces)
    w_pieces[-1] = after(join(w_pieces[-1:], 4), xn)
    (wt,) = call(
        functools.partial(assemble_kernel, offsets),
        "assemble",
        [VMEM] * len(w_pieces),
        [((5 * width, D), bf16, VMEM)],
        [pltpu.VMEM((D, 5 * width), bf16)],
        5,
    )(*w_pieces)
    dsilu, kx, kxt, qs, q, v, vt = call(
        functools.partial(project_kernel, heads),
        "project",
        [VMEM] * 4,
        [item + (VMEM,) for item in items],
        [],
        5,
    )(xn, wt, oh, oht)

    kept = nb * (nb + 1) // 2 * heads <= KEPT_TILES

    def attend(first, last, *before):
        count = (last * (last + 1) - first * (first + 1)) // 2
        return call(
            functools.partial(attend_kernel, heads, first, last, kept),
            "attend",
            [VMEM] * (len(before) + 6),
            [((last, width, TILE), f32, VMEM)] + [((count, TILE, heads * TILE), bf16, VMEM)] * (2 * kept),
            [],
            8,
        )(*before, kx, qs, trow, vt, pos, starts)

    split = nb - nb // 4
    attn, *kept_first = attend(0, split)
    cot_chips = after_all(cot_chips, attn)
    attn, *kept_last = attend(split, nb, after(attn, *cot_chips))
    kept_weights, kept_slopes = zip(kept_first, kept_last) if kept else ((), ())
    cot_pieces = gather_cores(cotangent, cot_chips)

    column = ((nb, width, TILE), f32, VMEM)
    p_gate, gg, stat, gb = call(
        functools.partial(gate_kernel, n_head),
        "gate",
        [VMEM] * (n_head + 3),
        [column, column, ((nb, 4, TILE), f32, VMEM), ((1, D), f32, VMEM)],
        [],
        5,
    )(*cot_pieces, attn, xn, wt)

    stats = [stat] + [swap(stat, "head", k) for k in range(1, n_head)]
    chips = n_head // 2
    split_shape = ((chips, here, D), bf16, VMEM)
    keep, send = call(
        functools.partial(branch_kernel, n_head), "branch", [VMEM] * (n_head + 3), [split_shape] * 2, [], 1
    )(*stats, attn, p_gate, wt)
    crossed = swap(send, "head", 1)
    da, dat, gun, wg_sum = call(
        functools.partial(middle_kernel, n_head),
        "middle",
        [VMEM] * (2 * n_head + 4),
        [
            ((nb, TILE, width), bf16, VMEM),
            ((nb, width, TILE), bf16, VMEM),
            ((nb, TILE, width), bf16, VMEM),
            ((2 * width, D), f32, VMEM),
        ],
        [],
        6,
    )(*stats, *cot_pieces, attn, p_gate, gg, xn)
    branch, *leaving = fold_cores(keep, crossed)
    received = [swap(sent, "head", 2 * (k + 1)) for k, sent in enumerate(leaving)]
    held = kept_weights if kept else (kx, qs, trow, pos, starts)
    gpv, *early_parts = call(
        functools.partial(values_kernel, heads, kept),
        "values",
        [VMEM] * (len(held) + 4),
        [((nb, TILE, width), bf16, VMEM)] + [((high, rows_here, 3 * width), bf16, VMEM)] * low,
        [pltpu.VMEM((D, 3 * width), f32)],
        VALUES,
    )(*held, da, dsilu, xn, wg_sum)
    early_received = [swap(early_parts[k], "dp", k) for k in range(1, low)]

    length = D + group + NTB
    extra = -(-length // (128 * n_dp))
    held = kept_slopes if kept else (qs, trow, pos, starts)
    gp, *late_parts = call(
        functools.partial(backward_kernel, heads, n_dp, extra, kept),
        "backward",
        [VMEM] * (len(held) + 8),
        [((nb, TILE, 2 * width), bf16, VMEM)] + [((high, rows_here + 16, 2 * width), bf16, VMEM)] * low,
        [
            pltpu.VMEM((nb, TILE, NTB + width), f32),
            pltpu.VMEM((nb, TILE, TILE), f32),
            pltpu.VMEM((2 * width, D), f32),
            pltpu.VMEM((n_dp * (rows_here + 16), 2 * width), f32),
            pltpu.VMEM((1, extra * n_dp * 128), f32),
        ],
        BACKWARD,
        ROOM,
    )(*held, kx, kxt, q, v, dat, dsilu, xn, gb)

    tied = lax.optimization_barrier((gp, *late_parts, *early_received, *received))
    gp, late_parts = tied[0], tied[1 : 1 + low]
    early_received, received = tied[1 + low : 2 * low], tied[2 * low :]
    late_received = [swap(late_parts[k], "dp", k) for k in range(1, low)]
    keep, send = call(
        functools.partial(input_kernel, n_head),
        "input_rows",
        [VMEM] * 4,
        [((n_head // 2, here, D), bf16, VMEM)] * 2,
        [],
        4,
    )(gp, gun, gpv, wt)
    early_blocks = scatter_high(after(early_parts[0], send), early_received, 1)
    crossed = swap(send, "head", 1)
    late_blocks = scatter_high(late_parts[0], late_received, 12, send, crossed)
    (early,) = call(
        sum_kernel, "sum", [VMEM] * high, [((rows_here, 3 * width), f32, VMEM)], [], 14
    )(*early_blocks)
    mine, *leaving = fold_cores(keep, after(crossed, late_blocks[0]))
    arrived = [swap(leaving[k - 1], "head", 2 * k) for k in range(1, chips)]
    n_all = n_dp * n_head
    grads_shape = ((rows_here, 5 * width), f32)
    grads, message = call(
        functools.partial(collect_kernel, high, extra),
        "collect",
        [VMEM] * (high + 1),
        [grads_shape + (VMEM,), ((n_all, 8, 128), f32, VMEM)],
        [],
        10,
    )(*late_blocks, early)
    message = after(message, *leaving)
    heard = lax.all_to_all(message, ("dp", "head"), 0, 0, tiled=True)
    (mixed,) = call(
        mix_kernel, "mix", [VMEM] * (2 + chips), [((here, D), bf16, VMEM)], [], 1
    )(tokens, small_rows, after(branch, message), *received)
    (input_grad,) = call(
        finish_kernel, "finish", [VMEM] * (2 + chips), [((here, D), f32, VMEM)], [], 1
    )(tokens, cotangent, mine, *arrived)
    heard = after(heard, input_grad)
    state = [proj_weight, proj_mean, proj_square, out_weight.T, out_mean.T, out_square.T]
    state += [x.reshape(-1, 128) for x in (small_params, small_mean, small_square)]
    proj_shape, out_shape, small_shape = proj_weight.shape, (rows_here, width), small_rows.shape
    shapes = [proj_shape, out_shape, small_shape, (1, 1)] + [proj_shape] * 3 + [out_shape] * 3 + [small_shape] * 3
    results = call(
        functools.partial(update_kernel, n_head, extra, group),
        "update",
        [VMEM] * (2 + len(state)),
        [(shape, f32, VMEM) for shape in shapes],
        [],
        0.1,
    )(heard, grads, *state)
    grad_proj, grad_out, grad_small, grad_norm = results[:4]
    grad_out, grad_small, grad_norm = grad_out.T, grad_small.reshape(-1), grad_norm.reshape(())
    new_proj, mean_proj, square_proj = results[4:7]
    new_out, mean_out, square_out = [x.T for x in results[7:10]]
    new_small, mean_small, square_small = [x.reshape(-1) for x in results[10:13]]
    return (
        mixed,
        input_grad,
        grad_proj,
        grad_out,
        grad_small,
        grad_norm,
        new_proj,
        mean_proj,
        square_proj,
        new_out,
        mean_out,
        square_out,
        new_small,
        mean_small,
        square_small,
    )


def solution(mesh):
    in_specs = (
        P(("dp", "head"), None),
        P(("dp", "head"), None),
        P("dp"),
        P("dp"),
        P("dp", None, "head"),
        P("head", "dp"),
        P(),
        P("dp", None, "head"),
        P("dp", None, "head"),
        P("head", "dp"),
        P("head", "dp"),
        P(),
        P(),
    )
    out_specs = (
        P(("dp", "head"), None),
        P(("dp", "head"), None),
        P("dp", None, "head"),
        P("head", "dp"),
        P(),
        P(),
        P("dp", None, "head"),
        P("dp", None, "head"),
        P("dp", None, "head"),
        P("head", "dp"),
        P("head", "dp"),
        P("head", "dp"),
        P(),
        P(),
        P(),
    )
    return jax.shard_map(shards, mesh=mesh, in_specs=in_specs, out_specs=out_specs, check_vma=False)
```

```python
import functools
import math

import jax
import jax.numpy as jnp
from jax import lax
from jax.experimental import pallas as pl
from jax.experimental.pallas import tpu as pltpu
from jax.sharding import PartitionSpec as P

D = 512
HEAD_DIM = 64
HD = 512
POS = 8192
NTB = 128
STEP = 10
TILE = 256
NEG = -1e9
ROOM = 16
KEPT_TILES = 72
VALUES = 12
BACKWARD = 2

norm_epsilon = 1e-06
adam_epsilon = 1e-08
beta_one = 0.9
beta_two = 0.999
clip_norm = 1.0
rate_matrix = 0.05
rate_small = 0.3
decay_matrix = 0.1

f32 = jnp.float32
bf16 = jnp.bfloat16
VMEM = pl.BlockSpec(memory_space=pltpu.VMEM)


def adam_step(weight, grad, first, second, factor, rate, decay):
    clipped = grad * factor
    first_new = beta_one * first + (1.0 - beta_one) * clipped
    second_new = beta_two * second + (1.0 - beta_two) * clipped * clipped
    update = (
        first_new
        / (1.0 - beta_one**STEP)
        / (jnp.sqrt(second_new / (1.0 - beta_two**STEP)) + adam_epsilon)
    )
    return (weight - rate * (update + decay * weight), first_new, second_new)


def swap(x, axis, k):
    n = lax.axis_size(axis)
    return lax.ppermute(x, axis, [(i, i ^ k) for i in range(n)])


def gather_chips(x):
    return [swap(x, "head", k) for k in range(2, lax.axis_size("head"), 2)]


def gather_cores(x, others):
    pieces = [x, swap(x, "head", 1)]
    for other in others:
        pieces += [other, swap(other, "head", 1)]
    return pieces


def after_all(arrays, *others):
    arrays = tuple(arrays)
    return lax.optimization_barrier(arrays + others)[: len(arrays)]


def after(x, *others):
    return lax.optimization_barrier((x,) + others)[0]


def gather_dp(x):
    n = lax.axis_size("dp")
    arrays, offsets, operands = [x], [[0]], []
    k = n // 2
    while k:
        operand = join(arrays) if len(arrays) > 1 else x
        operands.append(operand)
        arrays.append(swap(operand, "dp", k))
        offsets.append([o ^ k for group in offsets for o in group])
        k //= 2
    return arrays, offsets, operands


def join(arrays, us=2):
    shape = (sum(x.shape[0] for x in arrays), arrays[0].shape[1])
    return call(join_kernel, "join", [VMEM] * len(arrays), [(shape, arrays[0].dtype, VMEM)], [], us)(*arrays)[0]


def split_dp(n):
    low = 2 ** ((n.bit_length() - 1) // 2)
    return n // low, low


def scatter_high(own, received, us, *behind):
    high, rows, columns = own.shape
    low = 1 + len(received)
    mine, *leaving = call(
        fold_kernel,
        "fold",
        [VMEM] * low,
        [((rows, columns), f32, VMEM)] + [((rows, columns), bf16, VMEM)] * (high - 1),
        [],
        us,
    )(own, *received)
    leaving = after_all(leaving, *behind)
    order = sorted(range(1, high), key=lambda k: k != high // 2)
    return [mine] + [swap(leaving[k - 1], "dp", k * low) for k in order]


def fold_cores(keep, crossed, cuts=1):
    chips, rows, columns = keep.shape
    return call(
        functools.partial(rows_kernel, chips),
        "rows",
        [VMEM] * 2,
        [((rows, columns), f32, VMEM)] + [((rows // cuts, columns), bf16, VMEM)] * (cuts * (chips - 1)),
        [],
        0.1,
    )(keep, crossed)


def dot(a, b):
    return lax.dot_general(a, b, (((1,), (0,)), ((), ())), preferred_element_type=f32)


def dot_nt(a, b):
    return lax.dot_general(a, b, (((1,), (1,)), ((), ())), preferred_element_type=f32)


def flip(a):
    return jnp.transpose(a.astype(f32))


def lanes(i):
    return pl.ds(pl.multiple_of(i * TILE, TILE), TILE)


def by_head(block, heads):
    zero = jnp.zeros((HEAD_DIM, block.shape[1]), block.dtype)
    return jnp.concatenate(
        [
            jnp.concatenate(
                [block[g * HEAD_DIM : (g + 1) * HEAD_DIM] if g == h else zero for g in range(heads)], axis=0
            )
            for h in range(heads)
        ],
        axis=1,
    )


def query_columns(qs, trow, heads):
    return jnp.concatenate([jnp.concatenate([trow] * heads, axis=1), by_head(qs, heads)], axis=0)


def own_rows(block, heads):
    return jnp.concatenate(
        [block[h * HEAD_DIM : (h + 1) * HEAD_DIM, h * TILE : (h + 1) * TILE] for h in range(heads)], axis=0
    )


def own_lanes(block, heads):
    lane = lax.broadcasted_iota(jnp.int32, block.shape, 1) // HEAD_DIM
    return jnp.concatenate([jnp.where(lane == h, block, jnp.zeros_like(block)) for h in range(heads)], axis=0)


def masked(product, bias, start, j, heads):
    key = j * TILE + lax.broadcasted_iota(jnp.int32, (TILE, TILE), 0)
    seen = key >= start
    return jnp.where(
        jnp.concatenate([seen] * heads, axis=1), product + jnp.concatenate([bias] * heads, axis=1), NEG
    )


def diagonals(x):
    rows, cols = x.shape
    z = jnp.concatenate([x, jnp.zeros((rows, cols), f32)], axis=1)
    total = z[:8]
    for q in range(1, rows // 8):
        total = total + pltpu.roll(z[8 * q : 8 * q + 8], 2 * cols - 8 * q, 1)
    g = total[0:1]
    for r in range(1, 8):
        g = g + pltpu.roll(total, 2 * cols - r, 1)[r : r + 1]
    return g


def cast_kernel(w_in, o_in, low_ref, w_ref, o_ref, sems):
    copies = [pltpu.make_async_copy(w_in, w_ref, sems.at[0]), pltpu.make_async_copy(o_in, o_ref, sems.at[1])]
    for copy in copies:
        copy.start()
    for copy in copies:
        copy.wait()
    width = o_ref.shape[1]
    for c in range(4):
        low_ref[:, c * width : (c + 1) * width] = w_ref[:, c, :].astype(bf16)
    low_ref[:, 4 * width :] = o_ref[...].astype(bf16)


def row_lanes(ref, first, count):
    return jnp.concatenate([ref[pl.ds(first + k, 1), :] for k in range(count)], axis=1)


def prepare_kernel(tb_ref, small_ref, pos_ref, oh_ref, oht_ref, trow_ref):
    nb = pos_ref.shape[0]
    step = TILE // 128

    def tile(d, _):
        first = D // 128 + d * step
        row = jnp.concatenate([row_lanes(small_ref, first, step), row_lanes(small_ref, first - step, step)], axis=1)
        pos_ref[d] = pltpu.roll(
            jnp.broadcast_to(row * 0.5, (TILE, 2 * TILE)), 0, 1, stride=1, stride_axis=0
        )[:, :TILE]
        return 0

    lax.fori_loop(0, nb, tile, 0)
    b = lax.broadcasted_iota(jnp.int32, (TILE, TILE), 0)
    a = lax.broadcasted_iota(jnp.int32, (TILE, TILE), 1)
    pos_ref[0] = jnp.where(b <= a, pos_ref[0], NEG)
    table = row_lanes(small_ref, (D + POS) // 128, NTB // 128)
    row = jnp.concatenate([table, table], axis=1)
    upper = pltpu.roll(jnp.broadcast_to(row, (NTB, 2 * NTB)), 0, 1, stride=1, stride_axis=0)[:, :NTB]
    a = lax.broadcasted_iota(jnp.int32, (NTB, NTB), 0)
    b = lax.broadcasted_iota(jnp.int32, (NTB, NTB), 1)
    upper = jnp.where(b >= a, upper, 0.0)
    square = (jnp.where(b > a, upper, jnp.transpose(upper)) * 0.5).astype(bf16)

    def block(i, _):
        onehot = (lax.broadcasted_iota(jnp.int32, (NTB, TILE), 0) == tb_ref[:, lanes(i)]).astype(f32)
        low = onehot.astype(bf16)
        oht_ref[i] = low
        oh_ref[i] = flip(onehot).astype(bf16)
        trow_ref[i] = dot(square, low).astype(bf16)
        return 0

    lax.fori_loop(0, nb, block, 0)


def join_kernel(*refs):
    at = 0
    for ref in refs[:-1]:
        refs[-1][at : at + ref.shape[0]] = ref[...]
        at += ref.shape[0]


def normalize_kernel(*refs):
    x_pieces, xn_ref = refs[:-1], refs[-1]
    per = x_pieces[0].shape[0] // TILE
    for k, piece in enumerate(x_pieces):
        for r in range(per):
            x = piece[r * TILE : (r + 1) * TILE, :].astype(f32)
            x = x - jnp.sum(x, axis=1, keepdims=True) / D
            x = x * lax.rsqrt(jnp.sum(x * x, axis=1, keepdims=True) / D + norm_epsilon)
            xn_ref[(lax.axis_index("head") ^ k) * per + r] = x.astype(bf16)


def assemble_kernel(offsets, *refs):
    w_pieces, (wt_ref, w_ref) = refs[:-2], refs[-2:]
    for piece, group in zip(w_pieces, offsets):
        rows = piece.shape[0] // len(group)
        for at, offset in enumerate(group):
            start = pl.multiple_of((lax.axis_index("dp") ^ offset) * rows, 16)
            w_ref[pl.ds(start, rows), :] = piece[at * rows : (at + 1) * rows, :]
    wt_ref[...] = flip(w_ref[...]).astype(bf16)


def project_kernel(heads, *refs):
    refs = list(refs)
    take = lambda count: [refs.pop(0) for _ in range(count)]
    xn_ref, wt_ref, oh_ref, oht_ref = take(4)
    d_ref, kx_ref, kxt_ref, qs_ref, q_ref, v_ref, vt_ref = refs
    width = v_ref.shape[2]

    def project(i):
        x = xn_ref[i]
        p = dot_nt(wt_ref[width : 4 * width], x)
        sg = 0.5 + 0.5 * jnp.tanh(0.5 * p)
        act = p * sg
        d_ref[i] = (sg + act * (1.0 - sg)).astype(bf16)
        vt = act[:width]
        vt_ref[i] = vt.astype(bf16)
        v_ref[i] = flip(vt).astype(bf16)
        qt = act[width : 2 * width].astype(bf16)
        kt = act[2 * width :]
        kxt_ref[i, :NTB] = oht_ref[i]
        kxt_ref[i, NTB:] = kt.astype(bf16)
        kx_ref[i, :, :NTB] = oh_ref[i]
        kx_ref[i, :, NTB:] = flip(kt).astype(bf16)
        qs = (qt.astype(f32) * (0.5 / math.sqrt(HEAD_DIM))).astype(bf16)
        qs_ref[i] = qs
        q_ref[i] = flip(qt).astype(bf16)

    for i in range(xn_ref.shape[0]):
        project(i)

def tile_at(refs, i, j):
    at = i * (i + 1) // 2 + j
    for ref in refs:
        if at < ref.shape[0]:
            return ref[at]
        at -= ref.shape[0]


def weights_and_slope(h):
    th = jnp.tanh(h)
    u = 1.0 + th
    w = h * u
    return w, u + w * (1.0 - th)


def attend_kernel(heads, first, last, kept, *refs):
    if first:
        before_ref, refs = refs[0], refs[1:]
    kx_ref, qs_ref, trow_ref, vt_ref, pos_ref, ss_ref, attn_ref = refs[:7]
    if first:
        attn_ref[:first] = before_ref[...]
    tiles = [(i, j) for i in range(first, last) for j in range(i + 1)]
    scores, weights = {}, {}
    for t in range(len(tiles) + 3):
        if t < len(tiles):
            i, j = tiles[t]
            if j == 0:
                queries = query_columns(qs_ref[i], trow_ref[i], heads)
            scores[t] = dot(kx_ref[j], queries)
        if 0 <= t - 1 < len(tiles):
            i, j = tiles[t - 1]
            h = masked(scores.pop(t - 1), pos_ref[i - j], ss_ref[:, i * TILE : (i + 1) * TILE], j, heads)
            w, slope = weights_and_slope(h)
            weights[t - 1] = w.astype(bf16)
            if kept:
                refs[7][t - 1] = weights[t - 1]
                refs[8][t - 1] = slope.astype(bf16)
        if t >= 3:
            i, j = tiles[t - 3]
            more = dot(vt_ref[j], weights.pop(t - 3))
            total = more if j == 0 else total + more
            if i == j:
                attn_ref[i] = own_rows(total, heads)


def gate_kernel(n_head, *refs):
    refs = list(refs)
    take = lambda count: [refs.pop(0) for _ in range(count)]
    cot_pieces = take(n_head)
    attn_ref, xn_ref, wt_ref = take(3)
    p_ref, gg_ref, stat_ref, gb_ref = refs
    width = attn_ref.shape[1]
    per = cot_pieces[0].shape[0] // TILE
    gb_ref[...] = jnp.sum(cot_pieces[0][...].astype(f32), axis=0, keepdims=True)
    for k, piece in enumerate(cot_pieces):
        for r in range(per):
            i = (lax.axis_index("head") ^ k) * per + r
            p = dot_nt(wt_ref[:width], xn_ref[i])
            gate = p * (0.5 + 0.5 * jnp.tanh(0.5 * p))
            gg = dot_nt(wt_ref[4 * width :], piece[r * TILE : (r + 1) * TILE, :])
            grad = gg * gate
            p_ref[i] = p
            gg_ref[i] = gg
            at = attn_ref[i]
            mean = jnp.sum(at, axis=0, keepdims=True) / width
            centred = at - mean
            stat_ref[i] = jnp.concatenate(
                [
                    mean,
                    jnp.sum(centred * centred, axis=0, keepdims=True),
                    jnp.sum(grad, axis=0, keepdims=True),
                    jnp.sum(grad * centred, axis=0, keepdims=True),
                ],
                axis=0,
            )


def standardized(i, n_head, stats, attn_ref):
    width = attn_ref.shape[1]
    st = [s[i] for s in stats]
    mean = sum(p[0:1] for p in st) / n_head
    spread = sum(p[1:2] + width * (p[0:1] - mean) * (p[0:1] - mean) for p in st)
    scale = lax.rsqrt(spread / HD + norm_epsilon)
    first = sum(p[2:3] for p in st) / HD
    second = scale * sum(p[3:4] + (p[0:1] - mean) * p[2:3] for p in st) / HD
    return (attn_ref[i] - mean) * scale, scale, first, second


def branch_kernel(n_head, *refs):
    stats, (attn_ref, p_ref, wt_ref, keep, send) = refs[:n_head], refs[n_head:]
    width = attn_ref.shape[1]
    per = keep.shape[1] // TILE
    for k in range(n_head):
        device = lax.axis_index("head") ^ k
        for r in range(per):
            i = device * per + r
            normed = standardized(i, n_head, stats, attn_ref)[0]
            p = p_ref[i]
            gated = (normed * (p * (0.5 + 0.5 * jnp.tanh(0.5 * p)))).astype(bf16)
            (keep, send)[k % 2][device // 2, r * TILE : (r + 1) * TILE] = dot(
                flip(gated).astype(bf16), wt_ref[4 * width :]
            ).astype(bf16)


def middle_kernel(n_head, *refs):
    refs = list(refs)
    take = lambda count: [refs.pop(0) for _ in range(count)]
    stats = take(n_head)
    cot_pieces = take(n_head)
    attn_ref, p_ref, gg_ref, xn_ref = take(4)
    da_ref, dat_ref, gun_ref = take(3)
    (acc_ref,) = refs
    width = attn_ref.shape[1]
    per = cot_pieces[0].shape[0] // TILE
    for k, piece in enumerate(cot_pieces):
        for r in range(per):
            i = (lax.axis_index("head") ^ k) * per + r
            normed, scale, first, second = standardized(i, n_head, stats, attn_ref)
            p = p_ref[i]
            sg = 0.5 + 0.5 * jnp.tanh(0.5 * p)
            gate = p * sg
            gg = gg_ref[i]
            gated = (normed * gate).astype(bf16)
            grad = scale * (gg * gate - first - normed * second)
            da_ref[i] = flip(grad).astype(bf16)
            dat_ref[i] = (grad * 0.5).astype(bf16)
            gu = (gg * normed * (sg + gate * (1.0 - sg))).astype(bf16)
            gun_ref[i] = flip(gu).astype(bf16)
            add_gate, add_out = dot(gu, xn_ref[i]), dot(gated, piece[r * TILE : (r + 1) * TILE, :])
            if k + r == 0:
                acc_ref[:width] = add_gate
                acc_ref[width:] = add_out
            else:
                acc_ref[:width] += add_gate
                acc_ref[width:] += add_out


def send_parts(wg_ref, parts):
    low = len(parts)
    high, rows = parts[0].shape[0], parts[0].shape[1]
    me = lax.axis_index("dp") % low
    for k in range(low):
        for p in range(high):
            start = pl.multiple_of((p * low + (me ^ k)) * rows, 16)
            parts[k][p] = wg_ref[pl.ds(start, rows), :].astype(bf16)


def values_kernel(heads, kept, *refs):
    refs = list(refs)
    take = lambda count: [refs.pop(0) for _ in range(count)]
    held = take(2 if kept else 5)
    da_ref, d_ref, xn_ref, acc_in = take(4)
    gpv_ref = refs.pop(0)
    parts, wg_ref = refs[:-1], refs[-1]
    nb, width = da_ref.shape[0], da_ref.shape[2]
    das = [own_lanes(da_ref[i], heads) for i in range(nb)]
    queries = None if kept else [query_columns(held[1][i], held[2][i], heads) for i in range(nb)]
    acc = None
    for j in range(nb):
        if kept:
            tiles = [tile_at(held, i, j) for i in range(j, nb)]
        else:
            kx_ref, _, _, pos_ref, ss_ref = held
            tiles = [
                weights_and_slope(
                    masked(
                        dot(kx_ref[j], queries[i]), pos_ref[i - j], ss_ref[:, i * TILE : (i + 1) * TILE], j, heads
                    )
                )[0].astype(bf16)
                for i in range(j, nb)
            ]
        total = dot(jnp.concatenate(tiles, axis=1), jnp.concatenate(das[j:], axis=0))
        gv = (flip(total) * d_ref[j, :width]).astype(bf16)
        gpv_ref[j] = flip(gv).astype(bf16)
        more = dot(gv, xn_ref[j])
        acc = more if j == 0 else acc + more
    wg_ref[...] = flip(jnp.concatenate([acc_in[...], acc], axis=0))
    send_parts(wg_ref, parts)


def backward_kernel(heads, n_dp, extra, kept, *refs):
    refs = list(refs)
    take = lambda count: [refs.pop(0) for _ in range(count)]
    held = take(2 if kept else 4)
    kx_ref, kxt_ref, q_ref, v_ref, dat_ref = take(5)
    d_ref, xn_ref, gb_ref = take(3)
    gp_ref = refs.pop(0)
    parts = take(split_dp(n_dp)[1])
    acck_ref, posg_ref, acc_ref, wg_ref, small_ref = refs
    nb, width = v_ref.shape[0], v_ref.shape[2]
    factor = 1.0 / math.sqrt(HEAD_DIM)
    tiles = [(i, j) for i in reversed(range(nb)) for j in range(i + 1)]
    products, grads = {}, {}
    dq = m2 = None
    small_ref[...] = jnp.zeros_like(small_ref)
    small_ref[:, :D] = gb_ref[...]

    def add(ref, at, value, first):
        ref[at] = value if first else ref[at] + value

    for t in range(len(tiles) + 3):
        if t < len(tiles):
            i, j = tiles[t]
            if j == 0:
                backs = by_head(dat_ref[i], heads)
                queries = None if kept else query_columns(held[0][i], held[1][i], heads)
            products[t] = dot(v_ref[j], backs), None if kept else dot(kx_ref[j], queries)
        if 0 <= t - 1 < len(tiles):
            i, j = tiles[t - 1]
            back, product = products.pop(t - 1)
            if kept:
                slope = tile_at(held, i, j).astype(f32)
            else:
                start = held[3][:, i * TILE : (i + 1) * TILE]
                slope = weights_and_slope(masked(product, held[2][i - j], start, j, heads))[1]
            ds = back * slope
            grads[t - 1] = ds.astype(bf16)
            add(posg_ref, i - j, sum(ds[:, g * TILE : (g + 1) * TILE] for g in range(heads)), i == nb - 1)
        if t >= 3:
            i, j = tiles[t - 3]
            low = grads.pop(t - 3)
            if j == 0:
                times = jnp.concatenate([kx_ref[i, :, :NTB]] * heads, axis=0)
                q = jnp.concatenate([times, own_lanes(q_ref[i], heads)], axis=1)
            add(acck_ref, j, dot(low, q), i == nb - 1)
            more = dot(kxt_ref[j, NTB:], low)
            dq = more if j == 0 else dq + more
            if i == j:
                gp = jnp.concatenate([own_rows(dq, heads), flip(acck_ref[i, :, NTB:])], axis=0)
                gp = (gp * factor * d_ref[i, width:]).astype(bf16)
                gp_ref[i] = flip(gp).astype(bf16)
                more = dot(gp, xn_ref[i])
                acc_ref[...] = more if i == nb - 1 else acc_ref[...] + more
                part = acck_ref[i, :, :NTB]
                high = part.astype(bf16)
                rest = (part - high.astype(f32)).astype(bf16)
                onehot = kxt_ref[i, :NTB]
                part = dot(onehot, high) + dot(onehot, rest)
                m2 = part if i == nb - 1 else m2 + part
                g = diagonals(posg_ref[i])
                small_ref[:, D + i * TILE : D + (i + 1) * TILE] += g[:, :TILE]
                if i > 0:
                    small_ref[:, D + (i - 1) * TILE : D + i * TILE] += g[:, TILE:]
    g = diagonals(m2 + jnp.transpose(m2))[:, :NTB]
    zero = lax.broadcasted_iota(jnp.int32, (1, NTB), 1) == 0
    at = D + nb * TILE
    small_ref[:, at : at + NTB] = jnp.where(zero, 0.5 * g, g)
    step = D // n_dp
    grads = flip(acc_ref[...])
    for p in range(n_dp):
        here = jnp.concatenate(
            [small_ref[:, (p * extra + r) * 128 : (p * extra + r + 1) * 128] for r in range(extra)], axis=0
        )
        high = here.astype(bf16).astype(f32)
        block = jnp.concatenate([high, here - high, jnp.zeros((16 - 2 * extra, 128), f32)], axis=0)
        wg_ref[p * (step + 16) : p * (step + 16) + step] = grads[p * step : (p + 1) * step]
        if 2 * width > 128:
            block = jnp.concatenate([block, jnp.zeros((16, 2 * width - 128), f32)], axis=1)
        wg_ref[p * (step + 16) + step : (p + 1) * (step + 16)] = block
    send_parts(wg_ref, parts)


def input_kernel(n_head, gp_ref, gun_ref, gpv_ref, wt_ref, keep, send):
    width = gun_ref.shape[2]
    per = keep.shape[1] // TILE
    for k in range(n_head):
        device = lax.axis_index("head") ^ k
        target = (keep, send)[k % 2]
        for r in range(per):
            i = device * per + r
            rows = dot(jnp.concatenate([gun_ref[i], gpv_ref[i]], axis=1), wt_ref[: 2 * width])
            rows = rows + dot(gp_ref[i], wt_ref[2 * width : 4 * width])
            target[device // 2, r * TILE : (r + 1) * TILE] = rows.astype(bf16)


def fold_kernel(*refs):
    low = sum(len(ref.shape) == 3 for ref in refs)
    row = lax.axis_index("dp") // low
    for k, out in enumerate(refs[low:]):
        total = refs[0][row ^ k].astype(f32)
        for ref in refs[1:low]:
            total = total + ref[row ^ k].astype(f32)
        out[...] = total.astype(out.dtype)


def sum_kernel(*refs):
    total = refs[0][...]
    for ref in refs[1:-1]:
        total = total + ref[...].astype(f32)
    refs[-1][...] = total


def mix_kernel(tokens_ref, bias_ref, *refs):
    total = tokens_ref[...].astype(f32) + row_lanes(bias_ref, 0, D // 128)
    for ref in refs[:-1]:
        total = total + ref[...].astype(f32)
    refs[-1][...] = total.astype(bf16)


def finish_kernel(part, *refs):
    tokens_ref, cot_ref, mine_ref, *refs = refs[part:]
    x = tokens_ref[...].astype(f32)
    x = x - jnp.sum(x, axis=1, keepdims=True) / D
    scale = lax.rsqrt(jnp.sum(x * x, axis=1, keepdims=True) / D + norm_epsilon)
    x = x * scale
    grad = mine_ref[...]
    for ref in refs[:-1]:
        grad = grad + ref[...].astype(f32)
    mean = jnp.sum(grad, axis=1, keepdims=True) / D
    along = jnp.sum(grad * x, axis=1, keepdims=True) / D
    refs[-1][...] = cot_ref[...].astype(f32) + scale * (grad - mean - x * along)


def rows_kernel(chips, keep_ref, crossed_ref, mine_ref, *leaving):
    chip = lax.axis_index("head") // 2
    for k in range(chips):
        total = keep_ref[chip ^ k].astype(f32) + crossed_ref[chip ^ k].astype(f32)
        if k == 0:
            mine_ref[...] = total
        else:
            rows = leaving[0].shape[0]
            cuts = total.shape[0] // rows
            for c in range(cuts):
                leaving[(k - 1) * cuts + c][...] = total[c * rows : (c + 1) * rows].astype(bf16)


def collect_kernel(high, extra, *refs):
    late_blocks, (early_ref, grads_ref, message_ref) = refs[:high], refs[high:]
    rows = grads_ref.shape[0]
    total, early = late_blocks[0][...], early_ref[...]
    for k in range(1, high):
        total = total + late_blocks[k][...].astype(f32)
    grads = jnp.concatenate([total[:rows], early], axis=1)
    grads_ref[...] = grads
    squares = jnp.sum(jnp.sum(grads * grads, axis=0, keepdims=True), axis=1, keepdims=True)
    message = jnp.concatenate(
        [
            total[rows : rows + extra, :128] + total[rows + extra : rows + 2 * extra, :128],
            jnp.zeros((7 - extra, 128), f32),
            jnp.broadcast_to(squares, (1, 128)),
        ],
        axis=0,
    )
    for k in range(message_ref.shape[0]):
        message_ref[k] = message


def update_kernel(n_head, extra, group, heard_ref, grads_ref, *refs):
    state, outs = refs[:9], refs[9:]
    grad_proj_ref, grad_out_ref, grad_small_ref, norm_ref = outs[:4]
    n_all = heard_ref.shape[0]
    width = grad_out_ref.shape[1]
    lead, pos_rows, used = D // 128, POS // 128, (D + group) // 128
    grad_small_ref[...] = jnp.zeros_like(grad_small_ref)
    squares = heard_ref[0, 7:8, :]
    for k in range(1, n_all):
        squares = squares + heard_ref[k, 7:8, :]
    for p in range(n_all // n_head):
        rows = heard_ref[p * n_head, :extra, :]
        for h in range(1, n_head):
            rows = rows + heard_ref[p * n_head + h, :extra, :]
        for r in range(extra):
            at = p * extra + r
            if at < used:
                grad_small_ref[at : at + 1, :] = rows[r : r + 1]
            elif at == used:
                grad_small_ref[lead + pos_rows : lead + pos_rows + 1, :] = rows[r : r + 1]
    small = grad_small_ref[...]
    total = jnp.sum(jnp.sum(small * small, axis=0, keepdims=True), axis=1, keepdims=True) + squares[:, :1]
    norm = jnp.sqrt(total)
    norm_ref[...] = norm
    factor = jnp.minimum(1.0, clip_norm / (norm + 1e-06))

    def update(get, put, grad, rate, decay):
        for k, value in enumerate(adam_step(get(0), grad, get(1), get(2), factor, rate, decay)):
            put(k, value)

    for c in range(4):
        at = (2, 4, 0, 1)[c] * width
        grad = grads_ref[:, at : at + width]
        grad_proj_ref[:, c, :] = grad

        def put(k, value):
            outs[4 + k][:, c, :] = value

        update(lambda k: state[k][:, c, :], put, grad, rate_matrix, decay_matrix)
    grad = grads_ref[:, 3 * width : 4 * width]
    grad_out_ref[...] = grad

    def put_out(k, value):
        outs[7 + k][...] = value

    update(lambda k: state[3 + k][...], put_out, grad, rate_matrix, decay_matrix)

    def put_small(k, value):
        outs[10 + k][...] = value

    update(lambda k: state[6 + k][...], put_small, small, rate_small, 0.0)


def call(kernel, name, in_specs, outs, scratch, us, room=16, **more):
    return pl.pallas_call(
        kernel,
        out_shape=[jax.ShapeDtypeStruct(shape, dtype) for shape, dtype, _ in outs],
        in_specs=in_specs,
        out_specs=[spec for _, _, spec in outs],
        scratch_shapes=scratch,
        compiler_params=pltpu.CompilerParams(vmem_limit_bytes=room * 2**20 * max(1, lax.axis_size("head") // 4)),
        cost_estimate=pl.CostEstimate(flops=int(us * 1e9), bytes_accessed=int(us * 3e6), transcendentals=0),
        name=name,
        **more,
    )


def block(shape):
    return pl.BlockSpec((1,) + tuple(shape[1:]), lambda i: (i,) + (0,) * (len(shape) - 1))


def shards(
    tokens,
    cotangent,
    seq_start,
    time_bucket,
    proj_weight,
    out_weight,
    small_params,
    proj_mean,
    proj_square,
    out_mean,
    out_square,
    small_mean,
    small_square,
):
    n_head = lax.axis_size("head")
    n_dp = lax.axis_size("dp")
    here = tokens.shape[0]
    group = here * n_head
    nb = group // TILE
    per = here // TILE
    rows_here, _, width = proj_weight.shape
    heads = width // HEAD_DIM
    high, low = split_dp(n_dp)

    (weights,) = call(
        cast_kernel,
        "cast",
        [pl.BlockSpec(memory_space=pl.ANY)] * 2,
        [((rows_here, 5 * width), bf16, VMEM)],
        [
            pltpu.VMEM(proj_weight.shape, f32),
            pltpu.VMEM((rows_here, width), f32),
            pltpu.SemaphoreType.DMA((2,)),
        ],
        1,
    )(proj_weight, out_weight.T)
    x_pieces = gather_cores(tokens, gather_chips(after(tokens, weights)))
    w_pieces, offsets, operands = gather_dp(weights)
    cot_chips = gather_chips(after(cotangent, weights))
    starts = seq_start.reshape(1, group)
    small_rows = small_params.reshape(-1, 128)
    times = time_bucket.reshape(1, group)

    pos, oh, oht, trow = call(
        prepare_kernel,
        "prepare",
        [VMEM] * 2,
        [
            ((nb, TILE, TILE), f32, VMEM),
            ((nb, TILE, NTB), bf16, VMEM),
            ((nb, NTB, TILE), bf16, VMEM),
            ((nb, NTB, TILE), bf16, VMEM),
        ],
        [],
        5,
    )(after(times, operands[1]), small_rows)

    items = [
        ((nb, 3 * width, TILE), bf16),
        ((nb, TILE, NTB + width), bf16),
        ((nb, NTB + width, TILE), bf16),
        ((nb, width, TILE), bf16),
        ((nb, TILE, width), bf16),
        ((nb, TILE, width), bf16),
        ((nb, width, TILE), bf16),
    ]
    (xn,) = call(normalize_kernel, "normalize", [VMEM] * n_head, [((nb, TILE, D), bf16, VMEM)], [], 1)(*x_pieces)
    w_pieces[-1] = after(join(w_pieces[-1:], 4), xn)
    (wt,) = call(
        functools.partial(assemble_kernel, offsets),
        "assemble",
        [VMEM] * len(w_pieces),
        [((5 * width, D), bf16, VMEM)],
        [pltpu.VMEM((D, 5 * width), bf16)],
        5,
    )(*w_pieces)
    dsilu, kx, kxt, qs, q, v, vt = call(
        functools.partial(project_kernel, heads),
        "project",
        [VMEM] * 4,
        [item + (VMEM,) for item in items],
        [],
        5,
    )(xn, wt, oh, oht)

    kept = nb * (nb + 1) // 2 * heads <= KEPT_TILES

    def attend(first, last, *before):
        count = (last * (last + 1) - first * (first + 1)) // 2
        return call(
            functools.partial(attend_kernel, heads, first, last, kept),
            "attend",
            [VMEM] * (len(before) + 6),
            [((last, width, TILE), f32, VMEM)] + [((count, TILE, heads * TILE), bf16, VMEM)] * (2 * kept),
            [],
            8,
        )(*before, kx, qs, trow, vt, pos, starts)

    split = nb - nb // 4
    attn, *kept_first = attend(0, split)
    cot_chips = after_all(cot_chips, attn)
    attn, *kept_last = attend(split, nb, after(attn, *cot_chips))
    kept_weights, kept_slopes = zip(kept_first, kept_last) if kept else ((), ())
    cot_pieces = gather_cores(cotangent, cot_chips)

    column = ((nb, width, TILE), f32, VMEM)
    p_gate, gg, stat, gb = call(
        functools.partial(gate_kernel, n_head),
        "gate",
        [VMEM] * (n_head + 3),
        [column, column, ((nb, 4, TILE), f32, VMEM), ((1, D), f32, VMEM)],
        [],
        5,
    )(*cot_pieces, attn, xn, wt)

    stats = [stat] + [swap(stat, "head", k) for k in range(1, n_head)]
    chips = n_head // 2
    split_shape = ((chips, here, D), bf16, VMEM)
    keep, send = call(
        functools.partial(branch_kernel, n_head), "branch", [VMEM] * (n_head + 3), [split_shape] * 2, [], 1
    )(*stats, attn, p_gate, wt)
    crossed = swap(send, "head", 1)
    da, dat, gun, wg_sum = call(
        functools.partial(middle_kernel, n_head),
        "middle",
        [VMEM] * (2 * n_head + 4),
        [
            ((nb, TILE, width), bf16, VMEM),
            ((nb, width, TILE), bf16, VMEM),
            ((nb, TILE, width), bf16, VMEM),
            ((2 * width, D), f32, VMEM),
        ],
        [],
        6,
    )(*stats, *cot_pieces, attn, p_gate, gg, xn)
    branch, *leaving = fold_cores(keep, crossed)
    received = [swap(sent, "head", 2 * (k + 1)) for k, sent in enumerate(leaving)]
    held = kept_weights if kept else (kx, qs, trow, pos, starts)
    gpv, *early_parts = call(
        functools.partial(values_kernel, heads, kept),
        "values",
        [VMEM] * (len(held) + 4),
        [((nb, TILE, width), bf16, VMEM)] + [((high, rows_here, 3 * width), bf16, VMEM)] * low,
        [pltpu.VMEM((D, 3 * width), f32)],
        VALUES,
    )(*held, da, dsilu, xn, wg_sum)
    early_received = [swap(early_parts[k], "dp", k) for k in range(1, low)]

    length = D + group + NTB
    extra = -(-length // (128 * n_dp))
    held = kept_slopes if kept else (qs, trow, pos, starts)
    gp, *late_parts = call(
        functools.partial(backward_kernel, heads, n_dp, extra, kept),
        "backward",
        [VMEM] * (len(held) + 8),
        [((nb, TILE, 2 * width), bf16, VMEM)] + [((high, rows_here + 16, 2 * width), bf16, VMEM)] * low,
        [
            pltpu.VMEM((nb, TILE, NTB + width), f32),
            pltpu.VMEM((nb, TILE, TILE), f32),
            pltpu.VMEM((2 * width, D), f32),
            pltpu.VMEM((n_dp * (rows_here + 16), 2 * width), f32),
            pltpu.VMEM((1, extra * n_dp * 128), f32),
        ],
        BACKWARD,
        ROOM,
    )(*held, kx, kxt, q, v, dat, dsilu, xn, gb)

    tied = lax.optimization_barrier((gp, *late_parts, *early_received, *received))
    gp, late_parts = tied[0], tied[1 : 1 + low]
    early_received, received = tied[1 + low : 2 * low], tied[2 * low :]
    late_received = [swap(late_parts[k], "dp", k) for k in range(1, low)]
    keep, send = call(
        functools.partial(input_kernel, n_head),
        "input_rows",
        [VMEM] * 4,
        [((n_head // 2, here, D), bf16, VMEM)] * 2,
        [],
        4,
    )(gp, gun, gpv, wt)
    early_blocks = scatter_high(after(early_parts[0], send), early_received, 1)
    crossed = swap(send, "head", 1)
    late_blocks = scatter_high(late_parts[0], late_received, 12, send, crossed)
    (early,) = call(
        sum_kernel, "sum", [VMEM] * high, [((rows_here, 3 * width), f32, VMEM)], [], 14
    )(*early_blocks)
    mine, *leaving = fold_cores(keep, after(crossed, late_blocks[0]), 2)
    half = here // 2
    arrived = [[swap(leaving[2 * k - 2 + part], "head", 2 * k) for k in range(1, chips)] for part in range(2)]
    n_all = n_dp * n_head
    grads_shape = ((rows_here, 5 * width), f32)
    grads, message = call(
        functools.partial(collect_kernel, high, extra),
        "collect",
        [VMEM] * (high + 1),
        [grads_shape + (VMEM,), ((n_all, 8, 128), f32, VMEM)],
        [],
        10,
    )(*late_blocks, early)
    message = after(message, *leaving)
    heard = lax.all_to_all(message, ("dp", "head"), 0, 0, tiled=True)
    (mixed,) = call(
        mix_kernel, "mix", [VMEM] * (2 + chips), [((here, D), bf16, VMEM)], [], 1
    )(tokens, small_rows, after(branch, message), *received)
    input_grad = None
    for part in range(2):
        rows = pl.BlockSpec((half, D), lambda i, part=part: (part, 0))
        alone = pl.BlockSpec((half, D), lambda i: (0, 0))
        before = [] if part == 0 else [input_grad]
        (input_grad,) = call(
            functools.partial(finish_kernel, part),
            "finish",
            [pl.BlockSpec(memory_space=pl.ANY)] * len(before) + [rows] * 3 + [alone] * (chips - 1),
            [((here, D), f32, rows)],
            [],
            1,
            grid=(1,),
            input_output_aliases={0: 0} if before else {},
        )(*before, tokens, cotangent, mine, *arrived[part])
    heard = after(heard, input_grad)
    state = [proj_weight, proj_mean, proj_square, out_weight.T, out_mean.T, out_square.T]
    state += [x.reshape(-1, 128) for x in (small_params, small_mean, small_square)]
    proj_shape, out_shape, small_shape = proj_weight.shape, (rows_here, width), small_rows.shape
    shapes = [proj_shape, out_shape, small_shape, (1, 1)] + [proj_shape] * 3 + [out_shape] * 3 + [small_shape] * 3
    results = call(
        functools.partial(update_kernel, n_head, extra, group),
        "update",
        [VMEM] * (2 + len(state)),
        [(shape, f32, VMEM) for shape in shapes],
        [],
        0.1,
    )(heard, grads, *state)
    grad_proj, grad_out, grad_small, grad_norm = results[:4]
    grad_out, grad_small, grad_norm = grad_out.T, grad_small.reshape(-1), grad_norm.reshape(())
    new_proj, mean_proj, square_proj = results[4:7]
    new_out, mean_out, square_out = [x.T for x in results[7:10]]
    new_small, mean_small, square_small = [x.reshape(-1) for x in results[10:13]]
    return (
        mixed,
        input_grad,
        grad_proj,
        grad_out,
        grad_small,
        grad_norm,
        new_proj,
        mean_proj,
        square_proj,
        new_out,
        mean_out,
        square_out,
        new_small,
        mean_small,
        square_small,
    )


def solution(mesh):
    in_specs = (
        P(("dp", "head"), None),
        P(("dp", "head"), None),
        P("dp"),
        P("dp"),
        P("dp", None, "head"),
        P("head", "dp"),
        P(),
        P("dp", None, "head"),
        P("dp", None, "head"),
        P("head", "dp"),
        P("head", "dp"),
        P(),
        P(),
    )
    out_specs = (
        P(("dp", "head"), None),
        P(("dp", "head"), None),
        P("dp", None, "head"),
        P("head", "dp"),
        P(),
        P(),
        P("dp", None, "head"),
        P("dp", None, "head"),
        P("dp", None, "head"),
        P("head", "dp"),
        P("head", "dp"),
        P("head", "dp"),
        P(),
        P(),
        P(),
    )
    return jax.shard_map(shards, mesh=mesh, in_specs=in_specs, out_specs=out_specs, check_vma=False)
```

```python
import functools
import math

import jax
import jax.numpy as jnp
from jax import lax
from jax.experimental import pallas as pl
from jax.experimental.pallas import tpu as pltpu
from jax.sharding import PartitionSpec as P

D = 512
HEAD_DIM = 64
HD = 512
POS = 8192
NTB = 128
STEP = 10
TILE = 256
NEG = -1e9
ROOM = 16
KEPT_TILES = 72
VALUES = 12
BACKWARD = 2

norm_epsilon = 1e-06
adam_epsilon = 1e-08
beta_one = 0.9
beta_two = 0.999
clip_norm = 1.0
rate_matrix = 0.05
rate_small = 0.3
decay_matrix = 0.1

f32 = jnp.float32
bf16 = jnp.bfloat16
VMEM = pl.BlockSpec(memory_space=pltpu.VMEM)


def adam_step(weight, grad, first, second, factor, rate, decay):
    clipped = grad * factor
    first_new = beta_one * first + (1.0 - beta_one) * clipped
    second_new = beta_two * second + (1.0 - beta_two) * clipped * clipped
    update = (
        first_new
        / (1.0 - beta_one**STEP)
        / (jnp.sqrt(second_new / (1.0 - beta_two**STEP)) + adam_epsilon)
    )
    return (weight - rate * (update + decay * weight), first_new, second_new)


def swap(x, axis, k):
    n = lax.axis_size(axis)
    return lax.ppermute(x, axis, [(i, i ^ k) for i in range(n)])


def gather_chips(x):
    return [swap(x, "head", k) for k in range(2, lax.axis_size("head"), 2)]


def gather_cores(x, others):
    pieces = [x, swap(x, "head", 1)]
    for other in others:
        pieces += [other, swap(other, "head", 1)]
    return pieces


def after_all(arrays, *others):
    arrays = tuple(arrays)
    return lax.optimization_barrier(arrays + others)[: len(arrays)]


def after(x, *others):
    return lax.optimization_barrier((x,) + others)[0]


def gather_dp(x, behind):
    n = lax.axis_size("dp")
    arrays, offsets = [x], [[0]]
    k = n // 2
    while k:
        operand = join(arrays) if len(arrays) > 1 else x
        if k == 1:
            operand = after(operand, behind)
        arrays.append(swap(operand, "dp", k))
        offsets.append([o ^ k for group in offsets for o in group])
        k //= 2
    return arrays, offsets


def join(arrays, us=0.1):
    shape = (sum(x.shape[0] for x in arrays), arrays[0].shape[1])
    return call(join_kernel, "join", [VMEM] * len(arrays), [(shape, arrays[0].dtype, VMEM)], [], us)(*arrays)[0]


def split_dp(n):
    low = 2 ** ((n.bit_length() - 1) // 2)
    return n // low, low


def scatter_high(own, received, us, *behind):
    high, rows, columns = own.shape
    low = 1 + len(received)
    mine, *leaving = call(
        fold_kernel,
        "fold",
        [VMEM] * low,
        [((rows, columns), f32, VMEM)] + [((rows, columns), bf16, VMEM)] * (high - 1),
        [],
        us,
    )(own, *received)
    leaving = after_all(leaving, *behind)
    order = sorted(range(1, high), key=lambda k: k != high // 2)
    return [mine] + [swap(leaving[k - 1], "dp", k * low) for k in order]


def fold_cores(keep, crossed, cuts=1):
    chips, rows, columns = keep.shape
    return call(
        functools.partial(rows_kernel, chips),
        "rows",
        [VMEM] * 2,
        [((rows, columns), f32, VMEM)] + [((rows // cuts, columns), bf16, VMEM)] * (cuts * (chips - 1)),
        [],
        0.1,
    )(keep, crossed)


def dot(a, b):
    return lax.dot_general(a, b, (((1,), (0,)), ((), ())), preferred_element_type=f32)


def dot_nt(a, b):
    return lax.dot_general(a, b, (((1,), (1,)), ((), ())), preferred_element_type=f32)


def flip(a):
    return jnp.transpose(a.astype(f32))


def lanes(i):
    return pl.ds(pl.multiple_of(i * TILE, TILE), TILE)


def by_head(block, heads):
    zero = jnp.zeros((HEAD_DIM, block.shape[1]), block.dtype)
    return jnp.concatenate(
        [
            jnp.concatenate(
                [block[g * HEAD_DIM : (g + 1) * HEAD_DIM] if g == h else zero for g in range(heads)], axis=0
            )
            for h in range(heads)
        ],
        axis=1,
    )


def query_columns(qs, trow, heads):
    return jnp.concatenate([jnp.concatenate([trow] * heads, axis=1), by_head(qs, heads)], axis=0)


def own_rows(block, heads):
    return jnp.concatenate(
        [block[h * HEAD_DIM : (h + 1) * HEAD_DIM, h * TILE : (h + 1) * TILE] for h in range(heads)], axis=0
    )


def own_lanes(block, heads):
    lane = lax.broadcasted_iota(jnp.int32, block.shape, 1) // HEAD_DIM
    return jnp.concatenate([jnp.where(lane == h, block, jnp.zeros_like(block)) for h in range(heads)], axis=0)


def masked(product, bias, start, j, heads):
    key = j * TILE + lax.broadcasted_iota(jnp.int32, (TILE, TILE), 0)
    seen = key >= start
    return jnp.where(
        jnp.concatenate([seen] * heads, axis=1), product + jnp.concatenate([bias] * heads, axis=1), NEG
    )


def diagonals(x):
    rows, cols = x.shape
    z = jnp.concatenate([x, jnp.zeros((rows, cols), f32)], axis=1)
    total = z[:8]
    for q in range(1, rows // 8):
        total = total + pltpu.roll(z[8 * q : 8 * q + 8], 2 * cols - 8 * q, 1)
    g = total[0:1]
    for r in range(1, 8):
        g = g + pltpu.roll(total, 2 * cols - r, 1)[r : r + 1]
    return g


def cast_kernel(w_in, o_in, low_ref, w_ref, o_ref, sems):
    copies = [pltpu.make_async_copy(w_in, w_ref, sems.at[0]), pltpu.make_async_copy(o_in, o_ref, sems.at[1])]
    for copy in copies:
        copy.start()
    for copy in copies:
        copy.wait()
    width = o_ref.shape[1]
    for c in range(4):
        low_ref[:, c * width : (c + 1) * width] = w_ref[:, c, :].astype(bf16)
    low_ref[:, 4 * width :] = o_ref[...].astype(bf16)


def row_lanes(ref, first, count):
    return jnp.concatenate([ref[pl.ds(first + k, 1), :] for k in range(count)], axis=1)


def prepare_kernel(tb_ref, small_ref, pos_ref, oh_ref, oht_ref, trow_ref):
    nb = pos_ref.shape[0]
    step = TILE // 128

    def tile(d, _):
        first = D // 128 + d * step
        row = jnp.concatenate([row_lanes(small_ref, first, step), row_lanes(small_ref, first - step, step)], axis=1)
        pos_ref[d] = pltpu.roll(
            jnp.broadcast_to(row * 0.5, (TILE, 2 * TILE)), 0, 1, stride=1, stride_axis=0
        )[:, :TILE]
        return 0

    lax.fori_loop(0, nb, tile, 0)
    b = lax.broadcasted_iota(jnp.int32, (TILE, TILE), 0)
    a = lax.broadcasted_iota(jnp.int32, (TILE, TILE), 1)
    pos_ref[0] = jnp.where(b <= a, pos_ref[0], NEG)
    table = row_lanes(small_ref, (D + POS) // 128, NTB // 128)
    row = jnp.concatenate([table, table], axis=1)
    upper = pltpu.roll(jnp.broadcast_to(row, (NTB, 2 * NTB)), 0, 1, stride=1, stride_axis=0)[:, :NTB]
    a = lax.broadcasted_iota(jnp.int32, (NTB, NTB), 0)
    b = lax.broadcasted_iota(jnp.int32, (NTB, NTB), 1)
    upper = jnp.where(b >= a, upper, 0.0)
    square = (jnp.where(b > a, upper, jnp.transpose(upper)) * 0.5).astype(bf16)

    def block(i, _):
        onehot = (lax.broadcasted_iota(jnp.int32, (NTB, TILE), 0) == tb_ref[:, lanes(i)]).astype(f32)
        low = onehot.astype(bf16)
        oht_ref[i] = low
        oh_ref[i] = flip(onehot).astype(bf16)
        trow_ref[i] = dot(square, low).astype(bf16)
        return 0

    lax.fori_loop(0, nb, block, 0)


def join_kernel(*refs):
    at = 0
    for ref in refs[:-1]:
        refs[-1][at : at + ref.shape[0]] = ref[...]
        at += ref.shape[0]


def normalize_kernel(which, *refs):
    before = refs[: len(refs) - len(which) - 1]
    pieces, xn_ref = refs[len(before) : -1], refs[-1]
    per = pieces[0].shape[0] // TILE
    for ref in before:
        xn_ref[...] = ref[...]
    for k, piece in zip(which, pieces):
        for r in range(per):
            x = piece[r * TILE : (r + 1) * TILE, :].astype(f32)
            x = x - jnp.sum(x, axis=1, keepdims=True) / D
            x = x * lax.rsqrt(jnp.sum(x * x, axis=1, keepdims=True) / D + norm_epsilon)
            xn_ref[(lax.axis_index("head") ^ k) * per + r] = x.astype(bf16)


def assemble_kernel(offsets, *refs):
    w_pieces, (wt_ref, w_ref) = refs[:-2], refs[-2:]
    for piece, group in zip(w_pieces, offsets):
        rows = piece.shape[0] // len(group)
        for at, offset in enumerate(group):
            start = pl.multiple_of((lax.axis_index("dp") ^ offset) * rows, 16)
            w_ref[pl.ds(start, rows), :] = piece[at * rows : (at + 1) * rows, :]
    wt_ref[...] = flip(w_ref[...]).astype(bf16)


def project_kernel(heads, *refs):
    refs = list(refs)
    take = lambda count: [refs.pop(0) for _ in range(count)]
    xn_ref, wt_ref, oh_ref, oht_ref = take(4)
    d_ref, kx_ref, kxt_ref, qs_ref, q_ref, v_ref, vt_ref = refs
    width = v_ref.shape[2]

    def project(i):
        x = xn_ref[i]
        p = dot_nt(wt_ref[width : 4 * width], x)
        sg = 0.5 + 0.5 * jnp.tanh(0.5 * p)
        act = p * sg
        d_ref[i] = (sg + act * (1.0 - sg)).astype(bf16)
        vt = act[:width]
        vt_ref[i] = vt.astype(bf16)
        v_ref[i] = flip(vt).astype(bf16)
        qt = act[width : 2 * width].astype(bf16)
        kt = act[2 * width :]
        kxt_ref[i, :NTB] = oht_ref[i]
        kxt_ref[i, NTB:] = kt.astype(bf16)
        kx_ref[i, :, :NTB] = oh_ref[i]
        kx_ref[i, :, NTB:] = flip(kt).astype(bf16)
        qs = (qt.astype(f32) * (0.5 / math.sqrt(HEAD_DIM))).astype(bf16)
        qs_ref[i] = qs
        q_ref[i] = flip(qt).astype(bf16)

    for i in range(xn_ref.shape[0]):
        project(i)

def tile_at(refs, i, j):
    at = i * (i + 1) // 2 + j
    for ref in refs:
        if at < ref.shape[0]:
            return ref[at]
        at -= ref.shape[0]


def weights_and_slope(h):
    th = jnp.tanh(h)
    u = 1.0 + th
    w = h * u
    return w, u + w * (1.0 - th)


def attend_kernel(heads, first, last, kept, *refs):
    if first:
        before_ref, refs = refs[0], refs[1:]
    kx_ref, qs_ref, trow_ref, vt_ref, pos_ref, ss_ref, attn_ref = refs[:7]
    if first:
        attn_ref[:first] = before_ref[...]
    tiles = [(i, j) for i in range(first, last) for j in range(i + 1)]
    scores, weights = {}, {}
    for t in range(len(tiles) + 3):
        if t < len(tiles):
            i, j = tiles[t]
            if j == 0:
                queries = query_columns(qs_ref[i], trow_ref[i], heads)
            scores[t] = dot(kx_ref[j], queries)
        if 0 <= t - 1 < len(tiles):
            i, j = tiles[t - 1]
            h = masked(scores.pop(t - 1), pos_ref[i - j], ss_ref[:, i * TILE : (i + 1) * TILE], j, heads)
            w, slope = weights_and_slope(h)
            weights[t - 1] = w.astype(bf16)
            if kept:
                refs[7][t - 1] = weights[t - 1]
                refs[8][t - 1] = slope.astype(bf16)
        if t >= 3:
            i, j = tiles[t - 3]
            more = dot(vt_ref[j], weights.pop(t - 3))
            total = more if j == 0 else total + more
            if i == j:
                attn_ref[i] = own_rows(total, heads)


def gate_kernel(n_head, *refs):
    refs = list(refs)
    take = lambda count: [refs.pop(0) for _ in range(count)]
    cot_pieces = take(n_head)
    attn_ref, xn_ref, wt_ref = take(3)
    p_ref, gg_ref, stat_ref, gb_ref = refs
    width = attn_ref.shape[1]
    per = cot_pieces[0].shape[0] // TILE
    gb_ref[...] = jnp.sum(cot_pieces[0][...].astype(f32), axis=0, keepdims=True)
    for k, piece in enumerate(cot_pieces):
        for r in range(per):
            i = (lax.axis_index("head") ^ k) * per + r
            p = dot_nt(wt_ref[:width], xn_ref[i])
            gate = p * (0.5 + 0.5 * jnp.tanh(0.5 * p))
            gg = dot_nt(wt_ref[4 * width :], piece[r * TILE : (r + 1) * TILE, :])
            grad = gg * gate
            p_ref[i] = p
            gg_ref[i] = gg
            at = attn_ref[i]
            mean = jnp.sum(at, axis=0, keepdims=True) / width
            centred = at - mean
            stat_ref[i] = jnp.concatenate(
                [
                    mean,
                    jnp.sum(centred * centred, axis=0, keepdims=True),
                    jnp.sum(grad, axis=0, keepdims=True),
                    jnp.sum(grad * centred, axis=0, keepdims=True),
                ],
                axis=0,
            )


def standardized(i, n_head, stats, attn_ref):
    width = attn_ref.shape[1]
    st = [s[i] for s in stats]
    mean = sum(p[0:1] for p in st) / n_head
    spread = sum(p[1:2] + width * (p[0:1] - mean) * (p[0:1] - mean) for p in st)
    scale = lax.rsqrt(spread / HD + norm_epsilon)
    first = sum(p[2:3] for p in st) / HD
    second = scale * sum(p[3:4] + (p[0:1] - mean) * p[2:3] for p in st) / HD
    return (attn_ref[i] - mean) * scale, scale, first, second


def branch_kernel(n_head, *refs):
    stats, (attn_ref, p_ref, wt_ref, keep, send) = refs[:n_head], refs[n_head:]
    width = attn_ref.shape[1]
    per = keep.shape[1] // TILE
    for k in range(n_head):
        device = lax.axis_index("head") ^ k
        for r in range(per):
            i = device * per + r
            normed = standardized(i, n_head, stats, attn_ref)[0]
            p = p_ref[i]
            gated = (normed * (p * (0.5 + 0.5 * jnp.tanh(0.5 * p)))).astype(bf16)
            (keep, send)[k % 2][device // 2, r * TILE : (r + 1) * TILE] = dot(
                flip(gated).astype(bf16), wt_ref[4 * width :]
            ).astype(bf16)


def middle_kernel(n_head, *refs):
    refs = list(refs)
    take = lambda count: [refs.pop(0) for _ in range(count)]
    stats = take(n_head)
    cot_pieces = take(n_head)
    attn_ref, p_ref, gg_ref, xn_ref = take(4)
    da_ref, dat_ref, gun_ref = take(3)
    (acc_ref,) = refs
    width = attn_ref.shape[1]
    per = cot_pieces[0].shape[0] // TILE
    for k, piece in enumerate(cot_pieces):
        for r in range(per):
            i = (lax.axis_index("head") ^ k) * per + r
            normed, scale, first, second = standardized(i, n_head, stats, attn_ref)
            p = p_ref[i]
            sg = 0.5 + 0.5 * jnp.tanh(0.5 * p)
            gate = p * sg
            gg = gg_ref[i]
            gated = (normed * gate).astype(bf16)
            grad = scale * (gg * gate - first - normed * second)
            da_ref[i] = flip(grad).astype(bf16)
            dat_ref[i] = (grad * 0.5).astype(bf16)
            gu = (gg * normed * (sg + gate * (1.0 - sg))).astype(bf16)
            gun_ref[i] = flip(gu).astype(bf16)
            add_gate, add_out = dot(gu, xn_ref[i]), dot(gated, piece[r * TILE : (r + 1) * TILE, :])
            if k + r == 0:
                acc_ref[:width] = add_gate
                acc_ref[width:] = add_out
            else:
                acc_ref[:width] += add_gate
                acc_ref[width:] += add_out


def send_parts(wg_ref, parts):
    low = len(parts)
    high, rows = parts[0].shape[0], parts[0].shape[1]
    me = lax.axis_index("dp") % low
    for k in range(low):
        for p in range(high):
            start = pl.multiple_of((p * low + (me ^ k)) * rows, 16)
            parts[k][p] = wg_ref[pl.ds(start, rows), :].astype(bf16)


def values_kernel(heads, kept, *refs):
    refs = list(refs)
    take = lambda count: [refs.pop(0) for _ in range(count)]
    held = take(2 if kept else 5)
    da_ref, d_ref, xn_ref, acc_in = take(4)
    gpv_ref = refs.pop(0)
    parts, wg_ref = refs[:-1], refs[-1]
    nb, width = da_ref.shape[0], da_ref.shape[2]
    das = [own_lanes(da_ref[i], heads) for i in range(nb)]
    queries = None if kept else [query_columns(held[1][i], held[2][i], heads) for i in range(nb)]
    acc = None
    for j in range(nb):
        if kept:
            tiles = [tile_at(held, i, j) for i in range(j, nb)]
        else:
            kx_ref, _, _, pos_ref, ss_ref = held
            tiles = [
                weights_and_slope(
                    masked(
                        dot(kx_ref[j], queries[i]), pos_ref[i - j], ss_ref[:, i * TILE : (i + 1) * TILE], j, heads
                    )
                )[0].astype(bf16)
                for i in range(j, nb)
            ]
        total = dot(jnp.concatenate(tiles, axis=1), jnp.concatenate(das[j:], axis=0))
        gv = (flip(total) * d_ref[j, :width]).astype(bf16)
        gpv_ref[j] = flip(gv).astype(bf16)
        more = dot(gv, xn_ref[j])
        acc = more if j == 0 else acc + more
    wg_ref[...] = flip(jnp.concatenate([acc_in[...], acc], axis=0))
    send_parts(wg_ref, parts)


def backward_kernel(heads, n_dp, extra, kept, *refs):
    refs = list(refs)
    take = lambda count: [refs.pop(0) for _ in range(count)]
    held = take(2 if kept else 4)
    kx_ref, kxt_ref, q_ref, v_ref, dat_ref = take(5)
    d_ref, xn_ref, gb_ref = take(3)
    gp_ref = refs.pop(0)
    parts = take(split_dp(n_dp)[1])
    acck_ref, posg_ref, acc_ref, wg_ref, small_ref = refs
    nb, width = v_ref.shape[0], v_ref.shape[2]
    factor = 1.0 / math.sqrt(HEAD_DIM)
    tiles = [(i, j) for i in reversed(range(nb)) for j in range(i + 1)]
    products, grads = {}, {}
    dq = m2 = None
    small_ref[...] = jnp.zeros_like(small_ref)
    small_ref[:, :D] = gb_ref[...]

    def add(ref, at, value, first):
        ref[at] = value if first else ref[at] + value

    for t in range(len(tiles) + 3):
        if t < len(tiles):
            i, j = tiles[t]
            if j == 0:
                backs = by_head(dat_ref[i], heads)
                queries = None if kept else query_columns(held[0][i], held[1][i], heads)
            products[t] = dot(v_ref[j], backs), None if kept else dot(kx_ref[j], queries)
        if 0 <= t - 1 < len(tiles):
            i, j = tiles[t - 1]
            back, product = products.pop(t - 1)
            if kept:
                slope = tile_at(held, i, j).astype(f32)
            else:
                start = held[3][:, i * TILE : (i + 1) * TILE]
                slope = weights_and_slope(masked(product, held[2][i - j], start, j, heads))[1]
            ds = back * slope
            grads[t - 1] = ds.astype(bf16)
            add(posg_ref, i - j, sum(ds[:, g * TILE : (g + 1) * TILE] for g in range(heads)), i == nb - 1)
        if t >= 3:
            i, j = tiles[t - 3]
            low = grads.pop(t - 3)
            if j == 0:
                times = jnp.concatenate([kx_ref[i, :, :NTB]] * heads, axis=0)
                q = jnp.concatenate([times, own_lanes(q_ref[i], heads)], axis=1)
            add(acck_ref, j, dot(low, q), i == nb - 1)
            more = dot(kxt_ref[j, NTB:], low)
            dq = more if j == 0 else dq + more
            if i == j:
                gp = jnp.concatenate([own_rows(dq, heads), flip(acck_ref[i, :, NTB:])], axis=0)
                gp = (gp * factor * d_ref[i, width:]).astype(bf16)
                gp_ref[i] = flip(gp).astype(bf16)
                more = dot(gp, xn_ref[i])
                acc_ref[...] = more if i == nb - 1 else acc_ref[...] + more
                part = acck_ref[i, :, :NTB]
                high = part.astype(bf16)
                rest = (part - high.astype(f32)).astype(bf16)
                onehot = kxt_ref[i, :NTB]
                part = dot(onehot, high) + dot(onehot, rest)
                m2 = part if i == nb - 1 else m2 + part
                g = diagonals(posg_ref[i])
                small_ref[:, D + i * TILE : D + (i + 1) * TILE] += g[:, :TILE]
                if i > 0:
                    small_ref[:, D + (i - 1) * TILE : D + i * TILE] += g[:, TILE:]
    g = diagonals(m2 + jnp.transpose(m2))[:, :NTB]
    zero = lax.broadcasted_iota(jnp.int32, (1, NTB), 1) == 0
    at = D + nb * TILE
    small_ref[:, at : at + NTB] = jnp.where(zero, 0.5 * g, g)
    step = D // n_dp
    grads = flip(acc_ref[...])
    for p in range(n_dp):
        here = jnp.concatenate(
            [small_ref[:, (p * extra + r) * 128 : (p * extra + r + 1) * 128] for r in range(extra)], axis=0
        )
        high = here.astype(bf16).astype(f32)
        block = jnp.concatenate([high, here - high, jnp.zeros((16 - 2 * extra, 128), f32)], axis=0)
        wg_ref[p * (step + 16) : p * (step + 16) + step] = grads[p * step : (p + 1) * step]
        if 2 * width > 128:
            block = jnp.concatenate([block, jnp.zeros((16, 2 * width - 128), f32)], axis=1)
        wg_ref[p * (step + 16) + step : (p + 1) * (step + 16)] = block
    send_parts(wg_ref, parts)


def input_kernel(n_head, gp_ref, gun_ref, gpv_ref, wt_ref, keep, send):
    width = gun_ref.shape[2]
    per = keep.shape[1] // TILE
    for k in range(n_head):
        device = lax.axis_index("head") ^ k
        target = (keep, send)[k % 2]
        for r in range(per):
            i = device * per + r
            rows = dot(jnp.concatenate([gun_ref[i], gpv_ref[i]], axis=1), wt_ref[: 2 * width])
            rows = rows + dot(gp_ref[i], wt_ref[2 * width : 4 * width])
            target[device // 2, r * TILE : (r + 1) * TILE] = rows.astype(bf16)


def fold_kernel(*refs):
    low = sum(len(ref.shape) == 3 for ref in refs)
    row = lax.axis_index("dp") // low
    for k, out in enumerate(refs[low:]):
        total = refs[0][row ^ k].astype(f32)
        for ref in refs[1:low]:
            total = total + ref[row ^ k].astype(f32)
        out[...] = total.astype(out.dtype)


def sum_kernel(*refs):
    total = refs[0][...]
    for ref in refs[1:-1]:
        total = total + ref[...].astype(f32)
    refs[-1][...] = total


def mix_kernel(tokens_ref, bias_ref, *refs):
    total = tokens_ref[...].astype(f32) + row_lanes(bias_ref, 0, D // 128)
    for ref in refs[:-1]:
        total = total + ref[...].astype(f32)
    refs[-1][...] = total.astype(bf16)


def finish_kernel(part, *refs):
    tokens_ref, cot_ref, mine_ref, *refs = refs[part:]
    x = tokens_ref[...].astype(f32)
    x = x - jnp.sum(x, axis=1, keepdims=True) / D
    scale = lax.rsqrt(jnp.sum(x * x, axis=1, keepdims=True) / D + norm_epsilon)
    x = x * scale
    grad = mine_ref[...]
    for ref in refs[:-1]:
        grad = grad + ref[...].astype(f32)
    mean = jnp.sum(grad, axis=1, keepdims=True) / D
    along = jnp.sum(grad * x, axis=1, keepdims=True) / D
    refs[-1][...] = cot_ref[...].astype(f32) + scale * (grad - mean - x * along)


def rows_kernel(chips, keep_ref, crossed_ref, mine_ref, *leaving):
    chip = lax.axis_index("head") // 2
    for k in range(chips):
        total = keep_ref[chip ^ k].astype(f32) + crossed_ref[chip ^ k].astype(f32)
        if k == 0:
            mine_ref[...] = total
        else:
            rows = leaving[0].shape[0]
            cuts = total.shape[0] // rows
            for c in range(cuts):
                leaving[(k - 1) * cuts + c][...] = total[c * rows : (c + 1) * rows].astype(bf16)


def collect_kernel(high, extra, *refs):
    late_blocks, (early_ref, grads_ref, message_ref) = refs[:high], refs[high:]
    rows = grads_ref.shape[0]
    total, early = late_blocks[0][...], early_ref[...]
    for k in range(1, high):
        total = total + late_blocks[k][...].astype(f32)
    grads = jnp.concatenate([total[:rows], early], axis=1)
    grads_ref[...] = grads
    squares = jnp.sum(jnp.sum(grads * grads, axis=0, keepdims=True), axis=1, keepdims=True)
    message = jnp.concatenate(
        [
            total[rows : rows + extra, :128] + total[rows + extra : rows + 2 * extra, :128],
            jnp.broadcast_to(squares, (message_ref.shape[1] - extra, 128)),
        ],
        axis=0,
    )
    for k in range(message_ref.shape[0]):
        message_ref[k] = message


def update_kernel(n_head, extra, group, heard_ref, grads_ref, *refs):
    state, outs = refs[:9], refs[9:]
    grad_proj_ref, grad_out_ref, grad_small_ref, norm_ref = outs[:4]
    n_all = heard_ref.shape[0]
    width = grad_out_ref.shape[1]
    lead, pos_rows, used = D // 128, POS // 128, (D + group) // 128
    grad_small_ref[...] = jnp.zeros_like(grad_small_ref)
    last = heard_ref.shape[1] - 1
    squares = heard_ref[0, last:, :]
    for k in range(1, n_all):
        squares = squares + heard_ref[k, last:, :]
    for p in range(n_all // n_head):
        rows = heard_ref[p * n_head, :extra, :]
        for h in range(1, n_head):
            rows = rows + heard_ref[p * n_head + h, :extra, :]
        for r in range(extra):
            at = p * extra + r
            if at < used:
                grad_small_ref[at : at + 1, :] = rows[r : r + 1]
            elif at == used:
                grad_small_ref[lead + pos_rows : lead + pos_rows + 1, :] = rows[r : r + 1]
    small = grad_small_ref[...]
    total = jnp.sum(jnp.sum(small * small, axis=0, keepdims=True), axis=1, keepdims=True) + squares[:, :1]
    norm = jnp.sqrt(total)
    norm_ref[...] = norm
    factor = jnp.minimum(1.0, clip_norm / (norm + 1e-06))

    def update(get, put, grad, rate, decay):
        for k, value in enumerate(adam_step(get(0), grad, get(1), get(2), factor, rate, decay)):
            put(k, value)

    for c in range(4):
        at = (2, 4, 0, 1)[c] * width
        grad = grads_ref[:, at : at + width]
        grad_proj_ref[:, c, :] = grad

        def put(k, value):
            outs[4 + k][:, c, :] = value

        update(lambda k: state[k][:, c, :], put, grad, rate_matrix, decay_matrix)
    grad = grads_ref[:, 3 * width : 4 * width]
    grad_out_ref[...] = grad

    def put_out(k, value):
        outs[7 + k][...] = value

    update(lambda k: state[3 + k][...], put_out, grad, rate_matrix, decay_matrix)

    def put_small(k, value):
        outs[10 + k][...] = value

    update(lambda k: state[6 + k][...], put_small, small, rate_small, 0.0)


def call(kernel, name, in_specs, outs, scratch, us, room=16, **more):
    return pl.pallas_call(
        kernel,
        out_shape=[jax.ShapeDtypeStruct(shape, dtype) for shape, dtype, _ in outs],
        in_specs=in_specs,
        out_specs=[spec for _, _, spec in outs],
        scratch_shapes=scratch,
        compiler_params=pltpu.CompilerParams(vmem_limit_bytes=min(60, room * max(1, lax.axis_size("head") // 4)) * 2**20),
        cost_estimate=pl.CostEstimate(flops=int(us * 1e9), bytes_accessed=int(us * 3e6), transcendentals=0),
        name=name,
        **more,
    )


def block(shape):
    return pl.BlockSpec((1,) + tuple(shape[1:]), lambda i: (i,) + (0,) * (len(shape) - 1))


def shards(
    tokens,
    cotangent,
    seq_start,
    time_bucket,
    proj_weight,
    out_weight,
    small_params,
    proj_mean,
    proj_square,
    out_mean,
    out_square,
    small_mean,
    small_square,
):
    n_head = lax.axis_size("head")
    n_dp = lax.axis_size("dp")
    here = tokens.shape[0]
    group = here * n_head
    nb = group // TILE
    per = here // TILE
    rows_here, _, width = proj_weight.shape
    heads = width // HEAD_DIM
    high, low = split_dp(n_dp)

    (weights,) = call(
        cast_kernel,
        "cast",
        [pl.BlockSpec(memory_space=pl.ANY)] * 2,
        [((rows_here, 5 * width), bf16, VMEM)],
        [
            pltpu.VMEM(proj_weight.shape, f32),
            pltpu.VMEM((rows_here, width), f32),
            pltpu.SemaphoreType.DMA((2,)),
        ],
        1,
    )(proj_weight, out_weight.T)
    x_chips = gather_chips(after(tokens, weights))
    starts = seq_start.reshape(1, group)
    times = time_bucket.reshape(1, group)
    small_rows = small_params.reshape(-1, 128)
    pos, oh, oht, trow = call(
        prepare_kernel,
        "prepare",
        [VMEM] * 2,
        [
            ((nb, TILE, TILE), f32, VMEM),
            ((nb, TILE, NTB), bf16, VMEM),
            ((nb, NTB, TILE), bf16, VMEM),
            ((nb, NTB, TILE), bf16, VMEM),
        ],
        [],
        2,
    )(after(times, weights), small_rows)

    items = [
        ((nb, 3 * width, TILE), bf16),
        ((nb, TILE, NTB + width), bf16),
        ((nb, NTB + width, TILE), bf16),
        ((nb, width, TILE), bf16),
        ((nb, TILE, width), bf16),
        ((nb, TILE, width), bf16),
        ((nb, width, TILE), bf16),
    ]
    w_pieces, offsets = gather_dp(weights, pos)
    cot_chips = gather_chips(after(cotangent, weights))

    x_pieces = gather_cores(tokens, x_chips)
    near = [0, 1] + list(range(2, n_head, 2))
    far = list(range(3, n_head, 2))
    xn = []
    for which in (near, far):
        xn = call(
            functools.partial(normalize_kernel, which),
            "normalize",
            [VMEM] * (len(xn) + len(which)),
            [((nb, TILE, D), bf16, VMEM)],
            [],
            0.1,
        )(*xn, *[x_pieces[k] for k in which])
    (xn,) = xn
    w_pieces[-1] = after(join(w_pieces[-1:], 6), xn)
    (wt,) = call(
        functools.partial(assemble_kernel, offsets),
        "assemble",
        [VMEM] * len(w_pieces),
        [((5 * width, D), bf16, VMEM)],
        [pltpu.VMEM((D, 5 * width), bf16)],
        0.5,
    )(*w_pieces)
    dsilu, kx, kxt, qs, q, v, vt = call(
        functools.partial(project_kernel, heads),
        "project",
        [VMEM] * 4,
        [item + (VMEM,) for item in items],
        [],
        1,
    )(xn, wt, oh, oht)

    kept = nb * (nb + 1) // 2 * heads <= KEPT_TILES

    def attend(first, last, *before):
        count = (last * (last + 1) - first * (first + 1)) // 2
        return call(
            functools.partial(attend_kernel, heads, first, last, kept),
            "attend",
            [VMEM] * (len(before) + 6),
            [((last, width, TILE), f32, VMEM)] + [((count, TILE, heads * TILE), bf16, VMEM)] * (2 * kept),
            [],
            8 if before else 0.5,
        )(*before, kx, qs, trow, vt, pos, starts)

    split = nb - nb // 4
    attn, *kept_first = attend(0, split)
    cot_chips = after_all(cot_chips, attn)
    attn, *kept_last = attend(split, nb, after(attn, *cot_chips))
    kept_weights, kept_slopes = zip(kept_first, kept_last) if kept else ((), ())
    cot_pieces = gather_cores(cotangent, cot_chips)

    column = ((nb, width, TILE), f32, VMEM)
    p_gate, gg, stat, gb = call(
        functools.partial(gate_kernel, n_head),
        "gate",
        [VMEM] * (n_head + 3),
        [column, column, ((nb, 4, TILE), f32, VMEM), ((1, D), f32, VMEM)],
        [],
        5,
    )(*cot_pieces, attn, xn, wt)

    stats = [stat] + [swap(stat, "head", k) for k in range(1, n_head)]
    chips = n_head // 2
    split_shape = ((chips, here, D), bf16, VMEM)
    keep, send = call(
        functools.partial(branch_kernel, n_head), "branch", [VMEM] * (n_head + 3), [split_shape] * 2, [], 1
    )(*stats, attn, p_gate, wt)
    crossed = swap(send, "head", 1)
    da, dat, gun, wg_sum = call(
        functools.partial(middle_kernel, n_head),
        "middle",
        [VMEM] * (2 * n_head + 4),
        [
            ((nb, TILE, width), bf16, VMEM),
            ((nb, width, TILE), bf16, VMEM),
            ((nb, TILE, width), bf16, VMEM),
            ((2 * width, D), f32, VMEM),
        ],
        [],
        6,
    )(*stats, *cot_pieces, attn, p_gate, gg, xn)
    branch, *leaving = fold_cores(keep, crossed)
    received = [swap(sent, "head", 2 * (k + 1)) for k, sent in enumerate(leaving)]
    held = kept_weights if kept else (kx, qs, trow, pos, starts)
    gpv, *early_parts = call(
        functools.partial(values_kernel, heads, kept),
        "values",
        [VMEM] * (len(held) + 4),
        [((nb, TILE, width), bf16, VMEM)] + [((high, rows_here, 3 * width), bf16, VMEM)] * low,
        [pltpu.VMEM((D, 3 * width), f32)],
        VALUES,
    )(*held, da, dsilu, xn, wg_sum)
    early_received = [swap(early_parts[k], "dp", k) for k in range(1, low)]

    length = D + group + NTB
    extra = -(-length // (128 * n_dp))
    held = kept_slopes if kept else (qs, trow, pos, starts)
    gp, *late_parts = call(
        functools.partial(backward_kernel, heads, n_dp, extra, kept),
        "backward",
        [VMEM] * (len(held) + 8),
        [((nb, TILE, 2 * width), bf16, VMEM)] + [((high, rows_here + 16, 2 * width), bf16, VMEM)] * low,
        [
            pltpu.VMEM((nb, TILE, NTB + width), f32),
            pltpu.VMEM((nb, TILE, TILE), f32),
            pltpu.VMEM((2 * width, D), f32),
            pltpu.VMEM((n_dp * (rows_here + 16), 2 * width), f32),
            pltpu.VMEM((1, extra * n_dp * 128), f32),
        ],
        BACKWARD,
        ROOM,
    )(*held, kx, kxt, q, v, dat, dsilu, xn, gb)

    tied = lax.optimization_barrier((gp, *late_parts, *early_received, *received))
    gp, late_parts = tied[0], tied[1 : 1 + low]
    early_received, received = tied[1 + low : 2 * low], tied[2 * low :]
    late_received = [swap(late_parts[k], "dp", k) for k in range(1, low)]
    keep, send = call(
        functools.partial(input_kernel, n_head),
        "input_rows",
        [VMEM] * 4,
        [((n_head // 2, here, D), bf16, VMEM)] * 2,
        [],
        4,
    )(gp, gun, gpv, wt)
    early_blocks = scatter_high(after(early_parts[0], send), early_received, 1)
    crossed = swap(send, "head", 1)
    late_blocks = scatter_high(late_parts[0], late_received, 12, send, crossed)
    (early,) = call(
        sum_kernel, "sum", [VMEM] * high, [((rows_here, 3 * width), f32, VMEM)], [], 14
    )(*early_blocks)
    mine, *leaving = fold_cores(keep, after(crossed, late_blocks[0]), 2)
    half = here // 2
    arrived = [[swap(leaving[2 * k - 2 + part], "head", 2 * k) for k in range(1, chips)] for part in range(2)]
    n_all = n_dp * n_head
    grads_shape = ((rows_here, 5 * width), f32)
    grads, message = call(
        functools.partial(collect_kernel, high, extra),
        "collect",
        [VMEM] * (high + 1),
        [grads_shape + (VMEM,), ((n_all, 4 if extra < 4 else 8, 128), f32, VMEM)],
        [],
        10,
    )(*late_blocks, early)
    message = after(message, *leaving)
    heard = lax.all_to_all(message, ("dp", "head"), 0, 0, tiled=True)
    (mixed,) = call(
        mix_kernel, "mix", [VMEM] * (2 + chips), [((here, D), bf16, VMEM)], [], 1
    )(tokens, small_rows, after(branch, message), *received)
    input_grad = None
    for part in range(2):
        rows = pl.BlockSpec((half, D), lambda i, part=part: (part, 0))
        alone = pl.BlockSpec((half, D), lambda i: (0, 0))
        before = [] if part == 0 else [input_grad]
        (input_grad,) = call(
            functools.partial(finish_kernel, part),
            "finish",
            [pl.BlockSpec(memory_space=pl.ANY)] * len(before) + [rows] * 3 + [alone] * (chips - 1),
            [((here, D), f32, rows)],
            [],
            1,
            grid=(1,),
            input_output_aliases={0: 0} if before else {},
        )(*before, tokens, cotangent, mine, *arrived[part])
    heard = after(heard, input_grad)
    state = [proj_weight, proj_mean, proj_square, out_weight.T, out_mean.T, out_square.T]
    state += [x.reshape(-1, 128) for x in (small_params, small_mean, small_square)]
    proj_shape, out_shape, small_shape = proj_weight.shape, (rows_here, width), small_rows.shape
    shapes = [proj_shape, out_shape, small_shape, (1, 1)] + [proj_shape] * 3 + [out_shape] * 3 + [small_shape] * 3
    results = call(
        functools.partial(update_kernel, n_head, extra, group),
        "update",
        [VMEM] * (2 + len(state)),
        [(shape, f32, VMEM) for shape in shapes],
        [],
        0.1,
    )(heard, grads, *state)
    grad_proj, grad_out, grad_small, grad_norm = results[:4]
    grad_out, grad_small, grad_norm = grad_out.T, grad_small.reshape(-1), grad_norm.reshape(())
    new_proj, mean_proj, square_proj = results[4:7]
    new_out, mean_out, square_out = [x.T for x in results[7:10]]
    new_small, mean_small, square_small = [x.reshape(-1) for x in results[10:13]]
    return (
        mixed,
        input_grad,
        grad_proj,
        grad_out,
        grad_small,
        grad_norm,
        new_proj,
        mean_proj,
        square_proj,
        new_out,
        mean_out,
        square_out,
        new_small,
        mean_small,
        square_small,
    )


def solution(mesh):
    in_specs = (
        P(("dp", "head"), None),
        P(("dp", "head"), None),
        P("dp"),
        P("dp"),
        P("dp", None, "head"),
        P("head", "dp"),
        P(),
        P("dp", None, "head"),
        P("dp", None, "head"),
        P("head", "dp"),
        P("head", "dp"),
        P(),
        P(),
    )
    out_specs = (
        P(("dp", "head"), None),
        P(("dp", "head"), None),
        P("dp", None, "head"),
        P("head", "dp"),
        P(),
        P(),
        P("dp", None, "head"),
        P("dp", None, "head"),
        P("dp", None, "head"),
        P("head", "dp"),
        P("head", "dp"),
        P("head", "dp"),
        P(),
        P(),
        P(),
    )
    return jax.shard_map(shards, mesh=mesh, in_specs=in_specs, out_specs=out_specs, check_vma=False)
```

```python
import functools
import math

import jax
import jax.numpy as jnp
from jax import lax
from jax.experimental import pallas as pl
from jax.experimental.pallas import tpu as pltpu
from jax.sharding import PartitionSpec as P

D = 512
HEAD_DIM = 64
HD = 512
POS = 8192
NTB = 128
STEP = 10
TILE = 256
NEG = -1e9
ROOM = 16
KEPT_TILES = 72
VALUES = 12
BACKWARD = 2

norm_epsilon = 1e-06
adam_epsilon = 1e-08
beta_one = 0.9
beta_two = 0.999
clip_norm = 1.0
rate_matrix = 0.05
rate_small = 0.3
decay_matrix = 0.1

f32 = jnp.float32
bf16 = jnp.bfloat16
VMEM = pl.BlockSpec(memory_space=pltpu.VMEM)


def adam_step(weight, grad, first, second, factor, rate, decay):
    clipped = grad * factor
    first_new = beta_one * first + (1.0 - beta_one) * clipped
    second_new = beta_two * second + (1.0 - beta_two) * clipped * clipped
    update = (
        first_new
        / (1.0 - beta_one**STEP)
        / (jnp.sqrt(second_new / (1.0 - beta_two**STEP)) + adam_epsilon)
    )
    return (weight - rate * (update + decay * weight), first_new, second_new)


def swap(x, axis, k):
    n = lax.axis_size(axis)
    return lax.ppermute(x, axis, [(i, i ^ k) for i in range(n)])


def gather_chips(x):
    return [swap(x, "head", k) for k in range(2, lax.axis_size("head"), 2)]


def gather_cores(x, others):
    pieces = [x, swap(x, "head", 1)]
    for other in others:
        pieces += [other, swap(other, "head", 1)]
    return pieces


def after_all(arrays, *others):
    arrays = tuple(arrays)
    return lax.optimization_barrier(arrays + others)[: len(arrays)]


def after(x, *others):
    return lax.optimization_barrier((x,) + others)[0]


def gather_dp(x, behind):
    n = lax.axis_size("dp")
    arrays, offsets = [x], [[0]]
    k = n // 2
    while k:
        operand = join(arrays) if len(arrays) > 1 else x
        if k == 1:
            operand = after(operand, behind)
        arrays.append(swap(operand, "dp", k))
        offsets.append([o ^ k for group in offsets for o in group])
        k //= 2
    return arrays, offsets


def join(arrays, us=0.1):
    shape = (sum(x.shape[0] for x in arrays), arrays[0].shape[1])
    return call(join_kernel, "join", [VMEM] * len(arrays), [(shape, arrays[0].dtype, VMEM)], [], us)(*arrays)[0]


def split_dp(n):
    low = 2 ** ((n.bit_length() - 1) // 2)
    return n // low, low


def scatter_high(own, received, us, *behind):
    high, rows, columns = own.shape
    low = 1 + len(received)
    mine, *leaving = call(
        fold_kernel,
        "fold",
        [VMEM] * low,
        [((rows, columns), f32, VMEM)] + [((rows, columns), bf16, VMEM)] * (high - 1),
        [],
        us,
    )(own, *received)
    leaving = after_all(leaving, *behind)
    return [mine] + [swap(leaving[k - 1], "dp", k * low) for k in reversed(range(1, high))]


def fold_cores(keep, crossed, cuts=1):
    chips, rows, columns = keep.shape
    return call(
        functools.partial(rows_kernel, chips),
        "rows",
        [VMEM] * 2,
        [((rows, columns), f32, VMEM)] + [((rows // cuts, columns), bf16, VMEM)] * (cuts * (chips - 1)),
        [],
        0.1,
    )(keep, crossed)


def dot(a, b):
    return lax.dot_general(a, b, (((1,), (0,)), ((), ())), preferred_element_type=f32)


def dot_nt(a, b):
    return lax.dot_general(a, b, (((1,), (1,)), ((), ())), preferred_element_type=f32)


def flip(a):
    return jnp.transpose(a.astype(f32))


def lanes(i):
    return pl.ds(pl.multiple_of(i * TILE, TILE), TILE)


def by_head(block, heads):
    zero = jnp.zeros((HEAD_DIM, block.shape[1]), block.dtype)
    return jnp.concatenate(
        [
            jnp.concatenate(
                [block[g * HEAD_DIM : (g + 1) * HEAD_DIM] if g == h else zero for g in range(heads)], axis=0
            )
            for h in range(heads)
        ],
        axis=1,
    )


def query_columns(qs, trow, heads):
    return jnp.concatenate([jnp.concatenate([trow] * heads, axis=1), by_head(qs, heads)], axis=0)


def own_rows(block, heads):
    return jnp.concatenate(
        [block[h * HEAD_DIM : (h + 1) * HEAD_DIM, h * TILE : (h + 1) * TILE] for h in range(heads)], axis=0
    )


def own_lanes(block, heads):
    lane = lax.broadcasted_iota(jnp.int32, block.shape, 1) // HEAD_DIM
    return jnp.concatenate([jnp.where(lane == h, block, jnp.zeros_like(block)) for h in range(heads)], axis=0)


def masked(product, bias, start, j, heads):
    key = j * TILE + lax.broadcasted_iota(jnp.int32, (TILE, TILE), 0)
    seen = key >= start
    return jnp.where(
        jnp.concatenate([seen] * heads, axis=1), product + jnp.concatenate([bias] * heads, axis=1), NEG
    )


def diagonals(x):
    rows, cols = x.shape
    z = jnp.concatenate([x, jnp.zeros((rows, cols), f32)], axis=1)
    total = z[:8]
    for q in range(1, rows // 8):
        total = total + pltpu.roll(z[8 * q : 8 * q + 8], 2 * cols - 8 * q, 1)
    g = total[0:1]
    for r in range(1, 8):
        g = g + pltpu.roll(total, 2 * cols - r, 1)[r : r + 1]
    return g


def cast_kernel(w_in, o_in, low_ref, w_ref, o_ref, sems):
    copies = [pltpu.make_async_copy(w_in, w_ref, sems.at[0]), pltpu.make_async_copy(o_in, o_ref, sems.at[1])]
    for copy in copies:
        copy.start()
    for copy in copies:
        copy.wait()
    width = o_ref.shape[1]
    for c in range(4):
        low_ref[:, c * width : (c + 1) * width] = w_ref[:, c, :].astype(bf16)
    low_ref[:, 4 * width :] = o_ref[...].astype(bf16)


def row_lanes(ref, first, count):
    return jnp.concatenate([ref[pl.ds(first + k, 1), :] for k in range(count)], axis=1)


def prepare_kernel(tb_ref, small_ref, pos_ref, oh_ref, oht_ref, trow_ref):
    nb = pos_ref.shape[0]
    step = TILE // 128

    def tile(d, _):
        first = D // 128 + d * step
        row = jnp.concatenate([row_lanes(small_ref, first, step), row_lanes(small_ref, first - step, step)], axis=1)
        pos_ref[d] = pltpu.roll(
            jnp.broadcast_to(row * 0.5, (TILE, 2 * TILE)), 0, 1, stride=1, stride_axis=0
        )[:, :TILE]
        return 0

    lax.fori_loop(0, nb, tile, 0)
    b = lax.broadcasted_iota(jnp.int32, (TILE, TILE), 0)
    a = lax.broadcasted_iota(jnp.int32, (TILE, TILE), 1)
    pos_ref[0] = jnp.where(b <= a, pos_ref[0], NEG)
    table = row_lanes(small_ref, (D + POS) // 128, NTB // 128)
    row = jnp.concatenate([table, table], axis=1)
    upper = pltpu.roll(jnp.broadcast_to(row, (NTB, 2 * NTB)), 0, 1, stride=1, stride_axis=0)[:, :NTB]
    a = lax.broadcasted_iota(jnp.int32, (NTB, NTB), 0)
    b = lax.broadcasted_iota(jnp.int32, (NTB, NTB), 1)
    upper = jnp.where(b >= a, upper, 0.0)
    square = (jnp.where(b > a, upper, jnp.transpose(upper)) * 0.5).astype(bf16)

    def block(i, _):
        onehot = (lax.broadcasted_iota(jnp.int32, (NTB, TILE), 0) == tb_ref[:, lanes(i)]).astype(f32)
        low = onehot.astype(bf16)
        oht_ref[i] = low
        oh_ref[i] = flip(onehot).astype(bf16)
        trow_ref[i] = dot(square, low).astype(bf16)
        return 0

    lax.fori_loop(0, nb, block, 0)


def join_kernel(*refs):
    at = 0
    for ref in refs[:-1]:
        refs[-1][at : at + ref.shape[0]] = ref[...]
        at += ref.shape[0]


def normalize_kernel(which, *refs):
    before = refs[: len(refs) - len(which) - 1]
    pieces, xn_ref = refs[len(before) : -1], refs[-1]
    per = pieces[0].shape[0] // TILE
    for ref in before:
        xn_ref[...] = ref[...]
    for k, piece in zip(which, pieces):
        for r in range(per):
            x = piece[r * TILE : (r + 1) * TILE, :].astype(f32)
            x = x - jnp.sum(x, axis=1, keepdims=True) / D
            x = x * lax.rsqrt(jnp.sum(x * x, axis=1, keepdims=True) / D + norm_epsilon)
            xn_ref[(lax.axis_index("head") ^ k) * per + r] = x.astype(bf16)


def assemble_kernel(offsets, *refs):
    w_pieces, (wt_ref, w_ref) = refs[:-2], refs[-2:]
    for piece, group in zip(w_pieces, offsets):
        rows = piece.shape[0] // len(group)
        for at, offset in enumerate(group):
            start = pl.multiple_of((lax.axis_index("dp") ^ offset) * rows, 16)
            w_ref[pl.ds(start, rows), :] = piece[at * rows : (at + 1) * rows, :]
    wt_ref[...] = flip(w_ref[...]).astype(bf16)


def project_kernel(heads, *refs):
    refs = list(refs)
    take = lambda count: [refs.pop(0) for _ in range(count)]
    xn_ref, wt_ref, oh_ref, oht_ref = take(4)
    d_ref, kx_ref, kxt_ref, qs_ref, q_ref, v_ref, vt_ref = refs
    width = v_ref.shape[2]

    def project(i):
        x = xn_ref[i]
        p = dot_nt(wt_ref[width : 4 * width], x)
        sg = 0.5 + 0.5 * jnp.tanh(0.5 * p)
        act = p * sg
        d_ref[i] = (sg + act * (1.0 - sg)).astype(bf16)
        vt = act[:width]
        vt_ref[i] = vt.astype(bf16)
        v_ref[i] = flip(vt).astype(bf16)
        qt = act[width : 2 * width].astype(bf16)
        kt = act[2 * width :]
        kxt_ref[i, :NTB] = oht_ref[i]
        kxt_ref[i, NTB:] = kt.astype(bf16)
        kx_ref[i, :, :NTB] = oh_ref[i]
        kx_ref[i, :, NTB:] = flip(kt).astype(bf16)
        qs = (qt.astype(f32) * (0.5 / math.sqrt(HEAD_DIM))).astype(bf16)
        qs_ref[i] = qs
        q_ref[i] = flip(qt).astype(bf16)

    for i in range(xn_ref.shape[0]):
        project(i)

def tile_at(refs, i, j):
    at = i * (i + 1) // 2 + j
    for ref in refs:
        if at < ref.shape[0]:
            return ref[at]
        at -= ref.shape[0]


def weights_and_slope(h):
    th = jnp.tanh(h)
    u = 1.0 + th
    w = h * u
    return w, u + w * (1.0 - th)


def attend_kernel(heads, first, last, kept, *refs):
    if first:
        before_ref, refs = refs[0], refs[1:]
    kx_ref, qs_ref, trow_ref, vt_ref, pos_ref, ss_ref, attn_ref = refs[:7]
    if first:
        attn_ref[:first] = before_ref[...]
    tiles = [(i, j) for i in range(first, last) for j in range(i + 1)]
    scores, weights = {}, {}
    for t in range(len(tiles) + 3):
        if t < len(tiles):
            i, j = tiles[t]
            if j == 0:
                queries = query_columns(qs_ref[i], trow_ref[i], heads)
            scores[t] = dot(kx_ref[j], queries)
        if 0 <= t - 1 < len(tiles):
            i, j = tiles[t - 1]
            h = masked(scores.pop(t - 1), pos_ref[i - j], ss_ref[:, i * TILE : (i + 1) * TILE], j, heads)
            w, slope = weights_and_slope(h)
            weights[t - 1] = w.astype(bf16)
            if kept:
                refs[7][t - 1] = weights[t - 1]
                refs[8][t - 1] = slope.astype(bf16)
        if t >= 3:
            i, j = tiles[t - 3]
            more = dot(vt_ref[j], weights.pop(t - 3))
            total = more if j == 0 else total + more
            if i == j:
                attn_ref[i] = own_rows(total, heads)


def gate_kernel(n_head, *refs):
    refs = list(refs)
    take = lambda count: [refs.pop(0) for _ in range(count)]
    cot_pieces = take(n_head)
    attn_ref, xn_ref, wt_ref = take(3)
    p_ref, gg_ref, stat_ref, gb_ref = refs
    width = attn_ref.shape[1]
    per = cot_pieces[0].shape[0] // TILE
    gb_ref[...] = jnp.sum(cot_pieces[0][...].astype(f32), axis=0, keepdims=True)
    for k, piece in enumerate(cot_pieces):
        for r in range(per):
            i = (lax.axis_index("head") ^ k) * per + r
            p = dot_nt(wt_ref[:width], xn_ref[i])
            gate = p * (0.5 + 0.5 * jnp.tanh(0.5 * p))
            gg = dot_nt(wt_ref[4 * width :], piece[r * TILE : (r + 1) * TILE, :])
            grad = gg * gate
            p_ref[i] = p
            gg_ref[i] = gg
            at = attn_ref[i]
            mean = jnp.sum(at, axis=0, keepdims=True) / width
            centred = at - mean
            stat_ref[i] = jnp.concatenate(
                [
                    mean,
                    jnp.sum(centred * centred, axis=0, keepdims=True),
                    jnp.sum(grad, axis=0, keepdims=True),
                    jnp.sum(grad * centred, axis=0, keepdims=True),
                ],
                axis=0,
            )


def standardized(i, n_head, stats, attn_ref):
    width = attn_ref.shape[1]
    st = [s[i] for s in stats]
    mean = sum(p[0:1] for p in st) / n_head
    spread = sum(p[1:2] + width * (p[0:1] - mean) * (p[0:1] - mean) for p in st)
    scale = lax.rsqrt(spread / HD + norm_epsilon)
    first = sum(p[2:3] for p in st) / HD
    second = scale * sum(p[3:4] + (p[0:1] - mean) * p[2:3] for p in st) / HD
    return (attn_ref[i] - mean) * scale, scale, first, second


def branch_kernel(n_head, *refs):
    stats, (attn_ref, p_ref, wt_ref, keep, send) = refs[:n_head], refs[n_head:]
    width = attn_ref.shape[1]
    per = keep.shape[1] // TILE
    for k in range(n_head):
        device = lax.axis_index("head") ^ k
        for r in range(per):
            i = device * per + r
            normed = standardized(i, n_head, stats, attn_ref)[0]
            p = p_ref[i]
            gated = (normed * (p * (0.5 + 0.5 * jnp.tanh(0.5 * p)))).astype(bf16)
            (keep, send)[k % 2][device // 2, r * TILE : (r + 1) * TILE] = dot(
                flip(gated).astype(bf16), wt_ref[4 * width :]
            ).astype(bf16)


def middle_kernel(n_head, *refs):
    refs = list(refs)
    take = lambda count: [refs.pop(0) for _ in range(count)]
    stats = take(n_head)
    cot_pieces = take(n_head)
    attn_ref, p_ref, gg_ref, xn_ref = take(4)
    da_ref, dat_ref, gun_ref = take(3)
    (acc_ref,) = refs
    width = attn_ref.shape[1]
    per = cot_pieces[0].shape[0] // TILE
    for k, piece in enumerate(cot_pieces):
        for r in range(per):
            i = (lax.axis_index("head") ^ k) * per + r
            normed, scale, first, second = standardized(i, n_head, stats, attn_ref)
            p = p_ref[i]
            sg = 0.5 + 0.5 * jnp.tanh(0.5 * p)
            gate = p * sg
            gg = gg_ref[i]
            gated = (normed * gate).astype(bf16)
            grad = scale * (gg * gate - first - normed * second)
            da_ref[i] = flip(grad).astype(bf16)
            dat_ref[i] = (grad * 0.5).astype(bf16)
            gu = (gg * normed * (sg + gate * (1.0 - sg))).astype(bf16)
            gun_ref[i] = flip(gu).astype(bf16)
            add_gate, add_out = dot(gu, xn_ref[i]), dot(gated, piece[r * TILE : (r + 1) * TILE, :])
            if k + r == 0:
                acc_ref[:width] = add_gate
                acc_ref[width:] = add_out
            else:
                acc_ref[:width] += add_gate
                acc_ref[width:] += add_out


def send_parts(wg_ref, parts):
    low = len(parts)
    high, rows = parts[0].shape[0], parts[0].shape[1]
    me = lax.axis_index("dp") % low
    for k in range(low):
        for p in range(high):
            start = pl.multiple_of((p * low + (me ^ k)) * rows, 16)
            parts[k][p] = wg_ref[pl.ds(start, rows), :].astype(bf16)


def values_kernel(heads, kept, *refs):
    refs = list(refs)
    take = lambda count: [refs.pop(0) for _ in range(count)]
    held = take(2 if kept else 5)
    da_ref, d_ref, xn_ref, acc_in = take(4)
    gpv_ref = refs.pop(0)
    parts, wg_ref = refs[:-1], refs[-1]
    nb, width = da_ref.shape[0], da_ref.shape[2]
    das = [own_lanes(da_ref[i], heads) for i in range(nb)]
    queries = None if kept else [query_columns(held[1][i], held[2][i], heads) for i in range(nb)]
    acc = None
    for j in range(nb):
        if kept:
            tiles = [tile_at(held, i, j) for i in range(j, nb)]
        else:
            kx_ref, _, _, pos_ref, ss_ref = held
            tiles = [
                weights_and_slope(
                    masked(
                        dot(kx_ref[j], queries[i]), pos_ref[i - j], ss_ref[:, i * TILE : (i + 1) * TILE], j, heads
                    )
                )[0].astype(bf16)
                for i in range(j, nb)
            ]
        total = dot(jnp.concatenate(tiles, axis=1), jnp.concatenate(das[j:], axis=0))
        gv = (flip(total) * d_ref[j, :width]).astype(bf16)
        gpv_ref[j] = flip(gv).astype(bf16)
        more = dot(gv, xn_ref[j])
        acc = more if j == 0 else acc + more
    wg_ref[...] = flip(jnp.concatenate([acc_in[...], acc], axis=0))
    send_parts(wg_ref, parts)


def backward_kernel(heads, n_dp, extra, kept, *refs):
    refs = list(refs)
    take = lambda count: [refs.pop(0) for _ in range(count)]
    held = take(2 if kept else 4)
    kx_ref, kxt_ref, q_ref, v_ref, dat_ref = take(5)
    d_ref, xn_ref, gb_ref = take(3)
    gp_ref = refs.pop(0)
    parts = take(split_dp(n_dp)[1])
    acck_ref, posg_ref, acc_ref, wg_ref, small_ref = refs
    nb, width = v_ref.shape[0], v_ref.shape[2]
    factor = 1.0 / math.sqrt(HEAD_DIM)
    tiles = [(i, j) for i in reversed(range(nb)) for j in range(i + 1)]
    products, grads = {}, {}
    dq = m2 = None
    small_ref[...] = jnp.zeros_like(small_ref)
    small_ref[:, :D] = gb_ref[...]

    def add(ref, at, value, first):
        ref[at] = value if first else ref[at] + value

    for t in range(len(tiles) + 3):
        if t < len(tiles):
            i, j = tiles[t]
            if j == 0:
                backs = by_head(dat_ref[i], heads)
                queries = None if kept else query_columns(held[0][i], held[1][i], heads)
            products[t] = dot(v_ref[j], backs), None if kept else dot(kx_ref[j], queries)
        if 0 <= t - 1 < len(tiles):
            i, j = tiles[t - 1]
            back, product = products.pop(t - 1)
            if kept:
                slope = tile_at(held, i, j).astype(f32)
            else:
                start = held[3][:, i * TILE : (i + 1) * TILE]
                slope = weights_and_slope(masked(product, held[2][i - j], start, j, heads))[1]
            ds = back * slope
            grads[t - 1] = ds.astype(bf16)
            add(posg_ref, i - j, sum(ds[:, g * TILE : (g + 1) * TILE] for g in range(heads)), i == nb - 1)
        if t >= 3:
            i, j = tiles[t - 3]
            low = grads.pop(t - 3)
            if j == 0:
                times = jnp.concatenate([kx_ref[i, :, :NTB]] * heads, axis=0)
                q = jnp.concatenate([times, own_lanes(q_ref[i], heads)], axis=1)
            add(acck_ref, j, dot(low, q), i == nb - 1)
            more = dot(kxt_ref[j, NTB:], low)
            dq = more if j == 0 else dq + more
            if i == j:
                gp = jnp.concatenate([own_rows(dq, heads), flip(acck_ref[i, :, NTB:])], axis=0)
                gp = (gp * factor * d_ref[i, width:]).astype(bf16)
                gp_ref[i] = flip(gp).astype(bf16)
                more = dot(gp, xn_ref[i])
                acc_ref[...] = more if i == nb - 1 else acc_ref[...] + more
                part = acck_ref[i, :, :NTB]
                high = part.astype(bf16)
                rest = (part - high.astype(f32)).astype(bf16)
                onehot = kxt_ref[i, :NTB]
                part = dot(onehot, high) + dot(onehot, rest)
                m2 = part if i == nb - 1 else m2 + part
                g = diagonals(posg_ref[i])
                small_ref[:, D + i * TILE : D + (i + 1) * TILE] += g[:, :TILE]
                if i > 0:
                    small_ref[:, D + (i - 1) * TILE : D + i * TILE] += g[:, TILE:]
    g = diagonals(m2 + jnp.transpose(m2))[:, :NTB]
    zero = lax.broadcasted_iota(jnp.int32, (1, NTB), 1) == 0
    at = D + nb * TILE
    small_ref[:, at : at + NTB] = jnp.where(zero, 0.5 * g, g)
    step = D // n_dp
    grads = flip(acc_ref[...])
    for p in range(n_dp):
        here = jnp.concatenate(
            [small_ref[:, (p * extra + r) * 128 : (p * extra + r + 1) * 128] for r in range(extra)], axis=0
        )
        high = here.astype(bf16).astype(f32)
        block = jnp.concatenate([high, here - high, jnp.zeros((16 - 2 * extra, 128), f32)], axis=0)
        wg_ref[p * (step + 16) : p * (step + 16) + step] = grads[p * step : (p + 1) * step]
        if 2 * width > 128:
            block = jnp.concatenate([block, jnp.zeros((16, 2 * width - 128), f32)], axis=1)
        wg_ref[p * (step + 16) + step : (p + 1) * (step + 16)] = block
    send_parts(wg_ref, parts)


def input_kernel(n_head, gp_ref, gun_ref, gpv_ref, wt_ref, keep, send):
    width = gun_ref.shape[2]
    per = keep.shape[1] // TILE
    for k in range(n_head):
        device = lax.axis_index("head") ^ k
        target = (keep, send)[k % 2]
        for r in range(per):
            i = device * per + r
            rows = dot(jnp.concatenate([gun_ref[i], gpv_ref[i]], axis=1), wt_ref[: 2 * width])
            rows = rows + dot(gp_ref[i], wt_ref[2 * width : 4 * width])
            target[device // 2, r * TILE : (r + 1) * TILE] = rows.astype(bf16)


def fold_kernel(*refs):
    low = sum(len(ref.shape) == 3 for ref in refs)
    row = lax.axis_index("dp") // low
    for k, out in enumerate(refs[low:]):
        total = refs[0][row ^ k].astype(f32)
        for ref in refs[1:low]:
            total = total + ref[row ^ k].astype(f32)
        out[...] = total.astype(out.dtype)


def sum_kernel(*refs):
    total = refs[0][...]
    for ref in refs[1:-1]:
        total = total + ref[...].astype(f32)
    refs[-1][...] = total


def mix_kernel(tokens_ref, bias_ref, *refs):
    total = tokens_ref[...].astype(f32) + row_lanes(bias_ref, 0, D // 128)
    for ref in refs[:-1]:
        total = total + ref[...].astype(f32)
    refs[-1][...] = total.astype(bf16)


def finish_kernel(part, *refs):
    tokens_ref, cot_ref, mine_ref, *refs = refs[part:]
    x = tokens_ref[...].astype(f32)
    x = x - jnp.sum(x, axis=1, keepdims=True) / D
    scale = lax.rsqrt(jnp.sum(x * x, axis=1, keepdims=True) / D + norm_epsilon)
    x = x * scale
    grad = mine_ref[...]
    for ref in refs[:-1]:
        grad = grad + ref[...].astype(f32)
    mean = jnp.sum(grad, axis=1, keepdims=True) / D
    along = jnp.sum(grad * x, axis=1, keepdims=True) / D
    refs[-1][...] = cot_ref[...].astype(f32) + scale * (grad - mean - x * along)


def rows_kernel(chips, keep_ref, crossed_ref, mine_ref, *leaving):
    chip = lax.axis_index("head") // 2
    for k in range(chips):
        total = keep_ref[chip ^ k].astype(f32) + crossed_ref[chip ^ k].astype(f32)
        if k == 0:
            mine_ref[...] = total
        else:
            rows = leaving[0].shape[0]
            cuts = total.shape[0] // rows
            for c in range(cuts):
                leaving[(k - 1) * cuts + c][...] = total[c * rows : (c + 1) * rows].astype(bf16)


def collect_kernel(high, extra, *refs):
    late_blocks, (early_ref, grads_ref, message_ref) = refs[:high], refs[high:]
    rows = grads_ref.shape[0]
    total, early = late_blocks[0][...], early_ref[...]
    for k in range(1, high):
        total = total + late_blocks[k][...].astype(f32)
    grads = jnp.concatenate([total[:rows], early], axis=1)
    grads_ref[...] = grads
    squares = jnp.sum(jnp.sum(grads * grads, axis=0, keepdims=True), axis=1, keepdims=True)
    message = jnp.concatenate(
        [
            total[rows : rows + extra, :128] + total[rows + extra : rows + 2 * extra, :128],
            jnp.broadcast_to(squares, (message_ref.shape[1] - extra, 128)),
        ],
        axis=0,
    )
    for k in range(message_ref.shape[0]):
        message_ref[k] = message


def update_kernel(n_head, extra, group, heard_ref, grads_ref, *refs):
    state, outs = refs[:9], refs[9:]
    grad_proj_ref, grad_out_ref, grad_small_ref, norm_ref = outs[:4]
    n_all = heard_ref.shape[0]
    width = grad_out_ref.shape[1]
    lead, pos_rows, used = D // 128, POS // 128, (D + group) // 128
    grad_small_ref[...] = jnp.zeros_like(grad_small_ref)
    last = heard_ref.shape[1] - 1
    squares = heard_ref[0, last:, :]
    for k in range(1, n_all):
        squares = squares + heard_ref[k, last:, :]
    for p in range(n_all // n_head):
        rows = heard_ref[p * n_head, :extra, :]
        for h in range(1, n_head):
            rows = rows + heard_ref[p * n_head + h, :extra, :]
        for r in range(extra):
            at = p * extra + r
            if at < used:
                grad_small_ref[at : at + 1, :] = rows[r : r + 1]
            elif at == used:
                grad_small_ref[lead + pos_rows : lead + pos_rows + 1, :] = rows[r : r + 1]
    small = grad_small_ref[...]
    total = jnp.sum(jnp.sum(small * small, axis=0, keepdims=True), axis=1, keepdims=True) + squares[:, :1]
    norm = jnp.sqrt(total)
    norm_ref[...] = norm
    factor = jnp.minimum(1.0, clip_norm / (norm + 1e-06))

    def update(get, put, grad, rate, decay):
        for k, value in enumerate(adam_step(get(0), grad, get(1), get(2), factor, rate, decay)):
            put(k, value)

    for c in range(4):
        at = (2, 4, 0, 1)[c] * width
        grad = grads_ref[:, at : at + width]
        grad_proj_ref[:, c, :] = grad

        def put(k, value):
            outs[4 + k][:, c, :] = value

        update(lambda k: state[k][:, c, :], put, grad, rate_matrix, decay_matrix)
    grad = grads_ref[:, 3 * width : 4 * width]
    grad_out_ref[...] = grad

    def put_out(k, value):
        outs[7 + k][...] = value

    update(lambda k: state[3 + k][...], put_out, grad, rate_matrix, decay_matrix)

    def put_small(k, value):
        outs[10 + k][...] = value

    update(lambda k: state[6 + k][...], put_small, small, rate_small, 0.0)


def call(kernel, name, in_specs, outs, scratch, us, room=16, **more):
    return pl.pallas_call(
        kernel,
        out_shape=[jax.ShapeDtypeStruct(shape, dtype) for shape, dtype, _ in outs],
        in_specs=in_specs,
        out_specs=[spec for _, _, spec in outs],
        scratch_shapes=scratch,
        compiler_params=pltpu.CompilerParams(vmem_limit_bytes=min(60, room * max(1, lax.axis_size("head") // 4)) * 2**20),
        cost_estimate=pl.CostEstimate(flops=int(us * 1e9), bytes_accessed=int(us * 3e6), transcendentals=0),
        name=name,
        **more,
    )


def block(shape):
    return pl.BlockSpec((1,) + tuple(shape[1:]), lambda i: (i,) + (0,) * (len(shape) - 1))


def shards(
    tokens,
    cotangent,
    seq_start,
    time_bucket,
    proj_weight,
    out_weight,
    small_params,
    proj_mean,
    proj_square,
    out_mean,
    out_square,
    small_mean,
    small_square,
):
    n_head = lax.axis_size("head")
    n_dp = lax.axis_size("dp")
    here = tokens.shape[0]
    group = here * n_head
    nb = group // TILE
    per = here // TILE
    rows_here, _, width = proj_weight.shape
    heads = width // HEAD_DIM
    high, low = split_dp(n_dp)

    (weights,) = call(
        cast_kernel,
        "cast",
        [pl.BlockSpec(memory_space=pl.ANY)] * 2,
        [((rows_here, 5 * width), bf16, VMEM)],
        [
            pltpu.VMEM(proj_weight.shape, f32),
            pltpu.VMEM((rows_here, width), f32),
            pltpu.SemaphoreType.DMA((2,)),
        ],
        1,
    )(proj_weight, out_weight.T)
    x_chips = gather_chips(after(tokens, weights))
    starts = seq_start.reshape(1, group)
    times = time_bucket.reshape(1, group)
    small_rows = small_params.reshape(-1, 128)
    pos, oh, oht, trow = call(
        prepare_kernel,
        "prepare",
        [VMEM] * 2,
        [
            ((nb, TILE, TILE), f32, VMEM),
            ((nb, TILE, NTB), bf16, VMEM),
            ((nb, NTB, TILE), bf16, VMEM),
            ((nb, NTB, TILE), bf16, VMEM),
        ],
        [],
        2,
    )(after(times, weights), small_rows)

    items = [
        ((nb, 3 * width, TILE), bf16),
        ((nb, TILE, NTB + width), bf16),
        ((nb, NTB + width, TILE), bf16),
        ((nb, width, TILE), bf16),
        ((nb, TILE, width), bf16),
        ((nb, TILE, width), bf16),
        ((nb, width, TILE), bf16),
    ]
    w_pieces, offsets = gather_dp(weights, pos)
    cot_chips = gather_chips(after(cotangent, weights))

    x_pieces = gather_cores(tokens, x_chips)
    near = [0, 1] + list(range(2, n_head, 2))
    far = list(range(3, n_head, 2))
    xn = []
    for which in (near, far):
        xn = call(
            functools.partial(normalize_kernel, which),
            "normalize",
            [VMEM] * (len(xn) + len(which)),
            [((nb, TILE, D), bf16, VMEM)],
            [],
            0.1,
        )(*xn, *[x_pieces[k] for k in which])
    (xn,) = xn
    w_pieces[-1] = after(join(w_pieces[-1:], 6), xn)
    (wt,) = call(
        functools.partial(assemble_kernel, offsets),
        "assemble",
        [VMEM] * len(w_pieces),
        [((5 * width, D), bf16, VMEM)],
        [pltpu.VMEM((D, 5 * width), bf16)],
        0.5,
    )(*w_pieces)
    dsilu, kx, kxt, qs, q, v, vt = call(
        functools.partial(project_kernel, heads),
        "project",
        [VMEM] * 4,
        [item + (VMEM,) for item in items],
        [],
        1,
    )(xn, wt, oh, oht)

    kept = nb * (nb + 1) // 2 * heads <= KEPT_TILES

    def attend(first, last, *before):
        count = (last * (last + 1) - first * (first + 1)) // 2
        return call(
            functools.partial(attend_kernel, heads, first, last, kept),
            "attend",
            [VMEM] * (len(before) + 6),
            [((last, width, TILE), f32, VMEM)] + [((count, TILE, heads * TILE), bf16, VMEM)] * (2 * kept),
            [],
            8 if before else 0.5,
        )(*before, kx, qs, trow, vt, pos, starts)

    split = nb - nb // 4
    attn, *kept_first = attend(0, split)
    cot_chips = after_all(cot_chips, attn)
    attn, *kept_last = attend(split, nb, after(attn, *cot_chips))
    kept_weights, kept_slopes = zip(kept_first, kept_last) if kept else ((), ())
    cot_pieces = gather_cores(cotangent, cot_chips)

    column = ((nb, width, TILE), f32, VMEM)
    p_gate, gg, stat, gb = call(
        functools.partial(gate_kernel, n_head),
        "gate",
        [VMEM] * (n_head + 3),
        [column, column, ((nb, 4, TILE), f32, VMEM), ((1, D), f32, VMEM)],
        [],
        5,
    )(*cot_pieces, attn, xn, wt)

    stats = [stat] + [swap(stat, "head", k) for k in range(1, n_head)]
    chips = n_head // 2
    split_shape = ((chips, here, D), bf16, VMEM)
    keep, send = call(
        functools.partial(branch_kernel, n_head), "branch", [VMEM] * (n_head + 3), [split_shape] * 2, [], 1
    )(*stats, attn, p_gate, wt)
    crossed = swap(send, "head", 1)
    da, dat, gun, wg_sum = call(
        functools.partial(middle_kernel, n_head),
        "middle",
        [VMEM] * (2 * n_head + 4),
        [
            ((nb, TILE, width), bf16, VMEM),
            ((nb, width, TILE), bf16, VMEM),
            ((nb, TILE, width), bf16, VMEM),
            ((2 * width, D), f32, VMEM),
        ],
        [],
        6,
    )(*stats, *cot_pieces, attn, p_gate, gg, xn)
    branch, *leaving = fold_cores(keep, crossed)
    received = [swap(sent, "head", 2 * (k + 1)) for k, sent in enumerate(leaving)]
    held = kept_weights if kept else (kx, qs, trow, pos, starts)
    gpv, *early_parts = call(
        functools.partial(values_kernel, heads, kept),
        "values",
        [VMEM] * (len(held) + 4),
        [((nb, TILE, width), bf16, VMEM)] + [((high, rows_here, 3 * width), bf16, VMEM)] * low,
        [pltpu.VMEM((D, 3 * width), f32)],
        VALUES,
    )(*held, da, dsilu, xn, wg_sum)
    early_received = [swap(early_parts[k], "dp", k) for k in range(1, low)]

    length = D + group + NTB
    extra = -(-length // (128 * n_dp))
    held = kept_slopes if kept else (qs, trow, pos, starts)
    gp, *late_parts = call(
        functools.partial(backward_kernel, heads, n_dp, extra, kept),
        "backward",
        [VMEM] * (len(held) + 8),
        [((nb, TILE, 2 * width), bf16, VMEM)] + [((high, rows_here + 16, 2 * width), bf16, VMEM)] * low,
        [
            pltpu.VMEM((nb, TILE, NTB + width), f32),
            pltpu.VMEM((nb, TILE, TILE), f32),
            pltpu.VMEM((2 * width, D), f32),
            pltpu.VMEM((n_dp * (rows_here + 16), 2 * width), f32),
            pltpu.VMEM((1, extra * n_dp * 128), f32),
        ],
        BACKWARD,
        ROOM,
    )(*held, kx, kxt, q, v, dat, dsilu, xn, gb)

    tied = lax.optimization_barrier((gp, *late_parts, *early_received, *received))
    gp, late_parts = tied[0], tied[1 : 1 + low]
    early_received, received = tied[1 + low : 2 * low], tied[2 * low :]
    late_received = [swap(late_parts[k], "dp", k) for k in range(1, low)]
    keep, send = call(
        functools.partial(input_kernel, n_head),
        "input_rows",
        [VMEM] * 4,
        [((n_head // 2, here, D), bf16, VMEM)] * 2,
        [],
        4,
    )(gp, gun, gpv, wt)
    early_blocks = scatter_high(after(early_parts[0], send), early_received, 1)
    crossed = swap(send, "head", 1)
    late_blocks = scatter_high(late_parts[0], late_received, 12, send, crossed)
    (early,) = call(
        sum_kernel, "sum", [VMEM] * high, [((rows_here, 3 * width), f32, VMEM)], [], 14
    )(*early_blocks)
    mine, *leaving = fold_cores(keep, after(crossed, late_blocks[0]), 2)
    half = here // 2
    arrived = [[swap(leaving[2 * k - 2 + part], "head", 2 * k) for k in range(1, chips)] for part in range(2)]
    n_all = n_dp * n_head
    grads_shape = ((rows_here, 5 * width), f32)
    grads, message = call(
        functools.partial(collect_kernel, high, extra),
        "collect",
        [VMEM] * (high + 1),
        [grads_shape + (VMEM,), ((n_all, 4 if extra < 4 else 8, 128), f32, VMEM)],
        [],
        10,
    )(*late_blocks, early)
    message = after(message, *leaving)
    heard = lax.all_to_all(message, ("dp", "head"), 0, 0, tiled=True)
    (mixed,) = call(
        mix_kernel, "mix", [VMEM] * (2 + chips), [((here, D), bf16, VMEM)], [], 1
    )(tokens, small_rows, after(branch, message), *received)
    input_grad = None
    for part in range(2):
        rows = pl.BlockSpec((half, D), lambda i, part=part: (part, 0))
        alone = pl.BlockSpec((half, D), lambda i: (0, 0))
        before = [] if part == 0 else [input_grad]
        (input_grad,) = call(
            functools.partial(finish_kernel, part),
            "finish",
            [pl.BlockSpec(memory_space=pl.ANY)] * len(before) + [rows] * 3 + [alone] * (chips - 1),
            [((here, D), f32, rows)],
            [],
            1,
            grid=(1,),
            input_output_aliases={0: 0} if before else {},
        )(*before, tokens, cotangent, mine, *arrived[part])
    heard = after(heard, input_grad)
    state = [proj_weight, proj_mean, proj_square, out_weight.T, out_mean.T, out_square.T]
    state += [x.reshape(-1, 128) for x in (small_params, small_mean, small_square)]
    proj_shape, out_shape, small_shape = proj_weight.shape, (rows_here, width), small_rows.shape
    shapes = [proj_shape, out_shape, small_shape, (1, 1)] + [proj_shape] * 3 + [out_shape] * 3 + [small_shape] * 3
    results = call(
        functools.partial(update_kernel, n_head, extra, group),
        "update",
        [VMEM] * (2 + len(state)),
        [(shape, f32, VMEM) for shape in shapes],
        [],
        0.1,
    )(heard, grads, *state)
    grad_proj, grad_out, grad_small, grad_norm = results[:4]
    grad_out, grad_small, grad_norm = grad_out.T, grad_small.reshape(-1), grad_norm.reshape(())
    new_proj, mean_proj, square_proj = results[4:7]
    new_out, mean_out, square_out = [x.T for x in results[7:10]]
    new_small, mean_small, square_small = [x.reshape(-1) for x in results[10:13]]
    return (
        mixed,
        input_grad,
        grad_proj,
        grad_out,
        grad_small,
        grad_norm,
        new_proj,
        mean_proj,
        square_proj,
        new_out,
        mean_out,
        square_out,
        new_small,
        mean_small,
        square_small,
    )


def solution(mesh):
    in_specs = (
        P(("dp", "head"), None),
        P(("dp", "head"), None),
        P("dp"),
        P("dp"),
        P("dp", None, "head"),
        P("head", "dp"),
        P(),
        P("dp", None, "head"),
        P("dp", None, "head"),
        P("head", "dp"),
        P("head", "dp"),
        P(),
        P(),
    )
    out_specs = (
        P(("dp", "head"), None),
        P(("dp", "head"), None),
        P("dp", None, "head"),
        P("head", "dp"),
        P(),
        P(),
        P("dp", None, "head"),
        P("dp", None, "head"),
        P("dp", None, "head"),
        P("head", "dp"),
        P("head", "dp"),
        P("head", "dp"),
        P(),
        P(),
        P(),
    )
    return jax.shard_map(shards, mesh=mesh, in_specs=in_specs, out_specs=out_specs, check_vma=False)
```

```python
import functools
import math

import jax
import jax.numpy as jnp
from jax import lax
from jax.experimental import pallas as pl
from jax.experimental.pallas import tpu as pltpu
from jax.sharding import PartitionSpec as P

D = 512
HEAD_DIM = 64
HD = 512
POS = 8192
NTB = 128
STEP = 10
TILE = 256
NEG = -1e9
ROOM = 16
KEPT_TILES = 72
VALUES = 12
BACKWARD = 2

norm_epsilon = 1e-06
adam_epsilon = 1e-08
beta_one = 0.9
beta_two = 0.999
clip_norm = 1.0
rate_matrix = 0.05
rate_small = 0.3
decay_matrix = 0.1

f32 = jnp.float32
bf16 = jnp.bfloat16
VMEM = pl.BlockSpec(memory_space=pltpu.VMEM)


def adam_step(weight, grad, first, second, factor, rate, decay):
    clipped = grad * factor
    first_new = beta_one * first + (1.0 - beta_one) * clipped
    second_new = beta_two * second + (1.0 - beta_two) * clipped * clipped
    update = (
        first_new
        / (1.0 - beta_one**STEP)
        / (jnp.sqrt(second_new / (1.0 - beta_two**STEP)) + adam_epsilon)
    )
    return (weight - rate * (update + decay * weight), first_new, second_new)


def swap(x, axis, k):
    n = lax.axis_size(axis)
    return lax.ppermute(x, axis, [(i, i ^ k) for i in range(n)])


def gather_chips(x):
    return [swap(x, "head", k) for k in range(2, lax.axis_size("head"), 2)]


def gather_cores(x, others):
    pieces = [x, swap(x, "head", 1)]
    for other in others:
        pieces += [other, swap(other, "head", 1)]
    return pieces


def after_all(arrays, *others):
    arrays = tuple(arrays)
    return lax.optimization_barrier(arrays + others)[: len(arrays)]


def after(x, *others):
    return lax.optimization_barrier((x,) + others)[0]


def gather_dp(x, behind):
    n = lax.axis_size("dp")
    arrays, offsets = [x], [[0]]
    k = n // 2
    while k:
        operand = join(arrays) if len(arrays) > 1 else x
        if k == 1:
            operand = after(operand, behind)
        arrays.append(swap(operand, "dp", k))
        offsets.append([o ^ k for group in offsets for o in group])
        k //= 2
    return arrays, offsets


def join(arrays, us=0.1):
    shape = (sum(x.shape[0] for x in arrays), arrays[0].shape[1])
    return call(join_kernel, "join", [VMEM] * len(arrays), [(shape, arrays[0].dtype, VMEM)], [], us)(*arrays)[0]


def split_dp(n):
    low = 2 ** ((n.bit_length() - 1) // 2)
    return n // low, low


def scatter_high(own, received, us, *behind):
    high, rows, columns = own.shape
    low = 1 + len(received)
    mine, *leaving = call(
        fold_kernel,
        "fold",
        [VMEM] * low,
        [((rows, columns), f32, VMEM)] + [((rows, columns), bf16, VMEM)] * (high - 1),
        [],
        us,
    )(own, *received)
    leaving = after_all(leaving, *behind)
    return [mine] + [swap(leaving[k - 1], "dp", k * low) for k in reversed(range(1, high))]


def fold_cores(keep, crossed, cuts=1):
    chips, rows, columns = keep.shape
    return call(
        functools.partial(rows_kernel, chips),
        "rows",
        [VMEM] * 2,
        [((rows, columns), f32, VMEM)] + [((rows // cuts, columns), bf16, VMEM)] * (cuts * (chips - 1)),
        [],
        0.1,
    )(keep, crossed)


def dot(a, b):
    return lax.dot_general(a, b, (((1,), (0,)), ((), ())), preferred_element_type=f32)


def dot_nt(a, b):
    return lax.dot_general(a, b, (((1,), (1,)), ((), ())), preferred_element_type=f32)


def flip(a):
    return jnp.transpose(a.astype(f32))


def lanes(i):
    return pl.ds(pl.multiple_of(i * TILE, TILE), TILE)


def by_head(block, heads):
    zero = jnp.zeros((HEAD_DIM, block.shape[1]), block.dtype)
    return jnp.concatenate(
        [
            jnp.concatenate(
                [block[g * HEAD_DIM : (g + 1) * HEAD_DIM] if g == h else zero for g in range(heads)], axis=0
            )
            for h in range(heads)
        ],
        axis=1,
    )


def query_columns(qs, trow, heads):
    return jnp.concatenate([jnp.concatenate([trow] * heads, axis=1), by_head(qs, heads)], axis=0)


def own_rows(block, heads):
    return jnp.concatenate(
        [block[h * HEAD_DIM : (h + 1) * HEAD_DIM, h * TILE : (h + 1) * TILE] for h in range(heads)], axis=0
    )


def own_lanes(block, heads):
    lane = lax.broadcasted_iota(jnp.int32, block.shape, 1) // HEAD_DIM
    return jnp.concatenate([jnp.where(lane == h, block, jnp.zeros_like(block)) for h in range(heads)], axis=0)


def masked(product, bias, start, j, heads):
    key = j * TILE + lax.broadcasted_iota(jnp.int32, (TILE, TILE), 0)
    seen = key >= start
    return jnp.where(
        jnp.concatenate([seen] * heads, axis=1), product + jnp.concatenate([bias] * heads, axis=1), NEG
    )


def diagonals(x):
    rows, cols = x.shape
    z = jnp.concatenate([x, jnp.zeros((rows, cols), f32)], axis=1)
    total = z[:8]
    for q in range(1, rows // 8):
        total = total + pltpu.roll(z[8 * q : 8 * q + 8], 2 * cols - 8 * q, 1)
    g = total[0:1]
    for r in range(1, 8):
        g = g + pltpu.roll(total, 2 * cols - r, 1)[r : r + 1]
    return g


def cast_kernel(w_in, o_in, low_ref, w_ref, o_ref, sems):
    copies = [pltpu.make_async_copy(w_in, w_ref, sems.at[0]), pltpu.make_async_copy(o_in, o_ref, sems.at[1])]
    for copy in copies:
        copy.start()
    for copy in copies:
        copy.wait()
    width = o_ref.shape[1]
    for c in range(4):
        low_ref[:, c * width : (c + 1) * width] = w_ref[:, c, :].astype(bf16)
    low_ref[:, 4 * width :] = o_ref[...].astype(bf16)


def row_lanes(ref, first, count):
    return jnp.concatenate([ref[pl.ds(first + k, 1), :] for k in range(count)], axis=1)


def prepare_kernel(tb_ref, small_ref, pos_ref, oh_ref, oht_ref, trow_ref):
    nb = pos_ref.shape[0]
    step = TILE // 128

    def tile(d, _):
        first = D // 128 + d * step
        row = jnp.concatenate([row_lanes(small_ref, first, step), row_lanes(small_ref, first - step, step)], axis=1)
        pos_ref[d] = pltpu.roll(
            jnp.broadcast_to(row * 0.5, (TILE, 2 * TILE)), 0, 1, stride=1, stride_axis=0
        )[:, :TILE]
        return 0

    lax.fori_loop(0, nb, tile, 0)
    b = lax.broadcasted_iota(jnp.int32, (TILE, TILE), 0)
    a = lax.broadcasted_iota(jnp.int32, (TILE, TILE), 1)
    pos_ref[0] = jnp.where(b <= a, pos_ref[0], NEG)
    table = row_lanes(small_ref, (D + POS) // 128, NTB // 128)
    row = jnp.concatenate([table, table], axis=1)
    upper = pltpu.roll(jnp.broadcast_to(row, (NTB, 2 * NTB)), 0, 1, stride=1, stride_axis=0)[:, :NTB]
    a = lax.broadcasted_iota(jnp.int32, (NTB, NTB), 0)
    b = lax.broadcasted_iota(jnp.int32, (NTB, NTB), 1)
    upper = jnp.where(b >= a, upper, 0.0)
    square = (jnp.where(b > a, upper, jnp.transpose(upper)) * 0.5).astype(bf16)

    def block(i, _):
        onehot = (lax.broadcasted_iota(jnp.int32, (NTB, TILE), 0) == tb_ref[:, lanes(i)]).astype(f32)
        low = onehot.astype(bf16)
        oht_ref[i] = low
        oh_ref[i] = flip(onehot).astype(bf16)
        trow_ref[i] = dot(square, low).astype(bf16)
        return 0

    lax.fori_loop(0, nb, block, 0)


def join_kernel(*refs):
    at = 0
    for ref in refs[:-1]:
        refs[-1][at : at + ref.shape[0]] = ref[...]
        at += ref.shape[0]


def normalize_kernel(which, *refs):
    before = refs[: len(refs) - len(which) - 1]
    pieces, xn_ref = refs[len(before) : -1], refs[-1]
    per = pieces[0].shape[0] // TILE
    for ref in before:
        xn_ref[...] = ref[...]
    for k, piece in zip(which, pieces):
        for r in range(per):
            x = piece[r * TILE : (r + 1) * TILE, :].astype(f32)
            x = x - jnp.sum(x, axis=1, keepdims=True) / D
            x = x * lax.rsqrt(jnp.sum(x * x, axis=1, keepdims=True) / D + norm_epsilon)
            xn_ref[(lax.axis_index("head") ^ k) * per + r] = x.astype(bf16)


def assemble_kernel(offsets, *refs):
    w_pieces, (wt_ref, w_ref) = refs[:-2], refs[-2:]
    for piece, group in zip(w_pieces, offsets):
        rows = piece.shape[0] // len(group)
        for at, offset in enumerate(group):
            start = pl.multiple_of((lax.axis_index("dp") ^ offset) * rows, 16)
            w_ref[pl.ds(start, rows), :] = piece[at * rows : (at + 1) * rows, :]
    wt_ref[...] = flip(w_ref[...]).astype(bf16)


def project_kernel(heads, *refs):
    refs = list(refs)
    take = lambda count: [refs.pop(0) for _ in range(count)]
    xn_ref, wt_ref, oh_ref, oht_ref = take(4)
    d_ref, kx_ref, kxt_ref, qs_ref, q_ref, v_ref, vt_ref = refs
    width = v_ref.shape[2]

    def project(i):
        x = xn_ref[i]
        p = dot_nt(wt_ref[width : 4 * width], x)
        sg = 0.5 + 0.5 * jnp.tanh(0.5 * p)
        act = p * sg
        d_ref[i] = (sg + act * (1.0 - sg)).astype(bf16)
        vt = act[:width]
        vt_ref[i] = vt.astype(bf16)
        v_ref[i] = flip(vt).astype(bf16)
        qt = act[width : 2 * width].astype(bf16)
        kt = act[2 * width :]
        kxt_ref[i, :NTB] = oht_ref[i]
        kxt_ref[i, NTB:] = kt.astype(bf16)
        kx_ref[i, :, :NTB] = oh_ref[i]
        kx_ref[i, :, NTB:] = flip(kt).astype(bf16)
        qs = (qt.astype(f32) * (0.5 / math.sqrt(HEAD_DIM))).astype(bf16)
        qs_ref[i] = qs
        q_ref[i] = flip(qt).astype(bf16)

    for i in range(xn_ref.shape[0]):
        project(i)

def tile_at(refs, i, j):
    at = i * (i + 1) // 2 + j
    for ref in refs:
        if at < ref.shape[0]:
            return ref[at]
        at -= ref.shape[0]


def weights_and_slope(h):
    th = jnp.tanh(h)
    u = 1.0 + th
    w = h * u
    return w, u + w * (1.0 - th)


def attend_kernel(heads, first, last, kept, *refs):
    if first:
        before_ref, refs = refs[0], refs[1:]
    kx_ref, qs_ref, trow_ref, vt_ref, pos_ref, ss_ref, attn_ref = refs[:7]
    if first:
        attn_ref[:first] = before_ref[...]
    tiles = [(i, j) for i in range(first, last) for j in range(i + 1)]
    scores, weights = {}, {}
    for t in range(len(tiles) + 3):
        if t < len(tiles):
            i, j = tiles[t]
            if j == 0:
                queries = query_columns(qs_ref[i], trow_ref[i], heads)
            scores[t] = dot(kx_ref[j], queries)
        if 0 <= t - 1 < len(tiles):
            i, j = tiles[t - 1]
            h = masked(scores.pop(t - 1), pos_ref[i - j], ss_ref[:, i * TILE : (i + 1) * TILE], j, heads)
            w, slope = weights_and_slope(h)
            weights[t - 1] = w.astype(bf16)
            if kept:
                refs[7][t - 1] = weights[t - 1]
                refs[8][t - 1] = slope.astype(bf16)
        if t >= 3:
            i, j = tiles[t - 3]
            more = dot(vt_ref[j], weights.pop(t - 3))
            total = more if j == 0 else total + more
            if i == j:
                attn_ref[i] = own_rows(total, heads)


def gate_kernel(n_head, *refs):
    refs = list(refs)
    take = lambda count: [refs.pop(0) for _ in range(count)]
    cot_pieces = take(n_head)
    attn_ref, xn_ref, wt_ref = take(3)
    p_ref, gg_ref, stat_ref, gb_ref = refs
    width = attn_ref.shape[1]
    per = cot_pieces[0].shape[0] // TILE
    gb_ref[...] = jnp.sum(cot_pieces[0][...].astype(f32), axis=0, keepdims=True)
    for k, piece in enumerate(cot_pieces):
        for r in range(per):
            i = (lax.axis_index("head") ^ k) * per + r
            p = dot_nt(wt_ref[:width], xn_ref[i])
            gate = p * (0.5 + 0.5 * jnp.tanh(0.5 * p))
            gg = dot_nt(wt_ref[4 * width :], piece[r * TILE : (r + 1) * TILE, :])
            grad = gg * gate
            p_ref[i] = p
            gg_ref[i] = gg
            at = attn_ref[i]
            mean = jnp.sum(at, axis=0, keepdims=True) / width
            centred = at - mean
            stat_ref[i] = jnp.concatenate(
                [
                    mean,
                    jnp.sum(centred * centred, axis=0, keepdims=True),
                    jnp.sum(grad, axis=0, keepdims=True),
                    jnp.sum(grad * centred, axis=0, keepdims=True),
                ],
                axis=0,
            )


def standardized(i, n_head, stats, attn_ref):
    width = attn_ref.shape[1]
    st = [s[i] for s in stats]
    mean = sum(p[0:1] for p in st) / n_head
    spread = sum(p[1:2] + width * (p[0:1] - mean) * (p[0:1] - mean) for p in st)
    scale = lax.rsqrt(spread / HD + norm_epsilon)
    first = sum(p[2:3] for p in st) / HD
    second = scale * sum(p[3:4] + (p[0:1] - mean) * p[2:3] for p in st) / HD
    return (attn_ref[i] - mean) * scale, scale, first, second


def branch_kernel(n_head, *refs):
    stats, (attn_ref, p_ref, wt_ref, keep, send) = refs[:n_head], refs[n_head:]
    width = attn_ref.shape[1]
    per = keep.shape[1] // TILE
    for k in range(n_head):
        device = lax.axis_index("head") ^ k
        for r in range(per):
            i = device * per + r
            normed = standardized(i, n_head, stats, attn_ref)[0]
            p = p_ref[i]
            gated = (normed * (p * (0.5 + 0.5 * jnp.tanh(0.5 * p)))).astype(bf16)
            (keep, send)[k % 2][device // 2, r * TILE : (r + 1) * TILE] = dot(
                flip(gated).astype(bf16), wt_ref[4 * width :]
            ).astype(bf16)


def middle_kernel(n_head, *refs):
    refs = list(refs)
    take = lambda count: [refs.pop(0) for _ in range(count)]
    stats = take(n_head)
    cot_pieces = take(n_head)
    attn_ref, p_ref, gg_ref, xn_ref = take(4)
    da_ref, dat_ref, gun_ref = take(3)
    (acc_ref,) = refs
    width = attn_ref.shape[1]
    per = cot_pieces[0].shape[0] // TILE
    for k, piece in enumerate(cot_pieces):
        for r in range(per):
            i = (lax.axis_index("head") ^ k) * per + r
            normed, scale, first, second = standardized(i, n_head, stats, attn_ref)
            p = p_ref[i]
            sg = 0.5 + 0.5 * jnp.tanh(0.5 * p)
            gate = p * sg
            gg = gg_ref[i]
            gated = (normed * gate).astype(bf16)
            grad = scale * (gg * gate - first - normed * second)
            da_ref[i] = flip(grad).astype(bf16)
            dat_ref[i] = (grad * 0.5).astype(bf16)
            gu = (gg * normed * (sg + gate * (1.0 - sg))).astype(bf16)
            gun_ref[i] = flip(gu).astype(bf16)
            add_gate, add_out = dot(gu, xn_ref[i]), dot(gated, piece[r * TILE : (r + 1) * TILE, :])
            if k + r == 0:
                acc_ref[:width] = add_gate
                acc_ref[width:] = add_out
            else:
                acc_ref[:width] += add_gate
                acc_ref[width:] += add_out


def send_parts(wg_ref, parts):
    low = len(parts)
    high, rows = parts[0].shape[0], parts[0].shape[1]
    me = lax.axis_index("dp") % low
    for k in range(low):
        for p in range(high):
            start = pl.multiple_of((p * low + (me ^ k)) * rows, 16)
            parts[k][p] = wg_ref[pl.ds(start, rows), :].astype(bf16)


def values_kernel(heads, kept, *refs):
    refs = list(refs)
    take = lambda count: [refs.pop(0) for _ in range(count)]
    held = take(2 if kept else 5)
    da_ref, d_ref, xn_ref, acc_in = take(4)
    gpv_ref = refs.pop(0)
    parts, wg_ref = refs[:-1], refs[-1]
    nb, width = da_ref.shape[0], da_ref.shape[2]
    das = [own_lanes(da_ref[i], heads) for i in range(nb)]
    queries = None if kept else [query_columns(held[1][i], held[2][i], heads) for i in range(nb)]
    acc = None
    for j in range(nb):
        if kept:
            tiles = [tile_at(held, i, j) for i in range(j, nb)]
        else:
            kx_ref, _, _, pos_ref, ss_ref = held
            tiles = [
                weights_and_slope(
                    masked(
                        dot(kx_ref[j], queries[i]), pos_ref[i - j], ss_ref[:, i * TILE : (i + 1) * TILE], j, heads
                    )
                )[0].astype(bf16)
                for i in range(j, nb)
            ]
        total = dot(jnp.concatenate(tiles, axis=1), jnp.concatenate(das[j:], axis=0))
        gv = (flip(total) * d_ref[j, :width]).astype(bf16)
        gpv_ref[j] = flip(gv).astype(bf16)
        more = dot(gv, xn_ref[j])
        acc = more if j == 0 else acc + more
    wg_ref[...] = flip(jnp.concatenate([acc_in[...], acc], axis=0))
    send_parts(wg_ref, parts)


def backward_kernel(heads, n_dp, extra, kept, *refs):
    refs = list(refs)
    take = lambda count: [refs.pop(0) for _ in range(count)]
    held = take(2 if kept else 4)
    kx_ref, kxt_ref, q_ref, v_ref, dat_ref = take(5)
    d_ref, xn_ref, gb_ref = take(3)
    gp_ref = refs.pop(0)
    parts = take(split_dp(n_dp)[1])
    acck_ref, posg_ref, acc_ref, wg_ref, small_ref = refs
    nb, width = v_ref.shape[0], v_ref.shape[2]
    factor = 1.0 / math.sqrt(HEAD_DIM)
    tiles = [(i, j) for i in reversed(range(nb)) for j in range(i + 1)]
    products, grads = {}, {}
    dq = m2 = None
    small_ref[...] = jnp.zeros_like(small_ref)
    small_ref[:, :D] = gb_ref[...]

    def add(ref, at, value, first):
        ref[at] = value if first else ref[at] + value

    for t in range(len(tiles) + 3):
        if t < len(tiles):
            i, j = tiles[t]
            if j == 0:
                backs = by_head(dat_ref[i], heads)
                queries = None if kept else query_columns(held[0][i], held[1][i], heads)
            products[t] = dot(v_ref[j], backs), None if kept else dot(kx_ref[j], queries)
        if 0 <= t - 1 < len(tiles):
            i, j = tiles[t - 1]
            back, product = products.pop(t - 1)
            if kept:
                slope = tile_at(held, i, j).astype(f32)
            else:
                start = held[3][:, i * TILE : (i + 1) * TILE]
                slope = weights_and_slope(masked(product, held[2][i - j], start, j, heads))[1]
            ds = back * slope
            grads[t - 1] = ds.astype(bf16)
            add(posg_ref, i - j, sum(ds[:, g * TILE : (g + 1) * TILE] for g in range(heads)), i == nb - 1)
        if t >= 3:
            i, j = tiles[t - 3]
            low = grads.pop(t - 3)
            if j == 0:
                times = jnp.concatenate([kx_ref[i, :, :NTB]] * heads, axis=0)
                q = jnp.concatenate([times, own_lanes(q_ref[i], heads)], axis=1)
            add(acck_ref, j, dot(low, q), i == nb - 1)
            more = dot(kxt_ref[j, NTB:], low)
            dq = more if j == 0 else dq + more
            if i == j:
                gp = jnp.concatenate([own_rows(dq, heads), flip(acck_ref[i, :, NTB:])], axis=0)
                gp = (gp * factor * d_ref[i, width:]).astype(bf16)
                gp_ref[i] = flip(gp).astype(bf16)
                more = dot(gp, xn_ref[i])
                acc_ref[...] = more if i == nb - 1 else acc_ref[...] + more
                part = acck_ref[i, :, :NTB]
                high = part.astype(bf16)
                rest = (part - high.astype(f32)).astype(bf16)
                onehot = kxt_ref[i, :NTB]
                part = dot(onehot, high) + dot(onehot, rest)
                m2 = part if i == nb - 1 else m2 + part
                g = diagonals(posg_ref[i])
                small_ref[:, D + i * TILE : D + (i + 1) * TILE] += g[:, :TILE]
                if i > 0:
                    small_ref[:, D + (i - 1) * TILE : D + i * TILE] += g[:, TILE:]
    g = diagonals(m2 + jnp.transpose(m2))[:, :NTB]
    zero = lax.broadcasted_iota(jnp.int32, (1, NTB), 1) == 0
    at = D + nb * TILE
    small_ref[:, at : at + NTB] = jnp.where(zero, 0.5 * g, g)
    step = D // n_dp
    grads = flip(acc_ref[...])
    for p in range(n_dp):
        here = jnp.concatenate(
            [small_ref[:, (p * extra + r) * 128 : (p * extra + r + 1) * 128] for r in range(extra)], axis=0
        )
        high = here.astype(bf16).astype(f32)
        block = jnp.concatenate([high, here - high, jnp.zeros((16 - 2 * extra, 128), f32)], axis=0)
        wg_ref[p * (step + 16) : p * (step + 16) + step] = grads[p * step : (p + 1) * step]
        if 2 * width > 128:
            block = jnp.concatenate([block, jnp.zeros((16, 2 * width - 128), f32)], axis=1)
        wg_ref[p * (step + 16) + step : (p + 1) * (step + 16)] = block
    send_parts(wg_ref, parts)


def input_kernel(n_head, gp_ref, gun_ref, gpv_ref, wt_ref, keep, send):
    width = gun_ref.shape[2]
    per = keep.shape[1] // TILE
    for k in range(n_head):
        device = lax.axis_index("head") ^ k
        target = (keep, send)[k % 2]
        for r in range(per):
            i = device * per + r
            rows = dot(jnp.concatenate([gun_ref[i], gpv_ref[i]], axis=1), wt_ref[: 2 * width])
            rows = rows + dot(gp_ref[i], wt_ref[2 * width : 4 * width])
            target[device // 2, r * TILE : (r + 1) * TILE] = rows.astype(bf16)


def fold_kernel(*refs):
    low = sum(len(ref.shape) == 3 for ref in refs)
    row = lax.axis_index("dp") // low
    for k, out in enumerate(refs[low:]):
        total = refs[0][row ^ k].astype(f32)
        for ref in refs[1:low]:
            total = total + ref[row ^ k].astype(f32)
        out[...] = total.astype(out.dtype)


def sum_kernel(*refs):
    total = refs[0][...]
    for ref in refs[1:-1]:
        total = total + ref[...].astype(f32)
    refs[-1][...] = total


def mix_kernel(tokens_ref, bias_ref, *refs):
    total = tokens_ref[...].astype(f32) + row_lanes(bias_ref, 0, D // 128)
    for ref in refs[:-1]:
        total = total + ref[...].astype(f32)
    refs[-1][...] = total.astype(bf16)


def finish_kernel(part, *refs):
    tokens_ref, cot_ref, mine_ref, *refs = refs[part:]
    x = tokens_ref[...].astype(f32)
    x = x - jnp.sum(x, axis=1, keepdims=True) / D
    scale = lax.rsqrt(jnp.sum(x * x, axis=1, keepdims=True) / D + norm_epsilon)
    x = x * scale
    grad = mine_ref[...]
    for ref in refs[:-1]:
        grad = grad + ref[...].astype(f32)
    mean = jnp.sum(grad, axis=1, keepdims=True) / D
    along = jnp.sum(grad * x, axis=1, keepdims=True) / D
    refs[-1][...] = cot_ref[...].astype(f32) + scale * (grad - mean - x * along)


def rows_kernel(chips, keep_ref, crossed_ref, mine_ref, *leaving):
    chip = lax.axis_index("head") // 2
    for k in range(chips):
        total = keep_ref[chip ^ k].astype(f32) + crossed_ref[chip ^ k].astype(f32)
        if k == 0:
            mine_ref[...] = total
        else:
            rows = leaving[0].shape[0]
            cuts = total.shape[0] // rows
            for c in range(cuts):
                leaving[(k - 1) * cuts + c][...] = total[c * rows : (c + 1) * rows].astype(bf16)


def collect_kernel(high, extra, *refs):
    late_blocks, (early_ref, grads_ref, message_ref) = refs[:high], refs[high:]
    rows = grads_ref.shape[0]
    total, early = late_blocks[0][...], early_ref[...]
    for k in range(1, high):
        total = total + late_blocks[k][...].astype(f32)
    grads = jnp.concatenate([total[:rows], early], axis=1)
    grads_ref[...] = grads
    squares = jnp.sum(jnp.sum(grads * grads, axis=0, keepdims=True), axis=1, keepdims=True)
    message = jnp.concatenate(
        [
            total[rows : rows + extra, :128] + total[rows + extra : rows + 2 * extra, :128],
            jnp.broadcast_to(squares, (message_ref.shape[1] - extra, 128)),
        ],
        axis=0,
    )
    for k in range(message_ref.shape[0]):
        message_ref[k] = message


def update_kernel(n_head, extra, group, heard_ref, grads_ref, *refs):
    state, outs = refs[:9], refs[9:]
    grad_proj_ref, grad_out_ref, grad_small_ref, norm_ref = outs[:4]
    n_all = heard_ref.shape[0]
    width = grad_out_ref.shape[1]
    lead, pos_rows, used = D // 128, POS // 128, (D + group) // 128
    grad_small_ref[...] = jnp.zeros_like(grad_small_ref)
    last = heard_ref.shape[1] - 1
    squares = heard_ref[0, last:, :]
    for k in range(1, n_all):
        squares = squares + heard_ref[k, last:, :]
    for p in range(n_all // n_head):
        rows = heard_ref[p * n_head, :extra, :]
        for h in range(1, n_head):
            rows = rows + heard_ref[p * n_head + h, :extra, :]
        for r in range(extra):
            at = p * extra + r
            if at < used:
                grad_small_ref[at : at + 1, :] = rows[r : r + 1]
            elif at == used:
                grad_small_ref[lead + pos_rows : lead + pos_rows + 1, :] = rows[r : r + 1]
    small = grad_small_ref[...]
    total = jnp.sum(jnp.sum(small * small, axis=0, keepdims=True), axis=1, keepdims=True) + squares[:, :1]
    norm = jnp.sqrt(total)
    norm_ref[...] = norm
    factor = jnp.minimum(1.0, clip_norm / (norm + 1e-06))

    def update(get, put, grad, rate, decay):
        for k, value in enumerate(adam_step(get(0), grad, get(1), get(2), factor, rate, decay)):
            put(k, value)

    for c in range(4):
        at = (2, 4, 0, 1)[c] * width
        grad = grads_ref[:, at : at + width]
        grad_proj_ref[:, c, :] = grad

        def put(k, value):
            outs[4 + k][:, c, :] = value

        update(lambda k: state[k][:, c, :], put, grad, rate_matrix, decay_matrix)
    grad = grads_ref[:, 3 * width : 4 * width]
    grad_out_ref[...] = grad

    def put_out(k, value):
        outs[7 + k][...] = value

    update(lambda k: state[3 + k][...], put_out, grad, rate_matrix, decay_matrix)

    def put_small(k, value):
        outs[10 + k][...] = value

    update(lambda k: state[6 + k][...], put_small, small, rate_small, 0.0)


def call(kernel, name, in_specs, outs, scratch, us, room=16, **more):
    return pl.pallas_call(
        kernel,
        out_shape=[jax.ShapeDtypeStruct(shape, dtype) for shape, dtype, _ in outs],
        in_specs=in_specs,
        out_specs=[spec for _, _, spec in outs],
        scratch_shapes=scratch,
        compiler_params=pltpu.CompilerParams(vmem_limit_bytes=min(60, room * max(1, lax.axis_size("head") // 4)) * 2**20),
        cost_estimate=pl.CostEstimate(flops=int(us * 1e9), bytes_accessed=int(us * 3e6), transcendentals=0),
        name=name,
        **more,
    )


def block(shape):
    return pl.BlockSpec((1,) + tuple(shape[1:]), lambda i: (i,) + (0,) * (len(shape) - 1))


def shards(
    tokens,
    cotangent,
    seq_start,
    time_bucket,
    proj_weight,
    out_weight,
    small_params,
    proj_mean,
    proj_square,
    out_mean,
    out_square,
    small_mean,
    small_square,
):
    n_head = lax.axis_size("head")
    n_dp = lax.axis_size("dp")
    here = tokens.shape[0]
    group = here * n_head
    nb = group // TILE
    per = here // TILE
    rows_here, _, width = proj_weight.shape
    heads = width // HEAD_DIM
    high, low = split_dp(n_dp)

    (weights,) = call(
        cast_kernel,
        "cast",
        [pl.BlockSpec(memory_space=pl.ANY)] * 2,
        [((rows_here, 5 * width), bf16, VMEM)],
        [
            pltpu.VMEM(proj_weight.shape, f32),
            pltpu.VMEM((rows_here, width), f32),
            pltpu.SemaphoreType.DMA((2,)),
        ],
        1,
    )(proj_weight, out_weight.T)
    x_chips = gather_chips(after(tokens, weights))
    starts = seq_start.reshape(1, group)
    times = time_bucket.reshape(1, group)
    small_rows = small_params.reshape(-1, 128)
    pos, oh, oht, trow = call(
        prepare_kernel,
        "prepare",
        [VMEM] * 2,
        [
            ((nb, TILE, TILE), f32, VMEM),
            ((nb, TILE, NTB), bf16, VMEM),
            ((nb, NTB, TILE), bf16, VMEM),
            ((nb, NTB, TILE), bf16, VMEM),
        ],
        [],
        2,
    )(after(times, weights), small_rows)

    items = [
        ((nb, 3 * width, TILE), bf16),
        ((nb, TILE, NTB + width), bf16),
        ((nb, NTB + width, TILE), bf16),
        ((nb, width, TILE), bf16),
        ((nb, TILE, width), bf16),
        ((nb, TILE, width), bf16),
        ((nb, width, TILE), bf16),
    ]
    w_pieces, offsets = gather_dp(weights, pos)
    cot_chips = gather_chips(after(cotangent, weights))

    x_pieces = gather_cores(tokens, x_chips)
    near = [0, 1] + list(range(2, n_head, 2))
    far = list(range(3, n_head, 2))
    xn = []
    for which in (near, far):
        xn = call(
            functools.partial(normalize_kernel, which),
            "normalize",
            [VMEM] * (len(xn) + len(which)),
            [((nb, TILE, D), bf16, VMEM)],
            [],
            0.1,
        )(*xn, *[x_pieces[k] for k in which])
    (xn,) = xn
    w_pieces[-1] = after(join(w_pieces[-1:], 6), xn)
    (wt,) = call(
        functools.partial(assemble_kernel, offsets),
        "assemble",
        [VMEM] * len(w_pieces),
        [((5 * width, D), bf16, VMEM)],
        [pltpu.VMEM((D, 5 * width), bf16)],
        0.5,
    )(*w_pieces)
    dsilu, kx, kxt, qs, q, v, vt = call(
        functools.partial(project_kernel, heads),
        "project",
        [VMEM] * 4,
        [item + (VMEM,) for item in items],
        [],
        1,
    )(xn, wt, oh, oht)

    kept = nb * (nb + 1) // 2 * heads <= KEPT_TILES

    def attend(first, last, *before):
        count = (last * (last + 1) - first * (first + 1)) // 2
        return call(
            functools.partial(attend_kernel, heads, first, last, kept),
            "attend",
            [VMEM] * (len(before) + 6),
            [((last, width, TILE), f32, VMEM)] + [((count, TILE, heads * TILE), bf16, VMEM)] * (2 * kept),
            [],
            8 if before else 0.5,
        )(*before, kx, qs, trow, vt, pos, starts)

    split = nb - nb // 8
    attn, *kept_first = attend(0, split)
    cot_chips = after_all(cot_chips, attn)
    attn, *kept_last = attend(split, nb, after(attn, *cot_chips))
    kept_weights, kept_slopes = zip(kept_first, kept_last) if kept else ((), ())
    cot_pieces = gather_cores(cotangent, cot_chips)

    column = ((nb, width, TILE), f32, VMEM)
    p_gate, gg, stat, gb = call(
        functools.partial(gate_kernel, n_head),
        "gate",
        [VMEM] * (n_head + 3),
        [column, column, ((nb, 4, TILE), f32, VMEM), ((1, D), f32, VMEM)],
        [],
        5,
    )(*cot_pieces, attn, xn, wt)

    stats = [stat] + [swap(stat, "head", k) for k in range(1, n_head)]
    chips = n_head // 2
    split_shape = ((chips, here, D), bf16, VMEM)
    keep, send = call(
        functools.partial(branch_kernel, n_head), "branch", [VMEM] * (n_head + 3), [split_shape] * 2, [], 1
    )(*stats, attn, p_gate, wt)
    crossed = swap(send, "head", 1)
    da, dat, gun, wg_sum = call(
        functools.partial(middle_kernel, n_head),
        "middle",
        [VMEM] * (2 * n_head + 4),
        [
            ((nb, TILE, width), bf16, VMEM),
            ((nb, width, TILE), bf16, VMEM),
            ((nb, TILE, width), bf16, VMEM),
            ((2 * width, D), f32, VMEM),
        ],
        [],
        6,
    )(*stats, *cot_pieces, attn, p_gate, gg, xn)
    branch, *leaving = fold_cores(keep, crossed)
    received = [swap(sent, "head", 2 * (k + 1)) for k, sent in enumerate(leaving)]
    held = kept_weights if kept else (kx, qs, trow, pos, starts)
    gpv, *early_parts = call(
        functools.partial(values_kernel, heads, kept),
        "values",
        [VMEM] * (len(held) + 4),
        [((nb, TILE, width), bf16, VMEM)] + [((high, rows_here, 3 * width), bf16, VMEM)] * low,
        [pltpu.VMEM((D, 3 * width), f32)],
        VALUES,
    )(*held, da, dsilu, xn, wg_sum)
    early_received = [swap(early_parts[k], "dp", k) for k in range(1, low)]

    length = D + group + NTB
    extra = -(-length // (128 * n_dp))
    held = kept_slopes if kept else (qs, trow, pos, starts)
    gp, *late_parts = call(
        functools.partial(backward_kernel, heads, n_dp, extra, kept),
        "backward",
        [VMEM] * (len(held) + 8),
        [((nb, TILE, 2 * width), bf16, VMEM)] + [((high, rows_here + 16, 2 * width), bf16, VMEM)] * low,
        [
            pltpu.VMEM((nb, TILE, NTB + width), f32),
            pltpu.VMEM((nb, TILE, TILE), f32),
            pltpu.VMEM((2 * width, D), f32),
            pltpu.VMEM((n_dp * (rows_here + 16), 2 * width), f32),
            pltpu.VMEM((1, extra * n_dp * 128), f32),
        ],
        BACKWARD,
        ROOM,
    )(*held, kx, kxt, q, v, dat, dsilu, xn, gb)

    tied = lax.optimization_barrier((gp, *late_parts, *early_received, *received))
    gp, late_parts = tied[0], tied[1 : 1 + low]
    early_received, received = tied[1 + low : 2 * low], tied[2 * low :]
    late_received = [swap(late_parts[k], "dp", k) for k in range(1, low)]
    keep, send = call(
        functools.partial(input_kernel, n_head),
        "input_rows",
        [VMEM] * 4,
        [((n_head // 2, here, D), bf16, VMEM)] * 2,
        [],
        4,
    )(gp, gun, gpv, wt)
    early_blocks = scatter_high(after(early_parts[0], send), early_received, 1)
    crossed = swap(send, "head", 1)
    late_blocks = scatter_high(late_parts[0], late_received, 12, send, crossed)
    (early,) = call(
        sum_kernel, "sum", [VMEM] * high, [((rows_here, 3 * width), f32, VMEM)], [], 14
    )(*early_blocks)
    mine, *leaving = fold_cores(keep, after(crossed, late_blocks[0]), 2)
    half = here // 2
    arrived = [[swap(leaving[2 * k - 2 + part], "head", 2 * k) for k in range(1, chips)] for part in range(2)]
    n_all = n_dp * n_head
    grads_shape = ((rows_here, 5 * width), f32)
    grads, message = call(
        functools.partial(collect_kernel, high, extra),
        "collect",
        [VMEM] * (high + 1),
        [grads_shape + (VMEM,), ((n_all, 4 if extra < 4 else 8, 128), f32, VMEM)],
        [],
        10,
    )(*late_blocks, early)
    message = after(message, *leaving)
    heard = lax.all_to_all(message, ("dp", "head"), 0, 0, tiled=True)
    (mixed,) = call(
        mix_kernel, "mix", [VMEM] * (2 + chips), [((here, D), bf16, VMEM)], [], 1
    )(tokens, small_rows, after(branch, message), *received)
    input_grad = None
    for part in range(2):
        rows = pl.BlockSpec((half, D), lambda i, part=part: (part, 0))
        alone = pl.BlockSpec((half, D), lambda i: (0, 0))
        before = [] if part == 0 else [input_grad]
        (input_grad,) = call(
            functools.partial(finish_kernel, part),
            "finish",
            [pl.BlockSpec(memory_space=pl.ANY)] * len(before) + [rows] * 3 + [alone] * (chips - 1),
            [((here, D), f32, rows)],
            [],
            1,
            grid=(1,),
            input_output_aliases={0: 0} if before else {},
        )(*before, tokens, cotangent, mine, *arrived[part])
    heard = after(heard, input_grad)
    state = [proj_weight, proj_mean, proj_square, out_weight.T, out_mean.T, out_square.T]
    state += [x.reshape(-1, 128) for x in (small_params, small_mean, small_square)]
    proj_shape, out_shape, small_shape = proj_weight.shape, (rows_here, width), small_rows.shape
    shapes = [proj_shape, out_shape, small_shape, (1, 1)] + [proj_shape] * 3 + [out_shape] * 3 + [small_shape] * 3
    results = call(
        functools.partial(update_kernel, n_head, extra, group),
        "update",
        [VMEM] * (2 + len(state)),
        [(shape, f32, VMEM) for shape in shapes],
        [],
        0.1,
    )(heard, grads, *state)
    grad_proj, grad_out, grad_small, grad_norm = results[:4]
    grad_out, grad_small, grad_norm = grad_out.T, grad_small.reshape(-1), grad_norm.reshape(())
    new_proj, mean_proj, square_proj = results[4:7]
    new_out, mean_out, square_out = [x.T for x in results[7:10]]
    new_small, mean_small, square_small = [x.reshape(-1) for x in results[10:13]]
    return (
        mixed,
        input_grad,
        grad_proj,
        grad_out,
        grad_small,
        grad_norm,
        new_proj,
        mean_proj,
        square_proj,
        new_out,
        mean_out,
        square_out,
        new_small,
        mean_small,
        square_small,
    )


def solution(mesh):
    in_specs = (
        P(("dp", "head"), None),
        P(("dp", "head"), None),
        P("dp"),
        P("dp"),
        P("dp", None, "head"),
        P("head", "dp"),
        P(),
        P("dp", None, "head"),
        P("dp", None, "head"),
        P("head", "dp"),
        P("head", "dp"),
        P(),
        P(),
    )
    out_specs = (
        P(("dp", "head"), None),
        P(("dp", "head"), None),
        P("dp", None, "head"),
        P("head", "dp"),
        P(),
        P(),
        P("dp", None, "head"),
        P("dp", None, "head"),
        P("dp", None, "head"),
        P("head", "dp"),
        P("head", "dp"),
        P("head", "dp"),
        P(),
        P(),
        P(),
    )
    return jax.shard_map(shards, mesh=mesh, in_specs=in_specs, out_specs=out_specs, check_vma=False)
```

```python
import functools
import math

import jax
import jax.numpy as jnp
from jax import lax
from jax.experimental import pallas as pl
from jax.experimental.pallas import tpu as pltpu
from jax.sharding import PartitionSpec as P

D = 512
HEAD_DIM = 64
HD = 512
POS = 8192
NTB = 128
STEP = 10
TILE = 256
NEG = -1e9
ROOM = 16
KEPT_TILES = 72
VALUES = 12
BACKWARD = 2

norm_epsilon = 1e-06
adam_epsilon = 1e-08
beta_one = 0.9
beta_two = 0.999
clip_norm = 1.0
rate_matrix = 0.05
rate_small = 0.3
decay_matrix = 0.1

f32 = jnp.float32
bf16 = jnp.bfloat16
VMEM = pl.BlockSpec(memory_space=pltpu.VMEM)


def adam_step(weight, grad, first, second, factor, rate, decay):
    clipped = grad * factor
    first_new = beta_one * first + (1.0 - beta_one) * clipped
    second_new = beta_two * second + (1.0 - beta_two) * clipped * clipped
    update = (
        first_new
        / (1.0 - beta_one**STEP)
        / (jnp.sqrt(second_new / (1.0 - beta_two**STEP)) + adam_epsilon)
    )
    return (weight - rate * (update + decay * weight), first_new, second_new)


def swap(x, axis, k):
    n = lax.axis_size(axis)
    return lax.ppermute(x, axis, [(i, i ^ k) for i in range(n)])


def gather_chips(x):
    return [swap(x, "head", k) for k in range(2, lax.axis_size("head"), 2)]


def gather_cores(x, others):
    pieces = [x, swap(x, "head", 1)]
    for other in others:
        pieces += [other, swap(other, "head", 1)]
    return pieces


def after_all(arrays, *others):
    arrays = tuple(arrays)
    return lax.optimization_barrier(arrays + others)[: len(arrays)]


def after(x, *others):
    return lax.optimization_barrier((x,) + others)[0]


def gather_dp(x, behind):
    n = lax.axis_size("dp")
    arrays, offsets = [x], [[0]]
    k = n // 2
    while k:
        operand = join(arrays) if len(arrays) > 1 else x
        if k == 1:
            operand = after(operand, behind)
        arrays.append(swap(operand, "dp", k))
        offsets.append([o ^ k for group in offsets for o in group])
        k //= 2
    return arrays, offsets


def join(arrays, us=0.1):
    shape = (sum(x.shape[0] for x in arrays), arrays[0].shape[1])
    return call(join_kernel, "join", [VMEM] * len(arrays), [(shape, arrays[0].dtype, VMEM)], [], us)(*arrays)[0]


def split_dp(n):
    low = 2 ** ((n.bit_length() - 1) // 2)
    return n // low, low


def scatter_high(own, received, us, *behind):
    high, rows, columns = own.shape
    low = 1 + len(received)
    mine, *leaving = call(
        fold_kernel,
        "fold",
        [VMEM] * low,
        [((rows, columns), f32, VMEM)] + [((rows, columns), bf16, VMEM)] * (high - 1),
        [],
        us,
    )(own, *received)
    leaving = after_all(leaving, *behind)
    return [mine] + [swap(leaving[k - 1], "dp", k * low) for k in reversed(range(1, high))]


def fold_cores(keep, crossed, cuts=1):
    chips, rows, columns = keep.shape
    return call(
        functools.partial(rows_kernel, chips),
        "rows",
        [VMEM] * 2,
        [((rows, columns), f32, VMEM)] + [((rows // cuts, columns), bf16, VMEM)] * (cuts * (chips - 1)),
        [],
        0.1,
    )(keep, crossed)


def dot(a, b):
    return lax.dot_general(a, b, (((1,), (0,)), ((), ())), preferred_element_type=f32)


def dot_nt(a, b):
    return lax.dot_general(a, b, (((1,), (1,)), ((), ())), preferred_element_type=f32)


def flip(a):
    return jnp.transpose(a.astype(f32))


def lanes(i):
    return pl.ds(pl.multiple_of(i * TILE, TILE), TILE)


def by_head(block, heads):
    zero = jnp.zeros((HEAD_DIM, block.shape[1]), block.dtype)
    return jnp.concatenate(
        [
            jnp.concatenate(
                [block[g * HEAD_DIM : (g + 1) * HEAD_DIM] if g == h else zero for g in range(heads)], axis=0
            )
            for h in range(heads)
        ],
        axis=1,
    )


def query_columns(qs, trow, heads):
    return jnp.concatenate([jnp.concatenate([trow] * heads, axis=1), by_head(qs, heads)], axis=0)


def own_rows(block, heads):
    return jnp.concatenate(
        [block[h * HEAD_DIM : (h + 1) * HEAD_DIM, h * TILE : (h + 1) * TILE] for h in range(heads)], axis=0
    )


def own_lanes(block, heads):
    lane = lax.broadcasted_iota(jnp.int32, block.shape, 1) // HEAD_DIM
    return jnp.concatenate([jnp.where(lane == h, block, jnp.zeros_like(block)) for h in range(heads)], axis=0)


def masked(product, bias, start, j, heads):
    key = j * TILE + lax.broadcasted_iota(jnp.int32, (TILE, TILE), 0)
    seen = key >= start
    return jnp.where(
        jnp.concatenate([seen] * heads, axis=1), product + jnp.concatenate([bias] * heads, axis=1), NEG
    )


def diagonals(x):
    rows, cols = x.shape
    z = jnp.concatenate([x, jnp.zeros((rows, cols), f32)], axis=1)
    total = z[:8]
    for q in range(1, rows // 8):
        total = total + pltpu.roll(z[8 * q : 8 * q + 8], 2 * cols - 8 * q, 1)
    g = total[0:1]
    for r in range(1, 8):
        g = g + pltpu.roll(total, 2 * cols - r, 1)[r : r + 1]
    return g


def cast_kernel(w_in, o_in, low_ref, w_ref, o_ref, sems):
    copies = [pltpu.make_async_copy(w_in, w_ref, sems.at[0]), pltpu.make_async_copy(o_in, o_ref, sems.at[1])]
    for copy in copies:
        copy.start()
    for copy in copies:
        copy.wait()
    width = o_ref.shape[1]
    for c in range(4):
        low_ref[:, c * width : (c + 1) * width] = w_ref[:, c, :].astype(bf16)
    low_ref[:, 4 * width :] = o_ref[...].astype(bf16)


def row_lanes(ref, first, count):
    return jnp.concatenate([ref[pl.ds(first + k, 1), :] for k in range(count)], axis=1)


def prepare_kernel(tb_ref, small_ref, pos_ref, oh_ref, oht_ref, trow_ref):
    nb = pos_ref.shape[0]
    step = TILE // 128

    def tile(d, _):
        first = D // 128 + d * step
        row = jnp.concatenate([row_lanes(small_ref, first, step), row_lanes(small_ref, first - step, step)], axis=1)
        pos_ref[d] = pltpu.roll(
            jnp.broadcast_to(row * 0.5, (TILE, 2 * TILE)), 0, 1, stride=1, stride_axis=0
        )[:, :TILE]
        return 0

    lax.fori_loop(0, nb, tile, 0)
    b = lax.broadcasted_iota(jnp.int32, (TILE, TILE), 0)
    a = lax.broadcasted_iota(jnp.int32, (TILE, TILE), 1)
    pos_ref[0] = jnp.where(b <= a, pos_ref[0], NEG)
    table = row_lanes(small_ref, (D + POS) // 128, NTB // 128)
    row = jnp.concatenate([table, table], axis=1)
    upper = pltpu.roll(jnp.broadcast_to(row, (NTB, 2 * NTB)), 0, 1, stride=1, stride_axis=0)[:, :NTB]
    a = lax.broadcasted_iota(jnp.int32, (NTB, NTB), 0)
    b = lax.broadcasted_iota(jnp.int32, (NTB, NTB), 1)
    upper = jnp.where(b >= a, upper, 0.0)
    square = (jnp.where(b > a, upper, jnp.transpose(upper)) * 0.5).astype(bf16)

    def block(i, _):
        onehot = (lax.broadcasted_iota(jnp.int32, (NTB, TILE), 0) == tb_ref[:, lanes(i)]).astype(f32)
        low = onehot.astype(bf16)
        oht_ref[i] = low
        oh_ref[i] = flip(onehot).astype(bf16)
        trow_ref[i] = dot(square, low).astype(bf16)
        return 0

    lax.fori_loop(0, nb, block, 0)


def join_kernel(*refs):
    at = 0
    for ref in refs[:-1]:
        refs[-1][at : at + ref.shape[0]] = ref[...]
        at += ref.shape[0]


def normalize_kernel(which, *refs):
    before = refs[: len(refs) - len(which) - 1]
    pieces, xn_ref = refs[len(before) : -1], refs[-1]
    per = pieces[0].shape[0] // TILE
    for ref in before:
        xn_ref[...] = ref[...]
    for k, piece in zip(which, pieces):
        for r in range(per):
            x = piece[r * TILE : (r + 1) * TILE, :].astype(f32)
            x = x - jnp.sum(x, axis=1, keepdims=True) / D
            x = x * lax.rsqrt(jnp.sum(x * x, axis=1, keepdims=True) / D + norm_epsilon)
            xn_ref[(lax.axis_index("head") ^ k) * per + r] = x.astype(bf16)


def assemble_kernel(offsets, *refs):
    w_pieces, (wt_ref, w_ref) = refs[:-2], refs[-2:]
    for piece, group in zip(w_pieces, offsets):
        rows = piece.shape[0] // len(group)
        for at, offset in enumerate(group):
            start = pl.multiple_of((lax.axis_index("dp") ^ offset) * rows, 16)
            w_ref[pl.ds(start, rows), :] = piece[at * rows : (at + 1) * rows, :]
    wt_ref[...] = flip(w_ref[...]).astype(bf16)


def project_kernel(heads, *refs):
    refs = list(refs)
    take = lambda count: [refs.pop(0) for _ in range(count)]
    xn_ref, wt_ref, oh_ref, oht_ref = take(4)
    d_ref, kx_ref, kxt_ref, qs_ref, q_ref, v_ref, vt_ref = refs
    width = v_ref.shape[2]

    def project(i):
        x = xn_ref[i]
        p = dot_nt(wt_ref[width : 4 * width], x)
        sg = 0.5 + 0.5 * jnp.tanh(0.5 * p)
        act = p * sg
        d_ref[i] = (sg + act * (1.0 - sg)).astype(bf16)
        vt = act[:width]
        vt_ref[i] = vt.astype(bf16)
        v_ref[i] = flip(vt).astype(bf16)
        qt = act[width : 2 * width].astype(bf16)
        kt = act[2 * width :]
        kxt_ref[i, :NTB] = oht_ref[i]
        kxt_ref[i, NTB:] = kt.astype(bf16)
        kx_ref[i, :, :NTB] = oh_ref[i]
        kx_ref[i, :, NTB:] = flip(kt).astype(bf16)
        qs = (qt.astype(f32) * (0.5 / math.sqrt(HEAD_DIM))).astype(bf16)
        qs_ref[i] = qs
        q_ref[i] = flip(qt).astype(bf16)

    for i in range(xn_ref.shape[0]):
        project(i)

def tile_at(refs, i, j):
    at = i * (i + 1) // 2 + j
    for ref in refs:
        if at < ref.shape[0]:
            return ref[at]
        at -= ref.shape[0]


def weights_and_slope(h):
    th = jnp.tanh(h)
    u = 1.0 + th
    w = h * u
    return w, u + w * (1.0 - th)


def attend_kernel(heads, first, last, kept, *refs):
    if first:
        before_ref, refs = refs[0], refs[1:]
    kx_ref, qs_ref, trow_ref, vt_ref, pos_ref, ss_ref, attn_ref = refs[:7]
    if first:
        attn_ref[:first] = before_ref[...]
    tiles = [(i, j) for i in range(first, last) for j in range(i + 1)]
    scores, weights = {}, {}
    for t in range(len(tiles) + 3):
        if t < len(tiles):
            i, j = tiles[t]
            if j == 0:
                queries = query_columns(qs_ref[i], trow_ref[i], heads)
            scores[t] = dot(kx_ref[j], queries)
        if 0 <= t - 1 < len(tiles):
            i, j = tiles[t - 1]
            h = masked(scores.pop(t - 1), pos_ref[i - j], ss_ref[:, i * TILE : (i + 1) * TILE], j, heads)
            w, slope = weights_and_slope(h)
            weights[t - 1] = w.astype(bf16)
            if kept:
                refs[7][t - 1] = weights[t - 1]
                refs[8][t - 1] = slope.astype(bf16)
        if t >= 3:
            i, j = tiles[t - 3]
            more = dot(vt_ref[j], weights.pop(t - 3))
            total = more if j == 0 else total + more
            if i == j:
                attn_ref[i] = own_rows(total, heads)


def gate_kernel(n_head, *refs):
    refs = list(refs)
    take = lambda count: [refs.pop(0) for _ in range(count)]
    cot_pieces = take(n_head)
    attn_ref, xn_ref, wt_ref = take(3)
    p_ref, gg_ref, stat_ref, gb_ref = refs
    width = attn_ref.shape[1]
    per = cot_pieces[0].shape[0] // TILE
    gb_ref[...] = jnp.sum(cot_pieces[0][...].astype(f32), axis=0, keepdims=True)
    for k, piece in enumerate(cot_pieces):
        for r in range(per):
            i = (lax.axis_index("head") ^ k) * per + r
            p = dot_nt(wt_ref[:width], xn_ref[i])
            gate = p * (0.5 + 0.5 * jnp.tanh(0.5 * p))
            gg = dot_nt(wt_ref[4 * width :], piece[r * TILE : (r + 1) * TILE, :])
            grad = gg * gate
            p_ref[i] = p
            gg_ref[i] = gg
            at = attn_ref[i]
            mean = jnp.sum(at, axis=0, keepdims=True) / width
            centred = at - mean
            stat_ref[i] = jnp.concatenate(
                [
                    mean,
                    jnp.sum(centred * centred, axis=0, keepdims=True),
                    jnp.sum(grad, axis=0, keepdims=True),
                    jnp.sum(grad * centred, axis=0, keepdims=True),
                ],
                axis=0,
            )


def standardized(i, n_head, stats, attn_ref):
    width = attn_ref.shape[1]
    st = [s[i] for s in stats]
    mean = sum(p[0:1] for p in st) / n_head
    spread = sum(p[1:2] + width * (p[0:1] - mean) * (p[0:1] - mean) for p in st)
    scale = lax.rsqrt(spread / HD + norm_epsilon)
    first = sum(p[2:3] for p in st) / HD
    second = scale * sum(p[3:4] + (p[0:1] - mean) * p[2:3] for p in st) / HD
    return (attn_ref[i] - mean) * scale, scale, first, second


def branch_kernel(n_head, *refs):
    stats, (attn_ref, p_ref, wt_ref), branches = refs[:n_head], refs[n_head : n_head + 3], refs[n_head + 3 :]
    width = attn_ref.shape[1]
    per = branches[0].shape[0] // TILE
    for k in range(n_head):
        device = lax.axis_index("head") ^ k
        for r in range(per):
            i = device * per + r
            normed = standardized(i, n_head, stats, attn_ref)[0]
            p = p_ref[i]
            gated = (normed * (p * (0.5 + 0.5 * jnp.tanh(0.5 * p)))).astype(bf16)
            branches[k][r * TILE : (r + 1) * TILE, :] = dot(
                flip(gated).astype(bf16), wt_ref[4 * width :]
            ).astype(bf16)


def pair_kernel(keep_ref, crossed_ref, out_ref):
    out_ref[...] = (keep_ref[...].astype(f32) + crossed_ref[...].astype(f32)).astype(bf16)


def middle_kernel(n_head, *refs):
    refs = list(refs)
    take = lambda count: [refs.pop(0) for _ in range(count)]
    stats = take(n_head)
    cot_pieces = take(n_head)
    attn_ref, p_ref, gg_ref, xn_ref = take(4)
    da_ref, dat_ref, gun_ref = take(3)
    (acc_ref,) = refs
    width = attn_ref.shape[1]
    per = cot_pieces[0].shape[0] // TILE
    for k, piece in enumerate(cot_pieces):
        for r in range(per):
            i = (lax.axis_index("head") ^ k) * per + r
            normed, scale, first, second = standardized(i, n_head, stats, attn_ref)
            p = p_ref[i]
            sg = 0.5 + 0.5 * jnp.tanh(0.5 * p)
            gate = p * sg
            gg = gg_ref[i]
            gated = (normed * gate).astype(bf16)
            grad = scale * (gg * gate - first - normed * second)
            da_ref[i] = flip(grad).astype(bf16)
            dat_ref[i] = (grad * 0.5).astype(bf16)
            gu = (gg * normed * (sg + gate * (1.0 - sg))).astype(bf16)
            gun_ref[i] = flip(gu).astype(bf16)
            add_gate, add_out = dot(gu, xn_ref[i]), dot(gated, piece[r * TILE : (r + 1) * TILE, :])
            if k + r == 0:
                acc_ref[:width] = add_gate
                acc_ref[width:] = add_out
            else:
                acc_ref[:width] += add_gate
                acc_ref[width:] += add_out


def send_parts(wg_ref, parts):
    low = len(parts)
    high, rows = parts[0].shape[0], parts[0].shape[1]
    me = lax.axis_index("dp") % low
    for k in range(low):
        for p in range(high):
            start = pl.multiple_of((p * low + (me ^ k)) * rows, 16)
            parts[k][p] = wg_ref[pl.ds(start, rows), :].astype(bf16)


def values_kernel(heads, kept, *refs):
    refs = list(refs)
    take = lambda count: [refs.pop(0) for _ in range(count)]
    held = take(2 if kept else 5)
    da_ref, d_ref, xn_ref, acc_in = take(4)
    gpv_ref = refs.pop(0)
    parts, wg_ref = refs[:-1], refs[-1]
    nb, width = da_ref.shape[0], da_ref.shape[2]
    das = [own_lanes(da_ref[i], heads) for i in range(nb)]
    queries = None if kept else [query_columns(held[1][i], held[2][i], heads) for i in range(nb)]
    acc = None
    for j in range(nb):
        if kept:
            tiles = [tile_at(held, i, j) for i in range(j, nb)]
        else:
            kx_ref, _, _, pos_ref, ss_ref = held
            tiles = [
                weights_and_slope(
                    masked(
                        dot(kx_ref[j], queries[i]), pos_ref[i - j], ss_ref[:, i * TILE : (i + 1) * TILE], j, heads
                    )
                )[0].astype(bf16)
                for i in range(j, nb)
            ]
        total = dot(jnp.concatenate(tiles, axis=1), jnp.concatenate(das[j:], axis=0))
        gv = (flip(total) * d_ref[j, :width]).astype(bf16)
        gpv_ref[j] = flip(gv).astype(bf16)
        more = dot(gv, xn_ref[j])
        acc = more if j == 0 else acc + more
    wg_ref[...] = flip(jnp.concatenate([acc_in[...], acc], axis=0))
    send_parts(wg_ref, parts)


def backward_kernel(heads, n_dp, extra, kept, *refs):
    refs = list(refs)
    take = lambda count: [refs.pop(0) for _ in range(count)]
    held = take(2 if kept else 4)
    kx_ref, kxt_ref, q_ref, v_ref, dat_ref = take(5)
    d_ref, xn_ref, gb_ref = take(3)
    gp_ref = refs.pop(0)
    parts = take(split_dp(n_dp)[1])
    acck_ref, posg_ref, acc_ref, wg_ref, small_ref = refs
    nb, width = v_ref.shape[0], v_ref.shape[2]
    factor = 1.0 / math.sqrt(HEAD_DIM)
    tiles = [(i, j) for i in reversed(range(nb)) for j in range(i + 1)]
    products, grads = {}, {}
    dq = m2 = None
    small_ref[...] = jnp.zeros_like(small_ref)
    small_ref[:, :D] = gb_ref[...]

    def add(ref, at, value, first):
        ref[at] = value if first else ref[at] + value

    for t in range(len(tiles) + 3):
        if t < len(tiles):
            i, j = tiles[t]
            if j == 0:
                backs = by_head(dat_ref[i], heads)
                queries = None if kept else query_columns(held[0][i], held[1][i], heads)
            products[t] = dot(v_ref[j], backs), None if kept else dot(kx_ref[j], queries)
        if 0 <= t - 1 < len(tiles):
            i, j = tiles[t - 1]
            back, product = products.pop(t - 1)
            if kept:
                slope = tile_at(held, i, j).astype(f32)
            else:
                start = held[3][:, i * TILE : (i + 1) * TILE]
                slope = weights_and_slope(masked(product, held[2][i - j], start, j, heads))[1]
            ds = back * slope
            grads[t - 1] = ds.astype(bf16)
            add(posg_ref, i - j, sum(ds[:, g * TILE : (g + 1) * TILE] for g in range(heads)), i == nb - 1)
        if t >= 3:
            i, j = tiles[t - 3]
            low = grads.pop(t - 3)
            if j == 0:
                times = jnp.concatenate([kx_ref[i, :, :NTB]] * heads, axis=0)
                q = jnp.concatenate([times, own_lanes(q_ref[i], heads)], axis=1)
            add(acck_ref, j, dot(low, q), i == nb - 1)
            more = dot(kxt_ref[j, NTB:], low)
            dq = more if j == 0 else dq + more
            if i == j:
                gp = jnp.concatenate([own_rows(dq, heads), flip(acck_ref[i, :, NTB:])], axis=0)
                gp = (gp * factor * d_ref[i, width:]).astype(bf16)
                gp_ref[i] = flip(gp).astype(bf16)
                more = dot(gp, xn_ref[i])
                acc_ref[...] = more if i == nb - 1 else acc_ref[...] + more
                part = acck_ref[i, :, :NTB]
                high = part.astype(bf16)
                rest = (part - high.astype(f32)).astype(bf16)
                onehot = kxt_ref[i, :NTB]
                part = dot(onehot, high) + dot(onehot, rest)
                m2 = part if i == nb - 1 else m2 + part
                g = diagonals(posg_ref[i])
                small_ref[:, D + i * TILE : D + (i + 1) * TILE] += g[:, :TILE]
                if i > 0:
                    small_ref[:, D + (i - 1) * TILE : D + i * TILE] += g[:, TILE:]
    g = diagonals(m2 + jnp.transpose(m2))[:, :NTB]
    zero = lax.broadcasted_iota(jnp.int32, (1, NTB), 1) == 0
    at = D + nb * TILE
    small_ref[:, at : at + NTB] = jnp.where(zero, 0.5 * g, g)
    step = D // n_dp
    grads = flip(acc_ref[...])
    for p in range(n_dp):
        here = jnp.concatenate(
            [small_ref[:, (p * extra + r) * 128 : (p * extra + r + 1) * 128] for r in range(extra)], axis=0
        )
        high = here.astype(bf16).astype(f32)
        block = jnp.concatenate([high, here - high, jnp.zeros((16 - 2 * extra, 128), f32)], axis=0)
        wg_ref[p * (step + 16) : p * (step + 16) + step] = grads[p * step : (p + 1) * step]
        if 2 * width > 128:
            block = jnp.concatenate([block, jnp.zeros((16, 2 * width - 128), f32)], axis=1)
        wg_ref[p * (step + 16) + step : (p + 1) * (step + 16)] = block
    send_parts(wg_ref, parts)


def input_kernel(n_head, gp_ref, gun_ref, gpv_ref, wt_ref, keep, send):
    width = gun_ref.shape[2]
    per = keep.shape[1] // TILE
    for k in range(n_head):
        device = lax.axis_index("head") ^ k
        target = (keep, send)[k % 2]
        for r in range(per):
            i = device * per + r
            rows = dot(jnp.concatenate([gun_ref[i], gpv_ref[i]], axis=1), wt_ref[: 2 * width])
            rows = rows + dot(gp_ref[i], wt_ref[2 * width : 4 * width])
            target[device // 2, r * TILE : (r + 1) * TILE] = rows.astype(bf16)


def fold_kernel(*refs):
    low = sum(len(ref.shape) == 3 for ref in refs)
    row = lax.axis_index("dp") // low
    for k, out in enumerate(refs[low:]):
        total = refs[0][row ^ k].astype(f32)
        for ref in refs[1:low]:
            total = total + ref[row ^ k].astype(f32)
        out[...] = total.astype(out.dtype)


def sum_kernel(*refs):
    total = refs[0][...]
    for ref in refs[1:-1]:
        total = total + ref[...].astype(f32)
    refs[-1][...] = total


def mix_kernel(tokens_ref, bias_ref, *refs):
    total = tokens_ref[...].astype(f32) + row_lanes(bias_ref, 0, D // 128)
    for ref in refs[:-1]:
        total = total + ref[...].astype(f32)
    refs[-1][...] = total.astype(bf16)


def finish_kernel(part, *refs):
    tokens_ref, cot_ref, mine_ref, *refs = refs[part:]
    x = tokens_ref[...].astype(f32)
    x = x - jnp.sum(x, axis=1, keepdims=True) / D
    scale = lax.rsqrt(jnp.sum(x * x, axis=1, keepdims=True) / D + norm_epsilon)
    x = x * scale
    grad = mine_ref[...]
    for ref in refs[:-1]:
        grad = grad + ref[...].astype(f32)
    mean = jnp.sum(grad, axis=1, keepdims=True) / D
    along = jnp.sum(grad * x, axis=1, keepdims=True) / D
    refs[-1][...] = cot_ref[...].astype(f32) + scale * (grad - mean - x * along)


def rows_kernel(chips, keep_ref, crossed_ref, mine_ref, *leaving):
    chip = lax.axis_index("head") // 2
    for k in range(chips):
        total = keep_ref[chip ^ k].astype(f32) + crossed_ref[chip ^ k].astype(f32)
        if k == 0:
            mine_ref[...] = total
        else:
            rows = leaving[0].shape[0]
            cuts = total.shape[0] // rows
            for c in range(cuts):
                leaving[(k - 1) * cuts + c][...] = total[c * rows : (c + 1) * rows].astype(bf16)


def collect_kernel(high, extra, *refs):
    late_blocks, (early_ref, grads_ref, message_ref) = refs[:high], refs[high:]
    rows = grads_ref.shape[0]
    total, early = late_blocks[0][...], early_ref[...]
    for k in range(1, high):
        total = total + late_blocks[k][...].astype(f32)
    grads = jnp.concatenate([total[:rows], early], axis=1)
    grads_ref[...] = grads
    squares = jnp.sum(jnp.sum(grads * grads, axis=0, keepdims=True), axis=1, keepdims=True)
    message = jnp.concatenate(
        [
            total[rows : rows + extra, :128] + total[rows + extra : rows + 2 * extra, :128],
            jnp.broadcast_to(squares, (message_ref.shape[1] - extra, 128)),
        ],
        axis=0,
    )
    for k in range(message_ref.shape[0]):
        message_ref[k] = message


def update_kernel(n_head, extra, group, heard_ref, grads_ref, *refs):
    state, outs = refs[:9], refs[9:]
    grad_proj_ref, grad_out_ref, grad_small_ref, norm_ref = outs[:4]
    n_all = heard_ref.shape[0]
    width = grad_out_ref.shape[1]
    lead, pos_rows, used = D // 128, POS // 128, (D + group) // 128
    grad_small_ref[...] = jnp.zeros_like(grad_small_ref)
    last = heard_ref.shape[1] - 1
    squares = heard_ref[0, last:, :]
    for k in range(1, n_all):
        squares = squares + heard_ref[k, last:, :]
    for p in range(n_all // n_head):
        rows = heard_ref[p * n_head, :extra, :]
        for h in range(1, n_head):
            rows = rows + heard_ref[p * n_head + h, :extra, :]
        for r in range(extra):
            at = p * extra + r
            if at < used:
                grad_small_ref[at : at + 1, :] = rows[r : r + 1]
            elif at == used:
                grad_small_ref[lead + pos_rows : lead + pos_rows + 1, :] = rows[r : r + 1]
    small = grad_small_ref[...]
    total = jnp.sum(jnp.sum(small * small, axis=0, keepdims=True), axis=1, keepdims=True) + squares[:, :1]
    norm = jnp.sqrt(total)
    norm_ref[...] = norm
    factor = jnp.minimum(1.0, clip_norm / (norm + 1e-06))

    def update(get, put, grad, rate, decay):
        for k, value in enumerate(adam_step(get(0), grad, get(1), get(2), factor, rate, decay)):
            put(k, value)

    for c in range(4):
        at = (2, 4, 0, 1)[c] * width
        grad = grads_ref[:, at : at + width]
        grad_proj_ref[:, c, :] = grad

        def put(k, value):
            outs[4 + k][:, c, :] = value

        update(lambda k: state[k][:, c, :], put, grad, rate_matrix, decay_matrix)
    grad = grads_ref[:, 3 * width : 4 * width]
    grad_out_ref[...] = grad

    def put_out(k, value):
        outs[7 + k][...] = value

    update(lambda k: state[3 + k][...], put_out, grad, rate_matrix, decay_matrix)

    def put_small(k, value):
        outs[10 + k][...] = value

    update(lambda k: state[6 + k][...], put_small, small, rate_small, 0.0)


def call(kernel, name, in_specs, outs, scratch, us, room=16, **more):
    return pl.pallas_call(
        kernel,
        out_shape=[jax.ShapeDtypeStruct(shape, dtype) for shape, dtype, _ in outs],
        in_specs=in_specs,
        out_specs=[spec for _, _, spec in outs],
        scratch_shapes=scratch,
        compiler_params=pltpu.CompilerParams(vmem_limit_bytes=min(60, room * max(1, lax.axis_size("head") // 4)) * 2**20),
        cost_estimate=pl.CostEstimate(flops=int(us * 1e9), bytes_accessed=int(us * 3e6), transcendentals=0),
        name=name,
        **more,
    )


def block(shape):
    return pl.BlockSpec((1,) + tuple(shape[1:]), lambda i: (i,) + (0,) * (len(shape) - 1))


def shards(
    tokens,
    cotangent,
    seq_start,
    time_bucket,
    proj_weight,
    out_weight,
    small_params,
    proj_mean,
    proj_square,
    out_mean,
    out_square,
    small_mean,
    small_square,
):
    n_head = lax.axis_size("head")
    n_dp = lax.axis_size("dp")
    here = tokens.shape[0]
    group = here * n_head
    nb = group // TILE
    per = here // TILE
    rows_here, _, width = proj_weight.shape
    heads = width // HEAD_DIM
    high, low = split_dp(n_dp)

    (weights,) = call(
        cast_kernel,
        "cast",
        [pl.BlockSpec(memory_space=pl.ANY)] * 2,
        [((rows_here, 5 * width), bf16, VMEM)],
        [
            pltpu.VMEM(proj_weight.shape, f32),
            pltpu.VMEM((rows_here, width), f32),
            pltpu.SemaphoreType.DMA((2,)),
        ],
        1,
    )(proj_weight, out_weight.T)
    x_chips = gather_chips(after(tokens, weights))
    starts = seq_start.reshape(1, group)
    times = time_bucket.reshape(1, group)
    small_rows = small_params.reshape(-1, 128)
    pos, oh, oht, trow = call(
        prepare_kernel,
        "prepare",
        [VMEM] * 2,
        [
            ((nb, TILE, TILE), f32, VMEM),
            ((nb, TILE, NTB), bf16, VMEM),
            ((nb, NTB, TILE), bf16, VMEM),
            ((nb, NTB, TILE), bf16, VMEM),
        ],
        [],
        2,
    )(after(times, weights), small_rows)

    items = [
        ((nb, 3 * width, TILE), bf16),
        ((nb, TILE, NTB + width), bf16),
        ((nb, NTB + width, TILE), bf16),
        ((nb, width, TILE), bf16),
        ((nb, TILE, width), bf16),
        ((nb, TILE, width), bf16),
        ((nb, width, TILE), bf16),
    ]
    w_pieces, offsets = gather_dp(weights, pos)
    cot_chips = gather_chips(after(cotangent, weights))

    x_pieces = gather_cores(tokens, x_chips)
    near = [0, 1] + list(range(2, n_head, 2))
    far = list(range(3, n_head, 2))
    xn = []
    for which in (near, far):
        xn = call(
            functools.partial(normalize_kernel, which),
            "normalize",
            [VMEM] * (len(xn) + len(which)),
            [((nb, TILE, D), bf16, VMEM)],
            [],
            0.1,
        )(*xn, *[x_pieces[k] for k in which])
    (xn,) = xn
    w_pieces[-1] = after(join(w_pieces[-1:], 6), xn)
    (wt,) = call(
        functools.partial(assemble_kernel, offsets),
        "assemble",
        [VMEM] * len(w_pieces),
        [((5 * width, D), bf16, VMEM)],
        [pltpu.VMEM((D, 5 * width), bf16)],
        0.5,
    )(*w_pieces)
    dsilu, kx, kxt, qs, q, v, vt = call(
        functools.partial(project_kernel, heads),
        "project",
        [VMEM] * 4,
        [item + (VMEM,) for item in items],
        [],
        1,
    )(xn, wt, oh, oht)

    kept = nb * (nb + 1) // 2 * heads <= KEPT_TILES

    def attend(first, last, *before):
        count = (last * (last + 1) - first * (first + 1)) // 2
        return call(
            functools.partial(attend_kernel, heads, first, last, kept),
            "attend",
            [VMEM] * (len(before) + 6),
            [((last, width, TILE), f32, VMEM)] + [((count, TILE, heads * TILE), bf16, VMEM)] * (2 * kept),
            [],
            8 if before else 0.5,
        )(*before, kx, qs, trow, vt, pos, starts)

    split = nb - nb // 4
    attn, *kept_first = attend(0, split)
    cot_chips = after_all(cot_chips, attn)
    attn, *kept_last = attend(split, nb, after(attn, *cot_chips))
    kept_weights, kept_slopes = zip(kept_first, kept_last) if kept else ((), ())
    cot_pieces = gather_cores(cotangent, cot_chips)

    column = ((nb, width, TILE), f32, VMEM)
    p_gate, gg, stat, gb = call(
        functools.partial(gate_kernel, n_head),
        "gate",
        [VMEM] * (n_head + 3),
        [column, column, ((nb, 4, TILE), f32, VMEM), ((1, D), f32, VMEM)],
        [],
        5,
    )(*cot_pieces, attn, xn, wt)

    stats = [stat] + [swap(stat, "head", k) for k in range(1, n_head)]
    chips = n_head // 2
    share = ((here, D), bf16, VMEM)
    branches = call(
        functools.partial(branch_kernel, n_head), "branch", [VMEM] * (n_head + 3), [share] * n_head, [], 1
    )(*stats, attn, p_gate, wt)
    crossed = [swap(branches[2 * k + 1], "head", 1) for k in range(chips)]
    da, dat, gun, wg_sum = call(
        functools.partial(middle_kernel, n_head),
        "middle",
        [VMEM] * (2 * n_head + 4),
        [
            ((nb, TILE, width), bf16, VMEM),
            ((nb, width, TILE), bf16, VMEM),
            ((nb, TILE, width), bf16, VMEM),
            ((2 * width, D), f32, VMEM),
        ],
        [],
        6,
    )(*stats, *cot_pieces, attn, p_gate, gg, xn)
    received = [
        swap(call(pair_kernel, "pair", [VMEM] * 2, [share], [], 0.1)(branches[2 * k], crossed[k])[0], "head", 2 * k)
        for k in range(1, chips)
    ]
    branch = (branches[0], crossed[0])
    held = kept_weights if kept else (kx, qs, trow, pos, starts)
    gpv, *early_parts = call(
        functools.partial(values_kernel, heads, kept),
        "values",
        [VMEM] * (len(held) + 4),
        [((nb, TILE, width), bf16, VMEM)] + [((high, rows_here, 3 * width), bf16, VMEM)] * low,
        [pltpu.VMEM((D, 3 * width), f32)],
        VALUES,
    )(*held, da, dsilu, xn, wg_sum)
    early_received = [swap(early_parts[k], "dp", k) for k in range(1, low)]

    length = D + group + NTB
    extra = -(-length // (128 * n_dp))
    held = kept_slopes if kept else (qs, trow, pos, starts)
    gp, *late_parts = call(
        functools.partial(backward_kernel, heads, n_dp, extra, kept),
        "backward",
        [VMEM] * (len(held) + 8),
        [((nb, TILE, 2 * width), bf16, VMEM)] + [((high, rows_here + 16, 2 * width), bf16, VMEM)] * low,
        [
            pltpu.VMEM((nb, TILE, NTB + width), f32),
            pltpu.VMEM((nb, TILE, TILE), f32),
            pltpu.VMEM((2 * width, D), f32),
            pltpu.VMEM((n_dp * (rows_here + 16), 2 * width), f32),
            pltpu.VMEM((1, extra * n_dp * 128), f32),
        ],
        BACKWARD,
        ROOM,
    )(*held, kx, kxt, q, v, dat, dsilu, xn, gb)

    tied = lax.optimization_barrier((gp, *late_parts, *early_received, *received))
    gp, late_parts = tied[0], tied[1 : 1 + low]
    early_received, received = tied[1 + low : 2 * low], tied[2 * low :]
    late_received = [swap(late_parts[k], "dp", k) for k in range(1, low)]
    keep, send = call(
        functools.partial(input_kernel, n_head),
        "input_rows",
        [VMEM] * 4,
        [((n_head // 2, here, D), bf16, VMEM)] * 2,
        [],
        4,
    )(gp, gun, gpv, wt)
    early_blocks = scatter_high(after(early_parts[0], send), early_received, 1)
    crossed = swap(send, "head", 1)
    late_blocks = scatter_high(late_parts[0], late_received, 12, send, crossed)
    (early,) = call(
        sum_kernel, "sum", [VMEM] * high, [((rows_here, 3 * width), f32, VMEM)], [], 14
    )(*early_blocks)
    mine, *leaving = fold_cores(keep, after(crossed, late_blocks[0]), 2)
    half = here // 2
    arrived = [[swap(leaving[2 * k - 2 + part], "head", 2 * k) for k in range(1, chips)] for part in range(2)]
    n_all = n_dp * n_head
    grads_shape = ((rows_here, 5 * width), f32)
    grads, message = call(
        functools.partial(collect_kernel, high, extra),
        "collect",
        [VMEM] * (high + 1),
        [grads_shape + (VMEM,), ((n_all, 4 if extra < 4 else 8, 128), f32, VMEM)],
        [],
        10,
    )(*late_blocks, early)
    message = after(message, *leaving)
    heard = lax.all_to_all(message, ("dp", "head"), 0, 0, tiled=True)
    (mixed,) = call(
        mix_kernel, "mix", [VMEM] * (3 + chips), [((here, D), bf16, VMEM)], [], 1
    )(tokens, small_rows, after(branch[0], message), branch[1], *received)
    input_grad = None
    for part in range(2):
        rows = pl.BlockSpec((half, D), lambda i, part=part: (part, 0))
        alone = pl.BlockSpec((half, D), lambda i: (0, 0))
        before = [] if part == 0 else [input_grad]
        (input_grad,) = call(
            functools.partial(finish_kernel, part),
            "finish",
            [pl.BlockSpec(memory_space=pl.ANY)] * len(before) + [rows] * 3 + [alone] * (chips - 1),
            [((here, D), f32, rows)],
            [],
            1,
            grid=(1,),
            input_output_aliases={0: 0} if before else {},
        )(*before, tokens, cotangent, mine, *arrived[part])
    heard = after(heard, input_grad)
    state = [proj_weight, proj_mean, proj_square, out_weight.T, out_mean.T, out_square.T]
    state += [x.reshape(-1, 128) for x in (small_params, small_mean, small_square)]
    proj_shape, out_shape, small_shape = proj_weight.shape, (rows_here, width), small_rows.shape
    shapes = [proj_shape, out_shape, small_shape, (1, 1)] + [proj_shape] * 3 + [out_shape] * 3 + [small_shape] * 3
    results = call(
        functools.partial(update_kernel, n_head, extra, group),
        "update",
        [VMEM] * (2 + len(state)),
        [(shape, f32, VMEM) for shape in shapes],
        [],
        0.1,
    )(heard, grads, *state)
    grad_proj, grad_out, grad_small, grad_norm = results[:4]
    grad_out, grad_small, grad_norm = grad_out.T, grad_small.reshape(-1), grad_norm.reshape(())
    new_proj, mean_proj, square_proj = results[4:7]
    new_out, mean_out, square_out = [x.T for x in results[7:10]]
    new_small, mean_small, square_small = [x.reshape(-1) for x in results[10:13]]
    return (
        mixed,
        input_grad,
        grad_proj,
        grad_out,
        grad_small,
        grad_norm,
        new_proj,
        mean_proj,
        square_proj,
        new_out,
        mean_out,
        square_out,
        new_small,
        mean_small,
        square_small,
    )


def solution(mesh):
    in_specs = (
        P(("dp", "head"), None),
        P(("dp", "head"), None),
        P("dp"),
        P("dp"),
        P("dp", None, "head"),
        P("head", "dp"),
        P(),
        P("dp", None, "head"),
        P("dp", None, "head"),
        P("head", "dp"),
        P("head", "dp"),
        P(),
        P(),
    )
    out_specs = (
        P(("dp", "head"), None),
        P(("dp", "head"), None),
        P("dp", None, "head"),
        P("head", "dp"),
        P(),
        P(),
        P("dp", None, "head"),
        P("dp", None, "head"),
        P("dp", None, "head"),
        P("head", "dp"),
        P("head", "dp"),
        P("head", "dp"),
        P(),
        P(),
        P(),
    )
    return jax.shard_map(shards, mesh=mesh, in_specs=in_specs, out_specs=out_specs, check_vma=False)
```

```python
import functools
import math

import jax
import jax.numpy as jnp
from jax import lax
from jax.experimental import pallas as pl
from jax.experimental.pallas import tpu as pltpu
from jax.sharding import PartitionSpec as P

D = 512
HEAD_DIM = 64
HD = 512
POS = 8192
NTB = 128
STEP = 10
TILE = 256
NEG = -1e9
ROOM = 14
KEPT_TILES = 72
VALUES = 12
BACKWARD = 2

norm_epsilon = 1e-06
adam_epsilon = 1e-08
beta_one = 0.9
beta_two = 0.999
clip_norm = 1.0
rate_matrix = 0.05
rate_small = 0.3
decay_matrix = 0.1

f32 = jnp.float32
bf16 = jnp.bfloat16
VMEM = pl.BlockSpec(memory_space=pltpu.VMEM)


def adam_step(weight, grad, first, second, factor, rate, decay):
    clipped = grad * factor
    first_new = beta_one * first + (1.0 - beta_one) * clipped
    second_new = beta_two * second + (1.0 - beta_two) * clipped * clipped
    update = (
        first_new
        / (1.0 - beta_one**STEP)
        / (jnp.sqrt(second_new / (1.0 - beta_two**STEP)) + adam_epsilon)
    )
    return (weight - rate * (update + decay * weight), first_new, second_new)


def swap(x, axis, k):
    n = lax.axis_size(axis)
    return lax.ppermute(x, axis, [(i, i ^ k) for i in range(n)])


def gather_chips(x):
    return [swap(x, "head", k) for k in range(2, lax.axis_size("head"), 2)]


def gather_cores(x, others):
    pieces = [x, swap(x, "head", 1)]
    for other in others:
        pieces += [other, swap(other, "head", 1)]
    return pieces


def after_all(arrays, *others):
    arrays = tuple(arrays)
    return lax.optimization_barrier(arrays + others)[: len(arrays)]


def after(x, *others):
    return lax.optimization_barrier((x,) + others)[0]


def gather_dp(x, behind):
    n = lax.axis_size("dp")
    arrays, offsets = [x], [[0]]
    k = n // 2
    while k:
        operand = join(arrays) if len(arrays) > 1 else x
        if k == 1:
            operand = after(operand, behind)
        arrays.append(swap(operand, "dp", k))
        offsets.append([o ^ k for group in offsets for o in group])
        k //= 2
    return arrays, offsets


def join(arrays, us=0.1):
    shape = (sum(x.shape[0] for x in arrays), arrays[0].shape[1])
    return call(join_kernel, "join", [VMEM] * len(arrays), [(shape, arrays[0].dtype, VMEM)], [], us)(*arrays)[0]


def split_dp(n):
    low = 2 ** ((n.bit_length() - 1) // 2)
    return n // low, low


def scatter_high(own, received, us, *behind):
    high, rows, columns = own.shape
    low = 1 + len(received)
    mine, *leaving = call(
        fold_kernel,
        "fold",
        [VMEM] * low,
        [((rows, columns), f32, VMEM)] + [((rows, columns), bf16, VMEM)] * (high - 1),
        [],
        us,
    )(own, *received)
    leaving = after_all(leaving, *behind)
    return [mine] + [swap(leaving[k - 1], "dp", k * low) for k in reversed(range(1, high))]


def fold_cores(keep, crossed, cuts=1):
    chips, rows, columns = keep.shape
    return call(
        functools.partial(rows_kernel, chips),
        "rows",
        [VMEM] * 2,
        [((rows, columns), f32, VMEM)] + [((rows // cuts, columns), bf16, VMEM)] * (cuts * (chips - 1)),
        [],
        0.1,
    )(keep, crossed)


def dot(a, b):
    return lax.dot_general(a, b, (((1,), (0,)), ((), ())), preferred_element_type=f32)


def dot_nt(a, b):
    return lax.dot_general(a, b, (((1,), (1,)), ((), ())), preferred_element_type=f32)


def flip(a):
    return jnp.transpose(a.astype(f32))


def lanes(i):
    return pl.ds(pl.multiple_of(i * TILE, TILE), TILE)


def by_head(block, heads):
    zero = jnp.zeros((HEAD_DIM, block.shape[1]), block.dtype)
    return jnp.concatenate(
        [
            jnp.concatenate(
                [block[g * HEAD_DIM : (g + 1) * HEAD_DIM] if g == h else zero for g in range(heads)], axis=0
            )
            for h in range(heads)
        ],
        axis=1,
    )


def query_columns(qs, trow, heads):
    return jnp.concatenate([jnp.concatenate([trow] * heads, axis=1), by_head(qs, heads)], axis=0)


def own_rows(block, heads):
    return jnp.concatenate(
        [block[h * HEAD_DIM : (h + 1) * HEAD_DIM, h * TILE : (h + 1) * TILE] for h in range(heads)], axis=0
    )


def own_lanes(block, heads):
    lane = lax.broadcasted_iota(jnp.int32, block.shape, 1) // HEAD_DIM
    return jnp.concatenate([jnp.where(lane == h, block, jnp.zeros_like(block)) for h in range(heads)], axis=0)


def masked(product, bias, start, j, heads):
    key = j * TILE + lax.broadcasted_iota(jnp.int32, (TILE, TILE), 0)
    seen = key >= start
    return jnp.where(
        jnp.concatenate([seen] * heads, axis=1), product + jnp.concatenate([bias] * heads, axis=1), NEG
    )


def diagonals(x):
    rows, cols = x.shape
    z = jnp.concatenate([x, jnp.zeros((rows, cols), f32)], axis=1)
    total = z[:8]
    for q in range(1, rows // 8):
        total = total + pltpu.roll(z[8 * q : 8 * q + 8], 2 * cols - 8 * q, 1)
    g = total[0:1]
    for r in range(1, 8):
        g = g + pltpu.roll(total, 2 * cols - r, 1)[r : r + 1]
    return g


def cast_kernel(w_in, o_in, low_ref, w_ref, o_ref, sems):
    copies = [pltpu.make_async_copy(w_in, w_ref, sems.at[0]), pltpu.make_async_copy(o_in, o_ref, sems.at[1])]
    for copy in copies:
        copy.start()
    for copy in copies:
        copy.wait()
    width = o_ref.shape[1]
    for c in range(4):
        low_ref[:, c * width : (c + 1) * width] = w_ref[:, c, :].astype(bf16)
    low_ref[:, 4 * width :] = o_ref[...].astype(bf16)


def row_lanes(ref, first, count):
    return jnp.concatenate([ref[pl.ds(first + k, 1), :] for k in range(count)], axis=1)


def prepare_kernel(tb_ref, small_ref, pos_ref, oh_ref, oht_ref, trow_ref):
    nb = pos_ref.shape[0]
    step = TILE // 128

    def tile(d, _):
        first = D // 128 + d * step
        row = jnp.concatenate([row_lanes(small_ref, first, step), row_lanes(small_ref, first - step, step)], axis=1)
        pos_ref[d] = pltpu.roll(
            jnp.broadcast_to(row * 0.5, (TILE, 2 * TILE)), 0, 1, stride=1, stride_axis=0
        )[:, :TILE]
        return 0

    lax.fori_loop(0, nb, tile, 0)
    b = lax.broadcasted_iota(jnp.int32, (TILE, TILE), 0)
    a = lax.broadcasted_iota(jnp.int32, (TILE, TILE), 1)
    pos_ref[0] = jnp.where(b <= a, pos_ref[0], NEG)
    table = row_lanes(small_ref, (D + POS) // 128, NTB // 128)
    row = jnp.concatenate([table, table], axis=1)
    upper = pltpu.roll(jnp.broadcast_to(row, (NTB, 2 * NTB)), 0, 1, stride=1, stride_axis=0)[:, :NTB]
    a = lax.broadcasted_iota(jnp.int32, (NTB, NTB), 0)
    b = lax.broadcasted_iota(jnp.int32, (NTB, NTB), 1)
    upper = jnp.where(b >= a, upper, 0.0)
    square = (jnp.where(b > a, upper, jnp.transpose(upper)) * 0.5).astype(bf16)

    def block(i, _):
        onehot = (lax.broadcasted_iota(jnp.int32, (NTB, TILE), 0) == tb_ref[:, lanes(i)]).astype(f32)
        low = onehot.astype(bf16)
        oht_ref[i] = low
        oh_ref[i] = flip(onehot).astype(bf16)
        trow_ref[i] = dot(square, low).astype(bf16)
        return 0

    lax.fori_loop(0, nb, block, 0)


def join_kernel(*refs):
    at = 0
    for ref in refs[:-1]:
        refs[-1][at : at + ref.shape[0]] = ref[...]
        at += ref.shape[0]


def normalize_kernel(which, *refs):
    before = refs[: len(refs) - len(which) - 1]
    pieces, xn_ref = refs[len(before) : -1], refs[-1]
    per = pieces[0].shape[0] // TILE
    for ref in before:
        xn_ref[...] = ref[...]
    for k, piece in zip(which, pieces):
        for r in range(per):
            x = piece[r * TILE : (r + 1) * TILE, :].astype(f32)
            x = x - jnp.sum(x, axis=1, keepdims=True) / D
            x = x * lax.rsqrt(jnp.sum(x * x, axis=1, keepdims=True) / D + norm_epsilon)
            xn_ref[(lax.axis_index("head") ^ k) * per + r] = x.astype(bf16)


def assemble_kernel(offsets, *refs):
    w_pieces, (wt_ref, w_ref) = refs[:-2], refs[-2:]
    for piece, group in zip(w_pieces, offsets):
        rows = piece.shape[0] // len(group)
        for at, offset in enumerate(group):
            start = pl.multiple_of((lax.axis_index("dp") ^ offset) * rows, 16)
            w_ref[pl.ds(start, rows), :] = piece[at * rows : (at + 1) * rows, :]
    wt_ref[...] = flip(w_ref[...]).astype(bf16)


def project_kernel(heads, *refs):
    refs = list(refs)
    take = lambda count: [refs.pop(0) for _ in range(count)]
    xn_ref, wt_ref, oh_ref, oht_ref = take(4)
    d_ref, kx_ref, kxt_ref, qs_ref, q_ref, v_ref, vt_ref = refs
    width = v_ref.shape[2]

    def project(i):
        x = xn_ref[i]
        p = dot_nt(wt_ref[width : 4 * width], x)
        sg = 0.5 + 0.5 * jnp.tanh(0.5 * p)
        act = p * sg
        d_ref[i] = (sg + act * (1.0 - sg)).astype(bf16)
        vt = act[:width]
        vt_ref[i] = vt.astype(bf16)
        v_ref[i] = flip(vt).astype(bf16)
        qt = act[width : 2 * width].astype(bf16)
        kt = act[2 * width :]
        kxt_ref[i, :NTB] = oht_ref[i]
        kxt_ref[i, NTB:] = kt.astype(bf16)
        kx_ref[i, :, :NTB] = oh_ref[i]
        kx_ref[i, :, NTB:] = flip(kt).astype(bf16)
        qs = (qt.astype(f32) * (0.5 / math.sqrt(HEAD_DIM))).astype(bf16)
        qs_ref[i] = qs
        q_ref[i] = flip(qt).astype(bf16)

    for i in range(xn_ref.shape[0]):
        project(i)

def tile_at(refs, i, j):
    at = i * (i + 1) // 2 + j
    for ref in refs:
        if at < ref.shape[0]:
            return ref[at]
        at -= ref.shape[0]


def weights_and_slope(h):
    th = jnp.tanh(h)
    u = 1.0 + th
    w = h * u
    return w, u + w * (1.0 - th)


def attend_kernel(heads, first, last, kept, *refs):
    if first:
        before_ref, refs = refs[0], refs[1:]
    kx_ref, qs_ref, trow_ref, vt_ref, pos_ref, ss_ref, attn_ref = refs[:7]
    if first:
        attn_ref[:first] = before_ref[...]
    tiles = [(i, j) for i in range(first, last) for j in range(i + 1)]
    scores, weights = {}, {}
    for t in range(len(tiles) + 3):
        if t < len(tiles):
            i, j = tiles[t]
            if j == 0:
                queries = query_columns(qs_ref[i], trow_ref[i], heads)
            scores[t] = dot(kx_ref[j], queries)
        if 0 <= t - 1 < len(tiles):
            i, j = tiles[t - 1]
            h = masked(scores.pop(t - 1), pos_ref[i - j], ss_ref[:, i * TILE : (i + 1) * TILE], j, heads)
            w, slope = weights_and_slope(h)
            weights[t - 1] = w.astype(bf16)
            if kept:
                refs[7][t - 1] = weights[t - 1]
                refs[8][t - 1] = slope.astype(bf16)
        if t >= 3:
            i, j = tiles[t - 3]
            more = dot(vt_ref[j], weights.pop(t - 3))
            total = more if j == 0 else total + more
            if i == j:
                attn_ref[i] = own_rows(total, heads)


def gate_kernel(n_head, *refs):
    refs = list(refs)
    take = lambda count: [refs.pop(0) for _ in range(count)]
    cot_pieces = take(n_head)
    attn_ref, xn_ref, wt_ref = take(3)
    p_ref, gg_ref, stat_ref, gb_ref = refs
    width = attn_ref.shape[1]
    per = cot_pieces[0].shape[0] // TILE
    gb_ref[...] = jnp.sum(cot_pieces[0][...].astype(f32), axis=0, keepdims=True)
    for k, piece in enumerate(cot_pieces):
        for r in range(per):
            i = (lax.axis_index("head") ^ k) * per + r
            p = dot_nt(wt_ref[:width], xn_ref[i])
            gate = p * (0.5 + 0.5 * jnp.tanh(0.5 * p))
            gg = dot_nt(wt_ref[4 * width :], piece[r * TILE : (r + 1) * TILE, :])
            grad = gg * gate
            p_ref[i] = p
            gg_ref[i] = gg
            at = attn_ref[i]
            mean = jnp.sum(at, axis=0, keepdims=True) / width
            centred = at - mean
            stat_ref[i] = jnp.concatenate(
                [
                    mean,
                    jnp.sum(centred * centred, axis=0, keepdims=True),
                    jnp.sum(grad, axis=0, keepdims=True),
                    jnp.sum(grad * centred, axis=0, keepdims=True),
                ],
                axis=0,
            )


def standardized(i, n_head, stats, attn_ref):
    width = attn_ref.shape[1]
    st = [s[i] for s in stats]
    mean = sum(p[0:1] for p in st) / n_head
    spread = sum(p[1:2] + width * (p[0:1] - mean) * (p[0:1] - mean) for p in st)
    scale = lax.rsqrt(spread / HD + norm_epsilon)
    first = sum(p[2:3] for p in st) / HD
    second = scale * sum(p[3:4] + (p[0:1] - mean) * p[2:3] for p in st) / HD
    return (attn_ref[i] - mean) * scale, scale, first, second


def branch_kernel(n_head, *refs):
    stats, (attn_ref, p_ref, wt_ref), branches = refs[:n_head], refs[n_head : n_head + 3], refs[n_head + 3 :]
    width = attn_ref.shape[1]
    per = branches[0].shape[0] // TILE
    for k in range(n_head):
        device = lax.axis_index("head") ^ k
        for r in range(per):
            i = device * per + r
            normed = standardized(i, n_head, stats, attn_ref)[0]
            p = p_ref[i]
            gated = (normed * (p * (0.5 + 0.5 * jnp.tanh(0.5 * p)))).astype(bf16)
            branches[k][r * TILE : (r + 1) * TILE, :] = dot(
                flip(gated).astype(bf16), wt_ref[4 * width :]
            ).astype(bf16)


def pair_kernel(keep_ref, crossed_ref, out_ref):
    out_ref[...] = (keep_ref[...].astype(f32) + crossed_ref[...].astype(f32)).astype(bf16)


def middle_kernel(n_head, *refs):
    refs = list(refs)
    take = lambda count: [refs.pop(0) for _ in range(count)]
    stats = take(n_head)
    cot_pieces = take(n_head)
    attn_ref, p_ref, gg_ref, xn_ref = take(4)
    da_ref, dat_ref, gun_ref = take(3)
    (acc_ref,) = refs
    width = attn_ref.shape[1]
    per = cot_pieces[0].shape[0] // TILE
    for k, piece in enumerate(cot_pieces):
        for r in range(per):
            i = (lax.axis_index("head") ^ k) * per + r
            normed, scale, first, second = standardized(i, n_head, stats, attn_ref)
            p = p_ref[i]
            sg = 0.5 + 0.5 * jnp.tanh(0.5 * p)
            gate = p * sg
            gg = gg_ref[i]
            gated = (normed * gate).astype(bf16)
            grad = scale * (gg * gate - first - normed * second)
            da_ref[i] = flip(grad).astype(bf16)
            dat_ref[i] = (grad * 0.5).astype(bf16)
            gu = (gg * normed * (sg + gate * (1.0 - sg))).astype(bf16)
            gun_ref[i] = flip(gu).astype(bf16)
            add_gate, add_out = dot(gu, xn_ref[i]), dot(gated, piece[r * TILE : (r + 1) * TILE, :])
            if k + r == 0:
                acc_ref[:width] = add_gate
                acc_ref[width:] = add_out
            else:
                acc_ref[:width] += add_gate
                acc_ref[width:] += add_out


def send_parts(wg_ref, parts):
    low = len(parts)
    high, rows = parts[0].shape[0], parts[0].shape[1]
    me = lax.axis_index("dp") % low
    for k in range(low):
        for p in range(high):
            start = pl.multiple_of((p * low + (me ^ k)) * rows, 16)
            parts[k][p] = wg_ref[pl.ds(start, rows), :].astype(bf16)


def values_kernel(heads, kept, *refs):
    refs = list(refs)
    take = lambda count: [refs.pop(0) for _ in range(count)]
    held = take(2 if kept else 5)
    da_ref, d_ref, xn_ref, acc_in = take(4)
    gpv_ref = refs.pop(0)
    parts, wg_ref = refs[:-1], refs[-1]
    nb, width = da_ref.shape[0], da_ref.shape[2]
    das = [own_lanes(da_ref[i], heads) for i in range(nb)]
    queries = None if kept else [query_columns(held[1][i], held[2][i], heads) for i in range(nb)]
    acc = None
    for j in range(nb):
        if kept:
            tiles = [tile_at(held, i, j) for i in range(j, nb)]
        else:
            kx_ref, _, _, pos_ref, ss_ref = held
            tiles = [
                weights_and_slope(
                    masked(
                        dot(kx_ref[j], queries[i]), pos_ref[i - j], ss_ref[:, i * TILE : (i + 1) * TILE], j, heads
                    )
                )[0].astype(bf16)
                for i in range(j, nb)
            ]
        total = dot(jnp.concatenate(tiles, axis=1), jnp.concatenate(das[j:], axis=0))
        gv = (flip(total) * d_ref[j, :width]).astype(bf16)
        gpv_ref[j] = flip(gv).astype(bf16)
        more = dot(gv, xn_ref[j])
        acc = more if j == 0 else acc + more
    wg_ref[...] = flip(jnp.concatenate([acc_in[...], acc], axis=0))
    send_parts(wg_ref, parts)


def backward_kernel(heads, n_dp, extra, kept, *refs):
    refs = list(refs)
    take = lambda count: [refs.pop(0) for _ in range(count)]
    held = take(2 if kept else 4)
    kx_ref, kxt_ref, q_ref, v_ref, dat_ref = take(5)
    d_ref, xn_ref, gb_ref = take(3)
    gp_ref = refs.pop(0)
    parts = take(split_dp(n_dp)[1])
    acck_ref, posg_ref, acc_ref, wg_ref, small_ref = refs
    nb, width = v_ref.shape[0], v_ref.shape[2]
    factor = 1.0 / math.sqrt(HEAD_DIM)
    tiles = [(i, j) for i in reversed(range(nb)) for j in range(i + 1)]
    products, grads = {}, {}
    dq = m2 = None
    small_ref[...] = jnp.zeros_like(small_ref)
    small_ref[:, :D] = gb_ref[...]

    def add(ref, at, value, first):
        ref[at] = value if first else ref[at] + value

    for t in range(len(tiles) + 3):
        if t < len(tiles):
            i, j = tiles[t]
            if j == 0:
                backs = by_head(dat_ref[i], heads)
                queries = None if kept else query_columns(held[0][i], held[1][i], heads)
            products[t] = dot(v_ref[j], backs), None if kept else dot(kx_ref[j], queries)
        if 0 <= t - 1 < len(tiles):
            i, j = tiles[t - 1]
            back, product = products.pop(t - 1)
            if kept:
                slope = tile_at(held, i, j).astype(f32)
            else:
                start = held[3][:, i * TILE : (i + 1) * TILE]
                slope = weights_and_slope(masked(product, held[2][i - j], start, j, heads))[1]
            ds = back * slope
            grads[t - 1] = ds.astype(bf16)
            add(posg_ref, i - j, sum(ds[:, g * TILE : (g + 1) * TILE] for g in range(heads)), i == nb - 1)
        if t >= 3:
            i, j = tiles[t - 3]
            low = grads.pop(t - 3)
            if j == 0:
                times = jnp.concatenate([kx_ref[i, :, :NTB]] * heads, axis=0)
                q = jnp.concatenate([times, own_lanes(q_ref[i], heads)], axis=1)
            add(acck_ref, j, dot(low, q), i == nb - 1)
            more = dot(kxt_ref[j, NTB:], low)
            dq = more if j == 0 else dq + more
            if i == j:
                gp = jnp.concatenate([own_rows(dq, heads), flip(acck_ref[i, :, NTB:])], axis=0)
                gp = (gp * factor * d_ref[i, width:]).astype(bf16)
                gp_ref[i] = flip(gp).astype(bf16)
                more = dot(gp, xn_ref[i])
                acc_ref[...] = more if i == nb - 1 else acc_ref[...] + more
                part = acck_ref[i, :, :NTB]
                high = part.astype(bf16)
                rest = (part - high.astype(f32)).astype(bf16)
                onehot = kxt_ref[i, :NTB]
                part = dot(onehot, high) + dot(onehot, rest)
                m2 = part if i == nb - 1 else m2 + part
                g = diagonals(posg_ref[i])
                small_ref[:, D + i * TILE : D + (i + 1) * TILE] += g[:, :TILE]
                if i > 0:
                    small_ref[:, D + (i - 1) * TILE : D + i * TILE] += g[:, TILE:]
    g = diagonals(m2 + jnp.transpose(m2))[:, :NTB]
    zero = lax.broadcasted_iota(jnp.int32, (1, NTB), 1) == 0
    at = D + nb * TILE
    small_ref[:, at : at + NTB] = jnp.where(zero, 0.5 * g, g)
    step = D // n_dp
    grads = flip(acc_ref[...])
    for p in range(n_dp):
        here = jnp.concatenate(
            [small_ref[:, (p * extra + r) * 128 : (p * extra + r + 1) * 128] for r in range(extra)], axis=0
        )
        high = here.astype(bf16).astype(f32)
        block = jnp.concatenate([high, here - high, jnp.zeros((16 - 2 * extra, 128), f32)], axis=0)
        wg_ref[p * (step + 16) : p * (step + 16) + step] = grads[p * step : (p + 1) * step]
        if 2 * width > 128:
            block = jnp.concatenate([block, jnp.zeros((16, 2 * width - 128), f32)], axis=1)
        wg_ref[p * (step + 16) + step : (p + 1) * (step + 16)] = block
    send_parts(wg_ref, parts)


def input_kernel(n_head, gp_ref, gun_ref, gpv_ref, wt_ref, keep, send):
    width = gun_ref.shape[2]
    per = keep.shape[1] // TILE
    for k in range(n_head):
        device = lax.axis_index("head") ^ k
        target = (keep, send)[k % 2]
        for r in range(per):
            i = device * per + r
            rows = dot(jnp.concatenate([gun_ref[i], gpv_ref[i]], axis=1), wt_ref[: 2 * width])
            rows = rows + dot(gp_ref[i], wt_ref[2 * width : 4 * width])
            target[device // 2, r * TILE : (r + 1) * TILE] = rows.astype(bf16)


def fold_kernel(*refs):
    low = sum(len(ref.shape) == 3 for ref in refs)
    row = lax.axis_index("dp") // low
    for k, out in enumerate(refs[low:]):
        total = refs[0][row ^ k].astype(f32)
        for ref in refs[1:low]:
            total = total + ref[row ^ k].astype(f32)
        out[...] = total.astype(out.dtype)


def sum_kernel(*refs):
    total = refs[0][...]
    for ref in refs[1:-1]:
        total = total + ref[...].astype(f32)
    refs[-1][...] = total


def mix_kernel(tokens_ref, bias_ref, *refs):
    total = tokens_ref[...].astype(f32) + row_lanes(bias_ref, 0, D // 128)
    for ref in refs[:-1]:
        total = total + ref[...].astype(f32)
    refs[-1][...] = total.astype(bf16)


def finish_kernel(part, *refs):
    tokens_ref, cot_ref, mine_ref, *refs = refs[part:]
    x = tokens_ref[...].astype(f32)
    x = x - jnp.sum(x, axis=1, keepdims=True) / D
    scale = lax.rsqrt(jnp.sum(x * x, axis=1, keepdims=True) / D + norm_epsilon)
    x = x * scale
    grad = mine_ref[...]
    for ref in refs[:-1]:
        grad = grad + ref[...].astype(f32)
    mean = jnp.sum(grad, axis=1, keepdims=True) / D
    along = jnp.sum(grad * x, axis=1, keepdims=True) / D
    refs[-1][...] = cot_ref[...].astype(f32) + scale * (grad - mean - x * along)


def rows_kernel(chips, keep_ref, crossed_ref, mine_ref, *leaving):
    chip = lax.axis_index("head") // 2
    for k in range(chips):
        total = keep_ref[chip ^ k].astype(f32) + crossed_ref[chip ^ k].astype(f32)
        if k == 0:
            mine_ref[...] = total
        else:
            rows = leaving[0].shape[0]
            cuts = total.shape[0] // rows
            for c in range(cuts):
                leaving[(k - 1) * cuts + c][...] = total[c * rows : (c + 1) * rows].astype(bf16)


def collect_kernel(high, extra, *refs):
    late_blocks, (early_ref, grads_ref, message_ref) = refs[:high], refs[high:]
    rows = grads_ref.shape[0]
    total, early = late_blocks[0][...], early_ref[...]
    for k in range(1, high):
        total = total + late_blocks[k][...].astype(f32)
    grads = jnp.concatenate([total[:rows], early], axis=1)
    grads_ref[...] = grads
    squares = jnp.sum(jnp.sum(grads * grads, axis=0, keepdims=True), axis=1, keepdims=True)
    message = jnp.concatenate(
        [
            total[rows : rows + extra, :128] + total[rows + extra : rows + 2 * extra, :128],
            jnp.broadcast_to(squares, (message_ref.shape[1] - extra, 128)),
        ],
        axis=0,
    )
    for k in range(message_ref.shape[0]):
        message_ref[k] = message


def update_kernel(n_head, extra, group, heard_ref, grads_ref, *refs):
    state, outs = refs[:9], refs[9:]
    grad_proj_ref, grad_out_ref, grad_small_ref, norm_ref = outs[:4]
    n_all = heard_ref.shape[0]
    width = grad_out_ref.shape[1]
    lead, pos_rows, used = D // 128, POS // 128, (D + group) // 128
    grad_small_ref[...] = jnp.zeros_like(grad_small_ref)
    last = heard_ref.shape[1] - 1
    squares = heard_ref[0, last:, :]
    for k in range(1, n_all):
        squares = squares + heard_ref[k, last:, :]
    for p in range(n_all // n_head):
        rows = heard_ref[p * n_head, :extra, :]
        for h in range(1, n_head):
            rows = rows + heard_ref[p * n_head + h, :extra, :]
        for r in range(extra):
            at = p * extra + r
            if at < used:
                grad_small_ref[at : at + 1, :] = rows[r : r + 1]
            elif at == used:
                grad_small_ref[lead + pos_rows : lead + pos_rows + 1, :] = rows[r : r + 1]
    small = grad_small_ref[...]
    total = jnp.sum(jnp.sum(small * small, axis=0, keepdims=True), axis=1, keepdims=True) + squares[:, :1]
    norm = jnp.sqrt(total)
    norm_ref[...] = norm
    factor = jnp.minimum(1.0, clip_norm / (norm + 1e-06))

    def update(get, put, grad, rate, decay):
        for k, value in enumerate(adam_step(get(0), grad, get(1), get(2), factor, rate, decay)):
            put(k, value)

    for c in range(4):
        at = (2, 4, 0, 1)[c] * width
        grad = grads_ref[:, at : at + width]
        grad_proj_ref[:, c, :] = grad

        def put(k, value):
            outs[4 + k][:, c, :] = value

        update(lambda k: state[k][:, c, :], put, grad, rate_matrix, decay_matrix)
    grad = grads_ref[:, 3 * width : 4 * width]
    grad_out_ref[...] = grad

    def put_out(k, value):
        outs[7 + k][...] = value

    update(lambda k: state[3 + k][...], put_out, grad, rate_matrix, decay_matrix)

    def put_small(k, value):
        outs[10 + k][...] = value

    update(lambda k: state[6 + k][...], put_small, small, rate_small, 0.0)


def call(kernel, name, in_specs, outs, scratch, us, room=14, **more):
    return pl.pallas_call(
        kernel,
        out_shape=[jax.ShapeDtypeStruct(shape, dtype) for shape, dtype, _ in outs],
        in_specs=in_specs,
        out_specs=[spec for _, _, spec in outs],
        scratch_shapes=scratch,
        compiler_params=pltpu.CompilerParams(vmem_limit_bytes=min(60, room * max(1, lax.axis_size("head") // 4)) * 2**20),
        cost_estimate=pl.CostEstimate(flops=int(us * 1e9), bytes_accessed=int(us * 3e6), transcendentals=0),
        name=name,
        **more,
    )


def block(shape):
    return pl.BlockSpec((1,) + tuple(shape[1:]), lambda i: (i,) + (0,) * (len(shape) - 1))


def shards(
    tokens,
    cotangent,
    seq_start,
    time_bucket,
    proj_weight,
    out_weight,
    small_params,
    proj_mean,
    proj_square,
    out_mean,
    out_square,
    small_mean,
    small_square,
):
    n_head = lax.axis_size("head")
    n_dp = lax.axis_size("dp")
    here = tokens.shape[0]
    group = here * n_head
    nb = group // TILE
    per = here // TILE
    rows_here, _, width = proj_weight.shape
    heads = width // HEAD_DIM
    high, low = split_dp(n_dp)

    (weights,) = call(
        cast_kernel,
        "cast",
        [pl.BlockSpec(memory_space=pl.ANY)] * 2,
        [((rows_here, 5 * width), bf16, VMEM)],
        [
            pltpu.VMEM(proj_weight.shape, f32),
            pltpu.VMEM((rows_here, width), f32),
            pltpu.SemaphoreType.DMA((2,)),
        ],
        1,
    )(proj_weight, out_weight.T)
    x_chips = gather_chips(after(tokens, weights))
    starts = seq_start.reshape(1, group)
    times = time_bucket.reshape(1, group)
    small_rows = small_params.reshape(-1, 128)
    pos, oh, oht, trow = call(
        prepare_kernel,
        "prepare",
        [VMEM] * 2,
        [
            ((nb, TILE, TILE), f32, VMEM),
            ((nb, TILE, NTB), bf16, VMEM),
            ((nb, NTB, TILE), bf16, VMEM),
            ((nb, NTB, TILE), bf16, VMEM),
        ],
        [],
        2,
    )(after(times, weights), small_rows)

    items = [
        ((nb, 3 * width, TILE), bf16),
        ((nb, TILE, NTB + width), bf16),
        ((nb, NTB + width, TILE), bf16),
        ((nb, width, TILE), bf16),
        ((nb, TILE, width), bf16),
        ((nb, TILE, width), bf16),
        ((nb, width, TILE), bf16),
    ]
    w_pieces, offsets = gather_dp(weights, pos)
    cot_chips = gather_chips(after(cotangent, weights))

    x_pieces = gather_cores(tokens, x_chips)
    near = [0, 1] + list(range(2, n_head, 2))
    far = list(range(3, n_head, 2))
    xn = []
    for which in (near, far):
        xn = call(
            functools.partial(normalize_kernel, which),
            "normalize",
            [VMEM] * (len(xn) + len(which)),
            [((nb, TILE, D), bf16, VMEM)],
            [],
            0.1,
        )(*xn, *[x_pieces[k] for k in which])
    (xn,) = xn
    w_pieces[-1] = after(join(w_pieces[-1:], 6), xn)
    (wt,) = call(
        functools.partial(assemble_kernel, offsets),
        "assemble",
        [VMEM] * len(w_pieces),
        [((5 * width, D), bf16, VMEM)],
        [pltpu.VMEM((D, 5 * width), bf16)],
        0.5,
    )(*w_pieces)
    dsilu, kx, kxt, qs, q, v, vt = call(
        functools.partial(project_kernel, heads),
        "project",
        [VMEM] * 4,
        [item + (VMEM,) for item in items],
        [],
        1,
    )(xn, wt, oh, oht)

    kept = nb * (nb + 1) // 2 * heads <= KEPT_TILES

    def attend(first, last, *before):
        count = (last * (last + 1) - first * (first + 1)) // 2
        return call(
            functools.partial(attend_kernel, heads, first, last, kept),
            "attend",
            [VMEM] * (len(before) + 6),
            [((last, width, TILE), f32, VMEM)] + [((count, TILE, heads * TILE), bf16, VMEM)] * (2 * kept),
            [],
            8 if before else 0.5,
        )(*before, kx, qs, trow, vt, pos, starts)

    split = nb - nb // 4
    attn, *kept_first = attend(0, split)
    cot_chips = after_all(cot_chips, attn)
    attn, *kept_last = attend(split, nb, after(attn, *cot_chips))
    kept_weights, kept_slopes = zip(kept_first, kept_last) if kept else ((), ())
    cot_pieces = gather_cores(cotangent, cot_chips)

    column = ((nb, width, TILE), f32, VMEM)
    p_gate, gg, stat, gb = call(
        functools.partial(gate_kernel, n_head),
        "gate",
        [VMEM] * (n_head + 3),
        [column, column, ((nb, 4, TILE), f32, VMEM), ((1, D), f32, VMEM)],
        [],
        5,
    )(*cot_pieces, attn, xn, wt)

    stats = [stat] + [swap(stat, "head", k) for k in range(1, n_head)]
    chips = n_head // 2
    share = ((here, D), bf16, VMEM)
    branches = call(
        functools.partial(branch_kernel, n_head), "branch", [VMEM] * (n_head + 3), [share] * n_head, [], 1
    )(*stats, attn, p_gate, wt)
    crossed = [swap(branches[2 * k + 1], "head", 1) for k in range(chips)]
    da, dat, gun, wg_sum = call(
        functools.partial(middle_kernel, n_head),
        "middle",
        [VMEM] * (2 * n_head + 4),
        [
            ((nb, TILE, width), bf16, VMEM),
            ((nb, width, TILE), bf16, VMEM),
            ((nb, TILE, width), bf16, VMEM),
            ((2 * width, D), f32, VMEM),
        ],
        [],
        6,
    )(*stats, *cot_pieces, attn, p_gate, gg, xn)
    received = [
        swap(call(pair_kernel, "pair", [VMEM] * 2, [share], [], 0.1)(branches[2 * k], crossed[k])[0], "head", 2 * k)
        for k in range(1, chips)
    ]
    branch = (branches[0], crossed[0])
    held = kept_weights if kept else (kx, qs, trow, pos, starts)
    gpv, *early_parts = call(
        functools.partial(values_kernel, heads, kept),
        "values",
        [VMEM] * (len(held) + 4),
        [((nb, TILE, width), bf16, VMEM)] + [((high, rows_here, 3 * width), bf16, VMEM)] * low,
        [pltpu.VMEM((D, 3 * width), f32)],
        VALUES,
    )(*held, da, dsilu, xn, wg_sum)
    early_received = [swap(early_parts[k], "dp", k) for k in range(1, low)]

    length = D + group + NTB
    extra = -(-length // (128 * n_dp))
    held = kept_slopes if kept else (qs, trow, pos, starts)
    gp, *late_parts = call(
        functools.partial(backward_kernel, heads, n_dp, extra, kept),
        "backward",
        [VMEM] * (len(held) + 8),
        [((nb, TILE, 2 * width), bf16, VMEM)] + [((high, rows_here + 16, 2 * width), bf16, VMEM)] * low,
        [
            pltpu.VMEM((nb, TILE, NTB + width), f32),
            pltpu.VMEM((nb, TILE, TILE), f32),
            pltpu.VMEM((2 * width, D), f32),
            pltpu.VMEM((n_dp * (rows_here + 16), 2 * width), f32),
            pltpu.VMEM((1, extra * n_dp * 128), f32),
        ],
        BACKWARD,
        ROOM,
    )(*held, kx, kxt, q, v, dat, dsilu, xn, gb)

    tied = lax.optimization_barrier((gp, *late_parts, *early_received, *received))
    gp, late_parts = tied[0], tied[1 : 1 + low]
    early_received, received = tied[1 + low : 2 * low], tied[2 * low :]
    late_received = [swap(late_parts[k], "dp", k) for k in range(1, low)]
    keep, send = call(
        functools.partial(input_kernel, n_head),
        "input_rows",
        [VMEM] * 4,
        [((n_head // 2, here, D), bf16, VMEM)] * 2,
        [],
        4,
    )(gp, gun, gpv, wt)
    early_blocks = scatter_high(after(early_parts[0], send), early_received, 1)
    crossed = swap(send, "head", 1)
    late_blocks = scatter_high(late_parts[0], late_received, 12, send, crossed)
    (early,) = call(
        sum_kernel, "sum", [VMEM] * high, [((rows_here, 3 * width), f32, VMEM)], [], 14
    )(*early_blocks)
    mine, *leaving = fold_cores(keep, after(crossed, late_blocks[0]), 2)
    half = here // 2
    arrived = [[swap(leaving[2 * k - 2 + part], "head", 2 * k) for k in range(1, chips)] for part in range(2)]
    n_all = n_dp * n_head
    grads_shape = ((rows_here, 5 * width), f32)
    grads, message = call(
        functools.partial(collect_kernel, high, extra),
        "collect",
        [VMEM] * (high + 1),
        [grads_shape + (VMEM,), ((n_all, 4 if extra < 4 else 8, 128), f32, VMEM)],
        [],
        10,
    )(*late_blocks, early)
    message = after(message, *leaving)
    heard = lax.all_to_all(message, ("dp", "head"), 0, 0, tiled=True)
    (mixed,) = call(
        mix_kernel, "mix", [VMEM] * (3 + chips), [((here, D), bf16, VMEM)], [], 1
    )(tokens, small_rows, after(branch[0], message), branch[1], *received)
    input_grad = None
    for part in range(2):
        rows = pl.BlockSpec((half, D), lambda i, part=part: (part, 0))
        alone = pl.BlockSpec((half, D), lambda i: (0, 0))
        before = [] if part == 0 else [input_grad]
        (input_grad,) = call(
            functools.partial(finish_kernel, part),
            "finish",
            [pl.BlockSpec(memory_space=pl.ANY)] * len(before) + [rows] * 3 + [alone] * (chips - 1),
            [((here, D), f32, rows)],
            [],
            1,
            grid=(1,),
            input_output_aliases={0: 0} if before else {},
        )(*before, tokens, cotangent, mine, *arrived[part])
    heard = after(heard, input_grad)
    state = [proj_weight, proj_mean, proj_square, out_weight.T, out_mean.T, out_square.T]
    state += [x.reshape(-1, 128) for x in (small_params, small_mean, small_square)]
    proj_shape, out_shape, small_shape = proj_weight.shape, (rows_here, width), small_rows.shape
    shapes = [proj_shape, out_shape, small_shape, (1, 1)] + [proj_shape] * 3 + [out_shape] * 3 + [small_shape] * 3
    results = call(
        functools.partial(update_kernel, n_head, extra, group),
        "update",
        [VMEM] * (2 + len(state)),
        [(shape, f32, VMEM) for shape in shapes],
        [],
        0.1,
    )(heard, grads, *state)
    grad_proj, grad_out, grad_small, grad_norm = results[:4]
    grad_out, grad_small, grad_norm = grad_out.T, grad_small.reshape(-1), grad_norm.reshape(())
    new_proj, mean_proj, square_proj = results[4:7]
    new_out, mean_out, square_out = [x.T for x in results[7:10]]
    new_small, mean_small, square_small = [x.reshape(-1) for x in results[10:13]]
    return (
        mixed,
        input_grad,
        grad_proj,
        grad_out,
        grad_small,
        grad_norm,
        new_proj,
        mean_proj,
        square_proj,
        new_out,
        mean_out,
        square_out,
        new_small,
        mean_small,
        square_small,
    )


def solution(mesh):
    in_specs = (
        P(("dp", "head"), None),
        P(("dp", "head"), None),
        P("dp"),
        P("dp"),
        P("dp", None, "head"),
        P("head", "dp"),
        P(),
        P("dp", None, "head"),
        P("dp", None, "head"),
        P("head", "dp"),
        P("head", "dp"),
        P(),
        P(),
    )
    out_specs = (
        P(("dp", "head"), None),
        P(("dp", "head"), None),
        P("dp", None, "head"),
        P("head", "dp"),
        P(),
        P(),
        P("dp", None, "head"),
        P("dp", None, "head"),
        P("dp", None, "head"),
        P("head", "dp"),
        P("head", "dp"),
        P("head", "dp"),
        P(),
        P(),
        P(),
    )
    return jax.shard_map(shards, mesh=mesh, in_specs=in_specs, out_specs=out_specs, check_vma=False)
```
